32 devices in a mesh: lev: 4 (over z), gx: 2 (over x), gy: 4 (over y, core).
Axes of the slice: x: 2, y: 2, z: 4, core: 2. Of those that a mesh axis runs over, the one named last changes fastest.
Arguments:
- increment: float32 [2, 64, 128, 512], P(None, 'lev', 'gx', 'gy'), may hold values from -6 to 6
- norm_gain: float32 [2, 64, 128, 512], P(None, 'lev', 'gx', 'gy'), may hold values from 0.5 to 2
- diffusion_i: float32 [64, 128, 512], P('lev', 'gx', 'gy'), may hold values from 0.1 to 0.24
- diffusion_j: float32 [64, 128, 512], P('lev', 'gx', 'gy'), may hold values from 0.1 to 0.24
- sea_mask: int32 [64, 128, 512], P('lev', 'gx', 'gy'), may hold values from 0 to 1, as said below
- coupling: float32 [128, 128], replicated, may hold values from -0.5 to 0.5
Outputs:
- correlated: float32 [2, 64, 128, 512], P(None, 'lev', 'gx', 'gy')
The draws below stay inside these ranges and needn't reach their ends.
Inputs may be any that keep to these rules, and one draw needn't show every extreme that they name: `sea_mask`: in every column the sea cells are the levels from the top down to some depth, which may be zero.
All inputs are finite; a program needn't handle non-finite values.
Results may differ from the reference program's by a relative error of at most 0.00009.
Values sent between devices are 32-bit elements; how exact they have to be, the bound alone decides.
No kernel may reach another device: no remote copies, remote signals or barrier semaphores. Data moves between devices by JAX's collectives and lax.ppermute only.
A program may use at most 64 MiB of HBM per device.

```python
import math
import jax
import jax.numpy as jnp
from jax import lax

ITERS = 2
NLEV = 64
NI = 128
NJ = 512


def draw_sea_mask(key, part):
    bottom = jax.random.randint(key, (NI, NJ), 0, NLEV + 1)
    level = lax.broadcasted_iota(jnp.int32, (NLEV, NI, NJ), 0)
    return (level < bottom[None]).astype(jnp.int32)


def levels(stream_key, dims, pieces, least, high):
    def one(position, parts):
        draws = jax.random.uniform(jax.random.fold_in(jax.random.fold_in(stream_key, 6), position), (parts,), jnp.float32, least / len(pieces), high / len(pieces))
        return jnp.repeat(jnp.exp(draws), dims[position] // parts).reshape((-1,) + (1,) * (len(dims) - position - 1))

    loudness = one(*pieces[0])
    for cut in pieces[1:]:
        loudness = loudness * one(*cut)
    return loudness


def bell_draw(stream_key, dims, width, most, cuts=(), kind=jnp.bfloat16):
    level = levels(stream_key, dims, cuts, -0.22, 0.18) if cuts else 1.0
    result = jax.random.normal(stream_key, dims, jnp.float32) * width * level
    return jnp.minimum(jnp.maximum(result, -most), most).astype(kind)


def setup_inputs(seed: int = 0) -> dict:
    splits = jax.random.split(jax.random.key(seed), 7)
    increment = bell_draw(splits[0], (2, NLEV, NI, NJ), 1.0, 6.0, ((1, 4), (2, 2), (3, 4)), jnp.float32)
    norm_gain = jnp.clip(jnp.exp(math.log(2.0) - 1.3862944 * jax.random.uniform(splits[1], (2, NLEV, NI, NJ), jnp.float32) ** levels(splits[1], (2, NLEV, NI, NJ), ((1, 4), (2, 2), (3, 4)), -0.2, 0.2)), 0.5, 2.0)
    diffusion_i = jnp.clip(jnp.exp(math.log(0.24) - 0.8754687 * jax.random.uniform(splits[2], (NLEV, NI, NJ), jnp.float32) ** levels(splits[2], (NLEV, NI, NJ), ((0, 4), (1, 2), (2, 4)), -0.2, 0.2)), 0.1, 0.24)
    diffusion_j = jnp.clip(jnp.exp(math.log(0.24) - 0.8754687 * jax.random.uniform(splits[3], (NLEV, NI, NJ), jnp.float32) ** levels(splits[3], (NLEV, NI, NJ), ((0, 4), (1, 2), (2, 4)), -0.2, 0.2)), 0.1, 0.24)
    sea_mask = draw_sea_mask(jax.random.fold_in(splits[6], 71), 0)
    coupling = bell_draw(splits[5], (2 * NLEV, 2 * NLEV), (2 * NLEV) ** -0.5, 0.5, (), jnp.float32)
    return {"increment": increment, "norm_gain": norm_gain, "diffusion_i": diffusion_i, "diffusion_j": diffusion_j, "sea_mask": sea_mask, "coupling": coupling}


def extend(array, margin):
    array = jnp.concatenate([array[..., -margin:, :], array, array[..., :margin, :]], axis=-2)
    padding = [(0, 0)] * (array.ndim - 1) + [(margin, margin)]
    return jnp.pad(array, padding)


def diffuse(values, coefficients):
    along_i = coefficients[0]
    along_j = coefficients[1]
    ocean = coefficients[2]
    weight_i = along_i[:, :-1, :] * ocean[:, :-1, :] * ocean[:, 1:, :]
    flux_i = weight_i[None] * (values[:, :, 1:, :] - values[:, :, :-1, :])
    weight_j = along_j[:, :, :-1] * ocean[:, :, :-1] * ocean[:, :, 1:]
    flux_j = weight_j[None] * (values[:, :, :, 1:] - values[:, :, :, :-1])
    return (values[:, :, 1:-1, 1:-1] + flux_i[:, :, 1:, 1:-1] - flux_i[:, :, :-1, 1:-1]
            + flux_j[:, :, 1:-1, 1:] - flux_j[:, :, 1:-1, :-1])


def reference(increment, norm_gain, diffusion_i, diffusion_j, sea_mask, coupling):
    ocean = sea_mask.astype(jnp.float32)
    scaled = ocean[None] * norm_gain * increment
    order_count = coupling.shape[0]
    balance = jnp.eye(order_count, dtype=jnp.float32) + coupling
    forward = balance.reshape(2, NLEV, 2, NLEV)
    adjoint_mixed = jnp.einsum('cdab,cdij->abij', forward, scaled, precision=lax.Precision.HIGHEST) * ocean[None]
    coefficients = extend(jnp.stack([diffusion_i, diffusion_j, ocean]), 1)
    spread = adjoint_mixed
    for repeat in range(2 * ITERS):
        spread = diffuse(extend(spread, 1), coefficients)
    forward_mixed = jnp.einsum('abcd,cdij->abij', forward, spread, precision=lax.Precision.HIGHEST)
    return ocean[None] * norm_gain * forward_mixed
```

```python
import functools

import jax
import jax.numpy as jnp
from jax import lax
from jax.experimental import pallas as pl
from jax.experimental.pallas import tpu as pltpu
from jax.sharding import PartitionSpec as P

ITERS = 2
STEPS = 2 * ITERS
PAD = 8
VMEM_LIMIT = 40 * 1024 * 1024
HIGHEST = lax.Precision.HIGHEST


def params(**more):
    return pltpu.CompilerParams(vmem_limit_bytes=VMEM_LIMIT, **more)


def smem():
    return pl.BlockSpec(memory_space=pltpu.SMEM)


def vmem():
    return pl.BlockSpec(memory_space=pltpu.VMEM)


def scaled_kernel(slab, increment, gain, mask, out):
    fields, levels, rows, _ = increment.shape
    depth = jnp.zeros((rows, increment.shape[3]), jnp.float32)
    for level in range(levels):
        ocean = mask[level].astype(jnp.float32)
        depth = depth + ocean
        for field in range(fields):
            at = (field * levels + level) * rows
            out[pl.ds(at, rows), :] = ocean * gain[field, level] * increment[field, level]
    out[pl.ds(fields * levels * rows, rows), :] = depth


def scaled_message(slab, increment, gain, mask, rows):
    fields, levels, _, cols = increment.shape
    block = pl.BlockSpec((fields, levels, rows, cols), lambda step, slab: (0, 0, slab[0], 0))
    mask_block = pl.BlockSpec((levels, rows, cols), lambda step, slab: (0, slab[0], 0))
    shape = ((fields * levels + 1) * rows, cols)
    return pl.pallas_call(
        scaled_kernel,
        grid_spec=pltpu.PrefetchScalarGridSpec(
            num_scalar_prefetch=1,
            grid=(1,),
            in_specs=[block, block, mask_block],
            out_specs=pl.BlockSpec(shape, lambda step, slab: (0, 0)),
        ),
        out_shape=jax.ShapeDtypeStruct(shape, jnp.float32),
        compiler_params=params(),
        name="scaled_message",
    )(slab.reshape(1), increment, gain, mask)


def weight_kernel(slabs, along_i, along_j, mask, row_depth, col_depth, *refs):
    outs, (wi, wj) = refs[:-2], refs[-2:]
    levels, length, cols = along_i.shape
    lane = lax.broadcasted_iota(jnp.int32, (length, cols), 1)
    row = lax.broadcasted_iota(jnp.int32, (length, cols), 0)

    def one(level, carry):
        ocean = mask[level]
        next_row = jnp.broadcast_to((level < row_depth[...]).astype(jnp.int32), (length, cols))
        next_col = jnp.broadcast_to((level < col_depth[...]).astype(jnp.int32), (length, cols))
        below = jnp.where(row == length - 1, next_row, pltpu.roll(ocean, length - 1, 0))
        right = jnp.where(lane == cols - 1, next_col, pltpu.roll(ocean, cols - 1, 1))
        wi[level] = along_i[level] * (ocean * below).astype(jnp.float32)
        wj[level] = along_j[level] * (ocean * right).astype(jnp.float32)
        return carry

    lax.fori_loop(0, levels, one, 0)
    rows = outs[0].shape[0] // (2 * levels)
    for d, out in enumerate(outs):
        at = pl.multiple_of(slabs[d] * rows, rows)
        for level in range(levels):
            out[pl.ds(level * rows, rows), :] = wi[level, pl.ds(at, rows), :]
            out[pl.ds((levels + level) * rows, rows), :] = wj[level, pl.ds(at, rows), :]


def weight_messages(slabs, along_i, along_j, mask, row_depth, col_depth, rows):
    levels, _, cols = along_i.shape
    shape = jax.ShapeDtypeStruct((2 * levels * rows, cols), jnp.float32)
    return pl.pallas_call(
        weight_kernel,
        in_specs=[smem()] + [vmem()] * 5,
        out_specs=[vmem()] * slabs.shape[0],
        out_shape=[shape] * slabs.shape[0],
        scratch_shapes=[pltpu.VMEM(along_i.shape, jnp.float32)] * 2,
        compiler_params=params(),
        name="weight_messages",
    )(slabs, along_i, along_j, mask, row_depth, col_depth)


def adjoint_kernel(matrix, *refs):
    parts, out = refs[:-1], refs[-1]
    rows, cols, order = out.shape
    count = order // len(parts)
    level = lax.rem(lax.broadcasted_iota(jnp.int32, (order, cols), 0), order // 2).astype(jnp.float32)

    def one(i, carry):
        x = jnp.concatenate([part[pl.ds(i, count, rows), :] for part in parts], axis=0)
        depth = parts[0][pl.ds(count * rows + i, 1), :]
        for part in parts[1:]:
            depth = depth + part[pl.ds(count * rows + i, 1), :]
        y = jnp.dot(matrix[...], x, precision=HIGHEST, preferred_element_type=jnp.float32)
        out[i] = jnp.where(level < depth, y, 0.0).T
        return carry

    lax.fori_loop(0, rows, one, 0, unroll=4)


def adjoint_mix(matrix, parts, rows):
    order = matrix.shape[0]
    cols = parts[0].shape[1]
    return pl.pallas_call(
        adjoint_kernel,
        in_specs=[vmem()] * (1 + len(parts)),
        out_specs=vmem(),
        out_shape=jax.ShapeDtypeStruct((rows, cols, order), jnp.float32),
        compiler_params=params(),
        name="adjoint_mix",
    )(matrix, *parts)


def turn_kernel(sources, *refs):
    parts, out, held = refs[:-2], refs[-2], refs[-1]
    rows, cols, order = out.shape
    count = order // (2 * len(parts))

    def one(i, carry):
        for d, part in enumerate(parts):
            for side in range(2):
                at = pl.multiple_of(side * (order // 2) + sources[d] * count, 8)
                held[pl.ds(at, count), :] = part[pl.ds(side * count * rows + i, count, rows), :]
        out[i] = held[...].T
        return carry

    lax.fori_loop(0, rows, one, 0)


def turn_weights(sources, parts, rows):
    cols = parts[0].shape[1]
    order = parts[0].shape[0] // rows * len(parts)
    return pl.pallas_call(
        turn_kernel,
        in_specs=[smem()] + [vmem()] * len(parts),
        out_specs=vmem(),
        out_shape=jax.ShapeDtypeStruct((rows, cols, order), jnp.float32),
        scratch_shapes=[pltpu.VMEM((order, cols), jnp.float32)],
        compiler_params=params(),
        name="turn_weights",
    )(sources, *parts)


def spread_kernel(matrix, *refs):
    field, weight = refs[0:5], refs[5:10]
    outs, (a, b, wi, wj) = refs[10:-4], refs[-4:]
    rows, cols, order = field[0].shape
    half = order // 2
    ext = rows + 2 * STEPS
    wide = cols + 2 * PAD
    lane = lax.broadcasted_iota(jnp.int32, (wide, order), 1)

    def row_of(five, r):
        main, above, below, left, right = five
        if r < STEPS:
            mid = above[r]
        elif r < STEPS + rows:
            mid = main[r - STEPS]
        else:
            mid = below[r - STEPS - rows]
        return jnp.concatenate([left[r], mid, right[r]], axis=0)

    for r in range(ext):
        a[r] = row_of(field, r)
        w = row_of(weight, r)
        other = pltpu.roll(w, half, 1)
        wi[r] = jnp.where(lane < half, w, other)
        wj[r] = jnp.where(lane < half, other, w)

    src, dst = a, b
    for step in range(STEPS):
        first, last = step + 1, ext - 2 - step

        def one(r, carry, src=src, dst=dst):
            v, before = carry
            after = src[r + 1]
            flux = wi[r] * (after - v)
            across = wj[r] * (pltpu.roll(v, wide - 1, 0) - v)
            dst[r] = v + (flux - before) + (across - pltpu.roll(across, 1, 0))
            return after, flux

        v = src[first]
        lax.fori_loop(first, last + 1, one, (v, wi[first - 1] * (v - src[first - 1])))
        src, dst = dst, src

    count = order // len(outs)

    def mix(i, carry):
        x = src[STEPS + i, pl.ds(PAD, cols), :]
        y = lax.dot_general(
            matrix[...], x, (((1,), (1,)), ((), ())), precision=HIGHEST, preferred_element_type=jnp.float32
        )
        for d, out in enumerate(outs):
            out[pl.ds(i, count, rows), :] = y[d * count:(d + 1) * count]
        return carry

    lax.fori_loop(0, rows, mix, 0, unroll=4)


def spread_mix(matrix, field, weight, devices):
    rows, cols, order = field[0].shape
    shape = jax.ShapeDtypeStruct((order // devices * rows, cols), jnp.float32)
    ext = pltpu.VMEM((rows + 2 * STEPS, cols + 2 * PAD, order), jnp.float32)
    return pl.pallas_call(
        spread_kernel,
        in_specs=[vmem()] * 11,
        out_specs=[vmem()] * devices,
        out_shape=[shape] * devices,
        scratch_shapes=[ext] * 4,
        compiler_params=params(),
        name="spread_mix",
    )(matrix, *field, *weight)


def result_kernel(slabs, gain, mask, *refs):
    parts, out = refs[:-1], refs[-1]
    fields, levels, _, cols = gain.shape
    rows = parts[0].shape[0] // (fields * levels)
    for d, part in enumerate(parts):
        at = pl.multiple_of(slabs[d] * rows, rows)
        for level in range(levels):
            ocean = mask[level, pl.ds(at, rows), :].astype(jnp.float32)
            for field in range(fields):
                value = part[pl.ds((field * levels + level) * rows, rows), :]
                out[field, level, pl.ds(at, rows), :] = ocean * gain[field, level, pl.ds(at, rows), :] * value


def result(slabs, gain, mask, parts):
    return pl.pallas_call(
        result_kernel,
        in_specs=[smem()] + [vmem()] * (2 + len(parts)),
        out_specs=vmem(),
        out_shape=jax.ShapeDtypeStruct(gain.shape, jnp.float32),
        compiler_params=params(),
        name="result",
    )(slabs, gain, mask, *parts)


def shards(increment, norm_gain, diffusion_i, diffusion_j, sea_mask, coupling):
    devices = lax.axis_size("lev")
    gx_size = lax.axis_size("gx")
    gy_size = lax.axis_size("gy")
    me = lax.axis_index("lev")
    gx = lax.axis_index("gx")
    _, levels, length, cols = increment.shape
    rows = length // devices
    order = coupling.shape[0]

    snake = gx_size % 2 == 0

    def place(x, lev):
        return devices - 1 - lev if snake and x % 2 else lev

    def slab_of(lev):
        return jnp.where(gx % 2 == 1, devices - 1 - lev, lev) if snake else lev

    to = [lax.rem(me + d, devices) for d in range(devices)]
    source = [lax.rem(me + devices - d, devices) for d in range(devices)]
    to_slabs = jnp.stack([slab_of(t) for t in to]).astype(jnp.int32)
    source_slabs = jnp.stack([slab_of(s) for s in source]).astype(jnp.int32)
    sources = jnp.stack(source).astype(jnp.int32)

    def exchange(parts):
        moved = [parts[0]]
        for d in range(1, devices):
            moved.append(lax.ppermute(parts[d], "lev", [(k, (k + d) % devices) for k in range(devices)]))
        return moved

    chain = [place(x, s) * gx_size + x for x in range(gx_size) for s in range(devices)]
    ahead = [(chain[p], chain[(p + 1) % len(chain)]) for p in range(len(chain))]
    back = [(b, a) for a, b in ahead]
    right = [(k, k + 1) for k in range(gy_size - 1)]
    left = [(b, a) for a, b in right]

    def halo(x):
        above = lax.ppermute(x[-STEPS:], ("lev", "gx"), ahead)
        below = lax.ppermute(x[:STEPS], ("lev", "gx"), back)
        first = jnp.concatenate([above[:, :PAD], x[:, :PAD], below[:, :PAD]], axis=0)
        last = jnp.concatenate([above[:, -PAD:], x[:, -PAD:], below[:, -PAD:]], axis=0)
        from_left = lax.ppermute(last, "gy", right)
        from_right = lax.ppermute(first, "gy", left)
        return x, above, below, from_left, from_right

    scaled = [scaled_message(to_slabs[d], increment, norm_gain, sea_mask, rows) for d in range(devices)]
    scaled = exchange(scaled)

    depth = jnp.sum(sea_mask, axis=0)
    row_depth = lax.ppermute(depth[:1], "gx", [((k + 1) % gx_size, k) for k in range(gx_size)])
    col_depth = lax.ppermute(depth[:, :1], "gy", left)
    weights = weight_messages(to_slabs, diffusion_i, diffusion_j, sea_mask, row_depth, col_depth, rows)
    weights = exchange(weights)

    balance = jnp.eye(order, dtype=jnp.float32) + coupling
    by_device = balance.reshape(2, devices, levels, order)
    adjoint = jnp.concatenate(
        [by_device[:, s].reshape(2 * levels, order) for s in source], axis=0
    ).T
    forward = jnp.concatenate([by_device[:, t].reshape(2 * levels, order) for t in to], axis=0)

    field = halo(adjoint_mix(adjoint, scaled, rows))
    weight = halo(turn_weights(sources, weights, rows))
    mixed = exchange(spread_mix(forward, field, weight, devices))
    return result(source_slabs, norm_gain, sea_mask, mixed)


def solution(mesh):
    return jax.shard_map(
        shards,
        mesh=mesh,
        in_specs=(
            P(None, "lev", "gx", "gy"),
            P(None, "lev", "gx", "gy"),
            P("lev", "gx", "gy"),
            P("lev", "gx", "gy"),
            P("lev", "gx", "gy"),
            P(),
        ),
        out_specs=P(None, "lev", "gx", "gy"),
        check_vma=False,
    )
```

```python
import functools

import jax
import jax.numpy as jnp
from jax import lax
from jax.experimental import pallas as pl
from jax.experimental.pallas import tpu as pltpu
from jax.sharding import PartitionSpec as P

ITERS = 2
STEPS = 2 * ITERS
PAD = 8
VMEM_LIMIT = 40 * 1024 * 1024
VMEM_WHOLE = 60 * 1024 * 1024
HIGHEST = lax.Precision.HIGHEST


def params(limit=VMEM_LIMIT):
    return pltpu.CompilerParams(vmem_limit_bytes=limit)


def smem():
    return pl.BlockSpec(memory_space=pltpu.SMEM)


def vmem():
    return pl.BlockSpec(memory_space=pltpu.VMEM)


def scaled_kernel(slab, increment, gain, mask, out):
    fields, levels, rows, _ = increment.shape
    depth = jnp.zeros((rows, increment.shape[3]), jnp.float32)
    for level in range(levels):
        ocean = mask[level].astype(jnp.float32)
        depth = depth + ocean
        for field in range(fields):
            at = (field * levels + level) * rows
            out[pl.ds(at, rows), :] = ocean * gain[field, level] * increment[field, level]
    out[pl.ds(fields * levels * rows, rows), :] = depth


def scaled_message(slab, increment, gain, mask, rows):
    fields, levels, _, cols = increment.shape
    block = pl.BlockSpec((fields, levels, rows, cols), lambda step, slab: (0, 0, slab[0], 0))
    mask_block = pl.BlockSpec((levels, rows, cols), lambda step, slab: (0, slab[0], 0))
    shape = ((fields * levels + 1) * rows, cols)
    return pl.pallas_call(
        scaled_kernel,
        grid_spec=pltpu.PrefetchScalarGridSpec(
            num_scalar_prefetch=1,
            grid=(1,),
            in_specs=[block, block, mask_block],
            out_specs=pl.BlockSpec(shape, lambda step, slab: (0, 0)),
        ),
        out_shape=jax.ShapeDtypeStruct(shape, jnp.float32),
        compiler_params=params(VMEM_WHOLE),
        name="scaled_message",
    )(slab.reshape(1), increment, gain, mask)


def weight_kernel(slab, along_i, along_j, out):
    levels, rows, _ = along_i.shape
    for level in range(levels):
        out[pl.ds(level * rows, rows), :] = along_i[level]
        out[pl.ds((levels + level) * rows, rows), :] = along_j[level]


def weight_message(slab, along_i, along_j, rows):
    levels, _, cols = along_i.shape
    block = pl.BlockSpec((levels, rows, cols), lambda step, slab: (0, slab[0], 0))
    shape = (2 * levels * rows, cols)
    return pl.pallas_call(
        weight_kernel,
        grid_spec=pltpu.PrefetchScalarGridSpec(
            num_scalar_prefetch=1,
            grid=(1,),
            in_specs=[block, block],
            out_specs=pl.BlockSpec(shape, lambda step, slab: (0, 0)),
        ),
        out_shape=jax.ShapeDtypeStruct(shape, jnp.float32),
        compiler_params=params(VMEM_WHOLE),
        name="weight_message",
    )(slab.reshape(1), along_i, along_j)


def adjoint_kernel(matrix, *refs):
    parts, out, depths = refs[:-2], refs[-2], refs[-1]
    rows, cols, order = out.shape
    count = order // len(parts)
    depths[...] = sum(part[pl.ds(count * rows, rows), :] for part in parts)
    level = lax.rem(lax.broadcasted_iota(jnp.int32, (order, cols), 0), order // 2).astype(jnp.float32)

    def one(i, carry):
        x = jnp.concatenate([part[pl.ds(i, count, rows), :] for part in parts], axis=0)
        depth = depths[pl.ds(i, 1), :]
        y = jnp.dot(matrix[...], x, precision=HIGHEST, preferred_element_type=jnp.float32)
        out[i] = jnp.where(level < depth, y, 0.0).T
        return carry

    lax.fori_loop(0, rows, one, 0, unroll=4)


def adjoint_mix(matrix, parts, rows):
    order = matrix.shape[0]
    cols = parts[0].shape[1]
    return pl.pallas_call(
        adjoint_kernel,
        in_specs=[vmem()] * (1 + len(parts)),
        out_specs=[vmem()] * 2,
        out_shape=[
            jax.ShapeDtypeStruct((rows, cols, order), jnp.float32),
            jax.ShapeDtypeStruct((rows, cols), jnp.float32),
        ],
        compiler_params=params(),
        name="adjoint_mix",
    )(matrix, *parts)


def turn_kernel(sources, depth, depth_below, depth_right, *refs):
    parts, out, held = refs[:-2], refs[-2], refs[-1]
    rows, cols, order = out.shape
    half = order // 2
    count = half // len(parts)
    level = lax.broadcasted_iota(jnp.int32, (half, cols), 0).astype(jnp.float32)
    lane = lax.broadcasted_iota(jnp.int32, (1, cols), 1)
    for i in range(rows):
        for d, part in enumerate(parts):
            for side in range(2):
                at = pl.multiple_of(side * half + sources[d] * count, 8)
                held[i, pl.ds(at, count), :] = part[pl.ds(side * count * rows + i, count, rows), :]
    for i in range(rows):
        here = depth[pl.ds(i, 1), :]
        below = depth[pl.ds(i + 1, 1), :] if i + 1 < rows else depth_below[pl.ds(0, 1), :]
        right = jnp.where(
            lane == cols - 1, pltpu.roll(depth_right[pl.ds(i, 1), :], cols - 1, 1), pltpu.roll(here, cols - 1, 1)
        )
        along_i = jnp.where(level < jnp.minimum(here, below), held[i, pl.ds(0, half), :], 0.0)
        along_j = jnp.where(level < jnp.minimum(here, right), held[i, pl.ds(half, half), :], 0.0)
        out[i] = jnp.concatenate([along_i, along_j], axis=0).T


def turn_weights(sources, depth, depth_below, depth_right, parts, rows):
    cols = parts[0].shape[1]
    order = parts[0].shape[0] // rows * len(parts)
    return pl.pallas_call(
        turn_kernel,
        in_specs=[smem()] + [vmem()] * (3 + len(parts)),
        out_specs=vmem(),
        out_shape=jax.ShapeDtypeStruct((rows, cols, order), jnp.float32),
        scratch_shapes=[pltpu.VMEM((rows, order, cols), jnp.float32)],
        compiler_params=params(),
        name="turn_weights",
    )(sources, depth, depth_below, depth_right, *parts)


def spread_kernel(matrix, *refs):
    field, weight = refs[0:5], refs[5:10]
    outs, (a, b, wi, wj) = refs[10:-4], refs[-4:]
    rows, cols, order = field[0].shape
    half = order // 2
    ext = rows + 2 * STEPS
    wide = cols + 2 * PAD
    lane = lax.broadcasted_iota(jnp.int32, (wide, order), 1)

    def row_of(five, r):
        main, above, below, left, right = five
        if r < STEPS:
            mid = above[r]
        elif r < STEPS + rows:
            mid = main[r - STEPS]
        else:
            mid = below[r - STEPS - rows]
        return jnp.concatenate([left[r], mid, right[r]], axis=0)

    for r in range(ext):
        a[r] = row_of(field, r)
        w = row_of(weight, r)
        other = pltpu.roll(w, half, 1)
        wi[r] = jnp.where(lane < half, w, other)
        wj[r] = jnp.where(lane < half, other, w)

    src, dst = a, b
    for step in range(STEPS):
        first, last = step + 1, ext - 2 - step

        def one(r, carry, src=src, dst=dst):
            v, before = carry
            after = src[r + 1]
            flux = wi[r] * (after - v)
            across = wj[r] * (pltpu.roll(v, wide - 1, 0) - v)
            dst[r] = v + (flux - before) + (across - pltpu.roll(across, 1, 0))
            return after, flux

        v = src[first]
        lax.fori_loop(first, last + 1, one, (v, wi[first - 1] * (v - src[first - 1])))
        src, dst = dst, src

    count = order // len(outs)

    def mix(i, carry):
        x = src[STEPS + i, pl.ds(PAD, cols), :]
        y = lax.dot_general(
            matrix[...], x, (((1,), (1,)), ((), ())), precision=HIGHEST, preferred_element_type=jnp.float32
        )
        for d, out in enumerate(outs):
            out[pl.ds(i, count, rows), :] = y[d * count:(d + 1) * count]
        return carry

    lax.fori_loop(0, rows, mix, 0, unroll=4)


def spread_mix(matrix, field, weight, devices):
    rows, cols, order = field[0].shape
    shape = jax.ShapeDtypeStruct((order // devices * rows, cols), jnp.float32)
    ext = pltpu.VMEM((rows + 2 * STEPS, cols + 2 * PAD, order), jnp.float32)
    return pl.pallas_call(
        spread_kernel,
        in_specs=[vmem()] * 11,
        out_specs=[vmem()] * devices,
        out_shape=[shape] * devices,
        scratch_shapes=[ext] * 4,
        compiler_params=params(),
        name="spread_mix",
    )(matrix, *field, *weight)


def result_kernel(slabs, gain, mask, *refs):
    parts, out = refs[:-1], refs[-1]
    fields, levels, _, cols = gain.shape
    rows = parts[0].shape[0] // (fields * levels)
    for d, part in enumerate(parts):
        at = pl.multiple_of(slabs[d] * rows, rows)
        for level in range(levels):
            ocean = mask[level, pl.ds(at, rows), :].astype(jnp.float32)
            for field in range(fields):
                value = part[pl.ds((field * levels + level) * rows, rows), :]
                out[field, level, pl.ds(at, rows), :] = ocean * gain[field, level, pl.ds(at, rows), :] * value


def result(slabs, gain, mask, parts):
    return pl.pallas_call(
        result_kernel,
        in_specs=[smem()] + [vmem()] * (2 + len(parts)),
        out_specs=vmem(),
        out_shape=jax.ShapeDtypeStruct(gain.shape, jnp.float32),
        compiler_params=params(),
        name="result",
    )(slabs, gain, mask, *parts)


def shards(increment, norm_gain, diffusion_i, diffusion_j, sea_mask, coupling):
    devices = lax.axis_size("lev")
    gx_size = lax.axis_size("gx")
    gy_size = lax.axis_size("gy")
    me = lax.axis_index("lev")
    gx = lax.axis_index("gx")
    _, levels, length, cols = increment.shape
    rows = length // devices
    order = coupling.shape[0]

    snake = gx_size % 2 == 0

    def place(x, lev):
        return devices - 1 - lev if snake and x % 2 else lev

    def slab_of(lev):
        return jnp.where(gx % 2 == 1, devices - 1 - lev, lev) if snake else lev

    to = [lax.rem(me + d, devices) for d in range(devices)]
    source = [lax.rem(me + devices - d, devices) for d in range(devices)]
    to_slabs = jnp.stack([slab_of(t) for t in to]).astype(jnp.int32)
    source_slabs = jnp.stack([slab_of(s) for s in source]).astype(jnp.int32)
    sources = jnp.stack(source).astype(jnp.int32)

    def shift(x, d):
        return lax.ppermute(x, "lev", [(k, (k + d) % devices) for k in range(devices)])

    def exchange(parts):
        return [parts[0]] + [shift(parts[d], d) for d in range(1, devices)]

    chain = [place(x, s) * gx_size + x for x in range(gx_size) for s in range(devices)]
    ahead = [(chain[p], chain[(p + 1) % len(chain)]) for p in range(len(chain))]
    back = [(b, a) for a, b in ahead]
    right = [(k, k + 1) for k in range(gy_size - 1)]
    left = [(b, a) for a, b in right]

    def halo(x, depth=None):
        order = x.shape[2]
        tiles = 8
        first = x[:STEPS].reshape(STEPS * cols, order)
        if depth is not None:
            first = jnp.concatenate([first, depth[:tiles]], axis=0)
        above = lax.ppermute(x[-STEPS:], ("lev", "gx"), ahead)
        below = lax.ppermute(first, ("lev", "gx"), back)
        depth_below = below[STEPS * cols:]
        below = below[:STEPS * cols].reshape(STEPS, cols, order)
        first = jnp.concatenate([above[:, :PAD], x[:, :PAD], below[:, :PAD]], axis=0)
        last = jnp.concatenate([above[:, -PAD:], x[:, -PAD:], below[:, -PAD:]], axis=0)
        ext = first.shape[0]
        first = first.reshape(ext * PAD, order)
        if depth is not None:
            first = jnp.concatenate([first, depth], axis=0)
        from_left = lax.ppermute(last, "gy", right)
        from_right = lax.ppermute(first, "gy", left)
        depth_right = from_right[ext * PAD:]
        from_right = from_right[:ext * PAD].reshape(ext, PAD, order)
        return (x, above, below, from_left, from_right), depth_below, depth_right

    scaled = [scaled_message(to_slabs[d], increment, norm_gain, sea_mask, rows) for d in range(devices)]
    weights = [weight_message(to_slabs[d], diffusion_i, diffusion_j, rows) for d in range(devices)]
    scaled = exchange(scaled)
    early = shift(weights[1], 1)
    scaled, weights = lax.optimization_barrier((scaled, weights))
    weights = [weights[0], early] + [shift(weights[d], d) for d in range(2, devices)]

    balance = jnp.eye(order, dtype=jnp.float32) + coupling
    by_device = balance.reshape(2, devices, levels, order)
    adjoint = jnp.concatenate(
        [by_device[:, s].reshape(2 * levels, order) for s in source], axis=0
    ).T
    forward = jnp.concatenate([by_device[:, t].reshape(2 * levels, order) for t in to], axis=0)

    mixed, depth = adjoint_mix(adjoint, scaled, rows)
    field, depth_below, depth_right = halo(mixed, depth)
    field, weights = lax.optimization_barrier((field, weights))
    weight, _, _ = halo(turn_weights(sources, depth, depth_below, depth_right, weights, rows))
    mixed = exchange(spread_mix(forward, field, weight, devices))
    return result(source_slabs, norm_gain, sea_mask, mixed)


def solution(mesh):
    return jax.shard_map(
        shards,
        mesh=mesh,
        in_specs=(
            P(None, "lev", "gx", "gy"),
            P(None, "lev", "gx", "gy"),
            P("lev", "gx", "gy"),
            P("lev", "gx", "gy"),
            P("lev", "gx", "gy"),
            P(),
        ),
        out_specs=P(None, "lev", "gx", "gy"),
        check_vma=False,
    )
```

```python
import functools

import jax
import jax.numpy as jnp
from jax import lax
from jax.experimental import pallas as pl
from jax.experimental.pallas import tpu as pltpu
from jax.sharding import PartitionSpec as P

ITERS = 2
STEPS = 2 * ITERS
PAD = 8
PARTS = 2
VMEM_LIMIT = 40 * 1024 * 1024
VMEM_WHOLE = 60 * 1024 * 1024
HIGHEST = lax.Precision.HIGHEST


def params(limit=VMEM_LIMIT):
    return pltpu.CompilerParams(vmem_limit_bytes=limit)


def smem():
    return pl.BlockSpec(memory_space=pltpu.SMEM)


def vmem():
    return pl.BlockSpec(memory_space=pltpu.VMEM)


def groups_of(slots, d, groups, cols):
    width = cols // groups
    return [lax.rem((group - slots[d]) * width + cols, cols) for group in range(groups)]


def pack(blocks, shifts, group):
    out = pltpu.roll(blocks[0], shifts[0], 1)
    for a in range(1, len(blocks)):
        out = jnp.where(group == a, pltpu.roll(blocks[a], shifts[a], 1), out)
    return out


def scaled_kernel(slots, increment, gain, mask, *refs):
    outs, total = refs[:-1], refs[-1]
    fields, some, length, cols = increment.shape
    groups = len(outs)
    rows = length // groups
    count = outs[0].shape[0] // rows - 1
    levels = count // fields
    group = lax.broadcasted_iota(jnp.int32, (rows, cols), 1) // (cols // groups)
    step = pl.program_id(0)
    shifts = [groups_of(slots, d, groups, cols) for d in range(groups)]

    @pl.when(step == 0)
    def _():
        total[...] = jnp.zeros_like(total)

    for level in range(some):
        ocean = mask[level].astype(jnp.float32)
        total[...] += ocean
        for field in range(fields):
            x = ocean * gain[field, level] * increment[field, level]
            blocks = [x[a * rows:(a + 1) * rows] for a in range(groups)]
            at = pl.multiple_of((field * levels + step * some + level) * rows, rows)
            for d, out in enumerate(outs):
                out[pl.ds(at, rows), :] = pack(blocks, shifts[d], group)

    @pl.when(step == pl.num_programs(0) - 1)
    def _():
        blocks = [total[pl.ds(a * rows, rows), :] for a in range(groups)]
        for d, out in enumerate(outs):
            out[pl.ds(count * rows, rows), :] = pack(blocks, shifts[d], group)


def scaled_messages(slots, increment, gain, mask):
    fields, levels, length, cols = increment.shape
    groups = slots.shape[0]
    rows = length // groups
    some = 4
    block = pl.BlockSpec((fields, some, length, cols), lambda step, slots: (0, step, 0, 0))
    mask_block = pl.BlockSpec((some, length, cols), lambda step, slots: (step, 0, 0))
    shape = ((fields * levels + 1) * rows, cols)
    whole = lambda step, slots: (0, 0)
    *messages, depth = pl.pallas_call(
        scaled_kernel,
        grid_spec=pltpu.PrefetchScalarGridSpec(
            num_scalar_prefetch=1,
            grid=(levels // some,),
            in_specs=[block, block, mask_block],
            out_specs=[pl.BlockSpec(shape, whole)] * groups + [pl.BlockSpec((length, cols), whole)],
        ),
        out_shape=[jax.ShapeDtypeStruct(shape, jnp.float32)] * groups
        + [jax.ShapeDtypeStruct((length, cols), jnp.float32)],
        compiler_params=params(VMEM_WHOLE),
        name="scaled_messages",
    )(slots, increment, gain, mask)
    return messages, depth


def weight_kernel(along_i, along_j, mask, next_tile, right_tile, out, edge):
    levels, length, cols = along_i.shape
    lane = lax.broadcasted_iota(jnp.int32, (length, cols), 1)
    row = lax.broadcasted_iota(jnp.int32, (length, cols), 0)
    next_row = jnp.broadcast_to(next_tile[pl.ds(0, 1), :], (length, cols))
    next_col = pltpu.roll(right_tile[...], cols - 1, 1)

    def one(level, carry):
        at = level.astype(jnp.float32)
        ocean = mask[level].astype(jnp.float32)
        below = jnp.where(row == length - 1, (at < next_row).astype(jnp.float32), pltpu.roll(ocean, length - 1, 0))
        right = jnp.where(lane == cols - 1, (at < next_col).astype(jnp.float32), pltpu.roll(ocean, cols - 1, 1))
        for side, weight in ((0, along_i[level] * ocean * below), (1, along_j[level] * ocean * right)):
            index = side * levels + level
            out[index] = weight
            edge[index, pl.ds(0, STEPS), :] = weight[:STEPS]
            edge[index, pl.ds(STEPS, STEPS), :] = weight[length - STEPS:]
        return carry

    lax.fori_loop(0, levels, one, 0, unroll=2)


def tile_weights(along_i, along_j, mask, next_tile, right_tile):
    levels, length, cols = along_i.shape
    return pl.pallas_call(
        weight_kernel,
        in_specs=[vmem()] * 5,
        out_specs=[vmem()] * 2,
        out_shape=[
            jax.ShapeDtypeStruct((2 * levels, length, cols), jnp.float32),
            jax.ShapeDtypeStruct((2 * levels, 2 * STEPS, cols), jnp.float32),
        ],
        compiler_params=params(),
        name="tile_weights",
    )(along_i, along_j, mask, next_tile, right_tile)


def pack_kernel(first, slots, weight, above, below, *refs):
    outs, held = refs[:-1], refs[-1]
    count, length, cols = weight.shape
    groups = len(outs)
    rows = outs[0].shape[0] // count
    group = lax.broadcasted_iota(jnp.int32, (rows, cols), 1) // (cols // groups)
    shifts = [groups_of(slots, d, groups, cols) for d in range(groups)]
    unroll = held.shape[0]

    def some(outer, carry):
        for k in range(unroll):
            index = outer * unroll + k
            held[k, pl.ds(0, STEPS), :] = above[index]
            held[k, pl.ds(STEPS, length), :] = weight[index]
            held[k, pl.ds(STEPS + length, STEPS), :] = below[index]
        blocks = [[held[k, pl.ds(first + a * rows, rows), :] for a in range(groups)] for k in range(unroll)]
        at = pl.multiple_of(outer * unroll * rows, 8)
        for d, out in enumerate(outs):
            packed = [pack(blocks[k], shifts[d], group) for k in range(unroll)]
            out[pl.ds(at, unroll * rows), :] = jnp.concatenate(packed, axis=0)
        return carry

    lax.fori_loop(0, count // unroll, some, 0)


def weight_messages(first, rows, slots, weight, above, below):
    count, length, cols = weight.shape
    groups = slots.shape[0]
    shape = jax.ShapeDtypeStruct((count * rows // groups, cols), jnp.float32)

    def kernel(slots, weight, above, below, *refs):
        pack_kernel(first, slots, weight, above, below, *refs)

    return pl.pallas_call(
        kernel,
        in_specs=[smem()] + [vmem()] * 3,
        out_specs=[vmem()] * groups,
        out_shape=[shape] * groups,
        scratch_shapes=[pltpu.VMEM((4, length + 2 * STEPS, cols), jnp.float32)],
        compiler_params=params(),
        name="weight_messages",
    )(slots, weight, above, below)


def adjoint_kernel(matrix, *refs):
    parts, out = refs[:-1], refs[-1]
    length, width, order = out.shape
    groups = len(parts)
    rows = length // groups
    cols = groups * width
    count = order // groups
    level = lax.rem(lax.broadcasted_iota(jnp.int32, (order, cols), 0), order // 2).astype(jnp.float32)

    def one(i, carry):
        x = jnp.concatenate([part[pl.ds(i, count, rows), :] for part in parts], axis=0)
        depth = sum(part[pl.ds(count * rows + i, 1), :] for part in parts)
        y = jnp.dot(matrix[...], x, precision=HIGHEST, preferred_element_type=jnp.float32)
        y = jnp.where(level < depth, y, 0.0).T
        for a in range(groups):
            out[a * rows + i] = y[a * width:(a + 1) * width]
        return carry

    lax.fori_loop(0, rows, one, 0, unroll=4)


def adjoint_mix(matrix, parts, length, width):
    return pl.pallas_call(
        adjoint_kernel,
        in_specs=[vmem()] * (1 + len(parts)),
        out_specs=vmem(),
        out_shape=jax.ShapeDtypeStruct((length, width, matrix.shape[0]), jnp.float32),
        compiler_params=params(),
        name="adjoint_mix",
    )(matrix, *parts)


def turn_kernel(sources, *refs):
    parts, out, held = refs[:-2], refs[-2], refs[-1]
    length, width, order = out.shape
    groups = len(parts)
    rows = length // groups
    half = order // 2
    count = half // groups
    for i in range(rows):
        for d, part in enumerate(parts):
            for side in range(2):
                at = pl.multiple_of(side * half + sources[d] * count, 8)
                held[i, pl.ds(at, count), :] = part[pl.ds(side * count * rows + i, count, rows), :]
    for i in range(rows):
        turned = held[i].T
        for a in range(groups):
            out[a * rows + i] = turned[a * width:(a + 1) * width]


def turn_weights(sources, parts, order):
    groups = len(parts)
    cols = parts[0].shape[1]
    rows = parts[0].shape[0] * groups // order
    return pl.pallas_call(
        turn_kernel,
        in_specs=[smem()] + [vmem()] * groups,
        out_specs=vmem(),
        out_shape=jax.ShapeDtypeStruct((rows * groups, cols // groups, order), jnp.float32),
        scratch_shapes=[pltpu.VMEM((rows, order, cols), jnp.float32)],
        compiler_params=params(),
        name="turn_weights",
    )(sources, *parts)


def spread_kernel(first, pieces, matrix, *refs):
    field, weights = refs[:5], refs[5:5 + 3 * len(pieces)]
    outs, (a, b, wi, wj) = refs[5 + 3 * len(pieces):-4], refs[-4:]
    length, width, order = field[0].shape
    half = order // 2
    ext, wide, _ = a.shape
    lane = lax.broadcasted_iota(jnp.int32, (wide, order), 1)
    nothing = jnp.zeros((PAD - STEPS, order), jnp.float32)

    def widen(left, mid, right):
        return jnp.concatenate([nothing, left, mid, right, nothing], axis=0)

    for e in range(ext):
        r = first + e
        main, above, below, left, right = field
        if r < STEPS:
            mid = above[r]
        elif r < STEPS + length:
            mid = main[r - STEPS]
        else:
            mid = below[r - STEPS - length]
        a[e] = widen(left[r], mid, right[r])
        piece = [k for k, (at, rows) in enumerate(pieces) if at <= r < at + rows][0]
        main, left, right = weights[3 * piece:3 * piece + 3]
        k = r - pieces[piece][0]
        w = widen(left[k], main[k], right[k])
        other = pltpu.roll(w, half, 1)
        wi[e] = jnp.where(lane < half, w, other)
        wj[e] = jnp.where(lane < half, other, w)

    src, dst = a, b
    for step in range(STEPS):
        begin, last = step + 1, ext - 2 - step

        def one(r, carry, src=src, dst=dst):
            v, before = carry
            after = src[r + 1]
            flux = wi[r] * (after - v)
            across = wj[r] * (pltpu.roll(v, wide - 1, 0) - v)
            dst[r] = v + (flux - before) + (across - pltpu.roll(across, 1, 0))
            return after, flux

        v = src[begin]
        lax.fori_loop(begin, last + 1, one, (v, wi[begin - 1] * (v - src[begin - 1])), unroll=2)
        src, dst = dst, src

    groups = len(outs)
    count = order // groups
    rows = (ext - 2 * STEPS) // groups

    def mix(i, carry):
        x = jnp.concatenate([src[STEPS + g * rows + i, pl.ds(PAD, width), :] for g in range(groups)], axis=0)
        y = lax.dot_general(
            matrix[...], x, (((1,), (1,)), ((), ())), precision=HIGHEST, preferred_element_type=jnp.float32
        )
        for d, out in enumerate(outs):
            out[pl.ds(i, count, rows), :] = y[d * count:(d + 1) * count]
        return carry

    lax.fori_loop(0, rows, mix, 0, unroll=4)


def spread_mix(first, last, pieces, matrix, field, weights, groups):
    length, width, order = field[0].shape
    cols = width * groups
    rows = (last - first - 2 * STEPS) // groups
    shape = jax.ShapeDtypeStruct((order // groups * rows, cols), jnp.float32)
    ext = pltpu.VMEM((last - first, width + 2 * PAD, order), jnp.float32)

    def kernel(matrix, *refs):
        spread_kernel(first, pieces, matrix, *refs)

    return pl.pallas_call(
        kernel,
        in_specs=[vmem()] * (1 + len(field) + len(weights)),
        out_specs=[vmem()] * groups,
        out_shape=[shape] * groups,
        scratch_shapes=[ext] * 4,
        compiler_params=params(),
        name="spread_mix",
    )(matrix, *field, *weights)


def result_kernel(slots, gain, mask, *refs):
    parts, out = refs[:-1], refs[-1]
    fields, levels, length, cols = gain.shape
    groups = len(parts) // PARTS
    rows = parts[0].shape[0] // (fields * levels)
    group = lax.broadcasted_iota(jnp.int32, (rows, cols), 1) // (cols // groups)
    shifts = [[lax.rem((slots[d] - a) * (cols // groups) + cols, cols) for a in range(groups)] for d in range(groups)]

    def one(level, carry):
        for field in range(fields):
            at = pl.multiple_of((field * levels + level) * rows, rows)
            for part in range(PARTS):
                values = [parts[part * groups + d][pl.ds(at, rows), :] for d in range(groups)]
                for a in range(groups):
                    x = pltpu.roll(values[0], shifts[0][a], 1)
                    for d in range(1, groups):
                        x = jnp.where(group == slots[d], pltpu.roll(values[d], shifts[d][a], 1), x)
                    here = pl.ds((part * groups + a) * rows, rows)
                    ocean = mask[level, here, :].astype(jnp.float32)
                    out[field, level, here, :] = ocean * gain[field, level, here, :] * x
        return carry

    lax.fori_loop(0, levels, one, 0, unroll=2)


def result(slots, gain, mask, parts):
    return pl.pallas_call(
        result_kernel,
        in_specs=[smem()] + [vmem()] * (2 + len(parts)),
        out_specs=vmem(),
        out_shape=jax.ShapeDtypeStruct(gain.shape, jnp.float32),
        compiler_params=params(),
        name="result",
    )(slots, gain, mask, *parts)


def shards(increment, norm_gain, diffusion_i, diffusion_j, sea_mask, coupling):
    devices = lax.axis_size("lev")
    gx_size = lax.axis_size("gx")
    gy_size = lax.axis_size("gy")
    me = lax.axis_index("lev")
    gy = lax.axis_index("gy")
    _, levels, length, cols = increment.shape
    width = cols // devices
    order = coupling.shape[0]

    def place(y, slot):
        return devices - 1 - slot if y % 2 else slot

    def slot_of(lev):
        return jnp.where(gy % 2 == 1, devices - 1 - lev, lev)

    to = [lax.rem(me + d, devices) for d in range(devices)]
    source = [lax.rem(me + devices - d, devices) for d in range(devices)]
    to_slots = jnp.stack([slot_of(t) for t in to]).astype(jnp.int32)
    source_slots = jnp.stack([slot_of(s) for s in source]).astype(jnp.int32)
    sources = jnp.stack(source).astype(jnp.int32)

    def exchange(parts):
        return [parts[0]] + [
            lax.ppermute(parts[d], "lev", [(k, (k + d) % devices) for k in range(devices)]) for d in range(1, devices)
        ]

    up = [((k + 1) % gx_size, k) for k in range(gx_size)]
    down = [(b, a) for a, b in up]
    right = [(k, k + 1) for k in range(gy_size - 1)]
    left = [(b, a) for a, b in right]
    chain = [place(y, slot) * gy_size + y for y in range(gy_size) for slot in range(devices)]
    ahead = list(zip(chain[:-1], chain[1:]))
    back = [(b, a) for a, b in ahead]

    def halo_i(edge, axis):
        first, last = lax.split(edge, (STEPS, STEPS), axis)
        if gx_size == 2:
            below, above = lax.split(lax.ppermute(edge, "gx", up), (STEPS, STEPS), axis)
            return above, below
        return lax.ppermute(last, "gx", down), lax.ppermute(first, "gx", up)

    def halo_j(first, last):
        return lax.ppermute(last, ("lev", "gy"), ahead), lax.ppermute(first, ("lev", "gy"), back)

    messages, depth = scaled_messages(to_slots, increment, norm_gain, sea_mask)
    scaled = exchange(messages)
    next_tile = lax.ppermute(depth, "gx", up)
    right_tile = lax.ppermute(depth, "gy", left)
    weight, edge = tile_weights(diffusion_i, diffusion_j, sea_mask, next_tile, right_tile)
    weight_above, weight_below = halo_i(edge, 1)

    part = length // PARTS
    pieces = [(0, part + 2 * STEPS)] + [(k * part + 2 * STEPS, part) for k in range(1, PARTS)]

    def send(piece, weight):
        return exchange(weight_messages(*piece, to_slots, weight, weight_above, weight_below))

    arrived = [send(pieces[0], weight)]

    balance = jnp.eye(order, dtype=jnp.float32) + coupling
    by_device = balance.reshape(2, devices, levels, order)
    adjoint = jnp.concatenate([by_device[:, s].reshape(2 * levels, order) for s in source], axis=0).T
    forward = jnp.concatenate([by_device[:, t].reshape(2 * levels, order) for t in to], axis=0)

    mixed = adjoint_mix(adjoint, scaled, length, width)
    above, below = halo_i(jnp.concatenate([mixed[:STEPS], mixed[-STEPS:]], axis=0), 0)
    above, weight = lax.optimization_barrier((above, weight))
    tall = [above, mixed, below]
    field = [mixed, above, below] + list(
        halo_j(
            jnp.concatenate([x[:, :STEPS] for x in tall], axis=0),
            jnp.concatenate([x[:, -STEPS:] for x in tall], axis=0),
        )
    )

    field, arrived = lax.optimization_barrier((field, arrived))

    turned, out = [], []
    for k in range(PARTS):
        if k > 0:
            arrived.append(send(pieces[k], weight))
        here = turn_weights(sources, arrived[k], order)
        turned += [here, *halo_j(here[:, :STEPS], here[:, -STEPS:])]
        first, last = k * part, (k + 1) * part + 2 * STEPS
        out += exchange(spread_mix(first, last, pieces[:k + 1], forward, field, turned, devices))
    return result(source_slots, norm_gain, sea_mask, out)


def solution(mesh):
    return jax.shard_map(
        shards,
        mesh=mesh,
        in_specs=(
            P(None, "lev", "gx", "gy"),
            P(None, "lev", "gx", "gy"),
            P("lev", "gx", "gy"),
            P("lev", "gx", "gy"),
            P("lev", "gx", "gy"),
            P(),
        ),
        out_specs=P(None, "lev", "gx", "gy"),
        check_vma=False,
    )
```

```python
import functools

import jax
import jax.numpy as jnp
from jax import lax
from jax.experimental import pallas as pl
from jax.experimental.pallas import tpu as pltpu
from jax.sharding import PartitionSpec as P

ITERS = 2
STEPS = 2 * ITERS
PAD = 8
PARTS = 2
VMEM_LIMIT = 40 * 1024 * 1024
VMEM_WHOLE = 60 * 1024 * 1024
HIGHEST = lax.Precision.HIGHEST


def params(limit=VMEM_LIMIT):
    return pltpu.CompilerParams(vmem_limit_bytes=limit)


def smem():
    return pl.BlockSpec(memory_space=pltpu.SMEM)


def vmem():
    return pl.BlockSpec(memory_space=pltpu.VMEM)


def position():
    devices = lax.axis_size("lev")
    me = lax.axis_index("lev")
    flipped = lax.rem(lax.axis_index("gy"), 2) == 1

    def slot(lev):
        return jnp.where(flipped, devices - 1 - lev, lev)

    to = [lax.rem(me + d, devices) for d in range(devices)]
    source = [lax.rem(me + devices - d, devices) for d in range(devices)]
    return [slot(lev) for lev in to], [slot(lev) for lev in source], source


def swap(blocks, group, width):
    blocks = list(blocks)
    cols = blocks[0].shape[1]
    bit = len(blocks) // 2
    while bit:
        shift = bit * width
        low = (group & bit) == 0
        for a in range(len(blocks)):
            if not a & bit:
                x, y = blocks[a], blocks[a + bit]
                blocks[a] = jnp.where(low, x, pltpu.roll(y, shift, 1))
                blocks[a + bit] = jnp.where(low, pltpu.roll(x, cols - shift, 1), y)
        bit //= 2
    return blocks


def lane_groups(rows, cols, groups):
    return lax.broadcasted_iota(jnp.int32, (rows, cols), 1) // (cols // groups)


def copies(pairs, sems):
    made = [pltpu.make_async_copy(src, dst, sems.at[k]) for k, (src, dst) in enumerate(pairs)]
    for copy in made:
        copy.start()
    return made


SCALED_STEPS = 4


def scaled_kernel(increment, gain, mask, *refs):
    outs, (inc, gn, sea, held, sems, out_sems) = refs[:-6], refs[-6:]
    fields, levels, length, cols = increment.shape
    groups = len(outs)
    rows = length // groups
    some = levels // SCALED_STEPS
    group = lane_groups(rows, cols, groups)
    fetched = []
    for step in range(SCALED_STEPS):
        part = pl.ds(step * some, some)
        fetched.append(
            copies(
                [
                    (increment.at[:, part], inc.at[:, part]),
                    (gain.at[:, part], gn.at[:, part]),
                    (mask.at[part], sea.at[part]),
                ],
                sems.at[step],
            )
        )
    depth = jnp.zeros((length, cols), jnp.float32)

    def put(at, x):
        for slot, block in enumerate(swap([x[a * rows:(a + 1) * rows] for a in range(groups)], group, cols // groups)):
            held[slot, pl.ds(at, rows), :] = block

    for step in range(SCALED_STEPS):
        for copy in fetched[step]:
            copy.wait()

        def one(level, depth):
            ocean = sea[level].astype(jnp.float32)
            for field in range(fields):
                at = pl.multiple_of((field * levels + level) * rows, rows)
                put(at, ocean * gn[field, level] * inc[field, level])
            return depth + ocean

        depth = lax.fori_loop(step * some, (step + 1) * some, one, depth, unroll=True)
    put(fields * levels * rows, depth)
    slots = position()[0]
    for copy in copies([(held.at[slots[d]], out) for d, out in enumerate(outs)], out_sems):
        copy.wait()


def scaled_messages(increment, gain, mask, groups):
    fields, levels, length, cols = increment.shape
    shape = ((fields * levels + 1) * length // groups, cols)
    return pl.pallas_call(
        scaled_kernel,
        in_specs=[pl.BlockSpec(memory_space=pl.ANY)] * 3,
        out_specs=[pl.BlockSpec(memory_space=pl.ANY)] * groups,
        out_shape=[jax.ShapeDtypeStruct(shape, jnp.float32)] * groups,
        scratch_shapes=[
            pltpu.VMEM(increment.shape, jnp.float32),
            pltpu.VMEM(gain.shape, jnp.float32),
            pltpu.VMEM(mask.shape, mask.dtype),
            pltpu.VMEM((groups, *shape), jnp.float32),
            pltpu.SemaphoreType.DMA((SCALED_STEPS, 3)),
            pltpu.SemaphoreType.DMA((groups,)),
        ],
        compiler_params=params(VMEM_WHOLE),
        name="scaled_messages",
    )(increment, gain, mask)


def pack_kernel(first, along_i, along_j, above, below, *refs):
    outs, (held, slots_held, sems) = refs[:-3], refs[-3:]
    levels, length, cols = along_i.shape
    groups = len(outs)
    rows = outs[0].shape[0] // (2 * levels)
    group = lane_groups(rows, cols, groups)
    unroll = held.shape[0]

    for side, weight in enumerate((along_i, along_j)):

        def some(outer, carry, side=side, weight=weight):
            for k in range(unroll):
                level = outer * unroll + k
                held[k, pl.ds(0, STEPS), :] = above[side * levels + level]
                held[k, pl.ds(STEPS, length), :] = weight[level]
                held[k, pl.ds(STEPS + length, STEPS), :] = below[side * levels + level]
            packed = [
                swap([held[k, pl.ds(first + a * rows, rows), :] for a in range(groups)], group, cols // groups)
                for k in range(unroll)
            ]
            at = pl.multiple_of((side * levels + outer * unroll) * rows, 8)
            for slot in range(groups):
                block = jnp.concatenate([packed[k][slot] for k in range(unroll)], axis=0)
                slots_held[slot, pl.ds(at, unroll * rows), :] = block
            return carry

        lax.fori_loop(0, levels // unroll, some, 0)
    slots = position()[0]
    for copy in copies([(slots_held.at[slots[d]], out) for d, out in enumerate(outs)], sems):
        copy.wait()


def weight_messages(first, rows, along_i, along_j, above, below, groups):
    levels, length, cols = along_i.shape
    shape = (2 * levels * rows // groups, cols)
    unroll = 4
    return pl.pallas_call(
        functools.partial(pack_kernel, first),
        in_specs=[vmem()] * 4,
        out_specs=[pl.BlockSpec(memory_space=pl.ANY)] * groups,
        out_shape=[jax.ShapeDtypeStruct(shape, jnp.float32)] * groups,
        scratch_shapes=[
            pltpu.VMEM((unroll, length + 2 * STEPS, cols), jnp.float32),
            pltpu.VMEM((groups, *shape), jnp.float32),
            pltpu.SemaphoreType.DMA((groups,)),
        ],
        compiler_params=params(),
        name="weight_messages",
    )(along_i, along_j, above, below)


def adjoint_kernel(matrix, *refs):
    parts, out, depths = refs[:-2], refs[-2], refs[-1]
    length, width, order = out.shape
    groups = len(parts)
    rows = length // groups
    cols = groups * width
    count = order // groups
    depths[...] = sum(part[pl.ds(count * rows, rows), :] for part in parts)
    level = lax.rem(lax.broadcasted_iota(jnp.int32, (order, cols), 0), order // 2).astype(jnp.float32)

    def one(i, carry):
        x = jnp.concatenate([part[pl.ds(i, count, rows), :] for part in parts], axis=0)
        depth = depths[pl.ds(i, 1), :]
        y = jnp.dot(matrix[...], x, precision=HIGHEST, preferred_element_type=jnp.float32)
        y = jnp.where(level < depth, y, 0.0).T
        for a in range(groups):
            out[a * rows + i] = y[a * width:(a + 1) * width]
        return carry

    lax.fori_loop(0, rows, one, 0, unroll=4)


def adjoint_mix(matrix, parts, length, width):
    return pl.pallas_call(
        adjoint_kernel,
        in_specs=[vmem()] * (1 + len(parts)),
        out_specs=[vmem()] * 2,
        out_shape=[
            jax.ShapeDtypeStruct((length, width, matrix.shape[0]), jnp.float32),
            jax.ShapeDtypeStruct((length // len(parts), width * len(parts)), jnp.float32),
        ],
        compiler_params=params(),
        name="adjoint_mix",
    )(matrix, *parts)


def unfold(main, halo, groups):
    cols = main.shape[1]
    width = cols // groups
    below = halo[:STEPS]
    above = pltpu.roll(halo[STEPS:], width, 1)
    return jnp.concatenate(
        [above] + [main] + [pltpu.roll(main, cols - a * width, 1) for a in range(1, groups)] + [below], axis=0
    )


def turn_kernel(first, main, halo, right_main, right_halo, *refs):
    parts, (out, held, depth_i, depth_j) = refs[:-4], refs[-4:]
    length, width, order = out.shape
    groups = len(parts)
    rows = length // groups
    half = order // 2
    count = half // groups
    cols = width * groups
    source = position()[2]
    for i in range(rows):
        for d, part in enumerate(parts):
            for side in range(2):
                at = pl.multiple_of(side * half + source[d] * count, 8)
                held[i, pl.ds(at, count), :] = part[pl.ds(side * count * rows + i, count, rows), :]

    gy = lax.axis_index("gy")
    ends = (position()[0][0] == groups - 1) & (gy == lax.axis_size("gy") - 1)
    depth = unfold(main[...], halo[...], groups)
    right = jnp.where(ends, 0.0, unfold(right_main[...], right_halo[...], groups))
    tall = depth.shape[0]
    lane = lax.broadcasted_iota(jnp.int32, depth.shape, 1)
    right = jnp.where(lane == width - 1, pltpu.roll(right, width - 1, 1), pltpu.roll(depth, cols - 1, 1))
    depth_j[...] = jnp.minimum(depth, right)
    depth_i[pl.ds(0, tall - 1), :] = jnp.minimum(depth[:-1], depth[1:])
    depth_i[pl.ds(tall - 1, 1), :] = depth[tall - 1:]
    group = lane_groups(rows, cols, groups)

    def fold(ref):
        x = ref[pl.ds(first, rows), :]
        for a in range(1, groups):
            x = jnp.where(group == a, pltpu.roll(ref[pl.ds(first + a * rows, rows), :], a * width, 1), x)
        return x

    folded_i, folded_j = fold(depth_i), fold(depth_j)
    level = lax.broadcasted_iota(jnp.int32, (half, cols), 0).astype(jnp.float32)
    for i in range(rows):
        along_i = jnp.where(level < folded_i[i:i + 1], held[i, pl.ds(0, half), :], 0.0)
        along_j = jnp.where(level < folded_j[i:i + 1], held[i, pl.ds(half, half), :], 0.0)
        turned = jnp.concatenate([along_i, along_j], axis=0).T
        for a in range(groups):
            out[a * rows + i] = turned[a * width:(a + 1) * width]


def turn_weights(first, depths, parts, order):
    groups = len(parts)
    cols = parts[0].shape[1]
    rows = parts[0].shape[0] * groups // order
    tall = depths[0].shape[0] * groups + 2 * STEPS
    return pl.pallas_call(
        functools.partial(turn_kernel, first),
        in_specs=[vmem()] * (4 + groups),
        out_specs=vmem(),
        out_shape=jax.ShapeDtypeStruct((rows * groups, cols // groups, order), jnp.float32),
        scratch_shapes=[pltpu.VMEM((rows, order, cols), jnp.float32)] + [pltpu.VMEM((tall, cols), jnp.float32)] * 2,
        compiler_params=params(),
        name="turn_weights",
    )(*depths, *parts)


def spread_kernel(first, pieces, matrix, *refs):
    field, weights = refs[:5], refs[5:5 + 3 * len(pieces)]
    outs, (a, b, wi, wj) = refs[5 + 3 * len(pieces):-4], refs[-4:]
    length, width, order = field[0].shape
    half = order // 2
    ext, wide, _ = a.shape
    lane = lax.broadcasted_iota(jnp.int32, (wide, order), 1)
    nothing = jnp.zeros((PAD - STEPS, order), jnp.float32)

    def widen(left, mid, right):
        return jnp.concatenate([nothing, left, mid, right, nothing], axis=0)

    for e in range(ext):
        r = first + e
        main, above, below, left, right = field
        if r < STEPS:
            mid = above[r]
        elif r < STEPS + length:
            mid = main[r - STEPS]
        else:
            mid = below[r - STEPS - length]
        a[e] = widen(left[pl.ds(r * STEPS, STEPS), :], mid, right[pl.ds(r * STEPS, STEPS), :])
        piece = [k for k, (at, rows) in enumerate(pieces) if at <= r < at + rows][0]
        main, left, right = weights[3 * piece:3 * piece + 3]
        k = r - pieces[piece][0]
        w = widen(left[pl.ds(k * STEPS, STEPS), :], main[k], right[pl.ds(k * STEPS, STEPS), :])
        other = pltpu.roll(w, half, 1)
        wi[e] = jnp.where(lane < half, w, other)
        wj[e] = jnp.where(lane < half, other, w)

    src, dst = a, b
    for step in range(STEPS):
        begin, last = step + 1, ext - 2 - step

        def one(r, carry, src=src, dst=dst):
            v, before = carry
            after = src[r + 1]
            flux = wi[r] * (after - v)
            across = wj[r] * (pltpu.roll(v, wide - 1, 0) - v)
            dst[r] = v + (flux - before) + (across - pltpu.roll(across, 1, 0))
            return after, flux

        v = src[begin]
        lax.fori_loop(begin, last + 1, one, (v, wi[begin - 1] * (v - src[begin - 1])), unroll=2)
        src, dst = dst, src

    groups = len(outs)
    count = order // groups
    rows = (ext - 2 * STEPS) // groups

    def mix(i, carry):
        x = jnp.concatenate([src[STEPS + g * rows + i, pl.ds(PAD, width), :] for g in range(groups)], axis=0)
        y = lax.dot_general(
            matrix[...], x, (((1,), (1,)), ((), ())), precision=HIGHEST, preferred_element_type=jnp.float32
        )
        for d, out in enumerate(outs):
            out[pl.ds(i, count, rows), :] = y[d * count:(d + 1) * count]
        return carry

    lax.fori_loop(0, rows, mix, 0, unroll=4)


def spread_mix(first, last, pieces, matrix, field, weights, groups):
    length, width, order = field[0].shape
    cols = width * groups
    rows = (last - first - 2 * STEPS) // groups
    shape = jax.ShapeDtypeStruct((order // groups * rows, cols), jnp.float32)
    ext = pltpu.VMEM((last - first, width + 2 * PAD, order), jnp.float32)

    def kernel(matrix, *refs):
        spread_kernel(first, pieces, matrix, *refs)

    return pl.pallas_call(
        kernel,
        in_specs=[vmem()] * (1 + len(field) + len(weights)),
        out_specs=[vmem()] * groups,
        out_shape=[shape] * groups,
        scratch_shapes=[ext] * 4,
        compiler_params=params(),
        name="spread_mix",
    )(matrix, *field, *weights)


def result_kernel(gain, mask, *refs):
    parts, (out, held, sems) = refs[:-3], refs[-3:]
    fields, levels, length, cols = gain.shape
    groups = held.shape[0]
    rows = length // groups
    slots = position()[1]
    fetched = copies([(parts[d], held.at[slots[d]]) for d in range(groups)], sems)
    group = lane_groups(rows, cols, groups)
    for copy in fetched:
        copy.wait()

    def one(level, carry):
        ocean = mask[level].astype(jnp.float32)
        for field in range(fields):
            at = pl.multiple_of((field * levels + level) * rows, rows)
            blocks = swap([held[slot, pl.ds(at, rows), :] for slot in range(groups)], group, cols // groups)
            out[field, level] = ocean * gain[field, level] * jnp.concatenate(blocks, axis=0)
        return carry

    lax.fori_loop(0, levels, one, 0, unroll=4)


def result(part, gain, mask, parts, before):
    fields, levels, length, cols = gain.shape
    groups = len(parts)
    rows = length // PARTS
    block = pl.BlockSpec((fields, levels, rows, cols), lambda step: (0, 0, part, 0))
    mask_block = pl.BlockSpec((levels, rows, cols), lambda step: (0, part, 0))
    anywhere = pl.BlockSpec(memory_space=pl.ANY)
    more = [] if before is None else [before]
    return pl.pallas_call(
        result_kernel if before is None else lambda gain, mask, *refs: result_kernel(
            gain, mask, *refs[:groups], *refs[groups + 1:]
        ),
        grid=(1,),
        in_specs=[block, mask_block] + [anywhere] * (groups + len(more)),
        out_specs=block,
        out_shape=jax.ShapeDtypeStruct(gain.shape, jnp.float32),
        scratch_shapes=[
            pltpu.VMEM((groups, *parts[0].shape), jnp.float32),
            pltpu.SemaphoreType.DMA((groups,)),
        ],
        input_output_aliases={2 + groups: 0} if more else {},
        compiler_params=params(),
        name="result",
    )(gain, mask, *parts, *more)


def shards(increment, norm_gain, diffusion_i, diffusion_j, sea_mask, coupling):
    devices = lax.axis_size("lev")
    gx_size = lax.axis_size("gx")
    gy_size = lax.axis_size("gy")
    _, levels, length, cols = increment.shape
    width = cols // devices
    rows = length // devices
    order = coupling.shape[0]
    to = [lax.rem(lax.axis_index("lev") + d, devices) for d in range(devices)]
    source = [lax.rem(lax.axis_index("lev") + devices - d, devices) for d in range(devices)]

    def exchange(parts):
        return [parts[0]] + [
            lax.ppermute(parts[d], "lev", [(k, (k + d) % devices) for k in range(devices)]) for d in range(1, devices)
        ]

    up = [((k + 1) % gx_size, k) for k in range(gx_size)]
    down = [(b, a) for a, b in up]
    ring = [(devices - 1 - slot if y % 2 else slot) * gy_size + y for y in range(gy_size) for slot in range(devices)]
    ahead = list(zip(ring, ring[1:] + ring[:1]))
    back = [(b, a) for a, b in ahead]

    def halo_i(first, last, axis):
        if gx_size == 2:
            size = first.shape[axis]
            both = lax.ppermute(jnp.concatenate([first, last], axis=axis), "gx", up)
            below, above = lax.split(both, (size, size), axis)
            return above, below
        return lax.ppermute(last, "gx", down), lax.ppermute(first, "gx", up)

    def halo_j(first, last):
        return lax.ppermute(last, ("lev", "gy"), ahead), lax.ppermute(first, ("lev", "gy"), back)

    def flat(x):
        return x.reshape(-1, x.shape[-1])

    scaled = exchange(scaled_messages(increment, norm_gain, sea_mask, devices))

    above, below = halo_i(
        jnp.concatenate([diffusion_i[:, :STEPS], diffusion_j[:, :STEPS]], axis=0),
        jnp.concatenate([diffusion_i[:, -STEPS:], diffusion_j[:, -STEPS:]], axis=0),
        1,
    )
    part = length // PARTS
    pieces = [(0, part + 2 * STEPS)] + [(k * part + 2 * STEPS, part) for k in range(1, PARTS)]
    messages = [weight_messages(*piece, diffusion_i, diffusion_j, above, below, devices) for piece in pieces]
    arrived = exchange(messages[0])

    balance = jnp.eye(order, dtype=jnp.float32) + coupling
    by_device = balance.reshape(2, devices, levels, order)
    adjoint = jnp.concatenate([by_device[:, s].reshape(2 * levels, order) for s in source], axis=0).T
    forward = jnp.concatenate([by_device[:, t].reshape(2 * levels, order) for t in to], axis=0)

    mixed, depth = adjoint_mix(adjoint, scaled, length, width)
    above, below = halo_i(
        jnp.concatenate([flat(mixed[:STEPS]), depth[:STEPS]], axis=0),
        jnp.concatenate([flat(mixed[-STEPS:]), depth[-STEPS:]], axis=0),
        0,
    )
    size = STEPS * width
    halo_depth = jnp.concatenate([below[size:], above[size:]], axis=0)
    above, below = [x[:size].reshape(STEPS, width, order) for x in (above, below)]
    tall = [above, mixed, below]
    left, right = halo_j(
        jnp.concatenate([flat(jnp.concatenate([x[:, :STEPS] for x in tall], axis=0)), depth, halo_depth], axis=0),
        flat(jnp.concatenate([x[:, -STEPS:] for x in tall], axis=0)),
    )
    size = left.shape[0]
    depths = [depth, halo_depth, right[size:size + rows], right[size + rows:]]
    field = [mixed, above, below, left, right[:size]]

    turned, out = [], None
    for k, piece in enumerate(pieces):
        if k + 1 < PARTS:
            field, depths, arrived, messages = lax.optimization_barrier((field, depths, arrived, messages))
            coming = exchange(messages[k + 1])
        here = turn_weights(piece[0], depths, arrived, order)
        turned += [here, *halo_j(flat(here[:, :STEPS]), flat(here[:, -STEPS:]))]
        first, last = k * part, (k + 1) * part + 2 * STEPS
        mixed = exchange(spread_mix(first, last, pieces[:k + 1], forward, field, turned, devices))
        out = result(k, norm_gain, sea_mask, mixed, out)
        arrived = coming
    return out


def solution(mesh):
    return jax.shard_map(
        shards,
        mesh=mesh,
        in_specs=(
            P(None, "lev", "gx", "gy"),
            P(None, "lev", "gx", "gy"),
            P("lev", "gx", "gy"),
            P("lev", "gx", "gy"),
            P("lev", "gx", "gy"),
            P(),
        ),
        out_specs=P(None, "lev", "gx", "gy"),
        check_vma=False,
    )
```

```python
import functools

import jax
import jax.numpy as jnp
from jax import lax
from jax.experimental import pallas as pl
from jax.experimental.pallas import tpu as pltpu
from jax.sharding import PartitionSpec as P

ITERS = 2
STEPS = 2 * ITERS
PAD = 8
VMEM_LIMIT = 40 * 1024 * 1024
VMEM_WHOLE = 60 * 1024 * 1024
HIGHEST = lax.Precision.HIGHEST


def params(limit=VMEM_LIMIT):
    return pltpu.CompilerParams(vmem_limit_bytes=limit)


def smem():
    return pl.BlockSpec(memory_space=pltpu.SMEM)


def vmem():
    return pl.BlockSpec(memory_space=pltpu.VMEM)


def position():
    devices = lax.axis_size("lev")
    me = lax.axis_index("lev")
    flipped = lax.rem(lax.axis_index("gy"), 2) == 1

    def slot(lev):
        return jnp.where(flipped, devices - 1 - lev, lev)

    to = [lax.rem(me + d, devices) for d in range(devices)]
    source = [lax.rem(me + devices - d, devices) for d in range(devices)]
    return [slot(lev) for lev in to], [slot(lev) for lev in source], source


def swap(blocks, group, width):
    blocks = list(blocks)
    cols = blocks[0].shape[1]
    bit = len(blocks) // 2
    while bit:
        shift = bit * width
        low = (group & bit) == 0
        for a in range(len(blocks)):
            if not a & bit:
                x, y = blocks[a], blocks[a + bit]
                blocks[a] = jnp.where(low, x, pltpu.roll(y, shift, 1))
                blocks[a + bit] = jnp.where(low, pltpu.roll(x, cols - shift, 1), y)
        bit //= 2
    return blocks


def lane_groups(rows, cols, groups):
    return lax.broadcasted_iota(jnp.int32, (rows, cols), 1) // (cols // groups)


def copies(pairs, sems):
    made = [pltpu.make_async_copy(src, dst, sems.at[k]) for k, (src, dst) in enumerate(pairs)]
    for copy in made:
        copy.start()
    return made


SCALED_STEPS = 4


def scaled_kernel(increment, gain, mask, *refs):
    outs, (inc, gn, sea, held, sems, out_sems) = refs[:-6], refs[-6:]
    fields, levels, length, cols = increment.shape
    groups = len(outs)
    rows = length // groups
    some = levels // SCALED_STEPS
    group = lane_groups(rows, cols, groups)
    fetched = []
    for step in range(SCALED_STEPS):
        part = pl.ds(step * some, some)
        fetched.append(
            copies(
                [
                    (increment.at[:, part], inc.at[:, part]),
                    (gain.at[:, part], gn.at[:, part]),
                    (mask.at[part], sea.at[part]),
                ],
                sems.at[step],
            )
        )

    for step in range(SCALED_STEPS):
        for copy in fetched[step]:
            copy.wait()

        def one(level, carry):
            ocean = sea[level].astype(jnp.float32)
            for field in range(fields):
                at = pl.multiple_of((field * levels + level) * rows, rows)
                x = ocean * gn[field, level] * inc[field, level]
                blocks = swap([x[a * rows:(a + 1) * rows] for a in range(groups)], group, cols // groups)
                for slot, block in enumerate(blocks):
                    held[slot, pl.ds(at, rows), :] = block
            return carry

        lax.fori_loop(step * some, (step + 1) * some, one, 0, unroll=True)
    slots = position()[0]
    for copy in copies([(held.at[slots[d]], out) for d, out in enumerate(outs)], out_sems):
        copy.wait()


def scaled_messages(increment, gain, mask, groups):
    fields, levels, length, cols = increment.shape
    shape = (fields * levels * length // groups, cols)
    return pl.pallas_call(
        scaled_kernel,
        in_specs=[pl.BlockSpec(memory_space=pl.ANY)] * 3,
        out_specs=[pl.BlockSpec(memory_space=pl.ANY)] * groups,
        out_shape=[jax.ShapeDtypeStruct(shape, jnp.float32)] * groups,
        scratch_shapes=[
            pltpu.VMEM(increment.shape, jnp.float32),
            pltpu.VMEM(gain.shape, jnp.float32),
            pltpu.VMEM(mask.shape, mask.dtype),
            pltpu.VMEM((groups, *shape), jnp.float32),
            pltpu.SemaphoreType.DMA((SCALED_STEPS, 3)),
            pltpu.SemaphoreType.DMA((groups,)),
        ],
        compiler_params=params(VMEM_WHOLE),
        name="scaled_messages",
    )(increment, gain, mask)


def pack_kernel(starts, rows, masked, along_i, along_j, *refs):
    levels, length, cols = along_i.shape
    groups = len(starts)
    halos, outs = refs[masked:-4 - groups - 3 * masked], refs[-4 - groups - 3 * masked:-4 - 3 * masked]
    held, slots_held, sems, fetch_sems = refs[-4:]
    if masked:
        pairs = list(zip((along_i, along_j, refs[0]), refs[-7:-4]))
        fetched = copies(pairs, fetch_sems)
        along_i, along_j, sea = refs[-7:-4]
        for copy in fetched[:2]:
            copy.wait()
    group = lane_groups(rows, cols, groups)
    unroll = held.shape[0]

    for side, weight in enumerate((along_i, along_j)):

        def some(outer, carry, side=side, weight=weight):
            for halo, at in zip(halos, (0, STEPS + length)):
                size = unroll * STEPS
                block = halo[pl.ds(pl.multiple_of(side * levels * STEPS + outer * size, 8), size), :]
                for k in range(unroll):
                    held[k, pl.ds(at, STEPS), :] = block[k * STEPS:(k + 1) * STEPS]
            for k in range(unroll):
                held[k, pl.ds(STEPS, length), :] = weight[outer * unroll + k]
            packed = [
                swap([held[k, pl.ds(start, rows), :] for start in starts], group, cols // groups)
                for k in range(unroll)
            ]
            at = pl.multiple_of((side * levels + outer * unroll) * rows, 8)
            for slot in range(groups):
                block = jnp.concatenate([packed[k][slot] for k in range(unroll)], axis=0)
                slots_held[slot, pl.ds(at, unroll * rows), :] = block
            return carry

        lax.fori_loop(0, levels // unroll, some, 0)
    if masked:
        fetched[2].wait()
        depth = sea[0]
        for level in range(1, levels):
            depth = depth + sea[level]
        depth = depth.astype(jnp.float32)
        size = length // groups
        blocks = [depth[a * size:(a + 1) * size] for a in range(groups)]
        for slot, block in enumerate(swap(blocks, lane_groups(size, cols, groups), cols // groups)):
            slots_held[slot, pl.ds(2 * levels * rows, size), :] = block
    slots = position()[0]
    for copy in copies([(slots_held.at[slots[d]], out) for d, out in enumerate(outs)], sems):
        copy.wait()


def weight_messages(starts, rows, along_i, along_j, mask=(), halos=()):
    levels, length, cols = along_i.shape
    groups = len(starts)
    shape = (2 * levels * rows + len(mask) * length // groups, cols)
    unroll = 4
    return list(
        pl.pallas_call(
            functools.partial(pack_kernel, starts, rows, len(mask)),
            in_specs=[pl.BlockSpec(memory_space=pl.ANY) if mask else vmem()] * (2 + len(mask) + len(halos)),
            out_specs=[pl.BlockSpec(memory_space=pl.ANY)] * groups,
            out_shape=[jax.ShapeDtypeStruct(shape, jnp.float32)] * groups,
            scratch_shapes=[pltpu.VMEM(x.shape, x.dtype) for x in ([along_i, along_j, *mask] if mask else [])]
            + [
                pltpu.VMEM((unroll, length + 2 * STEPS, cols), jnp.float32),
                pltpu.VMEM((groups, *shape), jnp.float32),
                pltpu.SemaphoreType.DMA((groups,)),
                pltpu.SemaphoreType.DMA((3,)),
            ],
            compiler_params=params(VMEM_WHOLE if mask else VMEM_LIMIT),
            name="weight_messages",
        )(along_i, along_j, *mask, *halos)
    )


def adjoint_kernel(matrix, depths, *refs):
    parts, out = refs[:-1], refs[-1]
    length, width, order = out.shape
    groups = len(parts)
    rows = length // groups
    cols = groups * width
    count = order // groups
    level = lax.rem(lax.broadcasted_iota(jnp.int32, (order, cols), 0), order // 2).astype(jnp.float32)

    def one(i, carry):
        x = jnp.concatenate([part[pl.ds(i, count, rows), :] for part in parts], axis=0)
        depth = depths[pl.ds(i, 1), :]
        y = jnp.dot(matrix[...], x, precision=HIGHEST, preferred_element_type=jnp.float32)
        y = jnp.where(level < depth, y, 0.0).T
        for a in range(groups):
            out[a * rows + i] = y[a * width:(a + 1) * width]
        return carry

    lax.fori_loop(0, rows, one, 0, unroll=4)


def adjoint_mix(matrix, depths, parts, length, width):
    return pl.pallas_call(
        adjoint_kernel,
        in_specs=[vmem()] * (2 + len(parts)),
        out_specs=vmem(),
        out_shape=jax.ShapeDtypeStruct((length, width, matrix.shape[0]), jnp.float32),
        compiler_params=params(),
        name="adjoint_mix",
    )(matrix, depths, *parts)


def unfold(main, halo, groups):
    cols = main.shape[1]
    width = cols // groups
    below = halo[:STEPS]
    above = pltpu.roll(halo[STEPS:], width, 1)
    return jnp.concatenate(
        [above] + [main] + [pltpu.roll(main, cols - a * width, 1) for a in range(1, groups)] + [below], axis=0
    )


def turn_kernel(starts, *refs):
    depths, parts, (out, held, depth_i, depth_j) = refs[:-4 - len(starts)], refs[-4 - len(starts):-4], refs[-4:]
    length, width, order = out.shape
    groups = len(parts)
    rows = length // groups
    half = order // 2
    count = half // groups
    cols = width * groups
    source = position()[2]
    for i in range(rows):
        for d, part in enumerate(parts):
            for side in range(2):
                at = pl.multiple_of(side * half + source[d] * count, 8)
                held[i, pl.ds(at, count), :] = part[pl.ds(side * count * rows + i, count, rows), :]

    ends = (position()[0][0] == groups - 1) & (lax.axis_index("gy") == lax.axis_size("gy") - 1)
    no_halo = jnp.zeros((2 * STEPS, cols), jnp.float32)
    main, right_main = depths[0][...], depths[1][...]
    halo, right_halo = [ref[...] for ref in depths[2:]] or (no_halo, no_halo)
    depth = unfold(main, halo, groups)
    right = jnp.where(ends, 0.0, unfold(right_main, right_halo, groups))
    tall = depth.shape[0]
    lane = lax.broadcasted_iota(jnp.int32, depth.shape, 1)
    right = jnp.where(lane == width - 1, pltpu.roll(right, width - 1, 1), pltpu.roll(depth, cols - 1, 1))
    depth_j[...] = jnp.minimum(depth, right)
    depth_i[pl.ds(0, tall - 1), :] = jnp.minimum(depth[:-1], depth[1:])
    depth_i[pl.ds(tall - 1, 1), :] = depth[tall - 1:]
    group = lane_groups(rows, cols, groups)

    def fold(ref):
        x = ref[pl.ds(starts[0], rows), :]
        for a in range(1, groups):
            x = jnp.where(group == a, pltpu.roll(ref[pl.ds(starts[a], rows), :], a * width, 1), x)
        return x

    folded_i, folded_j = fold(depth_i), fold(depth_j)
    level = lax.broadcasted_iota(jnp.int32, (half, cols), 0).astype(jnp.float32)
    for i in range(rows):
        along_i = jnp.where(level < folded_i[i:i + 1], held[i, pl.ds(0, half), :], 0.0)
        along_j = jnp.where(level < folded_j[i:i + 1], held[i, pl.ds(half, half), :], 0.0)
        turned = jnp.concatenate([along_i, along_j], axis=0).T
        for a in range(groups):
            out[a * rows + i] = turned[a * width:(a + 1) * width]


def turn_weights(starts, rows, depths, parts, order):
    groups = len(parts)
    cols = parts[0].shape[1]
    tall = depths[0].shape[0] * groups + 2 * STEPS
    return pl.pallas_call(
        functools.partial(turn_kernel, starts),
        in_specs=[vmem()] * (len(depths) + groups),
        out_specs=vmem(),
        out_shape=jax.ShapeDtypeStruct((rows * groups, cols // groups, order), jnp.float32),
        scratch_shapes=[pltpu.VMEM((rows, order, cols), jnp.float32)] + [pltpu.VMEM((tall, cols), jnp.float32)] * 2,
        compiler_params=params(),
        name="turn_weights",
    )(*depths, *parts)


def spread_kernel(windows, field_rows, weight_rows, matrix, *refs):
    pieces = [refs[3 * k:3 * k + 3] for k in range(len(field_rows) + len(weight_rows))]
    outs, (a, b, wi, wj) = refs[3 * len(pieces):-4], refs[-4:]
    width, order = pieces[0][0].shape[1:]
    half = order // 2
    _, ext, wide, _ = a.shape
    lane = lax.broadcasted_iota(jnp.int32, (wide, order), 1)
    nothing = jnp.zeros((PAD - STEPS, order), jnp.float32)

    def row_of(some, rows, r):
        piece = [k for k in range(len(rows)) if r in rows[k]][0]
        main, left, right = some[piece]
        k = rows[piece].index(r)
        side = pl.ds(k * STEPS, STEPS)
        return jnp.concatenate([nothing, left[side, :], main[k], right[side, :], nothing], axis=0)

    for n, window in enumerate(windows):
        for e, r in enumerate(window):
            a[n, e] = row_of(pieces[:len(field_rows)], field_rows, r)
            w = row_of(pieces[len(field_rows):], weight_rows, r)
            other = pltpu.roll(w, half, 1)
            wi[n, e] = jnp.where(lane < half, w, other)
            wj[n, e] = jnp.where(lane < half, other, w)

    src, dst = a, b
    for step in range(STEPS):
        begin, last = step + 1, ext - 2 - step
        for n in range(len(windows)):

            def one(r, carry, n=n, src=src, dst=dst):
                v, before = carry
                after = src[n, r + 1]
                flux = wi[n, r] * (after - v)
                across = wj[n, r] * (pltpu.roll(v, wide - 1, 0) - v)
                dst[n, r] = v + (flux - before) + (across - pltpu.roll(across, 1, 0))
                return after, flux

            v = src[n, begin]
            lax.fori_loop(begin, last + 1, one, (v, wi[n, begin - 1] * (v - src[n, begin - 1])), unroll=2)
        src, dst = dst, src

    groups = len(outs)
    count = order // groups
    rows = len(windows) * (ext - 2 * STEPS) // groups
    each = groups // len(windows)

    def mix(i, carry):
        x = jnp.concatenate(
            [src[g // each, STEPS + g % each * rows + i, pl.ds(PAD, width), :] for g in range(groups)], axis=0
        )
        y = lax.dot_general(
            matrix[...], x, (((1,), (1,)), ((), ())), precision=HIGHEST, preferred_element_type=jnp.float32
        )
        for d, out in enumerate(outs):
            out[pl.ds(i, count, rows), :] = y[d * count:(d + 1) * count]
        return carry

    lax.fori_loop(0, rows, mix, 0, unroll=4)


def spread_mix(windows, matrix, field, weights, groups):
    width, order = field[0][1].shape[1:]
    cols = width * groups
    ext = len(windows[0])
    rows = len(windows) * (ext - 2 * STEPS) // groups
    shape = jax.ShapeDtypeStruct((order // groups * rows, cols), jnp.float32)
    arrays = [x for piece in field + weights for x in piece[1:]]
    return pl.pallas_call(
        functools.partial(spread_kernel, windows, [piece[0] for piece in field], [piece[0] for piece in weights]),
        in_specs=[vmem()] * (1 + len(arrays)),
        out_specs=[vmem()] * groups,
        out_shape=[shape] * groups,
        scratch_shapes=[pltpu.VMEM((len(windows), ext, width + 2 * PAD, order), jnp.float32)] * 4,
        compiler_params=params(),
        name="spread_mix",
    )(matrix, *arrays)


RESULT_STEPS = 4


def result_kernel(runs, gain, mask, *refs):
    parts, (out, held, done, sems, out_sems) = refs[:-5], refs[-5:]
    fields, levels, _, cols = gain.shape
    groups = held.shape[0]
    rows = done.shape[2] // groups
    some = levels // RESULT_STEPS
    slots = position()[1]
    fetched = copies([(parts[d], held.at[slots[d]]) for d in range(groups)], sems)
    group = lane_groups(rows, cols, groups)
    for copy in fetched:
        copy.wait()
    stored = []
    for step in range(RESULT_STEPS):

        def one(level, carry):
            ocean = jnp.concatenate([mask[level, pl.ds(*run), :] for run in runs], axis=0).astype(jnp.float32)
            for field in range(fields):
                at = pl.multiple_of((field * levels + level) * rows, rows)
                blocks = swap([held[slot, pl.ds(at, rows), :] for slot in range(groups)], group, cols // groups)
                gains = jnp.concatenate([gain[field, level, pl.ds(*run), :] for run in runs], axis=0)
                done[field, level] = ocean * gains * jnp.concatenate(blocks, axis=0)
            return carry

        lax.fori_loop(step * some, (step + 1) * some, one, 0, unroll=True)
        these = pl.ds(step * some, some)
        pairs, at = [], 0
        for first, number in runs:
            pairs.append((done.at[:, these, pl.ds(at, number)], out.at[:, these, pl.ds(first, number)]))
            at += number
        stored += copies(pairs, out_sems.at[step])
    for copy in stored:
        copy.wait()


def result(runs, gain, mask, parts, before):
    fields, levels, _, cols = gain.shape
    groups = len(parts)
    rows = sum(number for _, number in runs)
    anywhere = pl.BlockSpec(memory_space=pl.ANY)
    more = [] if before is None else [before]

    def kernel(gain, mask, *refs):
        result_kernel(runs, gain, mask, *refs[:groups], *refs[groups + len(more):])

    return pl.pallas_call(
        kernel,
        in_specs=[vmem()] * 2 + [anywhere] * (groups + len(more)),
        out_specs=anywhere,
        out_shape=jax.ShapeDtypeStruct(gain.shape, jnp.float32),
        scratch_shapes=[
            pltpu.VMEM((groups, *parts[0].shape), jnp.float32),
            pltpu.VMEM((fields, levels, rows, cols), jnp.float32),
            pltpu.SemaphoreType.DMA((groups,)),
            pltpu.SemaphoreType.DMA((RESULT_STEPS, len(runs))),
        ],
        input_output_aliases={2 + groups: 0} if more else {},
        compiler_params=params(),
        name="result",
    )(gain, mask, *parts, *more)


def shards(increment, norm_gain, diffusion_i, diffusion_j, sea_mask, coupling):
    devices = lax.axis_size("lev")
    gx_size = lax.axis_size("gx")
    gy_size = lax.axis_size("gy")
    _, levels, length, cols = increment.shape
    width = cols // devices
    rows = length // devices
    order = coupling.shape[0]
    to = [lax.rem(lax.axis_index("lev") + d, devices) for d in range(devices)]
    source = [lax.rem(lax.axis_index("lev") + devices - d, devices) for d in range(devices)]

    def shift(x, d):
        return lax.ppermute(x, "lev", [(k, (k + d) % devices) for k in range(devices)])

    def exchange(parts):
        return [parts[0]] + [shift(parts[d], d) for d in range(1, devices)]

    up = [((k + 1) % gx_size, k) for k in range(gx_size)]
    down = [(b, a) for a, b in up]
    ring = [(devices - 1 - slot if y % 2 else slot) * gy_size + y for y in range(gy_size) for slot in range(devices)]
    ahead = list(zip(ring, ring[1:] + ring[:1]))
    back = [(b, a) for a, b in ahead]

    def halo_i(first, last):
        if gx_size == 2:
            size = first.shape[0]
            both = lax.ppermute(jnp.concatenate([first, last], axis=0), "gx", up)
            return both[size:], both[:size]
        return lax.ppermute(last, "gx", down), lax.ppermute(first, "gx", up)

    def halo_j(first, last):
        return lax.ppermute(last, ("lev", "gy"), ahead), lax.ppermute(first, ("lev", "gy"), back)

    def flat(x):
        return x.reshape(-1, x.shape[-1])

    def cut(x, *sizes):
        return lax.split(x, sizes, 0)

    quarter = length // 4
    some = 2 * quarter // devices
    half = devices // 2
    inner = (quarter, 2 * quarter)
    outer = ((0, quarter), (3 * quarter, quarter))
    inner_rows = list(range(quarter - STEPS, 3 * quarter + STEPS))
    outer_rows = list(range(-STEPS, quarter - STEPS)) + list(range(3 * quarter + STEPS, length + STEPS))
    inner_starts = [quarter + a * len(inner_rows) // devices for a in range(devices)]
    outer_starts = [a * some for a in range(half)] + [3 * quarter + 2 * STEPS + a * some for a in range(half)]
    windows = [list(range(-STEPS, quarter + STEPS)), list(range(3 * quarter - STEPS, length + STEPS))]

    inner_size = len(inner_rows) // devices
    inner_messages = weight_messages(inner_starts, inner_size, diffusion_i, diffusion_j, [sea_mask])
    inner_parts = exchange(inner_messages)
    inner_messages, increment, norm_gain = lax.optimization_barrier((inner_messages, increment, norm_gain))
    scaled = exchange(scaled_messages(increment, norm_gain, sea_mask, devices))

    depth = sum(part[2 * levels * inner_size:] for part in inner_parts)
    right_depth = lax.ppermute(depth, ("lev", "gy"), back)
    depth, edge_i, edge_j = lax.optimization_barrier((depth, diffusion_i, diffusion_j))
    above, below = halo_i(
        *[
            jnp.concatenate([depth[at], flat(edge_i[:, at]), flat(edge_j[:, at])], axis=0)
            for at in (slice(0, STEPS), slice(-STEPS, None))
        ]
    )
    sizes = STEPS, 2 * levels * STEPS
    above_depth, above_weight = cut(above, *sizes)
    below_depth, below_weight = cut(below, *sizes)
    halo_depth = jnp.concatenate([below_depth, above_depth], axis=0)
    here = turn_weights(inner_starts, inner_size, [depth, right_depth], inner_parts, order)
    left, right = halo_j(
        jnp.concatenate([flat(here[:, :STEPS]), halo_depth], axis=0),
        flat(here[:, -STEPS:]),
    )
    right, right_halo_depth = cut(right, len(inner_rows) * STEPS, 2 * STEPS)
    outer_messages = weight_messages(
        outer_starts, some, diffusion_i, diffusion_j, halos=[above_weight, below_weight]
    )

    balance = jnp.eye(order, dtype=jnp.float32) + coupling
    by_device = balance.reshape(2, devices, levels, order)
    adjoint = jnp.concatenate([by_device[:, s].reshape(2 * levels, order) for s in source], axis=0).T
    forward = jnp.concatenate([by_device[:, t].reshape(2 * levels, order) for t in to], axis=0)

    scaled[1], left, right = lax.optimization_barrier((scaled[1], left, right))
    weights = [(inner_rows, here, left, right)]
    mixed = adjoint_mix(adjoint, depth, scaled, length, width)
    left, right = halo_j(flat(mixed[:, :STEPS]), flat(mixed[:, -STEPS:]))
    scaled[1], outer_messages[1] = lax.optimization_barrier((scaled[1], outer_messages[1]))
    early = shift(outer_messages[1], 1)
    left, right, outer_messages, early = lax.optimization_barrier((left, right, outer_messages, early))
    outer_parts = [outer_messages[0], early] + [shift(outer_messages[d], d) for d in range(2, devices)]
    field = [(list(range(length)), mixed, left, right)]
    inner_mixed = spread_mix([inner_rows], forward, field, weights, devices)
    _, outer_parts = lax.optimization_barrier((inner_mixed[0], outer_parts))
    inner_mixed = exchange(inner_mixed)
    out = result((inner,), norm_gain, sea_mask, inner_mixed, None)

    above, below = halo_i(flat(mixed[:STEPS]), flat(mixed[-STEPS:]))
    halo = jnp.concatenate([above, below], axis=0).reshape(2 * STEPS, width, order)
    here = turn_weights(outer_starts, some, [depth, right_depth, halo_depth, right_halo_depth], outer_parts, order)
    left, right = halo_j(
        jnp.concatenate([flat(here[:, :STEPS]), flat(halo[:, :STEPS])], axis=0),
        jnp.concatenate([flat(here[:, -STEPS:]), flat(halo[:, -STEPS:])], axis=0),
    )
    sizes = len(outer_rows) * STEPS, 2 * STEPS * STEPS
    left, halo_left = cut(left, *sizes)
    right, halo_right = cut(right, *sizes)
    weights.append((outer_rows, here, left, right))
    field.append((list(range(-STEPS, 0)) + list(range(length, length + STEPS)), halo, halo_left, halo_right))
    outer_mixed = exchange(spread_mix(windows, forward, field, weights, devices))
    return result(outer, norm_gain, sea_mask, outer_mixed, out)


def solution(mesh):
    return jax.shard_map(
        shards,
        mesh=mesh,
        in_specs=(
            P(None, "lev", "gx", "gy"),
            P(None, "lev", "gx", "gy"),
            P("lev", "gx", "gy"),
            P("lev", "gx", "gy"),
            P("lev", "gx", "gy"),
            P(),
        ),
        out_specs=P(None, "lev", "gx", "gy"),
        check_vma=False,
    )
```

```python
import functools

import jax
import jax.numpy as jnp
from jax import lax
from jax.experimental import pallas as pl
from jax.experimental.pallas import tpu as pltpu
from jax.sharding import PartitionSpec as P

ITERS = 2
STEPS = 2 * ITERS
PAD = 8
VMEM_LIMIT = 40 * 1024 * 1024
VMEM_WHOLE = 60 * 1024 * 1024
HIGHEST = lax.Precision.HIGHEST


def params(limit=VMEM_LIMIT):
    return pltpu.CompilerParams(vmem_limit_bytes=limit)


def smem():
    return pl.BlockSpec(memory_space=pltpu.SMEM)


def vmem():
    return pl.BlockSpec(memory_space=pltpu.VMEM)


def position():
    devices = lax.axis_size("lev")
    me = lax.axis_index("lev")
    flipped = lax.rem(lax.axis_index("gy"), 2) == 1

    def slot(lev):
        return jnp.where(flipped, devices - 1 - lev, lev)

    to = [lax.rem(me + d, devices) for d in range(devices)]
    source = [lax.rem(me + devices - d, devices) for d in range(devices)]
    return [slot(lev) for lev in to], [slot(lev) for lev in source], source


def swap(blocks, group, width):
    blocks = list(blocks)
    cols = blocks[0].shape[1]
    bit = len(blocks) // 2
    while bit:
        shift = bit * width
        low = (group & bit) == 0
        for a in range(len(blocks)):
            if not a & bit:
                x, y = blocks[a], blocks[a + bit]
                blocks[a] = jnp.where(low, x, pltpu.roll(y, shift, 1))
                blocks[a + bit] = jnp.where(low, pltpu.roll(x, cols - shift, 1), y)
        bit //= 2
    return blocks


def lane_groups(rows, cols, groups):
    return lax.broadcasted_iota(jnp.int32, (rows, cols), 1) // (cols // groups)


def copies(pairs, sems):
    made = [pltpu.make_async_copy(src, dst, sems.at[k]) for k, (src, dst) in enumerate(pairs)]
    for copy in made:
        copy.start()
    return made


SCALED_STEPS = 4


def scaled_kernel(increment, gain, mask, *refs):
    outs, (inc, gn, sea, held, sems, out_sems) = refs[:-6], refs[-6:]
    fields, levels, length, cols = increment.shape
    groups = len(outs)
    rows = length // groups
    some = levels // SCALED_STEPS
    group = lane_groups(rows, cols, groups)
    fetched = []
    for step in range(SCALED_STEPS):
        part = pl.ds(step * some, some)
        fetched.append(
            copies(
                [
                    (increment.at[:, part], inc.at[:, part]),
                    (gain.at[:, part], gn.at[:, part]),
                    (mask.at[part], sea.at[part]),
                ],
                sems.at[step],
            )
        )

    for step in range(SCALED_STEPS):
        for copy in fetched[step]:
            copy.wait()

        def one(level, carry):
            ocean = sea[level].astype(jnp.float32)
            for field in range(fields):
                at = pl.multiple_of((field * levels + level) * rows, rows)
                x = ocean * gn[field, level] * inc[field, level]
                blocks = swap([x[a * rows:(a + 1) * rows] for a in range(groups)], group, cols // groups)
                for slot, block in enumerate(blocks):
                    held[slot, pl.ds(at, rows), :] = block
            return carry

        lax.fori_loop(step * some, (step + 1) * some, one, 0, unroll=True)
    slots = position()[0]
    for copy in copies([(held.at[slots[d]], out) for d, out in enumerate(outs)], out_sems):
        copy.wait()


def scaled_messages(increment, gain, mask, groups):
    fields, levels, length, cols = increment.shape
    shape = (fields * levels * length // groups, cols)
    return pl.pallas_call(
        scaled_kernel,
        in_specs=[pl.BlockSpec(memory_space=pl.ANY)] * 3,
        out_specs=[pl.BlockSpec(memory_space=pl.ANY)] * groups,
        out_shape=[jax.ShapeDtypeStruct(shape, jnp.float32)] * groups,
        scratch_shapes=[
            pltpu.VMEM(increment.shape, jnp.float32),
            pltpu.VMEM(gain.shape, jnp.float32),
            pltpu.VMEM(mask.shape, mask.dtype),
            pltpu.VMEM((groups, *shape), jnp.float32),
            pltpu.SemaphoreType.DMA((SCALED_STEPS, 3)),
            pltpu.SemaphoreType.DMA((groups,)),
        ],
        compiler_params=params(VMEM_WHOLE),
        name="scaled_messages",
    )(increment, gain, mask)


def pack_kernel(starts, rows, masked, along_i, along_j, *refs):
    levels, length, cols = along_i.shape
    groups = len(starts)
    halos, outs = refs[masked:-4 - groups - 3 * masked], refs[-4 - groups - 3 * masked:-4 - 3 * masked]
    held, slots_held, sems, fetch_sems = refs[-4:]
    if masked:
        pairs = list(zip((along_i, along_j, refs[0]), refs[-7:-4]))
        fetched = copies(pairs, fetch_sems)
        along_i, along_j, sea = refs[-7:-4]
        for copy in fetched[:2]:
            copy.wait()
    group = lane_groups(rows, cols, groups)
    unroll = held.shape[0]

    for side, weight in enumerate((along_i, along_j)):

        def some(outer, carry, side=side, weight=weight):
            for halo, at in zip(halos, (0, STEPS + length)):
                size = unroll * STEPS
                block = halo[pl.ds(pl.multiple_of(side * levels * STEPS + outer * size, 8), size), :]
                for k in range(unroll):
                    held[k, pl.ds(at, STEPS), :] = block[k * STEPS:(k + 1) * STEPS]
            for k in range(unroll):
                held[k, pl.ds(STEPS, length), :] = weight[outer * unroll + k]
            packed = [
                swap([held[k, pl.ds(start, rows), :] for start in starts], group, cols // groups)
                for k in range(unroll)
            ]
            at = pl.multiple_of((side * levels + outer * unroll) * rows, 8)
            for slot in range(groups):
                block = jnp.concatenate([packed[k][slot] for k in range(unroll)], axis=0)
                slots_held[slot, pl.ds(at, unroll * rows), :] = block
            return carry

        lax.fori_loop(0, levels // unroll, some, 0)
    if masked:
        fetched[2].wait()
        depth = sea[0]
        for level in range(1, levels):
            depth = depth + sea[level]
        depth = depth.astype(jnp.float32)
        size = length // groups
        blocks = [depth[a * size:(a + 1) * size] for a in range(groups)]
        for slot, block in enumerate(swap(blocks, lane_groups(size, cols, groups), cols // groups)):
            slots_held[slot, pl.ds(2 * levels * rows, size), :] = block
    slots = position()[0]
    for copy in copies([(slots_held.at[slots[d]], out) for d, out in enumerate(outs)], sems):
        copy.wait()


def weight_messages(starts, rows, along_i, along_j, mask=(), halos=()):
    levels, length, cols = along_i.shape
    groups = len(starts)
    shape = (2 * levels * rows + len(mask) * length // groups, cols)
    unroll = 4
    return list(
        pl.pallas_call(
            functools.partial(pack_kernel, starts, rows, len(mask)),
            in_specs=[pl.BlockSpec(memory_space=pl.ANY) if mask else vmem()] * (2 + len(mask) + len(halos)),
            out_specs=[pl.BlockSpec(memory_space=pl.ANY)] * groups,
            out_shape=[jax.ShapeDtypeStruct(shape, jnp.float32)] * groups,
            scratch_shapes=[pltpu.VMEM(x.shape, x.dtype) for x in ([along_i, along_j, *mask] if mask else [])]
            + [
                pltpu.VMEM((unroll, length + 2 * STEPS, cols), jnp.float32),
                pltpu.VMEM((groups, *shape), jnp.float32),
                pltpu.SemaphoreType.DMA((groups,)),
                pltpu.SemaphoreType.DMA((3,)),
            ],
            compiler_params=params(VMEM_WHOLE if mask else VMEM_LIMIT),
            name="weight_messages",
        )(along_i, along_j, *mask, *halos)
    )


def adjoint_kernel(matrix, depths, *refs):
    parts, out = refs[:-1], refs[-1]
    length, width, order = out.shape
    groups = len(parts)
    rows = length // groups
    cols = groups * width
    count = order // groups
    level = lax.rem(lax.broadcasted_iota(jnp.int32, (order, cols), 0), order // 2).astype(jnp.float32)

    def one(i, carry):
        x = jnp.concatenate([part[pl.ds(i, count, rows), :] for part in parts], axis=0)
        depth = depths[pl.ds(i, 1), :]
        y = jnp.dot(matrix[...], x, precision=HIGHEST, preferred_element_type=jnp.float32)
        y = jnp.where(level < depth, y, 0.0).T
        for a in range(groups):
            out[a * rows + i] = y[a * width:(a + 1) * width]
        return carry

    lax.fori_loop(0, rows, one, 0, unroll=4)


def adjoint_mix(matrix, depths, parts, length, width):
    return pl.pallas_call(
        adjoint_kernel,
        in_specs=[vmem()] * (2 + len(parts)),
        out_specs=vmem(),
        out_shape=jax.ShapeDtypeStruct((length, width, matrix.shape[0]), jnp.float32),
        compiler_params=params(),
        name="adjoint_mix",
    )(matrix, depths, *parts)


def unfold(main, halo, groups):
    cols = main.shape[1]
    width = cols // groups
    below = halo[:STEPS]
    above = pltpu.roll(halo[STEPS:], width, 1)
    return jnp.concatenate(
        [above] + [main] + [pltpu.roll(main, cols - a * width, 1) for a in range(1, groups)] + [below], axis=0
    )


def turn_kernel(starts, *refs):
    depths, parts, (out, held, depth_i, depth_j) = refs[:-4 - len(starts)], refs[-4 - len(starts):-4], refs[-4:]
    length, width, order = out.shape
    groups = len(parts)
    rows = length // groups
    half = order // 2
    count = half // groups
    cols = width * groups
    source = position()[2]
    for i in range(rows):
        for d, part in enumerate(parts):
            for side in range(2):
                at = pl.multiple_of(side * half + source[d] * count, 8)
                held[i, pl.ds(at, count), :] = part[pl.ds(side * count * rows + i, count, rows), :]

    no_halo = jnp.zeros((2 * STEPS, cols), jnp.float32)
    depth = unfold(depths[0][...], depths[1][...] if len(depths) > 1 else no_halo, groups)
    tall = depth.shape[0]
    lane = lax.broadcasted_iota(jnp.int32, depth.shape, 1)
    right = jnp.where(lane == width - 1, depth, pltpu.roll(depth, cols - 1, 1))
    depth_j[...] = jnp.minimum(depth, right)
    depth_i[pl.ds(0, tall - 1), :] = jnp.minimum(depth[:-1], depth[1:])
    depth_i[pl.ds(tall - 1, 1), :] = depth[tall - 1:]
    group = lane_groups(rows, cols, groups)

    def fold(ref):
        x = ref[pl.ds(starts[0], rows), :]
        for a in range(1, groups):
            x = jnp.where(group == a, pltpu.roll(ref[pl.ds(starts[a], rows), :], a * width, 1), x)
        return x

    folded_i, folded_j = fold(depth_i), fold(depth_j)
    level = lax.broadcasted_iota(jnp.int32, (half, cols), 0).astype(jnp.float32)
    for i in range(rows):
        along_i = jnp.where(level < folded_i[i:i + 1], held[i, pl.ds(0, half), :], 0.0)
        along_j = jnp.where(level < folded_j[i:i + 1], held[i, pl.ds(half, half), :], 0.0)
        turned = jnp.concatenate([along_i, along_j], axis=0).T
        for a in range(groups):
            out[a * rows + i] = turned[a * width:(a + 1) * width]


def turn_weights(starts, rows, depths, parts, order):
    groups = len(parts)
    cols = parts[0].shape[1]
    tall = depths[0].shape[0] * groups + 2 * STEPS
    return pl.pallas_call(
        functools.partial(turn_kernel, starts),
        in_specs=[vmem()] * (len(depths) + groups),
        out_specs=vmem(),
        out_shape=jax.ShapeDtypeStruct((rows * groups, cols // groups, order), jnp.float32),
        scratch_shapes=[pltpu.VMEM((rows, order, cols), jnp.float32)] + [pltpu.VMEM((tall, cols), jnp.float32)] * 2,
        compiler_params=params(),
        name="turn_weights",
    )(*depths, *parts)


def edge_masks(depths, order):
    groups = lax.axis_size("lev")
    slot = position()[0][0]
    gy = lax.axis_index("gy")
    start = (slot == 0) & (gy == 0)
    end = (slot == groups - 1) & (gy == lax.axis_size("gy") - 1)
    no_halo = jnp.zeros((2 * STEPS, depths[0].shape[1]), jnp.float32)
    masks = []
    for k, out in enumerate((start, end)):
        x = unfold(depths[k][...], depths[2 + k][...] if len(depths) > 2 else no_halo, groups)
        x = jnp.where(out, 0.0, x)
        x = jnp.broadcast_to(x[:, :1], (x.shape[0], order))
        lane = lax.broadcasted_iota(jnp.int32, x.shape, 1)
        level = lax.rem(lane, order // 2).astype(jnp.float32)
        masks.append(jnp.where((lane < order // 2) | (level < x), 1.0, 0.0))
    return masks


def spread_kernel(windows, field_rows, weight_rows, count, matrix, *refs):
    depths, refs = refs[:count], refs[count:]
    pieces = [refs[3 * k:3 * k + 3] for k in range(len(field_rows) + len(weight_rows))]
    outs, (a, b, wi, wj, masks) = refs[3 * len(pieces):-5], refs[-5:]
    width, order = pieces[0][0].shape[1:]
    half = order // 2
    _, ext, wide, _ = a.shape
    lane = lax.broadcasted_iota(jnp.int32, (wide, order), 1)
    row = lax.broadcasted_iota(jnp.int32, (wide, order), 0)
    nothing = jnp.zeros((PAD - STEPS, order), jnp.float32)
    masks[0], masks[1] = edge_masks(depths, order)

    def row_of(some, rows, r):
        piece = [k for k in range(len(rows)) if r in rows[k]][0]
        main, left, right = some[piece]
        k = rows[piece].index(r)
        side = pl.ds(k * STEPS, STEPS)
        return jnp.concatenate([nothing, left[side, :], main[k], right[side, :], nothing], axis=0)

    for n, window in enumerate(windows):
        for e, r in enumerate(window):
            a[n, e] = row_of(pieces[:len(field_rows)], field_rows, r)
            w = row_of(pieces[len(field_rows):], weight_rows, r)
            at = pl.ds(STEPS + r, 1)
            w = w * jnp.where(row == PAD - 1, masks[0, at, :], 1.0)
            w = w * jnp.where(row == PAD + width - 1, masks[1, at, :], 1.0)
            other = pltpu.roll(w, half, 1)
            wi[n, e] = jnp.where(lane < half, w, other)
            wj[n, e] = jnp.where(lane < half, other, w)

    src, dst = a, b
    for step in range(STEPS):
        begin, last = step + 1, ext - 2 - step
        for n in range(len(windows)):

            def one(r, carry, n=n, src=src, dst=dst):
                v, before = carry
                after = src[n, r + 1]
                flux = wi[n, r] * (after - v)
                across = wj[n, r] * (pltpu.roll(v, wide - 1, 0) - v)
                dst[n, r] = v + (flux - before) + (across - pltpu.roll(across, 1, 0))
                return after, flux

            v = src[n, begin]
            lax.fori_loop(begin, last + 1, one, (v, wi[n, begin - 1] * (v - src[n, begin - 1])), unroll=2)
        src, dst = dst, src

    groups = len(outs)
    count = order // groups
    rows = len(windows) * (ext - 2 * STEPS) // groups
    each = groups // len(windows)

    def mix(i, carry):
        x = jnp.concatenate(
            [src[g // each, STEPS + g % each * rows + i, pl.ds(PAD, width), :] for g in range(groups)], axis=0
        )
        y = lax.dot_general(
            matrix[...], x, (((1,), (1,)), ((), ())), precision=HIGHEST, preferred_element_type=jnp.float32
        )
        for d, out in enumerate(outs):
            out[pl.ds(i, count, rows), :] = y[d * count:(d + 1) * count]
        return carry

    lax.fori_loop(0, rows, mix, 0, unroll=4)


def spread_mix(windows, matrix, depths, field, weights, groups):
    width, order = field[0][1].shape[1:]
    cols = width * groups
    ext = len(windows[0])
    rows = len(windows) * (ext - 2 * STEPS) // groups
    shape = jax.ShapeDtypeStruct((order // groups * rows, cols), jnp.float32)
    arrays = list(depths) + [x for piece in field + weights for x in piece[1:]]
    kernel = functools.partial(
        spread_kernel, windows, [piece[0] for piece in field], [piece[0] for piece in weights], len(depths)
    )
    tall = field[0][1].shape[0] + 2 * STEPS
    return pl.pallas_call(
        kernel,
        in_specs=[vmem()] * (1 + len(arrays)),
        out_specs=[vmem()] * groups,
        out_shape=[shape] * groups,
        scratch_shapes=[pltpu.VMEM((len(windows), ext, width + 2 * PAD, order), jnp.float32)] * 4
        + [pltpu.VMEM((2, tall, order), jnp.float32)],
        compiler_params=params(),
        name="spread_mix",
    )(matrix, *arrays)


RESULT_STEPS = 4


def result_kernel(runs, gain, mask, *refs):
    parts, (out, held, done, sems, out_sems) = refs[:-5], refs[-5:]
    fields, levels, _, cols = gain.shape
    groups = held.shape[0]
    rows = done.shape[2] // groups
    some = levels // RESULT_STEPS
    slots = position()[1]
    fetched = copies([(parts[d], held.at[slots[d]]) for d in range(groups)], sems)
    group = lane_groups(rows, cols, groups)
    for copy in fetched:
        copy.wait()
    stored = []
    for step in range(RESULT_STEPS):

        def one(level, carry):
            ocean = jnp.concatenate([mask[level, pl.ds(*run), :] for run in runs], axis=0).astype(jnp.float32)
            for field in range(fields):
                at = pl.multiple_of((field * levels + level) * rows, rows)
                blocks = swap([held[slot, pl.ds(at, rows), :] for slot in range(groups)], group, cols // groups)
                gains = jnp.concatenate([gain[field, level, pl.ds(*run), :] for run in runs], axis=0)
                done[field, level] = ocean * gains * jnp.concatenate(blocks, axis=0)
            return carry

        lax.fori_loop(step * some, (step + 1) * some, one, 0, unroll=True)
        these = pl.ds(step * some, some)
        pairs, at = [], 0
        for first, number in runs:
            pairs.append((done.at[:, these, pl.ds(at, number)], out.at[:, these, pl.ds(first, number)]))
            at += number
        stored += copies(pairs, out_sems.at[step])
    for copy in stored:
        copy.wait()


def result(runs, gain, mask, parts, before):
    fields, levels, _, cols = gain.shape
    groups = len(parts)
    rows = sum(number for _, number in runs)
    anywhere = pl.BlockSpec(memory_space=pl.ANY)
    more = [] if before is None else [before]

    def kernel(gain, mask, *refs):
        result_kernel(runs, gain, mask, *refs[:groups], *refs[groups + len(more):])

    return pl.pallas_call(
        kernel,
        in_specs=[vmem()] * 2 + [anywhere] * (groups + len(more)),
        out_specs=anywhere,
        out_shape=jax.ShapeDtypeStruct(gain.shape, jnp.float32),
        scratch_shapes=[
            pltpu.VMEM((groups, *parts[0].shape), jnp.float32),
            pltpu.VMEM((fields, levels, rows, cols), jnp.float32),
            pltpu.SemaphoreType.DMA((groups,)),
            pltpu.SemaphoreType.DMA((RESULT_STEPS, len(runs))),
        ],
        input_output_aliases={2 + groups: 0} if more else {},
        compiler_params=params(),
        name="result",
    )(gain, mask, *parts, *more)


def shards(increment, norm_gain, diffusion_i, diffusion_j, sea_mask, coupling):
    devices = lax.axis_size("lev")
    gx_size = lax.axis_size("gx")
    gy_size = lax.axis_size("gy")
    _, levels, length, cols = increment.shape
    width = cols // devices
    rows = length // devices
    order = coupling.shape[0]
    to = [lax.rem(lax.axis_index("lev") + d, devices) for d in range(devices)]
    source = [lax.rem(lax.axis_index("lev") + devices - d, devices) for d in range(devices)]

    def shift(x, d):
        return lax.ppermute(x, "lev", [(k, (k + d) % devices) for k in range(devices)])

    def exchange(parts):
        return [parts[0]] + [shift(parts[d], d) for d in range(1, devices)]

    up = [((k + 1) % gx_size, k) for k in range(gx_size)]
    down = [(b, a) for a, b in up]
    ring = [(devices - 1 - slot if y % 2 else slot) * gy_size + y for y in range(gy_size) for slot in range(devices)]
    ahead = list(zip(ring, ring[1:] + ring[:1]))
    back = [(b, a) for a, b in ahead]

    def halo_i(first, last):
        if gx_size == 2:
            size = first.shape[0]
            both = lax.ppermute(jnp.concatenate([first, last], axis=0), "gx", up)
            return both[size:], both[:size]
        return lax.ppermute(last, "gx", down), lax.ppermute(first, "gx", up)

    def halo_j(first, last):
        return lax.ppermute(last, ("lev", "gy"), ahead), lax.ppermute(first, ("lev", "gy"), back)

    def flat(x):
        return x.reshape(-1, x.shape[-1])

    def cut(x, *sizes):
        return lax.split(x, sizes, 0)

    quarter = length // 4
    some = 2 * quarter // devices
    half = devices // 2
    inner = (quarter, 2 * quarter)
    outer = ((0, quarter), (3 * quarter, quarter))
    inner_rows = list(range(quarter - STEPS, 3 * quarter + STEPS))
    outer_rows = list(range(-STEPS, quarter - STEPS)) + list(range(3 * quarter + STEPS, length + STEPS))
    inner_starts = [quarter + a * len(inner_rows) // devices for a in range(devices)]
    outer_starts = [a * some for a in range(half)] + [3 * quarter + 2 * STEPS + a * some for a in range(half)]
    windows = [list(range(-STEPS, quarter + STEPS)), list(range(3 * quarter - STEPS, length + STEPS))]

    inner_size = len(inner_rows) // devices
    inner_messages = weight_messages(inner_starts, inner_size, diffusion_i, diffusion_j, [sea_mask])
    inner_parts = exchange(inner_messages)
    inner_messages, edge_i, edge_j, increment, norm_gain = lax.optimization_barrier(
        (inner_messages, diffusion_i, diffusion_j, increment, norm_gain)
    )
    halos = halo_i(
        *[
            jnp.concatenate([flat(edge_i[:, at]), flat(edge_j[:, at])], axis=0)
            for at in (slice(0, STEPS), slice(-STEPS, None))
        ]
    )
    messages = scaled_messages(increment, norm_gain, sea_mask, devices)
    scaled = exchange(messages)
    messages, halos = lax.optimization_barrier((messages, halos))
    outer_messages = weight_messages(outer_starts, some, diffusion_i, diffusion_j, halos=halos)

    depth = sum(part[2 * levels * inner_size:] for part in inner_parts)
    here = turn_weights(inner_starts, inner_size, [depth], inner_parts, order)
    left, right = halo_j(
        jnp.concatenate([flat(here[:, :STEPS]), depth], axis=0),
        flat(here[:, -STEPS:]),
    )
    right, right_depth = cut(right, len(inner_rows) * STEPS, rows)

    balance = jnp.eye(order, dtype=jnp.float32) + coupling
    by_device = balance.reshape(2, devices, levels, order)
    adjoint = jnp.concatenate([by_device[:, s].reshape(2 * levels, order) for s in source], axis=0).T
    forward = jnp.concatenate([by_device[:, t].reshape(2 * levels, order) for t in to], axis=0)

    scaled[1], outer_messages = lax.optimization_barrier((scaled[1], outer_messages))
    early = shift(outer_messages[1], 1)
    mixed = adjoint_mix(adjoint, depth, scaled, length, width)
    edges = flat(mixed[:, :STEPS]), flat(mixed[:, -STEPS:])
    edges, inner_weights = lax.optimization_barrier((edges, (here, left, right)))
    left, right = halo_j(*edges)
    left, right, outer_messages, early = lax.optimization_barrier((left, right, outer_messages, early))
    outer_parts = [outer_messages[0], early] + [shift(outer_messages[d], d) for d in range(2, devices)]
    field = [(list(range(length)), mixed, left, right)]
    weights = [(inner_rows, *inner_weights)]
    depths = [depth, right_depth]
    inner_mixed = spread_mix([inner_rows], forward, depths, field, weights, devices)
    _, upper, lower = lax.optimization_barrier((left, mixed[:STEPS], mixed[-STEPS:]))
    _, outer_parts = lax.optimization_barrier((inner_mixed[0], outer_parts))
    inner_mixed = exchange(inner_mixed)
    out = result((inner,), norm_gain, sea_mask, inner_mixed, None)

    above, below = halo_i(
        jnp.concatenate([flat(upper), depth[:STEPS]], axis=0),
        jnp.concatenate([flat(lower), depth[-STEPS:]], axis=0),
    )
    above, above_depth = cut(above, STEPS * width, STEPS)
    below, below_depth = cut(below, STEPS * width, STEPS)
    halo_depth = jnp.concatenate([below_depth, above_depth], axis=0)
    halo = jnp.concatenate([above, below], axis=0).reshape(2 * STEPS, width, order)
    here = turn_weights(outer_starts, some, [depth, halo_depth], outer_parts, order)
    left, right = halo_j(
        jnp.concatenate([flat(here[:, :STEPS]), flat(halo[:, :STEPS]), halo_depth], axis=0),
        jnp.concatenate([flat(here[:, -STEPS:]), flat(halo[:, -STEPS:])], axis=0),
    )
    sizes = len(outer_rows) * STEPS, 2 * STEPS * STEPS
    left, halo_left = cut(left, *sizes)
    right, halo_right, right_halo_depth = cut(right, *sizes, 2 * STEPS)
    weights.append((outer_rows, here, left, right))
    field.append((list(range(-STEPS, 0)) + list(range(length, length + STEPS)), halo, halo_left, halo_right))
    depths += [halo_depth, right_halo_depth]
    outer_mixed = exchange(spread_mix(windows, forward, depths, field, weights, devices))
    return result(outer, norm_gain, sea_mask, outer_mixed, out)


def solution(mesh):
    return jax.shard_map(
        shards,
        mesh=mesh,
        in_specs=(
            P(None, "lev", "gx", "gy"),
            P(None, "lev", "gx", "gy"),
            P("lev", "gx", "gy"),
            P("lev", "gx", "gy"),
            P("lev", "gx", "gy"),
            P(),
        ),
        out_specs=P(None, "lev", "gx", "gy"),
        check_vma=False,
    )
```

```python
import functools

import jax
import jax.numpy as jnp
from jax import lax
from jax.experimental import pallas as pl
from jax.experimental.pallas import tpu as pltpu
from jax.sharding import PartitionSpec as P

ITERS = 2
STEPS = 2 * ITERS
PAD = 8
VMEM_LIMIT = 40 * 1024 * 1024
VMEM_WHOLE = 60 * 1024 * 1024
HIGHEST = lax.Precision.HIGHEST


def params(limit=VMEM_LIMIT):
    return pltpu.CompilerParams(vmem_limit_bytes=limit)


def smem():
    return pl.BlockSpec(memory_space=pltpu.SMEM)


def vmem():
    return pl.BlockSpec(memory_space=pltpu.VMEM)


def position():
    devices = lax.axis_size("lev")
    me = lax.axis_index("lev")
    flipped = lax.rem(lax.axis_index("gy"), 2) == 1

    def slot(lev):
        return jnp.where(flipped, devices - 1 - lev, lev)

    to = [lax.rem(me + d, devices) for d in range(devices)]
    source = [lax.rem(me + devices - d, devices) for d in range(devices)]
    return [slot(lev) for lev in to], [slot(lev) for lev in source], source


def swap(blocks, group, width):
    blocks = list(blocks)
    cols = blocks[0].shape[1]
    bit = len(blocks) // 2
    while bit:
        shift = bit * width
        low = (group & bit) == 0
        for a in range(len(blocks)):
            if not a & bit:
                x, y = blocks[a], blocks[a + bit]
                blocks[a] = jnp.where(low, x, pltpu.roll(y, shift, 1))
                blocks[a + bit] = jnp.where(low, pltpu.roll(x, cols - shift, 1), y)
        bit //= 2
    return blocks


def lane_groups(rows, cols, groups):
    return lax.broadcasted_iota(jnp.int32, (rows, cols), 1) // (cols // groups)


def copies(pairs, sems):
    made = [pltpu.make_async_copy(src, dst, sems.at[k]) for k, (src, dst) in enumerate(pairs)]
    for copy in made:
        copy.start()
    return made


SCALED_STEPS = 4


def scaled_kernel(increment, gain, mask, *refs):
    outs, (inc, gn, sea, held, sems, out_sems) = refs[:-6], refs[-6:]
    fields, levels, length, cols = increment.shape
    groups = len(outs)
    rows = length // groups
    some = levels // SCALED_STEPS
    group = lane_groups(rows, cols, groups)
    fetched = []
    for step in range(SCALED_STEPS):
        part = pl.ds(step * some, some)
        fetched.append(
            copies(
                [
                    (increment.at[:, part], inc.at[:, part]),
                    (gain.at[:, part], gn.at[:, part]),
                    (mask.at[part], sea.at[part]),
                ],
                sems.at[step],
            )
        )

    for step in range(SCALED_STEPS):
        for copy in fetched[step]:
            copy.wait()

        def one(level, carry):
            ocean = sea[level].astype(jnp.float32)
            for field in range(fields):
                at = pl.multiple_of((field * levels + level) * rows, rows)
                x = ocean * gn[field, level] * inc[field, level]
                blocks = swap([x[a * rows:(a + 1) * rows] for a in range(groups)], group, cols // groups)
                for slot, block in enumerate(blocks):
                    held[slot, pl.ds(at, rows), :] = block
            return carry

        lax.fori_loop(step * some, (step + 1) * some, one, 0, unroll=True)
    slots = position()[0]
    for copy in copies([(held.at[slots[d]], out) for d, out in enumerate(outs)], out_sems):
        copy.wait()


def scaled_messages(increment, gain, mask, groups):
    fields, levels, length, cols = increment.shape
    shape = (fields * levels * length // groups, cols)
    return pl.pallas_call(
        scaled_kernel,
        in_specs=[pl.BlockSpec(memory_space=pl.ANY)] * 3,
        out_specs=[pl.BlockSpec(memory_space=pl.ANY)] * groups,
        out_shape=[jax.ShapeDtypeStruct(shape, jnp.float32)] * groups,
        scratch_shapes=[
            pltpu.VMEM(increment.shape, jnp.float32),
            pltpu.VMEM(gain.shape, jnp.float32),
            pltpu.VMEM(mask.shape, mask.dtype),
            pltpu.VMEM((groups, *shape), jnp.float32),
            pltpu.SemaphoreType.DMA((SCALED_STEPS, 3)),
            pltpu.SemaphoreType.DMA((groups,)),
        ],
        compiler_params=params(VMEM_WHOLE),
        name="scaled_messages",
    )(increment, gain, mask)


def pack_kernel(starts, rows, masked, along_i, along_j, *refs):
    levels, length, cols = along_i.shape
    groups = len(starts)
    halos, outs = refs[masked:-4 - groups - 3 * masked], refs[-4 - groups - 3 * masked:-4 - 3 * masked]
    held, slots_held, sems, fetch_sems = refs[-4:]
    group = lane_groups(rows, cols, groups)
    unroll = held.shape[0]
    pieces = levels // unroll
    if masked:
        sources, (along_i, along_j, sea) = (along_i, along_j, refs[0]), refs[-7:-4]
        fetched = []
        for side, (source, target) in enumerate(zip(sources, (along_i, along_j, sea))):
            pairs = [(source.at[pl.ds(k * unroll, unroll)], target.at[pl.ds(k * unroll, unroll)]) for k in range(pieces)]
            fetched.append(copies(pairs, fetch_sems.at[side]))

    def put(at, blocks):
        for slot, block in enumerate(blocks):
            slots_held[slot, pl.ds(at, block.shape[0]), :] = block

    for side, weight in enumerate((along_i, along_j)):
        for outer in range(pieces):
            if masked:
                fetched[side][outer].wait()
            packed = []
            for k in range(unroll):
                level = outer * unroll + k
                if halos:
                    for halo, at in zip(halos, (0, STEPS + length)):
                        held[k, pl.ds(at, STEPS), :] = halo[pl.ds((side * levels + level) * STEPS, STEPS), :]
                    held[k, pl.ds(STEPS, length), :] = weight[level]
                    blocks = [held[k, pl.ds(start, rows), :] for start in starts]
                else:
                    blocks = [weight[level, pl.ds(start - STEPS, rows), :] for start in starts]
                packed.append(swap(blocks, group, cols // groups))
            put(
                (side * levels + outer * unroll) * rows,
                [jnp.concatenate([packed[k][slot] for k in range(unroll)], axis=0) for slot in range(groups)],
            )
    if masked:
        depth = jnp.zeros((length, cols), sea.dtype)
        for outer in range(pieces):
            fetched[2][outer].wait()
            for level in range(outer * unroll, (outer + 1) * unroll):
                depth = depth + sea[level]
        depth = depth.astype(jnp.float32)
        size = length // groups
        blocks = [depth[a * size:(a + 1) * size] for a in range(groups)]
        put(2 * levels * rows, swap(blocks, lane_groups(size, cols, groups), cols // groups))
    slots = position()[0]
    for copy in copies([(slots_held.at[slots[d]], out) for d, out in enumerate(outs)], sems):
        copy.wait()


def weight_messages(starts, rows, along_i, along_j, mask=(), halos=()):
    levels, length, cols = along_i.shape
    groups = len(starts)
    shape = (2 * levels * rows + len(mask) * length // groups, cols)
    unroll = 4
    return list(
        pl.pallas_call(
            functools.partial(pack_kernel, starts, rows, len(mask)),
            in_specs=[pl.BlockSpec(memory_space=pl.ANY) if mask else vmem()] * (2 + len(mask) + len(halos)),
            out_specs=[pl.BlockSpec(memory_space=pl.ANY)] * groups,
            out_shape=[jax.ShapeDtypeStruct(shape, jnp.float32)] * groups,
            scratch_shapes=[pltpu.VMEM(x.shape, x.dtype) for x in ([along_i, along_j, *mask] if mask else [])]
            + [
                pltpu.VMEM((unroll, length + 2 * STEPS, cols), jnp.float32),
                pltpu.VMEM((groups, *shape), jnp.float32),
                pltpu.SemaphoreType.DMA((groups,)),
                pltpu.SemaphoreType.DMA((3, levels // unroll)),
            ],
            compiler_params=params(VMEM_WHOLE if mask else VMEM_LIMIT),
            name="weight_messages",
        )(along_i, along_j, *mask, *halos)
    )


def adjoint_kernel(matrix, depths, *refs):
    parts, out = refs[:-1], refs[-1]
    length, width, order = out.shape
    groups = len(parts)
    rows = length // groups
    cols = groups * width
    count = order // groups
    level = lax.rem(lax.broadcasted_iota(jnp.int32, (order, cols), 0), order // 2).astype(jnp.float32)

    def one(i, carry):
        x = jnp.concatenate([part[pl.ds(i, count, rows), :] for part in parts], axis=0)
        depth = depths[pl.ds(i, 1), :]
        y = jnp.dot(matrix[...], x, precision=HIGHEST, preferred_element_type=jnp.float32)
        y = jnp.where(level < depth, y, 0.0).T
        for a in range(groups):
            out[a * rows + i] = y[a * width:(a + 1) * width]
        return carry

    lax.fori_loop(0, rows, one, 0, unroll=4)


def adjoint_mix(matrix, depths, parts, length, width):
    return pl.pallas_call(
        adjoint_kernel,
        in_specs=[vmem()] * (2 + len(parts)),
        out_specs=vmem(),
        out_shape=jax.ShapeDtypeStruct((length, width, matrix.shape[0]), jnp.float32),
        compiler_params=params(),
        name="adjoint_mix",
    )(matrix, depths, *parts)


def unfold(main, halo, groups):
    cols = main.shape[1]
    width = cols // groups
    below = halo[:STEPS]
    above = pltpu.roll(halo[STEPS:], width, 1)
    return jnp.concatenate(
        [above] + [main] + [pltpu.roll(main, cols - a * width, 1) for a in range(1, groups)] + [below], axis=0
    )


def turn_kernel(starts, *refs):
    depths, parts, (out, held, depth_i, depth_j) = refs[:-4 - len(starts)], refs[-4 - len(starts):-4], refs[-4:]
    length, width, order = out.shape
    groups = len(parts)
    rows = length // groups
    half = order // 2
    count = half // groups
    cols = width * groups
    source = position()[2]
    for i in range(rows):
        for d, part in enumerate(parts):
            for side in range(2):
                at = pl.multiple_of(side * half + source[d] * count, 8)
                held[i, pl.ds(at, count), :] = part[pl.ds(side * count * rows + i, count, rows), :]

    no_halo = jnp.zeros((2 * STEPS, cols), jnp.float32)
    depth = unfold(depths[0][...], depths[1][...] if len(depths) > 1 else no_halo, groups)
    tall = depth.shape[0]
    lane = lax.broadcasted_iota(jnp.int32, depth.shape, 1)
    right = jnp.where(lane == width - 1, depth, pltpu.roll(depth, cols - 1, 1))
    depth_j[...] = jnp.minimum(depth, right)
    depth_i[pl.ds(0, tall - 1), :] = jnp.minimum(depth[:-1], depth[1:])
    depth_i[pl.ds(tall - 1, 1), :] = depth[tall - 1:]
    group = lane_groups(rows, cols, groups)

    def fold(ref):
        x = ref[pl.ds(starts[0], rows), :]
        for a in range(1, groups):
            x = jnp.where(group == a, pltpu.roll(ref[pl.ds(starts[a], rows), :], a * width, 1), x)
        return x

    folded_i, folded_j = fold(depth_i), fold(depth_j)
    level = lax.broadcasted_iota(jnp.int32, (half, cols), 0).astype(jnp.float32)
    for i in range(rows):
        along_i = jnp.where(level < folded_i[i:i + 1], held[i, pl.ds(0, half), :], 0.0)
        along_j = jnp.where(level < folded_j[i:i + 1], held[i, pl.ds(half, half), :], 0.0)
        turned = jnp.concatenate([along_i, along_j], axis=0).T
        for a in range(groups):
            out[a * rows + i] = turned[a * width:(a + 1) * width]


def turn_weights(starts, rows, depths, parts, order):
    groups = len(parts)
    cols = parts[0].shape[1]
    tall = depths[0].shape[0] * groups + 2 * STEPS
    return pl.pallas_call(
        functools.partial(turn_kernel, starts),
        in_specs=[vmem()] * (len(depths) + groups),
        out_specs=vmem(),
        out_shape=jax.ShapeDtypeStruct((rows * groups, cols // groups, order), jnp.float32),
        scratch_shapes=[pltpu.VMEM((rows, order, cols), jnp.float32)] + [pltpu.VMEM((tall, cols), jnp.float32)] * 2,
        compiler_params=params(),
        name="turn_weights",
    )(*depths, *parts)


def edge_masks(depths, order):
    groups = lax.axis_size("lev")
    slot = position()[0][0]
    gy = lax.axis_index("gy")
    start = (slot == 0) & (gy == 0)
    end = (slot == groups - 1) & (gy == lax.axis_size("gy") - 1)
    no_halo = jnp.zeros((2 * STEPS, depths[0].shape[1]), jnp.float32)
    masks = []
    for k, out in enumerate((start, end)):
        x = unfold(depths[k][...], depths[2 + k][...] if len(depths) > 2 else no_halo, groups)
        x = jnp.where(out, 0.0, x)
        x = jnp.broadcast_to(x[:, :1], (x.shape[0], order))
        lane = lax.broadcasted_iota(jnp.int32, x.shape, 1)
        level = lax.rem(lane, order // 2).astype(jnp.float32)
        masks.append(jnp.where((lane < order // 2) | (level < x), 1.0, 0.0))
    return masks


def spread_kernel(windows, field_rows, weight_rows, count, matrix, *refs):
    depths, refs = refs[:count], refs[count:]
    pieces = [refs[3 * k:3 * k + 3] for k in range(len(field_rows) + len(weight_rows))]
    outs, (a, b, wi, wj, masks) = refs[3 * len(pieces):-5], refs[-5:]
    width, order = pieces[0][0].shape[1:]
    half = order // 2
    _, ext, wide, _ = a.shape
    lane = lax.broadcasted_iota(jnp.int32, (wide, order), 1)
    row = lax.broadcasted_iota(jnp.int32, (wide, order), 0)
    nothing = jnp.zeros((PAD - STEPS, order), jnp.float32)
    masks[0], masks[1] = edge_masks(depths, order)

    def row_of(some, rows, r):
        piece = [k for k in range(len(rows)) if r in rows[k]][0]
        main, left, right = some[piece]
        k = rows[piece].index(r)
        side = pl.ds(k * STEPS, STEPS)
        return jnp.concatenate([nothing, left[side, :], main[k], right[side, :], nothing], axis=0)

    for n, window in enumerate(windows):
        for e, r in enumerate(window):
            a[n, e] = row_of(pieces[:len(field_rows)], field_rows, r)
            w = row_of(pieces[len(field_rows):], weight_rows, r)
            at = pl.ds(STEPS + r, 1)
            w = w * jnp.where(row == PAD - 1, masks[0, at, :], 1.0)
            w = w * jnp.where(row == PAD + width - 1, masks[1, at, :], 1.0)
            other = pltpu.roll(w, half, 1)
            wi[n, e] = jnp.where(lane < half, w, other)
            wj[n, e] = jnp.where(lane < half, other, w)

    src, dst = a, b
    for step in range(STEPS):
        begin, last = step + 1, ext - 2 - step
        for n in range(len(windows)):

            def one(r, carry, n=n, src=src, dst=dst):
                v, before = carry
                after = src[n, r + 1]
                flux = wi[n, r] * (after - v)
                across = wj[n, r] * (pltpu.roll(v, wide - 1, 0) - v)
                dst[n, r] = v + (flux - before) + (across - pltpu.roll(across, 1, 0))
                return after, flux

            v = src[n, begin]
            lax.fori_loop(begin, last + 1, one, (v, wi[n, begin - 1] * (v - src[n, begin - 1])), unroll=2)
        src, dst = dst, src

    groups = len(outs)
    count = order // groups
    rows = len(windows) * (ext - 2 * STEPS) // groups
    each = groups // len(windows)

    def mix(i, carry):
        x = jnp.concatenate(
            [src[g // each, STEPS + g % each * rows + i, pl.ds(PAD, width), :] for g in range(groups)], axis=0
        )
        y = lax.dot_general(
            matrix[...], x, (((1,), (1,)), ((), ())), precision=HIGHEST, preferred_element_type=jnp.float32
        )
        for d, out in enumerate(outs):
            out[pl.ds(i, count, rows), :] = y[d * count:(d + 1) * count]
        return carry

    lax.fori_loop(0, rows, mix, 0, unroll=4)


def spread_mix(windows, matrix, depths, field, weights, groups):
    width, order = field[0][1].shape[1:]
    cols = width * groups
    ext = len(windows[0])
    rows = len(windows) * (ext - 2 * STEPS) // groups
    shape = jax.ShapeDtypeStruct((order // groups * rows, cols), jnp.float32)
    arrays = list(depths) + [x for piece in field + weights for x in piece[1:]]
    kernel = functools.partial(
        spread_kernel, windows, [piece[0] for piece in field], [piece[0] for piece in weights], len(depths)
    )
    tall = field[0][1].shape[0] + 2 * STEPS
    return pl.pallas_call(
        kernel,
        in_specs=[vmem()] * (1 + len(arrays)),
        out_specs=[vmem()] * groups,
        out_shape=[shape] * groups,
        scratch_shapes=[pltpu.VMEM((len(windows), ext, width + 2 * PAD, order), jnp.float32)] * 4
        + [pltpu.VMEM((2, tall, order), jnp.float32)],
        compiler_params=params(),
        name="spread_mix",
    )(matrix, *arrays)


RESULT_STEPS = 4


def result_kernel(runs, gain, mask, *refs):
    parts, (out, done, out_sems) = refs[:-3], refs[-3:]
    fields, levels, _, cols = gain.shape
    groups = len(parts)
    rows = done.shape[2] // groups
    some = levels // RESULT_STEPS
    slots = position()[1]
    group = lane_groups(rows, cols, groups)

    def of_slot(slot, at):
        x = parts[0][pl.ds(at, rows), :]
        for d in range(1, groups):
            x = jnp.where(slots[d] == slot, parts[d][pl.ds(at, rows), :], x)
        return x

    stored = []
    for step in range(RESULT_STEPS):
        for level in range(step * some, (step + 1) * some):
            ocean = jnp.concatenate([mask[level, pl.ds(*run), :] for run in runs], axis=0).astype(jnp.float32)
            for field in range(fields):
                at = (field * levels + level) * rows
                blocks = swap([of_slot(slot, at) for slot in range(groups)], group, cols // groups)
                gains = jnp.concatenate([gain[field, level, pl.ds(*run), :] for run in runs], axis=0)
                done[field, level] = ocean * gains * jnp.concatenate(blocks, axis=0)
        these = pl.ds(step * some, some)
        pairs, at = [], 0
        for first, number in runs:
            pairs.append((done.at[:, these, pl.ds(at, number)], out.at[:, these, pl.ds(first, number)]))
            at += number
        stored += copies(pairs, out_sems.at[step])
    for copy in stored:
        copy.wait()


def result(runs, gain, mask, parts, before):
    fields, levels, _, cols = gain.shape
    groups = len(parts)
    rows = sum(number for _, number in runs)
    anywhere = pl.BlockSpec(memory_space=pl.ANY)
    more = [] if before is None else [before]

    def kernel(gain, mask, *refs):
        result_kernel(runs, gain, mask, *refs[:groups], *refs[groups + len(more):])

    return pl.pallas_call(
        kernel,
        in_specs=[vmem()] * (2 + groups) + [anywhere] * len(more),
        out_specs=anywhere,
        out_shape=jax.ShapeDtypeStruct(gain.shape, jnp.float32),
        scratch_shapes=[
            pltpu.VMEM((fields, levels, rows, cols), jnp.float32),
            pltpu.SemaphoreType.DMA((RESULT_STEPS, len(runs))),
        ],
        input_output_aliases={2 + groups: 0} if more else {},
        compiler_params=params(),
        name="result",
    )(gain, mask, *parts, *more)


def shards(increment, norm_gain, diffusion_i, diffusion_j, sea_mask, coupling):
    devices = lax.axis_size("lev")
    gx_size = lax.axis_size("gx")
    gy_size = lax.axis_size("gy")
    _, levels, length, cols = increment.shape
    width = cols // devices
    rows = length // devices
    order = coupling.shape[0]
    to = [lax.rem(lax.axis_index("lev") + d, devices) for d in range(devices)]
    source = [lax.rem(lax.axis_index("lev") + devices - d, devices) for d in range(devices)]

    def shift(x, d):
        return lax.ppermute(x, "lev", [(k, (k + d) % devices) for k in range(devices)])

    def exchange(parts):
        return [parts[0]] + [shift(parts[d], d) for d in range(1, devices)]

    up = [((k + 1) % gx_size, k) for k in range(gx_size)]
    down = [(b, a) for a, b in up]
    ring = [(devices - 1 - slot if y % 2 else slot) * gy_size + y for y in range(gy_size) for slot in range(devices)]
    ahead = list(zip(ring, ring[1:] + ring[:1]))
    back = [(b, a) for a, b in ahead]

    def halo_i(first, last):
        if gx_size == 2:
            size = first.shape[0]
            both = lax.ppermute(jnp.concatenate([first, last], axis=0), "gx", up)
            return both[size:], both[:size]
        return lax.ppermute(last, "gx", down), lax.ppermute(first, "gx", up)

    def halo_j(first, last):
        return lax.ppermute(last, ("lev", "gy"), ahead), lax.ppermute(first, ("lev", "gy"), back)

    def flat(x):
        return x.reshape(-1, x.shape[-1])

    def cut(x, *sizes):
        return lax.split(x, sizes, 0)

    quarter = length // 4
    some = 2 * quarter // devices
    half = devices // 2
    inner = (quarter, 2 * quarter)
    outer = ((0, quarter), (3 * quarter, quarter))
    inner_rows = list(range(quarter - STEPS, 3 * quarter + STEPS))
    outer_rows = list(range(-STEPS, quarter - STEPS)) + list(range(3 * quarter + STEPS, length + STEPS))
    inner_starts = [quarter + a * len(inner_rows) // devices for a in range(devices)]
    outer_starts = [a * some for a in range(half)] + [3 * quarter + 2 * STEPS + a * some for a in range(half)]
    windows = [list(range(-STEPS, quarter + STEPS)), list(range(3 * quarter - STEPS, length + STEPS))]

    inner_size = len(inner_rows) // devices
    inner_messages = weight_messages(inner_starts, inner_size, diffusion_i, diffusion_j, [sea_mask])
    inner_parts = exchange(inner_messages)
    inner_messages, edge_i, edge_j, increment, norm_gain = lax.optimization_barrier(
        (inner_messages, diffusion_i, diffusion_j, increment, norm_gain)
    )
    halos = halo_i(
        *[
            jnp.concatenate([flat(edge_i[:, at]), flat(edge_j[:, at])], axis=0)
            for at in (slice(0, STEPS), slice(-STEPS, None))
        ]
    )
    messages = scaled_messages(increment, norm_gain, sea_mask, devices)
    scaled = exchange(messages)
    messages, halos = lax.optimization_barrier((messages, halos))
    outer_messages = weight_messages(outer_starts, some, diffusion_i, diffusion_j, halos=halos)

    depth = sum(part[2 * levels * inner_size:] for part in inner_parts)
    here = turn_weights(inner_starts, inner_size, [depth], inner_parts, order)
    left, right = halo_j(
        jnp.concatenate([flat(here[:, :STEPS]), depth], axis=0),
        flat(here[:, -STEPS:]),
    )
    right, right_depth = cut(right, len(inner_rows) * STEPS, rows)

    balance = jnp.eye(order, dtype=jnp.float32) + coupling
    by_device = balance.reshape(2, devices, levels, order)
    adjoint = jnp.concatenate([by_device[:, s].reshape(2 * levels, order) for s in source], axis=0).T
    forward = jnp.concatenate([by_device[:, t].reshape(2 * levels, order) for t in to], axis=0)

    scaled[1], outer_messages = lax.optimization_barrier((scaled[1], outer_messages))
    middle = devices // 2
    early = shift(outer_messages[middle], middle)
    mixed = adjoint_mix(adjoint, depth, scaled, length, width)
    edges = flat(mixed[:, :STEPS]), flat(mixed[:, -STEPS:])
    edges, inner_weights = lax.optimization_barrier((edges, (here, left, right)))
    left, right = halo_j(*edges)
    left, right, outer_messages, early = lax.optimization_barrier((left, right, outer_messages, early))
    outer_parts = [
        early if d == middle else shift(outer_messages[d], d) if d else outer_messages[0] for d in range(devices)
    ]
    field = [(list(range(length)), mixed, left, right)]
    weights = [(inner_rows, *inner_weights)]
    depths = [depth, right_depth]
    inner_mixed = spread_mix([inner_rows], forward, depths, field, weights, devices)
    _, upper, lower = lax.optimization_barrier((left, mixed[:STEPS], mixed[-STEPS:]))
    _, outer_parts = lax.optimization_barrier((inner_mixed[0], outer_parts))
    inner_mixed = exchange(inner_mixed)
    out = result((inner,), norm_gain, sea_mask, inner_mixed, None)

    above, below = halo_i(
        jnp.concatenate([flat(upper), depth[:STEPS]], axis=0),
        jnp.concatenate([flat(lower), depth[-STEPS:]], axis=0),
    )
    above, above_depth = cut(above, STEPS * width, STEPS)
    below, below_depth = cut(below, STEPS * width, STEPS)
    halo_depth = jnp.concatenate([below_depth, above_depth], axis=0)
    halo = jnp.concatenate([above, below], axis=0).reshape(2 * STEPS, width, order)
    here = turn_weights(outer_starts, some, [depth, halo_depth], outer_parts, order)
    left, right = halo_j(
        jnp.concatenate([flat(here[:, :STEPS]), flat(halo[:, :STEPS]), halo_depth], axis=0),
        jnp.concatenate([flat(here[:, -STEPS:]), flat(halo[:, -STEPS:])], axis=0),
    )
    sizes = len(outer_rows) * STEPS, 2 * STEPS * STEPS
    left, halo_left = cut(left, *sizes)
    right, halo_right, right_halo_depth = cut(right, *sizes, 2 * STEPS)
    weights.append((outer_rows, here, left, right))
    field.append((list(range(-STEPS, 0)) + list(range(length, length + STEPS)), halo, halo_left, halo_right))
    depths += [halo_depth, right_halo_depth]
    outer_mixed = exchange(spread_mix(windows, forward, depths, field, weights, devices))
    return result(outer, norm_gain, sea_mask, outer_mixed, out)


def solution(mesh):
    return jax.shard_map(
        shards,
        mesh=mesh,
        in_specs=(
            P(None, "lev", "gx", "gy"),
            P(None, "lev", "gx", "gy"),
            P("lev", "gx", "gy"),
            P("lev", "gx", "gy"),
            P("lev", "gx", "gy"),
            P(),
        ),
        out_specs=P(None, "lev", "gx", "gy"),
        check_vma=False,
    )
```

```python
import functools

import jax
import jax.numpy as jnp
from jax import lax
from jax.experimental import pallas as pl
from jax.experimental.pallas import tpu as pltpu
from jax.sharding import PartitionSpec as P

ITERS = 2
STEPS = 2 * ITERS
PAD = 8
VMEM_LIMIT = 40 * 1024 * 1024
VMEM_WHOLE = 60 * 1024 * 1024
HIGHEST = lax.Precision.HIGHEST


def params(limit=VMEM_LIMIT):
    return pltpu.CompilerParams(vmem_limit_bytes=limit)


def smem():
    return pl.BlockSpec(memory_space=pltpu.SMEM)


def vmem():
    return pl.BlockSpec(memory_space=pltpu.VMEM)


def distances(devices):
    return [0, devices // 2] + [d for d in range(1, devices) if d != devices // 2]


def position():
    devices = lax.axis_size("lev")
    me = lax.axis_index("lev")
    flipped = lax.rem(lax.axis_index("gy"), 2) == 1

    def slot(lev):
        return jnp.where(flipped, devices - 1 - lev, lev)

    to = [lax.rem(me + d, devices) for d in distances(devices)]
    source = [lax.rem(me + devices - d, devices) for d in distances(devices)]
    return [slot(lev) for lev in to], [slot(lev) for lev in source], source


def swap(blocks, group, width):
    blocks = list(blocks)
    cols = blocks[0].shape[1]
    bit = len(blocks) // 2
    while bit:
        shift = bit * width
        low = (group & bit) == 0
        for a in range(len(blocks)):
            if not a & bit:
                x, y = blocks[a], blocks[a + bit]
                blocks[a] = jnp.where(low, x, pltpu.roll(y, shift, 1))
                blocks[a + bit] = jnp.where(low, pltpu.roll(x, cols - shift, 1), y)
        bit //= 2
    return blocks


def lane_groups(rows, cols, groups):
    return lax.broadcasted_iota(jnp.int32, (rows, cols), 1) // (cols // groups)


def copies(pairs, sems):
    made = [pltpu.make_async_copy(src, dst, sems.at[k]) for k, (src, dst) in enumerate(pairs)]
    for copy in made:
        copy.start()
    return made


SCALED_STEPS = 4


def scaled_kernel(increment, gain, mask, *refs):
    outs, (inc, gn, sea, held, sems, out_sems) = refs[:-6], refs[-6:]
    fields, levels, length, cols = increment.shape
    groups = len(outs)
    rows = length // groups
    some = levels // SCALED_STEPS
    group = lane_groups(rows, cols, groups)
    fetched = []
    for step in range(SCALED_STEPS):
        part = pl.ds(step * some, some)
        fetched.append(
            copies(
                [
                    (increment.at[:, part], inc.at[:, part]),
                    (gain.at[:, part], gn.at[:, part]),
                    (mask.at[part], sea.at[part]),
                ],
                sems.at[step],
            )
        )

    depth = jnp.zeros((length, cols), jnp.float32)

    def put(at, x):
        blocks = swap([x[a * rows:(a + 1) * rows] for a in range(groups)], group, cols // groups)
        for slot, block in enumerate(blocks):
            held[slot, pl.ds(at, rows), :] = block

    for step in range(SCALED_STEPS):
        for copy in fetched[step]:
            copy.wait()
        for level in range(step * some, (step + 1) * some):
            ocean = sea[level].astype(jnp.float32)
            depth = depth + ocean
            for field in range(fields):
                put((field * levels + level) * rows, ocean * gn[field, level] * inc[field, level])
    put(fields * levels * rows, depth)
    slots = position()[0]
    for copy in copies([(held.at[slots[d]], out) for d, out in enumerate(outs)], out_sems):
        copy.wait()


def scaled_messages(increment, gain, mask, groups):
    fields, levels, length, cols = increment.shape
    shape = ((fields * levels + 1) * length // groups, cols)
    return pl.pallas_call(
        scaled_kernel,
        in_specs=[pl.BlockSpec(memory_space=pl.ANY)] * 3,
        out_specs=[pl.BlockSpec(memory_space=pl.ANY)] * groups,
        out_shape=[jax.ShapeDtypeStruct(shape, jnp.float32)] * groups,
        scratch_shapes=[
            pltpu.VMEM(increment.shape, jnp.float32),
            pltpu.VMEM(gain.shape, jnp.float32),
            pltpu.VMEM(mask.shape, mask.dtype),
            pltpu.VMEM((groups, *shape), jnp.float32),
            pltpu.SemaphoreType.DMA((SCALED_STEPS, 3)),
            pltpu.SemaphoreType.DMA((groups,)),
        ],
        compiler_params=params(VMEM_WHOLE),
        name="scaled_messages",
    )(increment, gain, mask)


def pack_kernel(starts, along_i, along_j, *refs):
    levels, length, cols = along_i.shape
    groups = len(starts)
    halos, outs, (held, slots_held, sems) = refs[:-3 - groups], refs[-3 - groups:-3], refs[-3:]
    rows = outs[0].shape[0] // (2 * levels)
    group = lane_groups(rows, cols, groups)
    unroll = held.shape[0]
    for side, weight in enumerate((along_i, along_j)):
        for outer in range(levels // unroll):
            packed = []
            for k in range(unroll):
                level = outer * unroll + k
                if halos:
                    for halo, at in zip(halos, (0, STEPS + length)):
                        held[k, pl.ds(at, STEPS), :] = halo[pl.ds((side * levels + level) * STEPS, STEPS), :]
                    held[k, pl.ds(STEPS, length), :] = weight[level]
                    blocks = [held[k, pl.ds(start, rows), :] for start in starts]
                else:
                    blocks = [weight[level, pl.ds(start - STEPS, rows), :] for start in starts]
                packed.append(swap(blocks, group, cols // groups))
            at = (side * levels + outer * unroll) * rows
            for slot in range(groups):
                block = jnp.concatenate([packed[k][slot] for k in range(unroll)], axis=0)
                slots_held[slot, pl.ds(at, unroll * rows), :] = block
    slots = position()[0]
    for copy in copies([(slots_held.at[slots[d]], out) for d, out in enumerate(outs)], sems):
        copy.wait()


def weight_messages(starts, rows, along_i, along_j, halos=()):
    levels, length, cols = along_i.shape
    groups = len(starts)
    shape = (2 * levels * rows, cols)
    unroll = 4
    return list(
        pl.pallas_call(
            functools.partial(pack_kernel, starts),
            in_specs=[vmem()] * (2 + len(halos)),
            out_specs=[pl.BlockSpec(memory_space=pl.ANY)] * groups,
            out_shape=[jax.ShapeDtypeStruct(shape, jnp.float32)] * groups,
            scratch_shapes=[
                pltpu.VMEM((unroll, length + 2 * STEPS, cols), jnp.float32),
                pltpu.VMEM((groups, *shape), jnp.float32),
                pltpu.SemaphoreType.DMA((groups,)),
            ],
            compiler_params=params(),
            name="weight_messages",
        )(along_i, along_j, *halos)
    )


def adjoint_kernel(matrix, *refs):
    parts, out, depths = refs[:-2], refs[-2], refs[-1]
    length, width, order = out.shape
    groups = len(parts)
    rows = length // groups
    cols = groups * width
    count = order // groups
    depths[...] = sum(part[pl.ds(count * rows, rows), :] for part in parts)
    level = lax.rem(lax.broadcasted_iota(jnp.int32, (order, cols), 0), order // 2).astype(jnp.float32)

    def one(i, carry):
        x = jnp.concatenate([part[pl.ds(i, count, rows), :] for part in parts], axis=0)
        depth = depths[pl.ds(i, 1), :]
        y = jnp.dot(matrix[...], x, precision=HIGHEST, preferred_element_type=jnp.float32)
        y = jnp.where(level < depth, y, 0.0).T
        for a in range(groups):
            out[a * rows + i] = y[a * width:(a + 1) * width]
        return carry

    lax.fori_loop(0, rows, one, 0, unroll=4)


def adjoint_mix(matrix, parts, length, width):
    return pl.pallas_call(
        adjoint_kernel,
        in_specs=[vmem()] * (1 + len(parts)),
        out_specs=[vmem()] * 2,
        out_shape=[
            jax.ShapeDtypeStruct((length, width, matrix.shape[0]), jnp.float32),
            jax.ShapeDtypeStruct((length // len(parts), width * len(parts)), jnp.float32),
        ],
        compiler_params=params(),
        name="adjoint_mix",
    )(matrix, *parts)


def unfold(main, halo, groups):
    cols = main.shape[1]
    width = cols // groups
    below = halo[:STEPS]
    above = pltpu.roll(halo[STEPS:], width, 1)
    return jnp.concatenate(
        [above] + [main] + [pltpu.roll(main, cols - a * width, 1) for a in range(1, groups)] + [below], axis=0
    )


def turn_kernel(starts, *refs):
    depths, parts, (out, held, depth_i, depth_j) = refs[:-4 - len(starts)], refs[-4 - len(starts):-4], refs[-4:]
    length, width, order = out.shape
    groups = len(parts)
    rows = length // groups
    half = order // 2
    count = half // groups
    cols = width * groups
    source = position()[2]
    for i in range(rows):
        for d, part in enumerate(parts):
            for side in range(2):
                at = pl.multiple_of(side * half + source[d] * count, 8)
                held[i, pl.ds(at, count), :] = part[pl.ds(side * count * rows + i, count, rows), :]

    no_halo = jnp.zeros((2 * STEPS, cols), jnp.float32)
    depth = unfold(depths[0][...], depths[1][...] if len(depths) > 1 else no_halo, groups)
    tall = depth.shape[0]
    lane = lax.broadcasted_iota(jnp.int32, depth.shape, 1)
    right = jnp.where(lane == width - 1, depth, pltpu.roll(depth, cols - 1, 1))
    depth_j[...] = jnp.minimum(depth, right)
    depth_i[pl.ds(0, tall - 1), :] = jnp.minimum(depth[:-1], depth[1:])
    depth_i[pl.ds(tall - 1, 1), :] = depth[tall - 1:]
    group = lane_groups(rows, cols, groups)

    def fold(ref):
        x = ref[pl.ds(starts[0], rows), :]
        for a in range(1, groups):
            x = jnp.where(group == a, pltpu.roll(ref[pl.ds(starts[a], rows), :], a * width, 1), x)
        return x

    folded_i, folded_j = fold(depth_i), fold(depth_j)
    level = lax.broadcasted_iota(jnp.int32, (half, cols), 0).astype(jnp.float32)
    for i in range(rows):
        along_i = jnp.where(level < folded_i[i:i + 1], held[i, pl.ds(0, half), :], 0.0)
        along_j = jnp.where(level < folded_j[i:i + 1], held[i, pl.ds(half, half), :], 0.0)
        turned = jnp.concatenate([along_i, along_j], axis=0).T
        for a in range(groups):
            out[a * rows + i] = turned[a * width:(a + 1) * width]


def turn_weights(starts, rows, depths, parts, order):
    groups = len(parts)
    cols = parts[0].shape[1]
    tall = depths[0].shape[0] * groups + 2 * STEPS
    return pl.pallas_call(
        functools.partial(turn_kernel, starts),
        in_specs=[vmem()] * (len(depths) + groups),
        out_specs=vmem(),
        out_shape=jax.ShapeDtypeStruct((rows * groups, cols // groups, order), jnp.float32),
        scratch_shapes=[pltpu.VMEM((rows, order, cols), jnp.float32)] + [pltpu.VMEM((tall, cols), jnp.float32)] * 2,
        compiler_params=params(),
        name="turn_weights",
    )(*depths, *parts)


def edge_masks(depths, order):
    groups = lax.axis_size("lev")
    slot = position()[0][0]
    gy = lax.axis_index("gy")
    start = (slot == 0) & (gy == 0)
    end = (slot == groups - 1) & (gy == lax.axis_size("gy") - 1)
    no_halo = jnp.zeros((2 * STEPS, depths[0].shape[1]), jnp.float32)
    masks = []
    for k, out in enumerate((start, end)):
        x = unfold(depths[k][...], depths[2 + k][...] if len(depths) > 2 else no_halo, groups)
        x = jnp.where(out, 0.0, x)
        x = jnp.broadcast_to(x[:, :1], (x.shape[0], order))
        lane = lax.broadcasted_iota(jnp.int32, x.shape, 1)
        level = lax.rem(lane, order // 2).astype(jnp.float32)
        masks.append(jnp.where((lane < order // 2) | (level < x), 1.0, 0.0))
    return masks


def spread_kernel(windows, field_rows, weight_rows, count, matrix, *refs):
    depths, refs = refs[:count], refs[count:]
    pieces = [refs[3 * k:3 * k + 3] for k in range(len(field_rows) + len(weight_rows))]
    outs, (a, b, wi, wj, masks) = refs[3 * len(pieces):-5], refs[-5:]
    width, order = pieces[0][0].shape[1:]
    half = order // 2
    _, ext, wide, _ = a.shape
    lane = lax.broadcasted_iota(jnp.int32, (wide, order), 1)
    row = lax.broadcasted_iota(jnp.int32, (wide, order), 0)
    nothing = jnp.zeros((PAD - STEPS, order), jnp.float32)
    masks[0], masks[1] = edge_masks(depths, order)

    def row_of(some, rows, r):
        piece = [k for k in range(len(rows)) if r in rows[k]][0]
        main, left, right = some[piece]
        k = rows[piece].index(r)
        side = pl.ds(k * STEPS, STEPS)
        return jnp.concatenate([nothing, left[side, :], main[k], right[side, :], nothing], axis=0)

    for n, window in enumerate(windows):
        for e, r in enumerate(window):
            a[n, e] = row_of(pieces[:len(field_rows)], field_rows, r)
            w = row_of(pieces[len(field_rows):], weight_rows, r)
            at = pl.ds(STEPS + r, 1)
            w = w * jnp.where(row == PAD - 1, masks[0, at, :], 1.0)
            w = w * jnp.where(row == PAD + width - 1, masks[1, at, :], 1.0)
            other = pltpu.roll(w, half, 1)
            wi[n, e] = jnp.where(lane < half, w, other)
            wj[n, e] = jnp.where(lane < half, other, w)

    src, dst = a, b
    for step in range(STEPS):
        begin, last = step + 1, ext - 2 - step
        for n in range(len(windows)):

            def one(r, carry, n=n, src=src, dst=dst):
                v, before = carry
                after = src[n, r + 1]
                flux = wi[n, r] * (after - v)
                across = wj[n, r] * (pltpu.roll(v, wide - 1, 0) - v)
                dst[n, r] = v + (flux - before) + (across - pltpu.roll(across, 1, 0))
                return after, flux

            v = src[n, begin]
            lax.fori_loop(begin, last + 1, one, (v, wi[n, begin - 1] * (v - src[n, begin - 1])), unroll=2)
        src, dst = dst, src

    groups = len(outs)
    count = order // groups
    rows = len(windows) * (ext - 2 * STEPS) // groups
    each = groups // len(windows)

    def mix(i, carry):
        x = jnp.concatenate(
            [src[g // each, STEPS + g % each * rows + i, pl.ds(PAD, width), :] for g in range(groups)], axis=0
        )
        y = lax.dot_general(
            matrix[...], x, (((1,), (1,)), ((), ())), precision=HIGHEST, preferred_element_type=jnp.float32
        )
        for d, out in enumerate(outs):
            out[pl.ds(i, count, rows), :] = y[d * count:(d + 1) * count]
        return carry

    lax.fori_loop(0, rows, mix, 0, unroll=4)


def spread_mix(windows, matrix, depths, field, weights, groups):
    width, order = field[0][1].shape[1:]
    cols = width * groups
    ext = len(windows[0])
    rows = len(windows) * (ext - 2 * STEPS) // groups
    shape = jax.ShapeDtypeStruct((order // groups * rows, cols), jnp.float32)
    arrays = list(depths) + [x for piece in field + weights for x in piece[1:]]
    kernel = functools.partial(
        spread_kernel, windows, [piece[0] for piece in field], [piece[0] for piece in weights], len(depths)
    )
    tall = field[0][1].shape[0] + 2 * STEPS
    return pl.pallas_call(
        kernel,
        in_specs=[vmem()] * (1 + len(arrays)),
        out_specs=[vmem()] * groups,
        out_shape=[shape] * groups,
        scratch_shapes=[pltpu.VMEM((len(windows), ext, width + 2 * PAD, order), jnp.float32)] * 4
        + [pltpu.VMEM((2, tall, order), jnp.float32)],
        compiler_params=params(),
        name="spread_mix",
    )(matrix, *arrays)


RESULT_STEPS = 4


def result_kernel(runs, gain, mask, *refs):
    parts, (out, done, out_sems) = refs[:-3], refs[-3:]
    fields, levels, _, cols = gain.shape
    groups = len(parts)
    rows = done.shape[2] // groups
    some = levels // RESULT_STEPS
    slots = position()[1]
    group = lane_groups(rows, cols, groups)

    def of_slot(slot, at):
        x = parts[0][pl.ds(at, rows), :]
        for d in range(1, groups):
            x = jnp.where(slots[d] == slot, parts[d][pl.ds(at, rows), :], x)
        return x

    stored = []
    for step in range(RESULT_STEPS):
        for level in range(step * some, (step + 1) * some):
            ocean = jnp.concatenate([mask[level, pl.ds(*run), :] for run in runs], axis=0).astype(jnp.float32)
            for field in range(fields):
                at = (field * levels + level) * rows
                blocks = swap([of_slot(slot, at) for slot in range(groups)], group, cols // groups)
                gains = jnp.concatenate([gain[field, level, pl.ds(*run), :] for run in runs], axis=0)
                done[field, level] = ocean * gains * jnp.concatenate(blocks, axis=0)
        these = pl.ds(step * some, some)
        pairs, at = [], 0
        for first, number in runs:
            pairs.append((done.at[:, these, pl.ds(at, number)], out.at[:, these, pl.ds(first, number)]))
            at += number
        stored += copies(pairs, out_sems.at[step])
    for copy in stored:
        copy.wait()


def result(runs, gain, mask, parts, before):
    fields, levels, _, cols = gain.shape
    groups = len(parts)
    rows = sum(number for _, number in runs)
    anywhere = pl.BlockSpec(memory_space=pl.ANY)
    more = [] if before is None else [before]

    def kernel(gain, mask, *refs):
        result_kernel(runs, gain, mask, *refs[:groups], *refs[groups + len(more):])

    return pl.pallas_call(
        kernel,
        in_specs=[vmem()] * (2 + groups) + [anywhere] * len(more),
        out_specs=anywhere,
        out_shape=jax.ShapeDtypeStruct(gain.shape, jnp.float32),
        scratch_shapes=[
            pltpu.VMEM((fields, levels, rows, cols), jnp.float32),
            pltpu.SemaphoreType.DMA((RESULT_STEPS, len(runs))),
        ],
        input_output_aliases={2 + groups: 0} if more else {},
        compiler_params=params(),
        name="result",
    )(gain, mask, *parts, *more)


def shards(increment, norm_gain, diffusion_i, diffusion_j, sea_mask, coupling):
    devices = lax.axis_size("lev")
    gx_size = lax.axis_size("gx")
    gy_size = lax.axis_size("gy")
    _, levels, length, cols = increment.shape
    width = cols // devices
    rows = length // devices
    order = coupling.shape[0]
    to = [lax.rem(lax.axis_index("lev") + d, devices) for d in distances(devices)]
    source = [lax.rem(lax.axis_index("lev") + devices - d, devices) for d in distances(devices)]

    def shift(x, d):
        return lax.ppermute(x, "lev", [(k, (k + d) % devices) for k in range(devices)])

    def exchange(parts):
        return [parts[0]] + [shift(x, d) for x, d in zip(parts[1:], distances(devices)[1:])]

    up = [((k + 1) % gx_size, k) for k in range(gx_size)]
    down = [(b, a) for a, b in up]
    ring = [(devices - 1 - slot if y % 2 else slot) * gy_size + y for y in range(gy_size) for slot in range(devices)]
    ahead = list(zip(ring, ring[1:] + ring[:1]))
    back = [(b, a) for a, b in ahead]

    def halo_i(first, last):
        if gx_size == 2:
            size = first.shape[0]
            both = lax.ppermute(jnp.concatenate([first, last], axis=0), "gx", up)
            return both[size:], both[:size]
        return lax.ppermute(last, "gx", down), lax.ppermute(first, "gx", up)

    def halo_j(first, last):
        return lax.ppermute(last, ("lev", "gy"), ahead), lax.ppermute(first, ("lev", "gy"), back)

    def flat(x):
        return x.reshape(-1, x.shape[-1])

    def cut(x, *sizes):
        return lax.split(x, sizes, 0)

    quarter = length // 4
    some = 2 * quarter // devices
    half = devices // 2
    inner = (quarter, 2 * quarter)
    outer = ((0, quarter), (3 * quarter, quarter))
    inner_rows = list(range(quarter - STEPS, 3 * quarter + STEPS))
    outer_rows = list(range(-STEPS, quarter - STEPS)) + list(range(3 * quarter + STEPS, length + STEPS))
    inner_starts = [quarter + a * len(inner_rows) // devices for a in range(devices)]
    outer_starts = [a * some for a in range(half)] + [3 * quarter + 2 * STEPS + a * some for a in range(half)]
    windows = [list(range(-STEPS, quarter + STEPS)), list(range(3 * quarter - STEPS, length + STEPS))]

    messages = scaled_messages(increment, norm_gain, sea_mask, devices)
    scaled = exchange(messages)
    _, diffusion_i, diffusion_j = lax.optimization_barrier((messages[0], diffusion_i, diffusion_j))
    inner_size = len(inner_rows) // devices
    inner_messages = weight_messages(inner_starts, inner_size, diffusion_i, diffusion_j)
    inner_parts = exchange(inner_messages)
    _, edge_i, edge_j = lax.optimization_barrier((inner_messages[0], diffusion_i, diffusion_j))
    halos = halo_i(
        *[
            jnp.concatenate([flat(edge_i[:, at]), flat(edge_j[:, at])], axis=0)
            for at in (slice(0, STEPS), slice(-STEPS, None))
        ]
    )
    outer_messages = weight_messages(outer_starts, some, diffusion_i, diffusion_j, halos)

    balance = jnp.eye(order, dtype=jnp.float32) + coupling
    by_device = balance.reshape(2, devices, levels, order)
    adjoint = jnp.concatenate([by_device[:, s].reshape(2 * levels, order) for s in source], axis=0).T
    forward = jnp.concatenate([by_device[:, t].reshape(2 * levels, order) for t in to], axis=0)

    mixed, depth = adjoint_mix(adjoint, scaled, length, width)
    left, right = halo_j(jnp.concatenate([flat(mixed[:, :STEPS]), depth], axis=0), flat(mixed[:, -STEPS:]))
    right, right_depth = cut(right, length * STEPS, rows)
    _, upper, lower = lax.optimization_barrier((left, mixed[:STEPS], mixed[-STEPS:]))
    inner_parts, left, right = lax.optimization_barrier((inner_parts, left, right))
    field = [(list(range(length)), mixed, left, right)]

    inner_parts[1], outer_messages = lax.optimization_barrier((inner_parts[1], outer_messages))
    early = shift(outer_messages[1], devices // 2)
    here = turn_weights(inner_starts, inner_size, [depth], inner_parts, order)
    left, right = halo_j(flat(here[:, :STEPS]), flat(here[:, -STEPS:]))
    left, right, outer_messages, early = lax.optimization_barrier((left, right, outer_messages, early))
    weights = [(inner_rows, here, left, right)]
    own, _, *others = outer_messages
    outer_parts = [own, early] + [shift(x, d) for x, d in zip(others, distances(devices)[2:])]
    depths = [depth, right_depth]
    inner_mixed = spread_mix([inner_rows], forward, depths, field, weights, devices)
    _, outer_parts = lax.optimization_barrier((inner_mixed[0], outer_parts))
    inner_mixed = exchange(inner_mixed)
    out = result((inner,), norm_gain, sea_mask, inner_mixed, None)

    above, below = halo_i(
        jnp.concatenate([flat(upper), depth[:STEPS]], axis=0),
        jnp.concatenate([flat(lower), depth[-STEPS:]], axis=0),
    )
    above, above_depth = cut(above, STEPS * width, STEPS)
    below, below_depth = cut(below, STEPS * width, STEPS)
    halo_depth = jnp.concatenate([below_depth, above_depth], axis=0)
    halo = jnp.concatenate([above, below], axis=0).reshape(2 * STEPS, width, order)
    here = turn_weights(outer_starts, some, [depth, halo_depth], outer_parts, order)
    left, right = halo_j(
        jnp.concatenate([flat(here[:, :STEPS]), flat(halo[:, :STEPS]), halo_depth], axis=0),
        jnp.concatenate([flat(here[:, -STEPS:]), flat(halo[:, -STEPS:])], axis=0),
    )
    sizes = len(outer_rows) * STEPS, 2 * STEPS * STEPS
    left, halo_left = cut(left, *sizes)
    right, halo_right, right_halo_depth = cut(right, *sizes, 2 * STEPS)
    weights.append((outer_rows, here, left, right))
    field.append((list(range(-STEPS, 0)) + list(range(length, length + STEPS)), halo, halo_left, halo_right))
    depths += [halo_depth, right_halo_depth]
    outer_mixed = exchange(spread_mix(windows, forward, depths, field, weights, devices))
    return result(outer, norm_gain, sea_mask, outer_mixed, out)


def solution(mesh):
    return jax.shard_map(
        shards,
        mesh=mesh,
        in_specs=(
            P(None, "lev", "gx", "gy"),
            P(None, "lev", "gx", "gy"),
            P("lev", "gx", "gy"),
            P("lev", "gx", "gy"),
            P("lev", "gx", "gy"),
            P(),
        ),
        out_specs=P(None, "lev", "gx", "gy"),
        check_vma=False,
    )
```

```python
import functools

import jax
import jax.numpy as jnp
from jax import lax
from jax.experimental import pallas as pl
from jax.experimental.pallas import tpu as pltpu
from jax.sharding import PartitionSpec as P

ITERS = 2
STEPS = 2 * ITERS
PAD = 8
VMEM_LIMIT = 40 * 1024 * 1024
VMEM_WHOLE = 60 * 1024 * 1024
HIGHEST = lax.Precision.HIGHEST


def params(limit=VMEM_LIMIT):
    return pltpu.CompilerParams(vmem_limit_bytes=limit)


def smem():
    return pl.BlockSpec(memory_space=pltpu.SMEM)


def vmem():
    return pl.BlockSpec(memory_space=pltpu.VMEM)


def distances(devices):
    return [0, devices // 2] + [d for d in range(1, devices) if d != devices // 2]


def position():
    devices = lax.axis_size("lev")
    me = lax.axis_index("lev")
    flipped = lax.rem(lax.axis_index("gy"), 2) == 1

    def slot(lev):
        return jnp.where(flipped, devices - 1 - lev, lev)

    to = [lax.rem(me + d, devices) for d in distances(devices)]
    source = [lax.rem(me + devices - d, devices) for d in distances(devices)]
    return [slot(lev) for lev in to], [slot(lev) for lev in source], source


def swap(blocks, group, width):
    blocks = list(blocks)
    cols = blocks[0].shape[1]
    bit = len(blocks) // 2
    while bit:
        shift = bit * width
        low = (group & bit) == 0
        for a in range(len(blocks)):
            if not a & bit:
                x, y = blocks[a], blocks[a + bit]
                blocks[a] = jnp.where(low, x, pltpu.roll(y, shift, 1))
                blocks[a + bit] = jnp.where(low, pltpu.roll(x, cols - shift, 1), y)
        bit //= 2
    return blocks


def lane_groups(rows, cols, groups):
    return lax.broadcasted_iota(jnp.int32, (rows, cols), 1) // (cols // groups)


def copies(pairs, sems):
    made = [pltpu.make_async_copy(src, dst, sems.at[k]) for k, (src, dst) in enumerate(pairs)]
    for copy in made:
        copy.start()
    return made


SCALED_STEPS = 4


def scaled_kernel(increment, gain, mask, *refs):
    outs, (inc, gn, sea, held, sems, out_sems) = refs[:-6], refs[-6:]
    fields, levels, length, cols = increment.shape
    groups = len(outs)
    rows = length // groups
    some = levels // SCALED_STEPS
    group = lane_groups(rows, cols, groups)
    fetched = []
    for step in range(SCALED_STEPS):
        part = pl.ds(step * some, some)
        fetched.append(
            copies(
                [
                    (increment.at[:, part], inc.at[:, part]),
                    (gain.at[:, part], gn.at[:, part]),
                    (mask.at[part], sea.at[part]),
                ],
                sems.at[step],
            )
        )

    for step in range(SCALED_STEPS):
        for copy in fetched[step]:
            copy.wait()

        def one(level, carry):
            ocean = sea[level].astype(jnp.float32)
            for field in range(fields):
                at = pl.multiple_of((field * levels + level) * rows, rows)
                x = ocean * gn[field, level] * inc[field, level]
                blocks = swap([x[a * rows:(a + 1) * rows] for a in range(groups)], group, cols // groups)
                for slot, block in enumerate(blocks):
                    held[slot, pl.ds(at, rows), :] = block
            return carry

        lax.fori_loop(step * some, (step + 1) * some, one, 0, unroll=True)
    slots = position()[0]
    for copy in copies([(held.at[slots[d]], out) for d, out in enumerate(outs)], out_sems):
        copy.wait()


def scaled_messages(increment, gain, mask, groups):
    fields, levels, length, cols = increment.shape
    shape = (fields * levels * length // groups, cols)
    return pl.pallas_call(
        scaled_kernel,
        in_specs=[pl.BlockSpec(memory_space=pl.ANY)] * 3,
        out_specs=[pl.BlockSpec(memory_space=pl.ANY)] * groups,
        out_shape=[jax.ShapeDtypeStruct(shape, jnp.float32)] * groups,
        scratch_shapes=[
            pltpu.VMEM(increment.shape, jnp.float32),
            pltpu.VMEM(gain.shape, jnp.float32),
            pltpu.VMEM(mask.shape, mask.dtype),
            pltpu.VMEM((groups, *shape), jnp.float32),
            pltpu.SemaphoreType.DMA((SCALED_STEPS, 3)),
            pltpu.SemaphoreType.DMA((groups,)),
        ],
        compiler_params=params(VMEM_WHOLE),
        name="scaled_messages",
    )(increment, gain, mask)


def pack_kernel(starts, rows, masked, along_i, along_j, *refs):
    levels, length, cols = along_i.shape
    groups = len(starts)
    halos, outs = refs[masked:-4 - groups - 3 * masked], refs[-4 - groups - 3 * masked:-4 - 3 * masked]
    held, slots_held, sems, fetch_sems = refs[-4:]
    group = lane_groups(rows, cols, groups)
    unroll = held.shape[0]
    pieces = levels // unroll
    if masked:
        sources, (along_i, along_j, sea) = (along_i, along_j, refs[0]), refs[-7:-4]
        fetched = []
        for side, (source, target) in enumerate(zip(sources, (along_i, along_j, sea))):
            pairs = [(source.at[pl.ds(k * unroll, unroll)], target.at[pl.ds(k * unroll, unroll)]) for k in range(pieces)]
            fetched.append(copies(pairs, fetch_sems.at[side]))

    def put(at, blocks):
        for slot, block in enumerate(blocks):
            slots_held[slot, pl.ds(at, block.shape[0]), :] = block

    for side, weight in enumerate((along_i, along_j)):
        for outer in range(pieces):
            if masked:
                fetched[side][outer].wait()
            packed = []
            for k in range(unroll):
                level = outer * unroll + k
                if halos:
                    for halo, at in zip(halos, (0, STEPS + length)):
                        held[k, pl.ds(at, STEPS), :] = halo[pl.ds((side * levels + level) * STEPS, STEPS), :]
                    held[k, pl.ds(STEPS, length), :] = weight[level]
                    blocks = [held[k, pl.ds(start, rows), :] for start in starts]
                else:
                    blocks = [weight[level, pl.ds(start - STEPS, rows), :] for start in starts]
                packed.append(swap(blocks, group, cols // groups))
            put(
                (side * levels + outer * unroll) * rows,
                [jnp.concatenate([packed[k][slot] for k in range(unroll)], axis=0) for slot in range(groups)],
            )
    if masked:
        depth = jnp.zeros((length, cols), sea.dtype)
        for outer in range(pieces):
            fetched[2][outer].wait()
            for level in range(outer * unroll, (outer + 1) * unroll):
                depth = depth + sea[level]
        depth = depth.astype(jnp.float32)
        size = length // groups
        blocks = [depth[a * size:(a + 1) * size] for a in range(groups)]
        put(2 * levels * rows, swap(blocks, lane_groups(size, cols, groups), cols // groups))
    slots = position()[0]
    for copy in copies([(slots_held.at[slots[d]], out) for d, out in enumerate(outs)], sems):
        copy.wait()


def weight_messages(starts, rows, along_i, along_j, mask=(), halos=()):
    levels, length, cols = along_i.shape
    groups = len(starts)
    shape = (2 * levels * rows + len(mask) * length // groups, cols)
    unroll = 4
    return list(
        pl.pallas_call(
            functools.partial(pack_kernel, starts, rows, len(mask)),
            in_specs=[pl.BlockSpec(memory_space=pl.ANY) if mask else vmem()] * (2 + len(mask) + len(halos)),
            out_specs=[pl.BlockSpec(memory_space=pl.ANY)] * groups,
            out_shape=[jax.ShapeDtypeStruct(shape, jnp.float32)] * groups,
            scratch_shapes=[pltpu.VMEM(x.shape, x.dtype) for x in ([along_i, along_j, *mask] if mask else [])]
            + [
                pltpu.VMEM((unroll, length + 2 * STEPS, cols), jnp.float32),
                pltpu.VMEM((groups, *shape), jnp.float32),
                pltpu.SemaphoreType.DMA((groups,)),
                pltpu.SemaphoreType.DMA((3, levels // unroll)),
            ],
            compiler_params=params(VMEM_WHOLE if mask else VMEM_LIMIT),
            name="weight_messages",
        )(along_i, along_j, *mask, *halos)
    )


def adjoint_kernel(matrix, depths, *refs):
    parts, out = refs[:-1], refs[-1]
    length, width, order = out.shape
    groups = len(parts)
    rows = length // groups
    cols = groups * width
    count = order // groups
    level = lax.rem(lax.broadcasted_iota(jnp.int32, (order, cols), 0), order // 2).astype(jnp.float32)

    def one(i, carry):
        x = jnp.concatenate([part[pl.ds(i, count, rows), :] for part in parts], axis=0)
        depth = depths[pl.ds(i, 1), :]
        y = jnp.dot(matrix[...], x, precision=HIGHEST, preferred_element_type=jnp.float32)
        y = jnp.where(level < depth, y, 0.0).T
        for a in range(groups):
            out[a * rows + i] = y[a * width:(a + 1) * width]
        return carry

    lax.fori_loop(0, rows, one, 0, unroll=4)


def adjoint_mix(matrix, depths, parts, length, width):
    return pl.pallas_call(
        adjoint_kernel,
        in_specs=[vmem()] * (2 + len(parts)),
        out_specs=vmem(),
        out_shape=jax.ShapeDtypeStruct((length, width, matrix.shape[0]), jnp.float32),
        compiler_params=params(),
        name="adjoint_mix",
    )(matrix, depths, *parts)


def unfold(main, halo, groups):
    cols = main.shape[1]
    width = cols // groups
    below = halo[:STEPS]
    above = pltpu.roll(halo[STEPS:], width, 1)
    return jnp.concatenate(
        [above] + [main] + [pltpu.roll(main, cols - a * width, 1) for a in range(1, groups)] + [below], axis=0
    )


def turn_kernel(starts, *refs):
    depths, parts, (out, held, depth_i, depth_j) = refs[:-4 - len(starts)], refs[-4 - len(starts):-4], refs[-4:]
    length, width, order = out.shape
    groups = len(parts)
    rows = length // groups
    half = order // 2
    count = half // groups
    cols = width * groups
    source = position()[2]
    for i in range(rows):
        for d, part in enumerate(parts):
            for side in range(2):
                at = pl.multiple_of(side * half + source[d] * count, 8)
                held[i, pl.ds(at, count), :] = part[pl.ds(side * count * rows + i, count, rows), :]

    no_halo = jnp.zeros((2 * STEPS, cols), jnp.float32)
    depth = unfold(depths[0][...], depths[1][...] if len(depths) > 1 else no_halo, groups)
    tall = depth.shape[0]
    lane = lax.broadcasted_iota(jnp.int32, depth.shape, 1)
    right = jnp.where(lane == width - 1, depth, pltpu.roll(depth, cols - 1, 1))
    depth_j[...] = jnp.minimum(depth, right)
    depth_i[pl.ds(0, tall - 1), :] = jnp.minimum(depth[:-1], depth[1:])
    depth_i[pl.ds(tall - 1, 1), :] = depth[tall - 1:]
    group = lane_groups(rows, cols, groups)

    def fold(ref):
        x = ref[pl.ds(starts[0], rows), :]
        for a in range(1, groups):
            x = jnp.where(group == a, pltpu.roll(ref[pl.ds(starts[a], rows), :], a * width, 1), x)
        return x

    folded_i, folded_j = fold(depth_i), fold(depth_j)
    level = lax.broadcasted_iota(jnp.int32, (half, cols), 0).astype(jnp.float32)
    for i in range(rows):
        along_i = jnp.where(level < folded_i[i:i + 1], held[i, pl.ds(0, half), :], 0.0)
        along_j = jnp.where(level < folded_j[i:i + 1], held[i, pl.ds(half, half), :], 0.0)
        turned = jnp.concatenate([along_i, along_j], axis=0).T
        for a in range(groups):
            out[a * rows + i] = turned[a * width:(a + 1) * width]


def turn_weights(starts, rows, depths, parts, order):
    groups = len(parts)
    cols = parts[0].shape[1]
    tall = depths[0].shape[0] * groups + 2 * STEPS
    return pl.pallas_call(
        functools.partial(turn_kernel, starts),
        in_specs=[vmem()] * (len(depths) + groups),
        out_specs=vmem(),
        out_shape=jax.ShapeDtypeStruct((rows * groups, cols // groups, order), jnp.float32),
        scratch_shapes=[pltpu.VMEM((rows, order, cols), jnp.float32)] + [pltpu.VMEM((tall, cols), jnp.float32)] * 2,
        compiler_params=params(),
        name="turn_weights",
    )(*depths, *parts)


def edge_masks(depths, order):
    groups = lax.axis_size("lev")
    slot = position()[0][0]
    gy = lax.axis_index("gy")
    start = (slot == 0) & (gy == 0)
    end = (slot == groups - 1) & (gy == lax.axis_size("gy") - 1)
    no_halo = jnp.zeros((2 * STEPS, depths[0].shape[1]), jnp.float32)
    masks = []
    for k, out in enumerate((start, end)):
        x = unfold(depths[k][...], depths[2 + k][...] if len(depths) > 2 else no_halo, groups)
        x = jnp.where(out, 0.0, x)
        x = jnp.broadcast_to(x[:, :1], (x.shape[0], order))
        lane = lax.broadcasted_iota(jnp.int32, x.shape, 1)
        level = lax.rem(lane, order // 2).astype(jnp.float32)
        masks.append(jnp.where((lane < order // 2) | (level < x), 1.0, 0.0))
    return masks


def spread_kernel(windows, field_rows, weight_rows, count, matrix, *refs):
    depths, refs = refs[:count], refs[count:]
    pieces = [refs[3 * k:3 * k + 3] for k in range(len(field_rows) + len(weight_rows))]
    outs, (a, b, wi, wj, masks) = refs[3 * len(pieces):-5], refs[-5:]
    width, order = pieces[0][0].shape[1:]
    half = order // 2
    _, ext, wide, _ = a.shape
    lane = lax.broadcasted_iota(jnp.int32, (wide, order), 1)
    last = lax.broadcasted_iota(jnp.int32, (PAD, order), 0) == PAD - 1
    nothing = jnp.zeros((PAD - STEPS, order), jnp.float32)
    masks[0], masks[1] = edge_masks(depths, order)

    def row_of(some, rows, r):
        piece = [k for k in range(len(rows)) if r in rows[k]][0]
        main, left, right = some[piece]
        k = rows[piece].index(r)
        side = pl.ds(k * STEPS, STEPS)
        return [jnp.concatenate([nothing, left[side, :]], axis=0), main[k], jnp.concatenate([right[side, :], nothing], axis=0)]

    for n, window in enumerate(windows):
        for e, r in enumerate(window):
            a[n, e] = jnp.concatenate(row_of(pieces[:len(field_rows)], field_rows, r), axis=0)
            left, mid, right = row_of(pieces[len(field_rows):], weight_rows, r)
            at = pl.ds(STEPS + r, 1)
            left = jnp.where(last, left * masks[0, at, :], left)
            end = mid[width - PAD:]
            end = jnp.where(last, end * masks[1, at, :], end)
            w = jnp.concatenate([left, mid[:width - PAD], end, right], axis=0)
            other = pltpu.roll(w, half, 1)
            wi[n, e] = jnp.where(lane < half, w, other)
            wj[n, e] = jnp.where(lane < half, other, w)

    src, dst = a, b
    for step in range(STEPS):
        begin, stop = step + 1, ext - 1 - step
        for n in range(len(windows)):

            def one(r, carry, n=n, src=src, dst=dst):
                v, before = carry
                after = src[n, r + 1]
                flux = wi[n, r] * (after - v)
                across = wj[n, r] * (pltpu.roll(v, wide - 1, 0) - v)
                dst[n, r] = v + (flux - before) + (across - pltpu.roll(across, 1, 0))
                return after, flux

            v = src[n, begin]
            lax.fori_loop(begin, stop, one, (v, wi[n, begin - 1] * (v - src[n, begin - 1])), unroll=2)
        src, dst = dst, src

    groups = len(outs)
    count = order // groups
    rows = len(windows) * (ext - 2 * STEPS) // groups
    each = groups // len(windows)

    def mix(i, carry):
        x = jnp.concatenate(
            [src[g // each, STEPS + g % each * rows + i, pl.ds(PAD, width), :] for g in range(groups)], axis=0
        )
        y = lax.dot_general(
            matrix[...], x, (((1,), (1,)), ((), ())), precision=HIGHEST, preferred_element_type=jnp.float32
        )
        for d, out in enumerate(outs):
            out[pl.ds(i, count, rows), :] = y[d * count:(d + 1) * count]
        return carry

    lax.fori_loop(0, rows, mix, 0, unroll=4)


def spread_mix(windows, matrix, depths, field, weights, groups):
    width, order = field[0][1].shape[1:]
    cols = width * groups
    ext = len(windows[0])
    rows = len(windows) * (ext - 2 * STEPS) // groups
    shape = jax.ShapeDtypeStruct((order // groups * rows, cols), jnp.float32)
    arrays = list(depths) + [x for piece in field + weights for x in piece[1:]]
    kernel = functools.partial(
        spread_kernel, windows, [piece[0] for piece in field], [piece[0] for piece in weights], len(depths)
    )
    tall = field[0][1].shape[0] + 2 * STEPS
    return pl.pallas_call(
        kernel,
        in_specs=[vmem()] * (1 + len(arrays)),
        out_specs=[vmem()] * groups,
        out_shape=[shape] * groups,
        scratch_shapes=[pltpu.VMEM((len(windows), ext, width + 2 * PAD, order), jnp.float32)] * 4
        + [pltpu.VMEM((2, tall, order), jnp.float32)],
        compiler_params=params(),
        name="spread_mix",
    )(matrix, *arrays)


RESULT_STEPS = 4


def result_kernel(runs, gain, mask, *refs):
    parts, (out, done, out_sems) = refs[:-3], refs[-3:]
    fields, levels, _, cols = gain.shape
    groups = len(parts)
    rows = done.shape[2] // groups
    some = levels // RESULT_STEPS
    slots = position()[1]
    group = lane_groups(rows, cols, groups)

    def of_slot(slot, at):
        x = parts[0][pl.ds(at, rows), :]
        for d in range(1, groups):
            x = jnp.where(slots[d] == slot, parts[d][pl.ds(at, rows), :], x)
        return x

    stored = []
    for step in range(RESULT_STEPS):
        for level in range(step * some, (step + 1) * some):
            ocean = jnp.concatenate([mask[level, pl.ds(*run), :] for run in runs], axis=0).astype(jnp.float32)
            for field in range(fields):
                at = (field * levels + level) * rows
                blocks = swap([of_slot(slot, at) for slot in range(groups)], group, cols // groups)
                gains = jnp.concatenate([gain[field, level, pl.ds(*run), :] for run in runs], axis=0)
                done[field, level] = ocean * gains * jnp.concatenate(blocks, axis=0)
        these = pl.ds(step * some, some)
        pairs, at = [], 0
        for first, number in runs:
            pairs.append((done.at[:, these, pl.ds(at, number)], out.at[:, these, pl.ds(first, number)]))
            at += number
        stored += copies(pairs, out_sems.at[step])
    for copy in stored:
        copy.wait()


def result(runs, gain, mask, parts, before):
    fields, levels, _, cols = gain.shape
    groups = len(parts)
    rows = sum(number for _, number in runs)
    anywhere = pl.BlockSpec(memory_space=pl.ANY)
    more = [] if before is None else [before]

    def kernel(gain, mask, *refs):
        result_kernel(runs, gain, mask, *refs[:groups], *refs[groups + len(more):])

    return pl.pallas_call(
        kernel,
        in_specs=[vmem()] * (2 + groups) + [anywhere] * len(more),
        out_specs=anywhere,
        out_shape=jax.ShapeDtypeStruct(gain.shape, jnp.float32),
        scratch_shapes=[
            pltpu.VMEM((fields, levels, rows, cols), jnp.float32),
            pltpu.SemaphoreType.DMA((RESULT_STEPS, len(runs))),
        ],
        input_output_aliases={2 + groups: 0} if more else {},
        compiler_params=params(),
        name="result",
    )(gain, mask, *parts, *more)


def shards(increment, norm_gain, diffusion_i, diffusion_j, sea_mask, coupling):
    devices = lax.axis_size("lev")
    gx_size = lax.axis_size("gx")
    gy_size = lax.axis_size("gy")
    _, levels, length, cols = increment.shape
    width = cols // devices
    rows = length // devices
    order = coupling.shape[0]
    to = [lax.rem(lax.axis_index("lev") + d, devices) for d in distances(devices)]
    source = [lax.rem(lax.axis_index("lev") + devices - d, devices) for d in distances(devices)]

    def shift(x, d):
        return lax.ppermute(x, "lev", [(k, (k + d) % devices) for k in range(devices)])

    def exchange(parts):
        return [parts[0]] + [shift(x, d) for x, d in zip(parts[1:], distances(devices)[1:])]

    up = [((k + 1) % gx_size, k) for k in range(gx_size)]
    down = [(b, a) for a, b in up]
    ring = [(devices - 1 - slot if y % 2 else slot) * gy_size + y for y in range(gy_size) for slot in range(devices)]
    ahead = list(zip(ring, ring[1:] + ring[:1]))
    back = [(b, a) for a, b in ahead]

    def halo_i(first, last):
        if gx_size == 2:
            size = first.shape[0]
            both = lax.ppermute(jnp.concatenate([first, last], axis=0), "gx", up)
            return both[size:], both[:size]
        return lax.ppermute(last, "gx", down), lax.ppermute(first, "gx", up)

    def halo_j(first, last):
        return lax.ppermute(last, ("lev", "gy"), ahead), lax.ppermute(first, ("lev", "gy"), back)

    def flat(x):
        return x.reshape(-1, x.shape[-1])

    def cut(x, *sizes):
        return lax.split(x, sizes, 0)

    quarter = length // 4
    some = 2 * quarter // devices
    half = devices // 2
    inner = (quarter, 2 * quarter)
    outer = ((0, quarter), (3 * quarter, quarter))
    inner_rows = list(range(quarter - STEPS, 3 * quarter + STEPS))
    outer_rows = list(range(-STEPS, quarter - STEPS)) + list(range(3 * quarter + STEPS, length + STEPS))
    inner_starts = [quarter + a * len(inner_rows) // devices for a in range(devices)]
    outer_starts = [a * some for a in range(half)] + [3 * quarter + 2 * STEPS + a * some for a in range(half)]
    windows = [list(range(-STEPS, quarter + STEPS)), list(range(3 * quarter - STEPS, length + STEPS))]

    inner_size = len(inner_rows) // devices
    inner_messages = weight_messages(inner_starts, inner_size, diffusion_i, diffusion_j, [sea_mask])
    inner_parts = exchange(inner_messages)
    inner_messages, edge_i, edge_j, increment, norm_gain = lax.optimization_barrier(
        (inner_messages, diffusion_i, diffusion_j, increment, norm_gain)
    )
    halos = halo_i(
        *[
            jnp.concatenate([flat(edge_i[:, at]), flat(edge_j[:, at])], axis=0)
            for at in (slice(0, STEPS), slice(-STEPS, None))
        ]
    )
    messages = scaled_messages(increment, norm_gain, sea_mask, devices)
    scaled = exchange(messages)
    messages, halos = lax.optimization_barrier((messages, halos))
    outer_messages = weight_messages(outer_starts, some, diffusion_i, diffusion_j, halos=halos)

    depth = sum(part[2 * levels * inner_size:] for part in inner_parts)
    here = turn_weights(inner_starts, inner_size, [depth], inner_parts, order)
    left, right = halo_j(
        jnp.concatenate([flat(here[:, :STEPS]), depth], axis=0),
        flat(here[:, -STEPS:]),
    )
    right, right_depth = cut(right, len(inner_rows) * STEPS, rows)

    balance = jnp.eye(order, dtype=jnp.float32) + coupling
    by_device = balance.reshape(2, devices, levels, order)
    adjoint = jnp.concatenate([by_device[:, s].reshape(2 * levels, order) for s in source], axis=0).T
    forward = jnp.concatenate([by_device[:, t].reshape(2 * levels, order) for t in to], axis=0)

    scaled[1], outer_messages = lax.optimization_barrier((scaled[1], outer_messages))
    early = shift(outer_messages[1], devices // 2)
    mixed = adjoint_mix(adjoint, depth, scaled, length, width)
    edges = flat(mixed[:, :STEPS]), flat(mixed[:, -STEPS:])
    edges, inner_weights = lax.optimization_barrier((edges, (here, left, right)))
    left, right = halo_j(*edges)
    left, right, outer_messages, early = lax.optimization_barrier((left, right, outer_messages, early))
    own, _, *others = outer_messages
    outer_parts = [own, early] + [shift(x, d) for x, d in zip(others, distances(devices)[2:])]
    field = [(list(range(length)), mixed, left, right)]
    weights = [(inner_rows, *inner_weights)]
    depths = [depth, right_depth]
    inner_mixed = spread_mix([inner_rows], forward, depths, field, weights, devices)
    _, upper, lower = lax.optimization_barrier((left, mixed[:STEPS], mixed[-STEPS:]))
    _, outer_parts = lax.optimization_barrier((inner_mixed[0], outer_parts))
    inner_mixed = exchange(inner_mixed)
    out = result((inner,), norm_gain, sea_mask, inner_mixed, None)

    above, below = halo_i(
        jnp.concatenate([flat(upper), depth[:STEPS]], axis=0),
        jnp.concatenate([flat(lower), depth[-STEPS:]], axis=0),
    )
    above, above_depth = cut(above, STEPS * width, STEPS)
    below, below_depth = cut(below, STEPS * width, STEPS)
    halo_depth = jnp.concatenate([below_depth, above_depth], axis=0)
    halo = jnp.concatenate([above, below], axis=0).reshape(2 * STEPS, width, order)
    here = turn_weights(outer_starts, some, [depth, halo_depth], outer_parts, order)
    left, right = halo_j(
        jnp.concatenate([flat(here[:, :STEPS]), flat(halo[:, :STEPS]), halo_depth], axis=0),
        jnp.concatenate([flat(here[:, -STEPS:]), flat(halo[:, -STEPS:])], axis=0),
    )
    sizes = len(outer_rows) * STEPS, 2 * STEPS * STEPS
    left, halo_left = cut(left, *sizes)
    right, halo_right, right_halo_depth = cut(right, *sizes, 2 * STEPS)
    weights.append((outer_rows, here, left, right))
    field.append((list(range(-STEPS, 0)) + list(range(length, length + STEPS)), halo, halo_left, halo_right))
    depths += [halo_depth, right_halo_depth]
    outer_mixed = exchange(spread_mix(windows, forward, depths, field, weights, devices))
    return result(outer, norm_gain, sea_mask, outer_mixed, out)


def solution(mesh):
    return jax.shard_map(
        shards,
        mesh=mesh,
        in_specs=(
            P(None, "lev", "gx", "gy"),
            P(None, "lev", "gx", "gy"),
            P("lev", "gx", "gy"),
            P("lev", "gx", "gy"),
            P("lev", "gx", "gy"),
            P(),
        ),
        out_specs=P(None, "lev", "gx", "gy"),
        check_vma=False,
    )
```

```python
import functools

import jax
import jax.numpy as jnp
from jax import lax
from jax.experimental import pallas as pl
from jax.experimental.pallas import tpu as pltpu
from jax.sharding import PartitionSpec as P

ITERS = 2
STEPS = 2 * ITERS
PAD = 8
VMEM_LIMIT = 40 * 1024 * 1024
VMEM_WHOLE = 60 * 1024 * 1024
HIGHEST = lax.Precision.HIGHEST


def params(limit=VMEM_LIMIT):
    return pltpu.CompilerParams(vmem_limit_bytes=limit)


def smem():
    return pl.BlockSpec(memory_space=pltpu.SMEM)


def vmem():
    return pl.BlockSpec(memory_space=pltpu.VMEM)


def distances(devices):
    return [0, devices // 2] + [d for d in range(1, devices) if d != devices // 2]


def position():
    devices = lax.axis_size("lev")
    me = lax.axis_index("lev")
    flipped = lax.rem(lax.axis_index("gy"), 2) == 1

    def slot(lev):
        return jnp.where(flipped, devices - 1 - lev, lev)

    to = [lax.rem(me + d, devices) for d in distances(devices)]
    source = [lax.rem(me + devices - d, devices) for d in distances(devices)]
    return [slot(lev) for lev in to], [slot(lev) for lev in source], source


def swap(blocks, group, width):
    blocks = list(blocks)
    cols = blocks[0].shape[1]
    bit = len(blocks) // 2
    while bit:
        shift = bit * width
        low = (group & bit) == 0
        for a in range(len(blocks)):
            if not a & bit:
                x, y = blocks[a], blocks[a + bit]
                blocks[a] = jnp.where(low, x, pltpu.roll(y, shift, 1))
                blocks[a + bit] = jnp.where(low, pltpu.roll(x, cols - shift, 1), y)
        bit //= 2
    return blocks


def lane_groups(rows, cols, groups):
    return lax.broadcasted_iota(jnp.int32, (rows, cols), 1) // (cols // groups)


def copies(pairs, sems):
    made = [pltpu.make_async_copy(src, dst, sems.at[k]) for k, (src, dst) in enumerate(pairs)]
    for copy in made:
        copy.start()
    return made


SCALED_STEPS = 4


def scaled_kernel(increment, gain, mask, *refs):
    outs, (inc, gn, sea, held, sems, out_sems) = refs[:-6], refs[-6:]
    fields, levels, length, cols = increment.shape
    groups = len(outs)
    rows = length // groups
    some = levels // SCALED_STEPS
    group = lane_groups(rows, cols, groups)
    fetched = []
    for step in range(SCALED_STEPS):
        part = pl.ds(step * some, some)
        fetched.append(
            copies(
                [
                    (increment.at[:, part], inc.at[:, part]),
                    (gain.at[:, part], gn.at[:, part]),
                    (mask.at[part], sea.at[part]),
                ],
                sems.at[step],
            )
        )

    for step in range(SCALED_STEPS):
        for copy in fetched[step]:
            copy.wait()

        def one(level, carry):
            ocean = sea[level].astype(jnp.float32)
            for field in range(fields):
                at = pl.multiple_of((field * levels + level) * rows, rows)
                x = ocean * gn[field, level] * inc[field, level]
                blocks = swap([x[a * rows:(a + 1) * rows] for a in range(groups)], group, cols // groups)
                for slot, block in enumerate(blocks):
                    held[slot, pl.ds(at, rows), :] = block
            return carry

        lax.fori_loop(step * some, (step + 1) * some, one, 0, unroll=True)
    slots = position()[0]
    for copy in copies([(held.at[slots[d]], out) for d, out in enumerate(outs)], out_sems):
        copy.wait()


def scaled_messages(increment, gain, mask, groups):
    fields, levels, length, cols = increment.shape
    shape = (fields * levels * length // groups, cols)
    return pl.pallas_call(
        scaled_kernel,
        in_specs=[pl.BlockSpec(memory_space=pl.ANY)] * 3,
        out_specs=[pl.BlockSpec(memory_space=pl.ANY)] * groups,
        out_shape=[jax.ShapeDtypeStruct(shape, jnp.float32)] * groups,
        scratch_shapes=[
            pltpu.VMEM(increment.shape, jnp.float32),
            pltpu.VMEM(gain.shape, jnp.float32),
            pltpu.VMEM(mask.shape, mask.dtype),
            pltpu.VMEM((groups, *shape), jnp.float32),
            pltpu.SemaphoreType.DMA((SCALED_STEPS, 3)),
            pltpu.SemaphoreType.DMA((groups,)),
        ],
        compiler_params=params(VMEM_WHOLE),
        name="scaled_messages",
    )(increment, gain, mask)


def pack_kernel(starts, rows, masked, along_i, along_j, *refs):
    levels, length, cols = along_i.shape
    groups = len(starts)
    halos, outs = refs[masked:-4 - groups - 3 * masked], refs[-4 - groups - 3 * masked:-4 - 3 * masked]
    held, slots_held, sems, fetch_sems = refs[-4:]
    group = lane_groups(rows, cols, groups)
    unroll = held.shape[0]
    pieces = levels // unroll
    if masked:
        sources, (along_i, along_j, sea) = (along_i, along_j, refs[0]), refs[-7:-4]
        fetched = []
        for side, (source, target) in enumerate(zip(sources, (along_i, along_j, sea))):
            pairs = [(source.at[pl.ds(k * unroll, unroll)], target.at[pl.ds(k * unroll, unroll)]) for k in range(pieces)]
            fetched.append(copies(pairs, fetch_sems.at[side]))

    def put(at, blocks):
        for slot, block in enumerate(blocks):
            slots_held[slot, pl.ds(at, block.shape[0]), :] = block

    for side, weight in enumerate((along_i, along_j)):
        for outer in range(pieces):
            if masked:
                fetched[side][outer].wait()
            packed = []
            for k in range(unroll):
                level = outer * unroll + k
                if halos:
                    for halo, at in zip(halos, (0, STEPS + length)):
                        held[k, pl.ds(at, STEPS), :] = halo[pl.ds((side * levels + level) * STEPS, STEPS), :]
                    held[k, pl.ds(STEPS, length), :] = weight[level]
                    blocks = [held[k, pl.ds(start, rows), :] for start in starts]
                else:
                    blocks = [weight[level, pl.ds(start - STEPS, rows), :] for start in starts]
                packed.append(swap(blocks, group, cols // groups))
            put(
                (side * levels + outer * unroll) * rows,
                [jnp.concatenate([packed[k][slot] for k in range(unroll)], axis=0) for slot in range(groups)],
            )
    if masked:
        depth = jnp.zeros((length, cols), sea.dtype)
        for outer in range(pieces):
            fetched[2][outer].wait()
            for level in range(outer * unroll, (outer + 1) * unroll):
                depth = depth + sea[level]
        depth = depth.astype(jnp.float32)
        size = length // groups
        blocks = [depth[a * size:(a + 1) * size] for a in range(groups)]
        put(2 * levels * rows, swap(blocks, lane_groups(size, cols, groups), cols // groups))
    slots = position()[0]
    for copy in copies([(slots_held.at[slots[d]], out) for d, out in enumerate(outs)], sems):
        copy.wait()


def weight_messages(starts, rows, along_i, along_j, mask=(), halos=()):
    levels, length, cols = along_i.shape
    groups = len(starts)
    shape = (2 * levels * rows + len(mask) * length // groups, cols)
    unroll = 4
    return list(
        pl.pallas_call(
            functools.partial(pack_kernel, starts, rows, len(mask)),
            in_specs=[pl.BlockSpec(memory_space=pl.ANY) if mask else vmem()] * (2 + len(mask) + len(halos)),
            out_specs=[pl.BlockSpec(memory_space=pl.ANY)] * groups,
            out_shape=[jax.ShapeDtypeStruct(shape, jnp.float32)] * groups,
            scratch_shapes=[pltpu.VMEM(x.shape, x.dtype) for x in ([along_i, along_j, *mask] if mask else [])]
            + [
                pltpu.VMEM((unroll, length + 2 * STEPS, cols), jnp.float32),
                pltpu.VMEM((groups, *shape), jnp.float32),
                pltpu.SemaphoreType.DMA((groups,)),
                pltpu.SemaphoreType.DMA((3, levels // unroll)),
            ],
            compiler_params=params(VMEM_WHOLE if mask else VMEM_LIMIT),
            name="weight_messages",
        )(along_i, along_j, *mask, *halos)
    )


def adjoint_kernel(matrix, depths, *refs):
    parts, out = refs[:-1], refs[-1]
    length, width, order = out.shape
    groups = len(parts)
    rows = length // groups
    cols = groups * width
    count = order // groups
    level = lax.rem(lax.broadcasted_iota(jnp.int32, (order, cols), 0), order // 2).astype(jnp.float32)

    def one(i, carry):
        x = jnp.concatenate([part[pl.ds(i, count, rows), :] for part in parts], axis=0)
        depth = depths[pl.ds(i, 1), :]
        y = jnp.dot(matrix[...], x, precision=HIGHEST, preferred_element_type=jnp.float32)
        y = jnp.where(level < depth, y, 0.0).T
        for a in range(groups):
            out[a * rows + i] = y[a * width:(a + 1) * width]
        return carry

    lax.fori_loop(0, rows, one, 0, unroll=4)


def adjoint_mix(matrix, depths, parts, length, width):
    return pl.pallas_call(
        adjoint_kernel,
        in_specs=[vmem()] * (2 + len(parts)),
        out_specs=vmem(),
        out_shape=jax.ShapeDtypeStruct((length, width, matrix.shape[0]), jnp.float32),
        compiler_params=params(),
        name="adjoint_mix",
    )(matrix, depths, *parts)


def unfold(main, halo, groups):
    cols = main.shape[1]
    width = cols // groups
    below = halo[:STEPS]
    above = pltpu.roll(halo[STEPS:], width, 1)
    return jnp.concatenate(
        [above] + [main] + [pltpu.roll(main, cols - a * width, 1) for a in range(1, groups)] + [below], axis=0
    )


def turn_kernel(starts, *refs):
    depths, parts, (out, held, depth_i, depth_j) = refs[:-4 - len(starts)], refs[-4 - len(starts):-4], refs[-4:]
    length, width, order = out.shape
    groups = len(parts)
    rows = length // groups
    half = order // 2
    count = half // groups
    cols = width * groups
    source = position()[2]
    for i in range(rows):
        for d, part in enumerate(parts):
            for side in range(2):
                at = pl.multiple_of(side * half + source[d] * count, 8)
                held[i, pl.ds(at, count), :] = part[pl.ds(side * count * rows + i, count, rows), :]

    no_halo = jnp.zeros((2 * STEPS, cols), jnp.float32)
    depth = unfold(depths[0][...], depths[1][...] if len(depths) > 1 else no_halo, groups)
    tall = depth.shape[0]
    lane = lax.broadcasted_iota(jnp.int32, depth.shape, 1)
    right = jnp.where(lane == width - 1, depth, pltpu.roll(depth, cols - 1, 1))
    depth_j[...] = jnp.minimum(depth, right)
    depth_i[pl.ds(0, tall - 1), :] = jnp.minimum(depth[:-1], depth[1:])
    depth_i[pl.ds(tall - 1, 1), :] = depth[tall - 1:]
    group = lane_groups(rows, cols, groups)

    def fold(ref):
        x = ref[pl.ds(starts[0], rows), :]
        for a in range(1, groups):
            x = jnp.where(group == a, pltpu.roll(ref[pl.ds(starts[a], rows), :], a * width, 1), x)
        return x

    folded_i, folded_j = fold(depth_i), fold(depth_j)
    level = lax.broadcasted_iota(jnp.int32, (half, cols), 0).astype(jnp.float32)
    for i in range(rows):
        along_i = jnp.where(level < folded_i[i:i + 1], held[i, pl.ds(0, half), :], 0.0)
        along_j = jnp.where(level < folded_j[i:i + 1], held[i, pl.ds(half, half), :], 0.0)
        turned = jnp.concatenate([along_i, along_j], axis=0).T
        for a in range(groups):
            out[a * rows + i] = turned[a * width:(a + 1) * width]


def turn_weights(starts, rows, depths, parts, order):
    groups = len(parts)
    cols = parts[0].shape[1]
    tall = depths[0].shape[0] * groups + 2 * STEPS
    return pl.pallas_call(
        functools.partial(turn_kernel, starts),
        in_specs=[vmem()] * (len(depths) + groups),
        out_specs=vmem(),
        out_shape=jax.ShapeDtypeStruct((rows * groups, cols // groups, order), jnp.float32),
        scratch_shapes=[pltpu.VMEM((rows, order, cols), jnp.float32)] + [pltpu.VMEM((tall, cols), jnp.float32)] * 2,
        compiler_params=params(),
        name="turn_weights",
    )(*depths, *parts)


def edge_masks(depths, order):
    groups = lax.axis_size("lev")
    slot = position()[0][0]
    gy = lax.axis_index("gy")
    start = (slot == 0) & (gy == 0)
    end = (slot == groups - 1) & (gy == lax.axis_size("gy") - 1)
    no_halo = jnp.zeros((2 * STEPS, depths[0].shape[1]), jnp.float32)
    masks = []
    for k, out in enumerate((start, end)):
        x = unfold(depths[k][...], depths[2 + k][...] if len(depths) > 2 else no_halo, groups)
        x = jnp.where(out, 0.0, x)
        x = jnp.broadcast_to(x[:, :1], (x.shape[0], order))
        lane = lax.broadcasted_iota(jnp.int32, x.shape, 1)
        level = lax.rem(lane, order // 2).astype(jnp.float32)
        masks.append(jnp.where((lane < order // 2) | (level < x), 1.0, 0.0))
    return masks


def spread_kernel(windows, field_rows, weight_rows, count, matrix, *refs):
    depths, refs = refs[:count], refs[count:]
    pieces = [refs[3 * k:3 * k + 3] for k in range(len(field_rows) + len(weight_rows))]
    outs, (a, b, wi, wj, masks) = refs[3 * len(pieces):-5], refs[-5:]
    width, order = pieces[0][0].shape[1:]
    half = order // 2
    _, ext, wide, _ = a.shape
    lane = lax.broadcasted_iota(jnp.int32, (wide, order), 1)
    last = lax.broadcasted_iota(jnp.int32, (PAD, order), 0) == PAD - 1
    nothing = jnp.zeros((PAD - STEPS, order), jnp.float32)
    masks[0], masks[1] = edge_masks(depths, order)

    def row_of(some, rows, r):
        piece = [k for k in range(len(rows)) if r in rows[k]][0]
        main, left, right = some[piece]
        k = rows[piece].index(r)
        side = pl.ds(k * STEPS, STEPS)
        return [jnp.concatenate([nothing, left[side, :]], axis=0), main[k], jnp.concatenate([right[side, :], nothing], axis=0)]

    for n, window in enumerate(windows):
        for e, r in enumerate(window):
            a[n, e] = jnp.concatenate(row_of(pieces[:len(field_rows)], field_rows, r), axis=0)
            left, mid, right = row_of(pieces[len(field_rows):], weight_rows, r)
            at = pl.ds(STEPS + r, 1)
            left = jnp.where(last, left * masks[0, at, :], left)
            end = mid[width - PAD:]
            end = jnp.where(last, end * masks[1, at, :], end)
            w = jnp.concatenate([left, mid[:width - PAD], end, right], axis=0)
            other = pltpu.roll(w, half, 1)
            wi[n, e] = jnp.where(lane < half, w, other)
            wj[n, e] = jnp.where(lane < half, other, w)

    src, dst = a, b
    for step in range(STEPS):
        begin, stop = step + 1, ext - 1 - step
        for n in range(len(windows)):

            def one(r, carry, n=n, src=src, dst=dst):
                v, before = carry
                after = src[n, r + 1]
                flux = wi[n, r] * (after - v)
                across = wj[n, r] * (pltpu.roll(v, wide - 1, 0) - v)
                dst[n, r] = v + (flux - before) + (across - pltpu.roll(across, 1, 0))
                return after, flux

            v = src[n, begin]
            lax.fori_loop(begin, stop, one, (v, wi[n, begin - 1] * (v - src[n, begin - 1])), unroll=2)
        src, dst = dst, src

    groups = len(outs)
    count = order // groups
    rows = len(windows) * (ext - 2 * STEPS) // groups
    each = groups // len(windows)

    def mix(i, carry):
        x = jnp.concatenate(
            [src[g // each, STEPS + g % each * rows + i, pl.ds(PAD, width), :] for g in range(groups)], axis=0
        )
        y = lax.dot_general(
            matrix[...], x, (((1,), (1,)), ((), ())), precision=HIGHEST, preferred_element_type=jnp.float32
        )
        for d, out in enumerate(outs):
            out[pl.ds(i, count, rows), :] = y[d * count:(d + 1) * count]
        return carry

    lax.fori_loop(0, rows, mix, 0, unroll=4)


def spread_mix(windows, matrix, depths, field, weights, groups):
    width, order = field[0][1].shape[1:]
    cols = width * groups
    ext = len(windows[0])
    rows = len(windows) * (ext - 2 * STEPS) // groups
    shape = jax.ShapeDtypeStruct((order // groups * rows, cols), jnp.float32)
    arrays = list(depths) + [x for piece in field + weights for x in piece[1:]]
    kernel = functools.partial(
        spread_kernel, windows, [piece[0] for piece in field], [piece[0] for piece in weights], len(depths)
    )
    tall = field[0][1].shape[0] + 2 * STEPS
    return pl.pallas_call(
        kernel,
        in_specs=[vmem()] * (1 + len(arrays)),
        out_specs=[vmem()] * groups,
        out_shape=[shape] * groups,
        scratch_shapes=[pltpu.VMEM((len(windows), ext, width + 2 * PAD, order), jnp.float32)] * 4
        + [pltpu.VMEM((2, tall, order), jnp.float32)],
        compiler_params=params(),
        name="spread_mix",
    )(matrix, *arrays)


RESULT_STEPS = 4


def result_kernel(runs, gain, mask, *refs):
    parts, (out, done, out_sems) = refs[:-3], refs[-3:]
    fields, levels, _, cols = gain.shape
    groups = len(parts)
    rows = done.shape[2] // groups
    some = levels // RESULT_STEPS
    slots = position()[1]
    group = lane_groups(rows, cols, groups)

    def of_slot(slot, at):
        x = parts[0][pl.ds(at, rows), :]
        for d in range(1, groups):
            x = jnp.where(slots[d] == slot, parts[d][pl.ds(at, rows), :], x)
        return x

    stored = []
    for step in range(RESULT_STEPS):
        for level in range(step * some, (step + 1) * some):
            ocean = jnp.concatenate([mask[level, pl.ds(*run), :] for run in runs], axis=0).astype(jnp.float32)
            for field in range(fields):
                at = (field * levels + level) * rows
                blocks = swap([of_slot(slot, at) for slot in range(groups)], group, cols // groups)
                gains = jnp.concatenate([gain[field, level, pl.ds(*run), :] for run in runs], axis=0)
                done[field, level] = ocean * gains * jnp.concatenate(blocks, axis=0)
        these = pl.ds(step * some, some)
        pairs, at = [], 0
        for first, number in runs:
            pairs.append((done.at[:, these, pl.ds(at, number)], out.at[:, these, pl.ds(first, number)]))
            at += number
        stored += copies(pairs, out_sems.at[step])
    for copy in stored:
        copy.wait()


def result(runs, gain, mask, parts, before):
    fields, levels, _, cols = gain.shape
    groups = len(parts)
    rows = sum(number for _, number in runs)
    anywhere = pl.BlockSpec(memory_space=pl.ANY)
    more = [] if before is None else [before]

    def kernel(gain, mask, *refs):
        result_kernel(runs, gain, mask, *refs[:groups], *refs[groups + len(more):])

    return pl.pallas_call(
        kernel,
        in_specs=[vmem()] * (2 + groups) + [anywhere] * len(more),
        out_specs=anywhere,
        out_shape=jax.ShapeDtypeStruct(gain.shape, jnp.float32),
        scratch_shapes=[
            pltpu.VMEM((fields, levels, rows, cols), jnp.float32),
            pltpu.SemaphoreType.DMA((RESULT_STEPS, len(runs))),
        ],
        input_output_aliases={2 + groups: 0} if more else {},
        compiler_params=params(),
        name="result",
    )(gain, mask, *parts, *more)


def shards(increment, norm_gain, diffusion_i, diffusion_j, sea_mask, coupling):
    devices = lax.axis_size("lev")
    gx_size = lax.axis_size("gx")
    gy_size = lax.axis_size("gy")
    _, levels, length, cols = increment.shape
    width = cols // devices
    rows = length // devices
    order = coupling.shape[0]
    to = [lax.rem(lax.axis_index("lev") + d, devices) for d in distances(devices)]
    source = [lax.rem(lax.axis_index("lev") + devices - d, devices) for d in distances(devices)]

    def shift(x, d):
        return lax.ppermute(x, "lev", [(k, (k + d) % devices) for k in range(devices)])

    def exchange(parts):
        return [parts[0]] + [shift(x, d) for x, d in zip(parts[1:], distances(devices)[1:])]

    up = [((k + 1) % gx_size, k) for k in range(gx_size)]
    down = [(b, a) for a, b in up]
    ring = [(devices - 1 - slot if y % 2 else slot) * gy_size + y for y in range(gy_size) for slot in range(devices)]
    ahead = list(zip(ring, ring[1:] + ring[:1]))
    back = [(b, a) for a, b in ahead]

    def halo_i(first, last):
        if gx_size == 2:
            size = first.shape[0]
            both = lax.ppermute(jnp.concatenate([first, last], axis=0), "gx", up)
            return both[size:], both[:size]
        return lax.ppermute(last, "gx", down), lax.ppermute(first, "gx", up)

    def halo_j(first, last):
        return lax.ppermute(last, ("lev", "gy"), ahead), lax.ppermute(first, ("lev", "gy"), back)

    def flat(x):
        return x.reshape(-1, x.shape[-1])

    def cut(x, *sizes):
        return lax.split(x, sizes, 0)

    quarter = length // 4
    some = 2 * quarter // devices
    half = devices // 2
    inner = (quarter, 2 * quarter)
    outer = ((0, quarter), (3 * quarter, quarter))
    inner_rows = list(range(quarter - STEPS, 3 * quarter + STEPS))
    outer_rows = list(range(-STEPS, quarter - STEPS)) + list(range(3 * quarter + STEPS, length + STEPS))
    inner_starts = [quarter + a * len(inner_rows) // devices for a in range(devices)]
    outer_starts = [a * some for a in range(half)] + [3 * quarter + 2 * STEPS + a * some for a in range(half)]
    windows = [list(range(-STEPS, quarter + STEPS)), list(range(3 * quarter - STEPS, length + STEPS))]

    inner_size = len(inner_rows) // devices
    inner_messages = weight_messages(inner_starts, inner_size, diffusion_i, diffusion_j, [sea_mask])
    inner_parts = exchange(inner_messages)
    inner_messages, edge_i, edge_j, increment, norm_gain = lax.optimization_barrier(
        (inner_messages, diffusion_i, diffusion_j, increment, norm_gain)
    )
    halos = halo_i(
        *[
            jnp.concatenate([flat(edge_i[:, at]), flat(edge_j[:, at])], axis=0)
            for at in (slice(0, STEPS), slice(-STEPS, None))
        ]
    )
    messages = scaled_messages(increment, norm_gain, sea_mask, devices)
    scaled = exchange(messages)
    messages, halos = lax.optimization_barrier((messages, halos))
    outer_messages = weight_messages(outer_starts, some, diffusion_i, diffusion_j, halos=halos)

    depth = sum(part[2 * levels * inner_size:] for part in inner_parts)
    here = turn_weights(inner_starts, inner_size, [depth], inner_parts, order)
    left, right = halo_j(
        jnp.concatenate([flat(here[:, :STEPS]), depth], axis=0),
        flat(here[:, -STEPS:]),
    )
    right, right_depth = cut(right, len(inner_rows) * STEPS, rows)

    balance = jnp.eye(order, dtype=jnp.float32) + coupling
    by_device = balance.reshape(2, devices, levels, order)
    adjoint = jnp.concatenate([by_device[:, s].reshape(2 * levels, order) for s in source], axis=0).T
    forward = jnp.concatenate([by_device[:, t].reshape(2 * levels, order) for t in to], axis=0)

    scaled[1], outer_messages = lax.optimization_barrier((scaled[1], outer_messages))
    outer_parts = exchange(outer_messages)
    mixed = adjoint_mix(adjoint, depth, scaled, length, width)
    edges = flat(mixed[:, :STEPS]), flat(mixed[:, -STEPS:])
    edges, inner_weights = lax.optimization_barrier((edges, (here, left, right)))
    left, right = halo_j(*edges)
    left, right, outer_parts = lax.optimization_barrier((left, right, outer_parts))
    field = [(list(range(length)), mixed, left, right)]
    weights = [(inner_rows, *inner_weights)]
    depths = [depth, right_depth]
    inner_mixed = spread_mix([inner_rows], forward, depths, field, weights, devices)
    _, upper, lower = lax.optimization_barrier((left, mixed[:STEPS], mixed[-STEPS:]))
    _, outer_parts = lax.optimization_barrier((inner_mixed[0], outer_parts))
    inner_mixed = exchange(inner_mixed)
    out = result((inner,), norm_gain, sea_mask, inner_mixed, None)

    above, below = halo_i(
        jnp.concatenate([flat(upper), depth[:STEPS]], axis=0),
        jnp.concatenate([flat(lower), depth[-STEPS:]], axis=0),
    )
    above, above_depth = cut(above, STEPS * width, STEPS)
    below, below_depth = cut(below, STEPS * width, STEPS)
    halo_depth = jnp.concatenate([below_depth, above_depth], axis=0)
    halo = jnp.concatenate([above, below], axis=0).reshape(2 * STEPS, width, order)
    here = turn_weights(outer_starts, some, [depth, halo_depth], outer_parts, order)
    left, right = halo_j(
        jnp.concatenate([flat(here[:, :STEPS]), flat(halo[:, :STEPS]), halo_depth], axis=0),
        jnp.concatenate([flat(here[:, -STEPS:]), flat(halo[:, -STEPS:])], axis=0),
    )
    sizes = len(outer_rows) * STEPS, 2 * STEPS * STEPS
    left, halo_left = cut(left, *sizes)
    right, halo_right, right_halo_depth = cut(right, *sizes, 2 * STEPS)
    weights.append((outer_rows, here, left, right))
    field.append((list(range(-STEPS, 0)) + list(range(length, length + STEPS)), halo, halo_left, halo_right))
    depths += [halo_depth, right_halo_depth]
    outer_mixed = exchange(spread_mix(windows, forward, depths, field, weights, devices))
    return result(outer, norm_gain, sea_mask, outer_mixed, out)


def solution(mesh):
    return jax.shard_map(
        shards,
        mesh=mesh,
        in_specs=(
            P(None, "lev", "gx", "gy"),
            P(None, "lev", "gx", "gy"),
            P("lev", "gx", "gy"),
            P("lev", "gx", "gy"),
            P("lev", "gx", "gy"),
            P(),
        ),
        out_specs=P(None, "lev", "gx", "gy"),
        check_vma=False,
    )
```

```python
import functools

import jax
import jax.numpy as jnp
from jax import lax
from jax.experimental import pallas as pl
from jax.experimental.pallas import tpu as pltpu
from jax.sharding import PartitionSpec as P

ITERS = 2
STEPS = 2 * ITERS
PAD = 8
VMEM_LIMIT = 40 * 1024 * 1024
VMEM_WHOLE = 60 * 1024 * 1024
HIGHEST = lax.Precision.HIGHEST


def params(limit=VMEM_LIMIT):
    return pltpu.CompilerParams(vmem_limit_bytes=limit)


def smem():
    return pl.BlockSpec(memory_space=pltpu.SMEM)


def vmem():
    return pl.BlockSpec(memory_space=pltpu.VMEM)


def distances(devices):
    return list(range(devices))


def position():
    devices = lax.axis_size("lev")
    me = lax.axis_index("lev")
    flipped = lax.rem(lax.axis_index("gy"), 2) == 1

    def slot(lev):
        return jnp.where(flipped, devices - 1 - lev, lev)

    to = [lax.rem(me + d, devices) for d in distances(devices)]
    source = [lax.rem(me + devices - d, devices) for d in distances(devices)]
    return [slot(lev) for lev in to], [slot(lev) for lev in source], source


def swap(blocks, group, width):
    blocks = list(blocks)
    cols = blocks[0].shape[1]
    bit = len(blocks) // 2
    while bit:
        shift = bit * width
        low = (group & bit) == 0
        for a in range(len(blocks)):
            if not a & bit:
                x, y = blocks[a], blocks[a + bit]
                blocks[a] = jnp.where(low, x, pltpu.roll(y, shift, 1))
                blocks[a + bit] = jnp.where(low, pltpu.roll(x, cols - shift, 1), y)
        bit //= 2
    return blocks


def lane_groups(rows, cols, groups):
    return lax.broadcasted_iota(jnp.int32, (rows, cols), 1) // (cols // groups)


def copies(pairs, sems):
    made = [pltpu.make_async_copy(src, dst, sems.at[k]) for k, (src, dst) in enumerate(pairs)]
    for copy in made:
        copy.start()
    return made


SCALED_STEPS = 4


def scaled_kernel(increment, gain, mask, *refs):
    outs, (inc, gn, sea, held, sems, out_sems) = refs[:-6], refs[-6:]
    fields, levels, length, cols = increment.shape
    groups = len(outs)
    rows = length // groups
    some = levels // SCALED_STEPS
    group = lane_groups(rows, cols, groups)
    fetched = []
    for step in range(SCALED_STEPS):
        part = pl.ds(step * some, some)
        fetched.append(
            copies(
                [
                    (increment.at[:, part], inc.at[:, part]),
                    (gain.at[:, part], gn.at[:, part]),
                    (mask.at[part], sea.at[part]),
                ],
                sems.at[step],
            )
        )

    for step in range(SCALED_STEPS):
        for copy in fetched[step]:
            copy.wait()

        def one(level, carry):
            ocean = sea[level].astype(jnp.float32)
            for field in range(fields):
                at = pl.multiple_of((field * levels + level) * rows, rows)
                x = ocean * gn[field, level] * inc[field, level]
                blocks = swap([x[a * rows:(a + 1) * rows] for a in range(groups)], group, cols // groups)
                for slot, block in enumerate(blocks):
                    held[slot, pl.ds(at, rows), :] = block
            return carry

        lax.fori_loop(step * some, (step + 1) * some, one, 0, unroll=True)
    slots = position()[0]
    for copy in copies([(held.at[slots[d]], out) for d, out in enumerate(outs)], out_sems):
        copy.wait()


def scaled_messages(increment, gain, mask, groups):
    fields, levels, length, cols = increment.shape
    shape = (fields * levels * length // groups, cols)
    return pl.pallas_call(
        scaled_kernel,
        in_specs=[pl.BlockSpec(memory_space=pl.ANY)] * 3,
        out_specs=[pl.BlockSpec(memory_space=pl.ANY)] * groups,
        out_shape=[jax.ShapeDtypeStruct(shape, jnp.float32)] * groups,
        scratch_shapes=[
            pltpu.VMEM(increment.shape, jnp.float32),
            pltpu.VMEM(gain.shape, jnp.float32),
            pltpu.VMEM(mask.shape, mask.dtype),
            pltpu.VMEM((groups, *shape), jnp.float32),
            pltpu.SemaphoreType.DMA((SCALED_STEPS, 3)),
            pltpu.SemaphoreType.DMA((groups,)),
        ],
        compiler_params=params(VMEM_WHOLE),
        name="scaled_messages",
    )(increment, gain, mask)


def pack_kernel(starts, rows, masked, along_i, along_j, *refs):
    levels, length, cols = along_i.shape
    groups = len(starts)
    halos, outs = refs[masked:-4 - groups - 3 * masked], refs[-4 - groups - 3 * masked:-4 - 3 * masked]
    held, slots_held, sems, fetch_sems = refs[-4:]
    group = lane_groups(rows, cols, groups)
    unroll = held.shape[0]
    pieces = levels // unroll
    if masked:
        sources, (along_i, along_j, sea) = (along_i, along_j, refs[0]), refs[-7:-4]
        fetched = []
        for side, (source, target) in enumerate(zip(sources, (along_i, along_j, sea))):
            pairs = [(source.at[pl.ds(k * unroll, unroll)], target.at[pl.ds(k * unroll, unroll)]) for k in range(pieces)]
            fetched.append(copies(pairs, fetch_sems.at[side]))

    def put(at, blocks):
        for slot, block in enumerate(blocks):
            slots_held[slot, pl.ds(at, block.shape[0]), :] = block

    for side, weight in enumerate((along_i, along_j)):
        for outer in range(pieces):
            if masked:
                fetched[side][outer].wait()
            packed = []
            for k in range(unroll):
                level = outer * unroll + k
                if halos:
                    for halo, at in zip(halos, (0, STEPS + length)):
                        held[k, pl.ds(at, STEPS), :] = halo[pl.ds((side * levels + level) * STEPS, STEPS), :]
                    held[k, pl.ds(STEPS, length), :] = weight[level]
                    blocks = [held[k, pl.ds(start, rows), :] for start in starts]
                else:
                    blocks = [weight[level, pl.ds(start - STEPS, rows), :] for start in starts]
                packed.append(swap(blocks, group, cols // groups))
            put(
                (side * levels + outer * unroll) * rows,
                [jnp.concatenate([packed[k][slot] for k in range(unroll)], axis=0) for slot in range(groups)],
            )
    if masked:
        depth = jnp.zeros((length, cols), sea.dtype)
        for outer in range(pieces):
            fetched[2][outer].wait()
            for level in range(outer * unroll, (outer + 1) * unroll):
                depth = depth + sea[level]
        depth = depth.astype(jnp.float32)
        size = length // groups
        blocks = [depth[a * size:(a + 1) * size] for a in range(groups)]
        put(2 * levels * rows, swap(blocks, lane_groups(size, cols, groups), cols // groups))
    slots = position()[0]
    for copy in copies([(slots_held.at[slots[d]], out) for d, out in enumerate(outs)], sems):
        copy.wait()


def weight_messages(starts, rows, along_i, along_j, mask=(), halos=()):
    levels, length, cols = along_i.shape
    groups = len(starts)
    shape = (2 * levels * rows + len(mask) * length // groups, cols)
    unroll = 4
    return list(
        pl.pallas_call(
            functools.partial(pack_kernel, starts, rows, len(mask)),
            in_specs=[pl.BlockSpec(memory_space=pl.ANY) if mask else vmem()] * (2 + len(mask) + len(halos)),
            out_specs=[pl.BlockSpec(memory_space=pl.ANY)] * groups,
            out_shape=[jax.ShapeDtypeStruct(shape, jnp.float32)] * groups,
            scratch_shapes=[pltpu.VMEM(x.shape, x.dtype) for x in ([along_i, along_j, *mask] if mask else [])]
            + [
                pltpu.VMEM((unroll, length + 2 * STEPS, cols), jnp.float32),
                pltpu.VMEM((groups, *shape), jnp.float32),
                pltpu.SemaphoreType.DMA((groups,)),
                pltpu.SemaphoreType.DMA((3, levels // unroll)),
            ],
            compiler_params=params(VMEM_WHOLE if mask else VMEM_LIMIT),
            name="weight_messages",
        )(along_i, along_j, *mask, *halos)
    )


def adjoint_kernel(matrix, depths, *refs):
    parts, out = refs[:-1], refs[-1]
    length, width, order = out.shape
    groups = len(parts)
    rows = length // groups
    cols = groups * width
    count = order // groups
    level = lax.rem(lax.broadcasted_iota(jnp.int32, (order, cols), 0), order // 2).astype(jnp.float32)

    def one(i, carry):
        x = jnp.concatenate([part[pl.ds(i, count, rows), :] for part in parts], axis=0)
        depth = depths[pl.ds(i, 1), :]
        y = jnp.dot(matrix[...], x, precision=HIGHEST, preferred_element_type=jnp.float32)
        y = jnp.where(level < depth, y, 0.0).T
        for a in range(groups):
            out[a * rows + i] = y[a * width:(a + 1) * width]
        return carry

    lax.fori_loop(0, rows, one, 0, unroll=4)


def adjoint_mix(matrix, depths, parts, length, width):
    return pl.pallas_call(
        adjoint_kernel,
        in_specs=[vmem()] * (2 + len(parts)),
        out_specs=vmem(),
        out_shape=jax.ShapeDtypeStruct((length, width, matrix.shape[0]), jnp.float32),
        compiler_params=params(),
        name="adjoint_mix",
    )(matrix, depths, *parts)


def unfold(main, halo, groups):
    cols = main.shape[1]
    width = cols // groups
    below = halo[:STEPS]
    above = pltpu.roll(halo[STEPS:], width, 1)
    return jnp.concatenate(
        [above] + [main] + [pltpu.roll(main, cols - a * width, 1) for a in range(1, groups)] + [below], axis=0
    )


def turn_kernel(starts, *refs):
    depths, parts, (out, held, depth_i, depth_j) = refs[:-4 - len(starts)], refs[-4 - len(starts):-4], refs[-4:]
    length, width, order = out.shape
    groups = len(parts)
    rows = length // groups
    half = order // 2
    count = half // groups
    cols = width * groups
    source = position()[2]
    for i in range(rows):
        for d, part in enumerate(parts):
            for side in range(2):
                at = pl.multiple_of(side * half + source[d] * count, 8)
                held[i, pl.ds(at, count), :] = part[pl.ds(side * count * rows + i, count, rows), :]

    no_halo = jnp.zeros((2 * STEPS, cols), jnp.float32)
    depth = unfold(depths[0][...], depths[1][...] if len(depths) > 1 else no_halo, groups)
    tall = depth.shape[0]
    lane = lax.broadcasted_iota(jnp.int32, depth.shape, 1)
    right = jnp.where(lane == width - 1, depth, pltpu.roll(depth, cols - 1, 1))
    depth_j[...] = jnp.minimum(depth, right)
    depth_i[pl.ds(0, tall - 1), :] = jnp.minimum(depth[:-1], depth[1:])
    depth_i[pl.ds(tall - 1, 1), :] = depth[tall - 1:]
    group = lane_groups(rows, cols, groups)

    def fold(ref):
        x = ref[pl.ds(starts[0], rows), :]
        for a in range(1, groups):
            x = jnp.where(group == a, pltpu.roll(ref[pl.ds(starts[a], rows), :], a * width, 1), x)
        return x

    folded_i, folded_j = fold(depth_i), fold(depth_j)
    level = lax.broadcasted_iota(jnp.int32, (half, cols), 0).astype(jnp.float32)
    for i in range(rows):
        along_i = jnp.where(level < folded_i[i:i + 1], held[i, pl.ds(0, half), :], 0.0)
        along_j = jnp.where(level < folded_j[i:i + 1], held[i, pl.ds(half, half), :], 0.0)
        turned = jnp.concatenate([along_i, along_j], axis=0).T
        for a in range(groups):
            out[a * rows + i] = turned[a * width:(a + 1) * width]


def turn_weights(starts, rows, depths, parts, order):
    groups = len(parts)
    cols = parts[0].shape[1]
    tall = depths[0].shape[0] * groups + 2 * STEPS
    return pl.pallas_call(
        functools.partial(turn_kernel, starts),
        in_specs=[vmem()] * (len(depths) + groups),
        out_specs=vmem(),
        out_shape=jax.ShapeDtypeStruct((rows * groups, cols // groups, order), jnp.float32),
        scratch_shapes=[pltpu.VMEM((rows, order, cols), jnp.float32)] + [pltpu.VMEM((tall, cols), jnp.float32)] * 2,
        compiler_params=params(),
        name="turn_weights",
    )(*depths, *parts)


def edge_masks(depths, order):
    groups = lax.axis_size("lev")
    slot = position()[0][0]
    gy = lax.axis_index("gy")
    start = (slot == 0) & (gy == 0)
    end = (slot == groups - 1) & (gy == lax.axis_size("gy") - 1)
    no_halo = jnp.zeros((2 * STEPS, depths[0].shape[1]), jnp.float32)
    masks = []
    for k, out in enumerate((start, end)):
        x = unfold(depths[k][...], depths[2 + k][...] if len(depths) > 2 else no_halo, groups)
        x = jnp.where(out, 0.0, x)
        x = jnp.broadcast_to(x[:, :1], (x.shape[0], order))
        lane = lax.broadcasted_iota(jnp.int32, x.shape, 1)
        level = lax.rem(lane, order // 2).astype(jnp.float32)
        masks.append(jnp.where((lane < order // 2) | (level < x), 1.0, 0.0))
    return masks


def spread_kernel(windows, field_rows, weight_rows, count, matrix, *refs):
    depths, refs = refs[:count], refs[count:]
    pieces = [refs[3 * k:3 * k + 3] for k in range(len(field_rows) + len(weight_rows))]
    outs, (a, b, wi, wj, masks) = refs[3 * len(pieces):-5], refs[-5:]
    width, order = pieces[0][0].shape[1:]
    half = order // 2
    _, ext, wide, _ = a.shape
    lane = lax.broadcasted_iota(jnp.int32, (wide, order), 1)
    last = lax.broadcasted_iota(jnp.int32, (PAD, order), 0) == PAD - 1
    nothing = jnp.zeros((PAD - STEPS, order), jnp.float32)
    masks[0], masks[1] = edge_masks(depths, order)

    def row_of(some, rows, r):
        piece = [k for k in range(len(rows)) if r in rows[k]][0]
        main, left, right = some[piece]
        k = rows[piece].index(r)
        side = pl.ds(k * STEPS, STEPS)
        return [jnp.concatenate([nothing, left[side, :]], axis=0), main[k], jnp.concatenate([right[side, :], nothing], axis=0)]

    for n, window in enumerate(windows):
        for e, r in enumerate(window):
            a[n, e] = jnp.concatenate(row_of(pieces[:len(field_rows)], field_rows, r), axis=0)
            left, mid, right = row_of(pieces[len(field_rows):], weight_rows, r)
            at = pl.ds(STEPS + r, 1)
            left = jnp.where(last, left * masks[0, at, :], left)
            end = mid[width - PAD:]
            end = jnp.where(last, end * masks[1, at, :], end)
            w = jnp.concatenate([left, mid[:width - PAD], end, right], axis=0)
            other = pltpu.roll(w, half, 1)
            wi[n, e] = jnp.where(lane < half, w, other)
            wj[n, e] = jnp.where(lane < half, other, w)

    src, dst = a, b
    for step in range(STEPS):
        begin, stop = step + 1, ext - 1 - step
        for n in range(len(windows)):

            def one(r, carry, n=n, src=src, dst=dst):
                v, before = carry
                after = src[n, r + 1]
                flux = wi[n, r] * (after - v)
                across = wj[n, r] * (pltpu.roll(v, wide - 1, 0) - v)
                dst[n, r] = v + (flux - before) + (across - pltpu.roll(across, 1, 0))
                return after, flux

            v = src[n, begin]
            lax.fori_loop(begin, stop, one, (v, wi[n, begin - 1] * (v - src[n, begin - 1])), unroll=2)
        src, dst = dst, src

    groups = len(outs)
    count = order // groups
    rows = len(windows) * (ext - 2 * STEPS) // groups
    each = groups // len(windows)

    def mix(i, carry):
        x = jnp.concatenate(
            [src[g // each, STEPS + g % each * rows + i, pl.ds(PAD, width), :] for g in range(groups)], axis=0
        )
        y = lax.dot_general(
            matrix[...], x, (((1,), (1,)), ((), ())), precision=HIGHEST, preferred_element_type=jnp.float32
        )
        for d, out in enumerate(outs):
            out[pl.ds(i, count, rows), :] = y[d * count:(d + 1) * count]
        return carry

    lax.fori_loop(0, rows, mix, 0, unroll=4)


def spread_mix(windows, matrix, depths, field, weights, groups):
    width, order = field[0][1].shape[1:]
    cols = width * groups
    ext = len(windows[0])
    rows = len(windows) * (ext - 2 * STEPS) // groups
    shape = jax.ShapeDtypeStruct((order // groups * rows, cols), jnp.float32)
    arrays = list(depths) + [x for piece in field + weights for x in piece[1:]]
    kernel = functools.partial(
        spread_kernel, windows, [piece[0] for piece in field], [piece[0] for piece in weights], len(depths)
    )
    tall = field[0][1].shape[0] + 2 * STEPS
    return pl.pallas_call(
        kernel,
        in_specs=[vmem()] * (1 + len(arrays)),
        out_specs=[vmem()] * groups,
        out_shape=[shape] * groups,
        scratch_shapes=[pltpu.VMEM((len(windows), ext, width + 2 * PAD, order), jnp.float32)] * 4
        + [pltpu.VMEM((2, tall, order), jnp.float32)],
        compiler_params=params(),
        name="spread_mix",
    )(matrix, *arrays)


RESULT_STEPS = 4


def result_kernel(runs, gain, mask, *refs):
    parts, (out, done, out_sems) = refs[:-3], refs[-3:]
    fields, levels, _, cols = gain.shape
    groups = len(parts)
    rows = done.shape[2] // groups
    some = levels // RESULT_STEPS
    slots = position()[1]
    group = lane_groups(rows, cols, groups)

    def of_slot(slot, at):
        x = parts[0][pl.ds(at, rows), :]
        for d in range(1, groups):
            x = jnp.where(slots[d] == slot, parts[d][pl.ds(at, rows), :], x)
        return x

    stored = []
    for step in range(RESULT_STEPS):
        for level in range(step * some, (step + 1) * some):
            ocean = jnp.concatenate([mask[level, pl.ds(*run), :] for run in runs], axis=0).astype(jnp.float32)
            for field in range(fields):
                at = (field * levels + level) * rows
                blocks = swap([of_slot(slot, at) for slot in range(groups)], group, cols // groups)
                gains = jnp.concatenate([gain[field, level, pl.ds(*run), :] for run in runs], axis=0)
                done[field, level] = ocean * gains * jnp.concatenate(blocks, axis=0)
        these = pl.ds(step * some, some)
        pairs, at = [], 0
        for first, number in runs:
            pairs.append((done.at[:, these, pl.ds(at, number)], out.at[:, these, pl.ds(first, number)]))
            at += number
        stored += copies(pairs, out_sems.at[step])
    for copy in stored:
        copy.wait()


def result(runs, gain, mask, parts, before):
    fields, levels, _, cols = gain.shape
    groups = len(parts)
    rows = sum(number for _, number in runs)
    anywhere = pl.BlockSpec(memory_space=pl.ANY)
    more = [] if before is None else [before]

    def kernel(gain, mask, *refs):
        result_kernel(runs, gain, mask, *refs[:groups], *refs[groups + len(more):])

    return pl.pallas_call(
        kernel,
        in_specs=[vmem()] * (2 + groups) + [anywhere] * len(more),
        out_specs=anywhere,
        out_shape=jax.ShapeDtypeStruct(gain.shape, jnp.float32),
        scratch_shapes=[
            pltpu.VMEM((fields, levels, rows, cols), jnp.float32),
            pltpu.SemaphoreType.DMA((RESULT_STEPS, len(runs))),
        ],
        input_output_aliases={2 + groups: 0} if more else {},
        compiler_params=params(),
        name="result",
    )(gain, mask, *parts, *more)


def shards(increment, norm_gain, diffusion_i, diffusion_j, sea_mask, coupling):
    devices = lax.axis_size("lev")
    gx_size = lax.axis_size("gx")
    gy_size = lax.axis_size("gy")
    _, levels, length, cols = increment.shape
    width = cols // devices
    rows = length // devices
    order = coupling.shape[0]
    to = [lax.rem(lax.axis_index("lev") + d, devices) for d in distances(devices)]
    source = [lax.rem(lax.axis_index("lev") + devices - d, devices) for d in distances(devices)]

    def shift(x, d):
        return lax.ppermute(x, "lev", [(k, (k + d) % devices) for k in range(devices)])

    def exchange(parts):
        return [parts[0]] + [shift(x, d) for x, d in zip(parts[1:], distances(devices)[1:])]

    up = [((k + 1) % gx_size, k) for k in range(gx_size)]
    down = [(b, a) for a, b in up]
    ring = [(devices - 1 - slot if y % 2 else slot) * gy_size + y for y in range(gy_size) for slot in range(devices)]
    ahead = list(zip(ring, ring[1:] + ring[:1]))
    back = [(b, a) for a, b in ahead]

    def halo_i(first, last):
        if gx_size == 2:
            size = first.shape[0]
            both = lax.ppermute(jnp.concatenate([first, last], axis=0), "gx", up)
            return both[size:], both[:size]
        return lax.ppermute(last, "gx", down), lax.ppermute(first, "gx", up)

    def halo_j(first, last):
        return lax.ppermute(last, ("lev", "gy"), ahead), lax.ppermute(first, ("lev", "gy"), back)

    def flat(x):
        return x.reshape(-1, x.shape[-1])

    def cut(x, *sizes):
        return lax.split(x, sizes, 0)

    quarter = length // 4
    some = 2 * quarter // devices
    half = devices // 2
    inner = (quarter, 2 * quarter)
    outer = ((0, quarter), (3 * quarter, quarter))
    inner_rows = list(range(quarter - STEPS, 3 * quarter + STEPS))
    outer_rows = list(range(-STEPS, quarter - STEPS)) + list(range(3 * quarter + STEPS, length + STEPS))
    inner_starts = [quarter + a * len(inner_rows) // devices for a in range(devices)]
    outer_starts = [a * some for a in range(half)] + [3 * quarter + 2 * STEPS + a * some for a in range(half)]
    windows = [list(range(-STEPS, quarter + STEPS)), list(range(3 * quarter - STEPS, length + STEPS))]

    inner_size = len(inner_rows) // devices
    inner_messages = weight_messages(inner_starts, inner_size, diffusion_i, diffusion_j, [sea_mask])
    inner_parts = exchange(inner_messages)
    inner_messages, edge_i, edge_j, increment, norm_gain = lax.optimization_barrier(
        (inner_messages, diffusion_i, diffusion_j, increment, norm_gain)
    )
    halos = halo_i(
        *[
            jnp.concatenate([flat(edge_i[:, at]), flat(edge_j[:, at])], axis=0)
            for at in (slice(0, STEPS), slice(-STEPS, None))
        ]
    )
    messages = scaled_messages(increment, norm_gain, sea_mask, devices)
    scaled = exchange(messages)
    messages, halos = lax.optimization_barrier((messages, halos))
    outer_messages = weight_messages(outer_starts, some, diffusion_i, diffusion_j, halos=halos)

    depth = sum(part[2 * levels * inner_size:] for part in inner_parts)
    here = turn_weights(inner_starts, inner_size, [depth], inner_parts, order)
    left, right = halo_j(
        jnp.concatenate([flat(here[:, :STEPS]), depth], axis=0),
        flat(here[:, -STEPS:]),
    )
    right, right_depth = cut(right, len(inner_rows) * STEPS, rows)

    balance = jnp.eye(order, dtype=jnp.float32) + coupling
    by_device = balance.reshape(2, devices, levels, order)
    adjoint = jnp.concatenate([by_device[:, s].reshape(2 * levels, order) for s in source], axis=0).T
    forward = jnp.concatenate([by_device[:, t].reshape(2 * levels, order) for t in to], axis=0)

    middle = devices // 2
    scaled, outer_messages = lax.optimization_barrier((scaled, outer_messages))
    early = shift(outer_messages[middle], middle)
    mixed = adjoint_mix(adjoint, depth, scaled, length, width)
    edges = flat(mixed[:, :STEPS]), flat(mixed[:, -STEPS:])
    edges, inner_weights = lax.optimization_barrier((edges, (here, left, right)))
    left, right = halo_j(*edges)
    left, right, outer_messages, early = lax.optimization_barrier((left, right, outer_messages, early))
    outer_parts = [
        early if d == middle else shift(outer_messages[d], d) if d else outer_messages[0] for d in range(devices)
    ]
    field = [(list(range(length)), mixed, left, right)]
    weights = [(inner_rows, *inner_weights)]
    depths = [depth, right_depth]
    inner_mixed = spread_mix([inner_rows], forward, depths, field, weights, devices)
    _, upper, lower = lax.optimization_barrier((left, mixed[:STEPS], mixed[-STEPS:]))
    _, outer_parts = lax.optimization_barrier((inner_mixed[0], outer_parts))
    above, below = halo_i(
        jnp.concatenate([flat(upper), depth[:STEPS]], axis=0),
        jnp.concatenate([flat(lower), depth[-STEPS:]], axis=0),
    )
    above, above_depth = cut(above, STEPS * width, STEPS)
    below, below_depth = cut(below, STEPS * width, STEPS)
    halo_depth = jnp.concatenate([below_depth, above_depth], axis=0)
    halo = jnp.concatenate([above, below], axis=0).reshape(2 * STEPS, width, order)
    here = turn_weights(outer_starts, some, [depth, halo_depth], outer_parts, order)
    left, right = halo_j(
        jnp.concatenate([flat(here[:, :STEPS]), flat(halo[:, :STEPS]), halo_depth], axis=0),
        jnp.concatenate([flat(here[:, -STEPS:]), flat(halo[:, -STEPS:])], axis=0),
    )
    sizes = len(outer_rows) * STEPS, 2 * STEPS * STEPS
    left, halo_left = cut(left, *sizes)
    right, halo_right, right_halo_depth = cut(right, *sizes, 2 * STEPS)
    weights.append((outer_rows, here, left, right))
    field.append((list(range(-STEPS, 0)) + list(range(length, length + STEPS)), halo, halo_left, halo_right))
    depths += [halo_depth, right_halo_depth]
    outer_mixed = spread_mix(windows, forward, depths, field, weights, devices)
    _, last = lax.optimization_barrier((outer_mixed[0], inner_mixed[-1]))
    inner_mixed = exchange(list(inner_mixed[:-1]) + [last])
    out = result((inner,), norm_gain, sea_mask, inner_mixed, None)
    outer_mixed = exchange(outer_mixed)
    return result(outer, norm_gain, sea_mask, outer_mixed, out)


def solution(mesh):
    return jax.shard_map(
        shards,
        mesh=mesh,
        in_specs=(
            P(None, "lev", "gx", "gy"),
            P(None, "lev", "gx", "gy"),
            P("lev", "gx", "gy"),
            P("lev", "gx", "gy"),
            P("lev", "gx", "gy"),
            P(),
        ),
        out_specs=P(None, "lev", "gx", "gy"),
        check_vma=False,
    )
```

```python
import functools

import jax
import jax.numpy as jnp
from jax import lax
from jax.experimental import pallas as pl
from jax.experimental.pallas import tpu as pltpu
from jax.sharding import PartitionSpec as P

ITERS = 2
STEPS = 2 * ITERS
PAD = 8
VMEM_LIMIT = 40 * 1024 * 1024
VMEM_WHOLE = 60 * 1024 * 1024
HIGHEST = lax.Precision.HIGHEST


def params(limit=VMEM_LIMIT):
    return pltpu.CompilerParams(vmem_limit_bytes=limit)


def smem():
    return pl.BlockSpec(memory_space=pltpu.SMEM)


def vmem():
    return pl.BlockSpec(memory_space=pltpu.VMEM)


def distances(devices):
    return [0, devices // 2] + [d for d in range(1, devices) if d != devices // 2]


def position():
    devices = lax.axis_size("lev")
    me = lax.axis_index("lev")
    flipped = lax.rem(lax.axis_index("gy"), 2) == 1

    def slot(lev):
        return jnp.where(flipped, devices - 1 - lev, lev)

    to = [lax.rem(me + d, devices) for d in distances(devices)]
    source = [lax.rem(me + devices - d, devices) for d in distances(devices)]
    return [slot(lev) for lev in to], [slot(lev) for lev in source], source


def swap(blocks, group, width, axis=1):
    blocks = list(blocks)
    cols = blocks[0].shape[axis]
    bit = len(blocks) // 2
    while bit:
        shift = bit * width
        low = (group & bit) == 0
        for a in range(len(blocks)):
            if not a & bit:
                x, y = blocks[a], blocks[a + bit]
                blocks[a] = jnp.where(low, x, pltpu.roll(y, shift, axis))
                blocks[a + bit] = jnp.where(low, pltpu.roll(x, cols - shift, axis), y)
        bit //= 2
    return blocks


def lane_groups(rows, cols, groups):
    return lax.broadcasted_iota(jnp.int32, (rows, cols), 1) // (cols // groups)


def copies(pairs, sems):
    made = [pltpu.make_async_copy(src, dst, sems.at[k]) for k, (src, dst) in enumerate(pairs)]
    for copy in made:
        copy.start()
    return made


SCALED_STEPS = 4


def scaled_kernel(increment, gain, mask, *refs):
    outs, (inc, gn, sea, held, sems, out_sems) = refs[:-6], refs[-6:]
    fields, levels, length, cols = increment.shape
    groups = len(outs)
    rows = length // groups
    some = levels // SCALED_STEPS
    group = lane_groups(rows, cols, groups)
    fetched = []
    for step in range(SCALED_STEPS):
        part = pl.ds(step * some, some)
        fetched.append(
            copies(
                [
                    (increment.at[:, part], inc.at[:, part]),
                    (gain.at[:, part], gn.at[:, part]),
                    (mask.at[part], sea.at[part]),
                ],
                sems.at[step],
            )
        )

    for step in range(SCALED_STEPS):
        for copy in fetched[step]:
            copy.wait()

        def one(level, carry):
            ocean = sea[level].astype(jnp.float32)
            for field in range(fields):
                at = pl.multiple_of((field * levels + level) * rows, rows)
                x = ocean * gn[field, level] * inc[field, level]
                blocks = swap([x[a * rows:(a + 1) * rows] for a in range(groups)], group, cols // groups)
                for slot, block in enumerate(blocks):
                    held[slot, pl.ds(at, rows), :] = block
            return carry

        lax.fori_loop(step * some, (step + 1) * some, one, 0, unroll=True)
    slots = position()[0]
    for copy in copies([(held.at[slots[d]], out) for d, out in enumerate(outs)], out_sems):
        copy.wait()


def scaled_messages(increment, gain, mask, groups):
    fields, levels, length, cols = increment.shape
    shape = (fields * levels * length // groups, cols)
    return pl.pallas_call(
        scaled_kernel,
        in_specs=[pl.BlockSpec(memory_space=pl.ANY)] * 3,
        out_specs=[pl.BlockSpec(memory_space=pl.ANY)] * groups,
        out_shape=[jax.ShapeDtypeStruct(shape, jnp.float32)] * groups,
        scratch_shapes=[
            pltpu.VMEM(increment.shape, jnp.float32),
            pltpu.VMEM(gain.shape, jnp.float32),
            pltpu.VMEM(mask.shape, mask.dtype),
            pltpu.VMEM((groups, *shape), jnp.float32),
            pltpu.SemaphoreType.DMA((SCALED_STEPS, 3)),
            pltpu.SemaphoreType.DMA((groups,)),
        ],
        compiler_params=params(VMEM_WHOLE),
        name="scaled_messages",
    )(increment, gain, mask)


def pack_kernel(pieces, masked, along_i, along_j, *refs):
    levels, length, cols = along_i.shape
    groups = len(pieces[0][0])
    width = cols // groups
    halos, outs = refs[masked:-4 - groups - 3 * masked], refs[-4 - groups - 3 * masked:-4 - 3 * masked]
    held, slots_held, sems, fetch_sems = refs[-4:]
    unroll = held.shape[0]
    number = levels // unroll
    starts, rows = pieces[0]
    group = lane_groups(rows, cols, groups)
    if masked:
        sources, (along_i, along_j, sea) = (along_i, along_j, refs[0]), refs[-7:-4]
        fetched = []
        for side, (source, target) in enumerate(zip(sources, (along_i, along_j, sea))):
            pairs = [(source.at[pl.ds(k * unroll, unroll)], target.at[pl.ds(k * unroll, unroll)]) for k in range(number)]
            fetched.append(copies(pairs, fetch_sems.at[side]))

    def put(at, blocks):
        for slot, block in enumerate(blocks):
            slots_held[slot, pl.ds(at, block.shape[0]), :] = block

    for side, weight in enumerate((along_i, along_j)):
        for outer in range(number):
            if masked:
                fetched[side][outer].wait()
            edges = []
            for k in range(unroll):
                level = outer * unroll + k
                index = side * levels + level
                if halos:
                    for halo, at in zip(halos, (0, STEPS + length)):
                        held[k, pl.ds(at, STEPS), :] = halo[pl.ds(index * STEPS, STEPS), :]
                    held[k, pl.ds(STEPS, length), :] = weight[level]
                    blocks = [held[k, pl.ds(start, rows), :] for start in starts]
                else:
                    blocks = [weight[level, pl.ds(start - STEPS, rows), :] for start in starts]
                put(index * rows, swap(blocks, group, width))
                if len(pieces) > 1:
                    small = pieces[1][0]
                    low, high = small[0] - 2 * STEPS, small[groups // 2] - STEPS
                    row = lax.broadcasted_iota(jnp.int32, (2 * STEPS, cols), 0)
                    upper = pltpu.roll(weight[level, pl.ds(low, 2 * STEPS), :], STEPS, 0)
                    lower = pltpu.roll(weight[level, pl.ds(high, 2 * STEPS), :], STEPS, 0)
                    edges.append(jnp.where(row < STEPS, upper, lower))
            if edges:
                each = pieces[1][1]
                pairs = lax.broadcasted_iota(jnp.int32, edges[0].shape, 0) // each
                edges = swap(edges, pairs, each, 0)
                at = 2 * levels * rows + (side * levels + outer * unroll) * each
                put(at, swap(edges, lane_groups(unroll * each, cols, groups), width))
    if masked:
        depth = jnp.zeros((length, cols), sea.dtype)
        for outer in range(number):
            fetched[2][outer].wait()
            for level in range(outer * unroll, (outer + 1) * unroll):
                depth = depth + sea[level]
        depth = depth.astype(jnp.float32)
        size = length // groups
        blocks = [depth[a * size:(a + 1) * size] for a in range(groups)]
        put(2 * levels * sum(n for _, n in pieces), swap(blocks, lane_groups(size, cols, groups), width))
    slots = position()[0]
    for copy in copies([(slots_held.at[slots[d]], out) for d, out in enumerate(outs)], sems):
        copy.wait()


def weight_messages(pieces, along_i, along_j, mask=(), halos=()):
    levels, length, cols = along_i.shape
    groups = len(pieces[0][0])
    shape = (2 * levels * sum(rows for _, rows in pieces) + len(mask) * length // groups, cols)
    unroll = 4
    return list(
        pl.pallas_call(
            functools.partial(pack_kernel, pieces, len(mask)),
            in_specs=[pl.BlockSpec(memory_space=pl.ANY) if mask else vmem()] * (2 + len(mask) + len(halos)),
            out_specs=[pl.BlockSpec(memory_space=pl.ANY)] * groups,
            out_shape=[jax.ShapeDtypeStruct(shape, jnp.float32)] * groups,
            scratch_shapes=[pltpu.VMEM(x.shape, x.dtype) for x in ([along_i, along_j, *mask] if mask else [])]
            + [
                pltpu.VMEM((unroll, length + 2 * STEPS, cols), jnp.float32),
                pltpu.VMEM((groups, *shape), jnp.float32),
                pltpu.SemaphoreType.DMA((groups,)),
                pltpu.SemaphoreType.DMA((3, levels // unroll)),
            ],
            compiler_params=params(VMEM_WHOLE if mask else VMEM_LIMIT),
            name="weight_messages",
        )(along_i, along_j, *mask, *halos)
    )


def three(x):
    high = x.astype(jnp.bfloat16)
    rest = x - high.astype(jnp.float32)
    middle = rest.astype(jnp.bfloat16)
    return high, middle, (rest - middle.astype(jnp.float32)).astype(jnp.bfloat16)


def left_terms(x):
    high, middle, low = three(x)
    return jnp.concatenate([high, middle, low, high, middle, high], axis=1)


def right_terms(x, axis):
    high, middle, low = three(x)
    return jnp.concatenate([high, high, high, middle, middle, low], axis=axis)


def adjoint_kernel(matrix, depths, *refs):
    parts, out, terms = refs[:-2], refs[-2], refs[-1]
    length, width, order = out.shape
    groups = len(parts)
    rows = length // groups
    cols = groups * width
    count = order // groups
    level = lax.rem(lax.broadcasted_iota(jnp.int32, (order, cols), 0), order // 2).astype(jnp.float32)

    terms[...] = left_terms(matrix[...])

    def two(pair, carry):
        planes = [2 * pair, 2 * pair + 1]
        x = jnp.concatenate(
            [jnp.concatenate([part[pl.ds(i, count, rows), :] for part in parts], axis=0) for i in planes], axis=1
        )
        y = jnp.dot(terms[...], right_terms(x, 0), preferred_element_type=jnp.float32)
        for k, i in enumerate(planes):
            z = jnp.where(level < depths[pl.ds(i, 1), :], y[:, k * cols:(k + 1) * cols], 0.0).T
            for a in range(groups):
                out[a * rows + i] = z[a * width:(a + 1) * width]
        return carry

    lax.fori_loop(0, rows // 2, two, 0, unroll=2)


def adjoint_mix(matrix, depths, parts, length, width):
    return pl.pallas_call(
        adjoint_kernel,
        in_specs=[vmem()] * (2 + len(parts)),
        out_specs=vmem(),
        out_shape=jax.ShapeDtypeStruct((length, width, matrix.shape[0]), jnp.float32),
        scratch_shapes=[pltpu.VMEM((matrix.shape[0], 6 * matrix.shape[0]), jnp.bfloat16)],
        compiler_params=params(),
        name="adjoint_mix",
    )(matrix, depths, *parts)


def unfold(main, halo, groups):
    cols = main.shape[1]
    width = cols // groups
    below = halo[:STEPS]
    above = pltpu.roll(halo[STEPS:], width, 1)
    return jnp.concatenate(
        [above] + [main] + [pltpu.roll(main, cols - a * width, 1) for a in range(1, groups)] + [below], axis=0
    )


def turn_kernel(pieces, *refs):
    groups = len(pieces[0][0])
    depths, parts, (out, held, depth_i, depth_j) = refs[:-4 - groups], refs[-4 - groups:-4], refs[-4:]
    _, width, order = out.shape
    half = order // 2
    count = half // groups
    cols = width * groups
    source = position()[2]
    planes, base = [], 0
    for starts, rows in pieces:
        planes += [(base + i, rows, i, starts) for i in range(rows)]
        base += 2 * count * rows
    for k, (first, rows, _, _) in enumerate(planes):
        for d, part in enumerate(parts):
            for side in range(2):
                at = pl.multiple_of(side * half + source[d] * count, 8)
                held[k, pl.ds(at, count), :] = part[pl.ds(first + side * count * rows, count, rows), :]

    no_halo = jnp.zeros((2 * STEPS, cols), jnp.float32)
    depth = unfold(depths[0][...], depths[1][...] if len(depths) > 1 else no_halo, groups)
    tall = depth.shape[0]
    lane = lax.broadcasted_iota(jnp.int32, depth.shape, 1)
    right = jnp.where(lane == width - 1, depth, pltpu.roll(depth, cols - 1, 1))
    depth_j[...] = jnp.minimum(depth, right)
    depth_i[pl.ds(0, tall - 1), :] = jnp.minimum(depth[:-1], depth[1:])
    depth_i[pl.ds(tall - 1, 1), :] = depth[tall - 1:]

    def fold(ref, starts, rows):
        group = lane_groups(rows, cols, groups)
        x = ref[pl.ds(starts[0], rows), :]
        for a in range(1, groups):
            x = jnp.where(group == a, pltpu.roll(ref[pl.ds(starts[a], rows), :], a * width, 1), x)
        return x

    folded = [(fold(depth_i, *piece), fold(depth_j, *piece)) for piece in pieces]
    level = lax.broadcasted_iota(jnp.int32, (half, cols), 0).astype(jnp.float32)
    at = 0
    for n, (starts, rows) in enumerate(pieces):
        for i in range(rows):
            k = at // groups + i
            along_i = jnp.where(level < folded[n][0][i:i + 1], held[k, pl.ds(0, half), :], 0.0)
            along_j = jnp.where(level < folded[n][1][i:i + 1], held[k, pl.ds(half, half), :], 0.0)
            turned = jnp.concatenate([along_i, along_j], axis=0).T
            for a in range(groups):
                out[at + a * rows + i] = turned[a * width:(a + 1) * width]
        at += groups * rows


def turn_weights(pieces, depths, parts, order):
    groups = len(parts)
    cols = parts[0].shape[1]
    rows = sum(n for _, n in pieces)
    tall = depths[0].shape[0] * groups + 2 * STEPS
    return pl.pallas_call(
        functools.partial(turn_kernel, pieces),
        in_specs=[vmem()] * (len(depths) + groups),
        out_specs=vmem(),
        out_shape=jax.ShapeDtypeStruct((rows * groups, cols // groups, order), jnp.float32),
        scratch_shapes=[pltpu.VMEM((rows, order, cols), jnp.float32)] + [pltpu.VMEM((tall, cols), jnp.float32)] * 2,
        compiler_params=params(),
        name="turn_weights",
    )(*depths, *parts)


def edge_masks(depths, order):
    groups = lax.axis_size("lev")
    slot = position()[0][0]
    gy = lax.axis_index("gy")
    start = (slot == 0) & (gy == 0)
    end = (slot == groups - 1) & (gy == lax.axis_size("gy") - 1)
    no_halo = jnp.zeros((2 * STEPS, depths[0].shape[1]), jnp.float32)
    masks = []
    for k, out in enumerate((start, end)):
        x = unfold(depths[k][...], depths[2 + k][...] if len(depths) > 2 else no_halo, groups)
        x = jnp.where(out, 0.0, x)
        x = jnp.broadcast_to(x[:, :1], (x.shape[0], order))
        lane = lax.broadcasted_iota(jnp.int32, x.shape, 1)
        level = lax.rem(lane, order // 2).astype(jnp.float32)
        masks.append(jnp.where((lane < order // 2) | (level < x), 1.0, 0.0))
    return masks


def spread_kernel(windows, field_rows, weight_rows, count, matrix, *refs):
    depths, refs = refs[:count], refs[count:]
    pieces = [refs[3 * k:3 * k + 3] for k in range(len(field_rows) + len(weight_rows))]
    outs, (a, b, wi, wj, masks, terms) = refs[3 * len(pieces):-6], refs[-6:]
    width, order = pieces[0][0].shape[1:]
    half = order // 2
    _, ext, wide, _ = a.shape
    lane = lax.broadcasted_iota(jnp.int32, (wide, order), 1)
    last = lax.broadcasted_iota(jnp.int32, (PAD, order), 0) == PAD - 1
    nothing = jnp.zeros((PAD - STEPS, order), jnp.float32)
    masks[0], masks[1] = edge_masks(depths, order)

    def row_of(some, rows, r):
        piece = [k for k in range(len(rows)) if r in rows[k]][0]
        main, left, right = some[piece]
        k = rows[piece].index(r)
        side = pl.ds(k * STEPS, STEPS)
        return [jnp.concatenate([nothing, left[side, :]], axis=0), main[k], jnp.concatenate([right[side, :], nothing], axis=0)]

    for n, window in enumerate(windows):
        for e, r in enumerate(window):
            a[n, e] = jnp.concatenate(row_of(pieces[:len(field_rows)], field_rows, r), axis=0)
            left, mid, right = row_of(pieces[len(field_rows):], weight_rows, r)
            at = pl.ds(STEPS + r, 1)
            left = jnp.where(last, left * masks[0, at, :], left)
            end = mid[width - PAD:]
            end = jnp.where(last, end * masks[1, at, :], end)
            w = jnp.concatenate([left, mid[:width - PAD], end, right], axis=0)
            other = pltpu.roll(w, half, 1)
            wi[n, e] = jnp.where(lane < half, w, other)
            wj[n, e] = jnp.where(lane < half, other, w)

    src, dst = a, b
    for step in range(STEPS):
        begin, stop = step + 1, ext - 1 - step
        for n in range(len(windows)):

            def one(r, carry, n=n, src=src, dst=dst):
                v, before = carry
                after = src[n, r + 1]
                flux = wi[n, r] * (after - v)
                across = wj[n, r] * (pltpu.roll(v, wide - 1, 0) - v)
                dst[n, r] = v + (flux - before) + (across - pltpu.roll(across, 1, 0))
                return after, flux

            v = src[n, begin]
            lax.fori_loop(begin, stop, one, (v, wi[n, begin - 1] * (v - src[n, begin - 1])), unroll=2)
        src, dst = dst, src

    groups = len(outs)
    count = order // groups
    rows = len(windows) * (ext - 2 * STEPS) // groups
    each = groups // len(windows)

    terms[...] = left_terms(matrix[...])

    def mix(pair, carry):
        planes = [2 * pair, 2 * pair + 1]
        x = jnp.concatenate(
            [src[g // each, STEPS + g % each * rows + i, pl.ds(PAD, width), :] for i in planes for g in range(groups)],
            axis=0,
        )
        y = lax.dot_general(
            terms[...], right_terms(x, 1), (((1,), (1,)), ((), ())), preferred_element_type=jnp.float32
        )
        cols = groups * width
        for k, i in enumerate(planes):
            for d, out in enumerate(outs):
                out[pl.ds(i, count, rows), :] = y[d * count:(d + 1) * count, k * cols:(k + 1) * cols]
        return carry

    lax.fori_loop(0, rows // 2, mix, 0, unroll=2)


def spread_mix(windows, matrix, depths, field, weights, groups):
    width, order = field[0][1].shape[1:]
    cols = width * groups
    ext = len(windows[0])
    rows = len(windows) * (ext - 2 * STEPS) // groups
    shape = jax.ShapeDtypeStruct((order // groups * rows, cols), jnp.float32)
    arrays = list(depths) + [x for piece in field + weights for x in piece[1:]]
    kernel = functools.partial(
        spread_kernel, windows, [piece[0] for piece in field], [piece[0] for piece in weights], len(depths)
    )
    tall = field[0][1].shape[0] + 2 * STEPS
    return pl.pallas_call(
        kernel,
        in_specs=[vmem()] * (1 + len(arrays)),
        out_specs=[vmem()] * groups,
        out_shape=[shape] * groups,
        scratch_shapes=[pltpu.VMEM((len(windows), ext, width + 2 * PAD, order), jnp.float32)] * 4
        + [pltpu.VMEM((2, tall, order), jnp.float32), pltpu.VMEM((order, 6 * order), jnp.bfloat16)],
        compiler_params=params(),
        name="spread_mix",
    )(matrix, *arrays)


RESULT_STEPS = 4


def result_kernel(runs, gain, mask, *refs):
    parts, (out, done, out_sems) = refs[:-3], refs[-3:]
    fields, levels, _, cols = gain.shape
    groups = len(parts)
    rows = done.shape[2] // groups
    some = levels // RESULT_STEPS
    slots = position()[1]
    group = lane_groups(rows, cols, groups)

    def of_slot(slot, at):
        x = parts[0][pl.ds(at, rows), :]
        for d in range(1, groups):
            x = jnp.where(slots[d] == slot, parts[d][pl.ds(at, rows), :], x)
        return x

    stored = []
    for step in range(RESULT_STEPS):
        for level in range(step * some, (step + 1) * some):
            ocean = jnp.concatenate([mask[level, pl.ds(*run), :] for run in runs], axis=0).astype(jnp.float32)
            for field in range(fields):
                at = (field * levels + level) * rows
                blocks = swap([of_slot(slot, at) for slot in range(groups)], group, cols // groups)
                gains = jnp.concatenate([gain[field, level, pl.ds(*run), :] for run in runs], axis=0)
                done[field, level] = ocean * gains * jnp.concatenate(blocks, axis=0)
        these = pl.ds(step * some, some)
        pairs, at = [], 0
        for first, number in runs:
            pairs.append((done.at[:, these, pl.ds(at, number)], out.at[:, these, pl.ds(first, number)]))
            at += number
        stored += copies(pairs, out_sems.at[step])
    for copy in stored:
        copy.wait()


def result(runs, gain, mask, parts, before):
    fields, levels, _, cols = gain.shape
    groups = len(parts)
    rows = sum(number for _, number in runs)
    anywhere = pl.BlockSpec(memory_space=pl.ANY)
    more = [] if before is None else [before]

    def kernel(gain, mask, *refs):
        result_kernel(runs, gain, mask, *refs[:groups], *refs[groups + len(more):])

    return pl.pallas_call(
        kernel,
        in_specs=[vmem()] * (2 + groups) + [anywhere] * len(more),
        out_specs=anywhere,
        out_shape=jax.ShapeDtypeStruct(gain.shape, jnp.float32),
        scratch_shapes=[
            pltpu.VMEM((fields, levels, rows, cols), jnp.float32),
            pltpu.SemaphoreType.DMA((RESULT_STEPS, len(runs))),
        ],
        input_output_aliases={2 + groups: 0} if more else {},
        compiler_params=params(),
        name="result",
    )(gain, mask, *parts, *more)


def shards(increment, norm_gain, diffusion_i, diffusion_j, sea_mask, coupling):
    devices = lax.axis_size("lev")
    gx_size = lax.axis_size("gx")
    gy_size = lax.axis_size("gy")
    _, levels, length, cols = increment.shape
    width = cols // devices
    rows = length // devices
    order = coupling.shape[0]
    to = [lax.rem(lax.axis_index("lev") + d, devices) for d in distances(devices)]
    source = [lax.rem(lax.axis_index("lev") + devices - d, devices) for d in distances(devices)]

    def shift(x, d):
        return lax.ppermute(x, "lev", [(k, (k + d) % devices) for k in range(devices)])

    def exchange(parts):
        return [parts[0]] + [shift(x, d) for x, d in zip(parts[1:], distances(devices)[1:])]

    up = [((k + 1) % gx_size, k) for k in range(gx_size)]
    down = [(b, a) for a, b in up]
    ring = [(devices - 1 - slot if y % 2 else slot) * gy_size + y for y in range(gy_size) for slot in range(devices)]
    ahead = list(zip(ring, ring[1:] + ring[:1]))
    back = [(b, a) for a, b in ahead]

    def halo_i(first, last):
        if gx_size == 2:
            size = first.shape[0]
            both = lax.ppermute(jnp.concatenate([first, last], axis=0), "gx", up)
            return both[size:], both[:size]
        return lax.ppermute(last, "gx", down), lax.ppermute(first, "gx", up)

    def halo_j(first, last):
        return lax.ppermute(last, ("lev", "gy"), ahead), lax.ppermute(first, ("lev", "gy"), back)

    def flat(x):
        return x.reshape(-1, x.shape[-1])

    def cut(x, *sizes):
        return lax.split(x, sizes, 0)

    quarter = length // 4
    some = 2 * quarter // devices
    half = devices // 2
    inner = (quarter, 2 * quarter)
    outer = ((0, quarter), (3 * quarter, quarter))
    inner_pieces = [
        ([STEPS + quarter + a * some for a in range(devices)], some),
        ([quarter + 2 * a for a in range(half)] + [STEPS + 3 * quarter + 2 * a for a in range(half)], 2),
    ]
    outer_pieces = [([a * some for a in range(half)] + [3 * quarter + 2 * STEPS + a * some for a in range(half)], some)]

    def rows_of(pieces):
        return [start - STEPS + i for starts, number in pieces for start in starts for i in range(number)]

    inner_rows, outer_rows = rows_of(inner_pieces), rows_of(outer_pieces)
    windows = [list(range(-STEPS, quarter + STEPS)), list(range(3 * quarter - STEPS, length + STEPS))]

    inner_size = len(inner_rows) // devices
    inner_messages = weight_messages(inner_pieces, diffusion_i, diffusion_j, [sea_mask])
    inner_parts = exchange(inner_messages)
    inner_messages, edge_i, edge_j, increment, norm_gain = lax.optimization_barrier(
        (inner_messages, diffusion_i, diffusion_j, increment, norm_gain)
    )
    halos = halo_i(
        *[
            jnp.concatenate([flat(edge_i[:, at]), flat(edge_j[:, at])], axis=0)
            for at in (slice(0, STEPS), slice(-STEPS, None))
        ]
    )
    messages = scaled_messages(increment, norm_gain, sea_mask, devices)
    scaled = exchange(messages)
    messages, halos = lax.optimization_barrier((messages, halos))
    outer_messages = weight_messages(outer_pieces, diffusion_i, diffusion_j, halos=halos)

    depth = sum(part[2 * levels * inner_size:] for part in inner_parts)
    here = turn_weights(inner_pieces, [depth], inner_parts, order)
    left, right = halo_j(
        jnp.concatenate([flat(here[:, :STEPS]), depth], axis=0),
        flat(here[:, -STEPS:]),
    )
    right, right_depth = cut(right, len(inner_rows) * STEPS, rows)

    balance = jnp.eye(order, dtype=jnp.float32) + coupling
    by_device = balance.reshape(2, devices, levels, order)
    adjoint = jnp.concatenate([by_device[:, s].reshape(2 * levels, order) for s in source], axis=0).T
    forward = jnp.concatenate([by_device[:, t].reshape(2 * levels, order) for t in to], axis=0)

    scaled[1], outer_messages = lax.optimization_barrier((scaled[1], outer_messages))
    early = shift(outer_messages[1], devices // 2)
    mixed = adjoint_mix(adjoint, depth, scaled, length, width)
    edges = flat(mixed[:, :STEPS]), flat(mixed[:, -STEPS:])
    edges, inner_weights = lax.optimization_barrier((edges, (here, left, right)))
    left, right = halo_j(*edges)
    left, right, outer_messages, early = lax.optimization_barrier((left, right, outer_messages, early))
    own, _, *others = outer_messages
    outer_parts = [own, early] + [shift(x, d) for x, d in zip(others, distances(devices)[2:])]
    field = [(list(range(length)), mixed, left, right)]
    weights = [(inner_rows, *inner_weights)]
    depths = [depth, right_depth]
    inner_mixed = spread_mix([sorted(inner_rows)], forward, depths, field, weights, devices)
    _, upper, lower = lax.optimization_barrier((left, mixed[:STEPS], mixed[-STEPS:]))
    _, outer_parts = lax.optimization_barrier((inner_mixed[0], outer_parts))
    inner_mixed = exchange(inner_mixed)
    out = result((inner,), norm_gain, sea_mask, inner_mixed, None)

    above, below = halo_i(
        jnp.concatenate([flat(upper), depth[:STEPS]], axis=0),
        jnp.concatenate([flat(lower), depth[-STEPS:]], axis=0),
    )
    above, above_depth = cut(above, STEPS * width, STEPS)
    below, below_depth = cut(below, STEPS * width, STEPS)
    halo_depth = jnp.concatenate([below_depth, above_depth], axis=0)
    halo = jnp.concatenate([above, below], axis=0).reshape(2 * STEPS, width, order)
    here = turn_weights(outer_pieces, [depth, halo_depth], outer_parts, order)
    left, right = halo_j(
        jnp.concatenate([flat(here[:, :STEPS]), flat(halo[:, :STEPS]), halo_depth], axis=0),
        jnp.concatenate([flat(here[:, -STEPS:]), flat(halo[:, -STEPS:])], axis=0),
    )
    sizes = len(outer_rows) * STEPS, 2 * STEPS * STEPS
    left, halo_left = cut(left, *sizes)
    right, halo_right, right_halo_depth = cut(right, *sizes, 2 * STEPS)
    weights.append((outer_rows, here, left, right))
    field.append((list(range(-STEPS, 0)) + list(range(length, length + STEPS)), halo, halo_left, halo_right))
    depths += [halo_depth, right_halo_depth]
    outer_mixed = exchange(spread_mix(windows, forward, depths, field, weights, devices))
    return result(outer, norm_gain, sea_mask, outer_mixed, out)


def solution(mesh):
    return jax.shard_map(
        shards,
        mesh=mesh,
        in_specs=(
            P(None, "lev", "gx", "gy"),
            P(None, "lev", "gx", "gy"),
            P("lev", "gx", "gy"),
            P("lev", "gx", "gy"),
            P("lev", "gx", "gy"),
            P(),
        ),
        out_specs=P(None, "lev", "gx", "gy"),
        check_vma=False,
    )
```

```python
import functools

import jax
import jax.numpy as jnp
from jax import lax
from jax.experimental import pallas as pl
from jax.experimental.pallas import tpu as pltpu
from jax.sharding import PartitionSpec as P

ITERS = 2
STEPS = 2 * ITERS
PAD = 8
VMEM_LIMIT = 40 * 1024 * 1024
VMEM_WHOLE = 60 * 1024 * 1024
HIGHEST = lax.Precision.HIGHEST


def params(limit=VMEM_LIMIT):
    return pltpu.CompilerParams(vmem_limit_bytes=limit)


def smem():
    return pl.BlockSpec(memory_space=pltpu.SMEM)


def vmem():
    return pl.BlockSpec(memory_space=pltpu.VMEM)


def distances(devices):
    return [0, devices // 2] + [d for d in range(1, devices) if d != devices // 2]


def position():
    devices = lax.axis_size("lev")
    me = lax.axis_index("lev")
    flipped = lax.rem(lax.axis_index("gy"), 2) == 1

    def slot(lev):
        return jnp.where(flipped, devices - 1 - lev, lev)

    to = [lax.rem(me + d, devices) for d in distances(devices)]
    source = [lax.rem(me + devices - d, devices) for d in distances(devices)]
    return [slot(lev) for lev in to], [slot(lev) for lev in source], source


def swap(blocks, group, width, axis=1):
    blocks = list(blocks)
    cols = blocks[0].shape[axis]
    bit = len(blocks) // 2
    while bit:
        shift = bit * width
        low = (group & bit) == 0
        for a in range(len(blocks)):
            if not a & bit:
                x, y = blocks[a], blocks[a + bit]
                blocks[a] = jnp.where(low, x, pltpu.roll(y, shift, axis))
                blocks[a + bit] = jnp.where(low, pltpu.roll(x, cols - shift, axis), y)
        bit //= 2
    return blocks


def lane_groups(rows, cols, groups):
    return lax.broadcasted_iota(jnp.int32, (rows, cols), 1) // (cols // groups)


def copies(pairs, sems):
    made = [pltpu.make_async_copy(src, dst, sems.at[k]) for k, (src, dst) in enumerate(pairs)]
    for copy in made:
        copy.start()
    return made


SCALED_STEPS = 4


def scaled_kernel(increment, gain, mask, *refs):
    outs, (inc, gn, sea, held, sems, out_sems) = refs[:-6], refs[-6:]
    fields, levels, length, cols = increment.shape
    groups = len(outs)
    rows = length // groups
    some = levels // SCALED_STEPS
    group = lane_groups(rows, cols, groups)
    fetched = []
    for step in range(SCALED_STEPS):
        part = pl.ds(step * some, some)
        fetched.append(
            copies(
                [
                    (increment.at[:, part], inc.at[:, part]),
                    (gain.at[:, part], gn.at[:, part]),
                    (mask.at[part], sea.at[part]),
                ],
                sems.at[step],
            )
        )

    for step in range(SCALED_STEPS):
        for copy in fetched[step]:
            copy.wait()

        def one(level, carry):
            ocean = sea[level].astype(jnp.float32)
            for field in range(fields):
                at = pl.multiple_of((field * levels + level) * rows, rows)
                x = ocean * gn[field, level] * inc[field, level]
                blocks = swap([x[a * rows:(a + 1) * rows] for a in range(groups)], group, cols // groups)
                for slot, block in enumerate(blocks):
                    held[slot, pl.ds(at, rows), :] = block
            return carry

        lax.fori_loop(step * some, (step + 1) * some, one, 0)
    slots = position()[0]
    for copy in copies([(held.at[slots[d]], out) for d, out in enumerate(outs)], out_sems):
        copy.wait()


def scaled_messages(increment, gain, mask, groups):
    fields, levels, length, cols = increment.shape
    shape = (fields * levels * length // groups, cols)
    return pl.pallas_call(
        scaled_kernel,
        in_specs=[pl.BlockSpec(memory_space=pl.ANY)] * 3,
        out_specs=[pl.BlockSpec(memory_space=pl.ANY)] * groups,
        out_shape=[jax.ShapeDtypeStruct(shape, jnp.float32)] * groups,
        scratch_shapes=[
            pltpu.VMEM(increment.shape, jnp.float32),
            pltpu.VMEM(gain.shape, jnp.float32),
            pltpu.VMEM(mask.shape, mask.dtype),
            pltpu.VMEM((groups, *shape), jnp.float32),
            pltpu.SemaphoreType.DMA((SCALED_STEPS, 3)),
            pltpu.SemaphoreType.DMA((groups,)),
        ],
        compiler_params=params(VMEM_WHOLE),
        name="scaled_messages",
    )(increment, gain, mask)


def pack_kernel(pieces, masked, along_i, along_j, *refs):
    levels, length, cols = along_i.shape
    groups = len(pieces[0][0])
    width = cols // groups
    extra, refs = refs[:1 if masked else 2], refs[1 if masked else 2:]
    outs, refs = refs[:groups], refs[groups:]
    ends, refs = refs[:masked], refs[masked:]
    held, slots_held, sems, fetch_sems = refs[-4:]
    unroll = held.shape[0]
    number = levels // unroll
    starts, rows = pieces[0]
    group = lane_groups(rows, cols, groups)
    sources = (along_i, along_j) + (extra if masked else ())
    targets = refs[:-4]
    fetched = []
    for side, (source, target) in enumerate(zip(sources, targets)):
        pairs = [(source.at[pl.ds(k * unroll, unroll)], target.at[pl.ds(k * unroll, unroll)]) for k in range(number)]
        fetched.append(copies(pairs, fetch_sems.at[side]))

    def put(at, blocks):
        for slot, block in enumerate(blocks):
            slots_held[slot, pl.ds(at, block.shape[0]), :] = block

    for side, weight in enumerate(targets[:2]):
        for copy in fetched[side]:
            copy.wait()

        def some(outer, carry, side=side, weight=weight):
            edges = []
            first = side * levels + outer * unroll
            if masked:
                for end, at in enumerate((0, length - STEPS)):
                    block = [weight[outer * unroll + k, pl.ds(at, STEPS), :] for k in range(unroll)]
                    to = pl.multiple_of((end * 2 * levels + first) * STEPS, 8)
                    ends[0][pl.ds(to, unroll * STEPS), :] = jnp.concatenate(block, axis=0)
            else:
                to = pl.multiple_of(first * STEPS, 8)
                blocks = [halo[pl.ds(to, unroll * STEPS), :] for halo in extra]
            for k in range(unroll):
                level = outer * unroll + k
                if masked:
                    mine = [weight[level, pl.ds(start - STEPS, rows), :] for start in starts]
                else:
                    for block, at in zip(blocks, (0, STEPS + length)):
                        held[k, pl.ds(at, STEPS), :] = block[k * STEPS:(k + 1) * STEPS]
                    held[k, pl.ds(STEPS, length), :] = weight[level]
                    mine = [held[k, pl.ds(start, rows), :] for start in starts]
                put(pl.multiple_of((first + k) * rows, 8), swap(mine, group, width))
                if len(pieces) > 1:
                    small = pieces[1][0]
                    low, high = small[0] - 2 * STEPS, small[groups // 2] - STEPS
                    row = lax.broadcasted_iota(jnp.int32, (2 * STEPS, cols), 0)
                    upper = pltpu.roll(weight[level, pl.ds(low, 2 * STEPS), :], STEPS, 0)
                    lower = pltpu.roll(weight[level, pl.ds(high, 2 * STEPS), :], STEPS, 0)
                    edges.append(jnp.where(row < STEPS, upper, lower))
            if edges:
                each = pieces[1][1]
                pairs = lax.broadcasted_iota(jnp.int32, edges[0].shape, 0) // each
                edges = swap(edges, pairs, each, 0)
                to = pl.multiple_of(2 * levels * rows + first * each, 8)
                put(to, swap(edges, lane_groups(unroll * each, cols, groups), width))
            return carry

        lax.fori_loop(0, number, some, 0)
    if masked:
        for copy in fetched[2]:
            copy.wait()
        sea = targets[2]
        depth = lax.fori_loop(0, levels, lambda level, x: x + sea[level], jnp.zeros((length, cols), sea.dtype), unroll=4)
        depth = depth.astype(jnp.float32)
        size = length // groups
        blocks = [depth[a * size:(a + 1) * size] for a in range(groups)]
        put(2 * levels * sum(n for _, n in pieces), swap(blocks, lane_groups(size, cols, groups), width))
    slots = position()[0]
    for copy in copies([(slots_held.at[slots[d]], out) for d, out in enumerate(outs)], sems):
        copy.wait()


def weight_messages(pieces, along_i, along_j, mask=(), halos=()):
    levels, length, cols = along_i.shape
    groups = len(pieces[0][0])
    shape = (2 * levels * sum(rows for _, rows in pieces) + len(mask) * length // groups, cols)
    ends = [(4 * levels * STEPS, cols)] * len(mask)
    unroll = 4
    anywhere = pl.BlockSpec(memory_space=pl.ANY)
    return list(
        pl.pallas_call(
            functools.partial(pack_kernel, pieces, len(mask)),
            in_specs=[anywhere] * (2 + len(mask)) + [vmem()] * len(halos),
            out_specs=[anywhere] * groups + [vmem()] * len(ends),
            out_shape=[jax.ShapeDtypeStruct(x, jnp.float32) for x in [shape] * groups + ends],
            scratch_shapes=[pltpu.VMEM(x.shape, x.dtype) for x in (along_i, along_j, *mask)]
            + [
                pltpu.VMEM((unroll, length + 2 * STEPS, cols), jnp.float32),
                pltpu.VMEM((groups, *shape), jnp.float32),
                pltpu.SemaphoreType.DMA((groups,)),
                pltpu.SemaphoreType.DMA((3, levels // unroll)),
            ],
            compiler_params=params(VMEM_WHOLE if mask else VMEM_LIMIT),
            name="weight_messages",
        )(along_i, along_j, *mask, *halos)
    )


def three(x):
    high = x.astype(jnp.bfloat16)
    rest = x - high.astype(jnp.float32)
    middle = rest.astype(jnp.bfloat16)
    return high, middle, (rest - middle.astype(jnp.float32)).astype(jnp.bfloat16)


def left_terms(x):
    high, middle, low = three(x)
    return jnp.concatenate([high, middle, low, high, middle, high], axis=1)


def right_terms(x, axis):
    high, middle, low = three(x)
    return jnp.concatenate([high, high, high, middle, middle, low], axis=axis)


def adjoint_kernel(matrix, depths, *refs):
    parts, out, terms = refs[:-2], refs[-2], refs[-1]
    length, width, order = out.shape
    groups = len(parts)
    rows = length // groups
    cols = groups * width
    count = order // groups
    level = lax.rem(lax.broadcasted_iota(jnp.int32, (order, cols), 0), order // 2).astype(jnp.float32)

    terms[...] = left_terms(matrix[...])

    def two(pair, carry):
        planes = [2 * pair, 2 * pair + 1]
        x = jnp.concatenate(
            [jnp.concatenate([part[pl.ds(i, count, rows), :] for part in parts], axis=0) for i in planes], axis=1
        )
        y = jnp.dot(terms[...], right_terms(x, 0), preferred_element_type=jnp.float32)
        for k, i in enumerate(planes):
            z = jnp.where(level < depths[pl.ds(i, 1), :], y[:, k * cols:(k + 1) * cols], 0.0).T
            for a in range(groups):
                out[a * rows + i] = z[a * width:(a + 1) * width]
        return carry

    lax.fori_loop(0, rows // 2, two, 0, unroll=2)


def adjoint_mix(matrix, depths, parts, length, width):
    return pl.pallas_call(
        adjoint_kernel,
        in_specs=[vmem()] * (2 + len(parts)),
        out_specs=vmem(),
        out_shape=jax.ShapeDtypeStruct((length, width, matrix.shape[0]), jnp.float32),
        scratch_shapes=[pltpu.VMEM((matrix.shape[0], 6 * matrix.shape[0]), jnp.bfloat16)],
        compiler_params=params(),
        name="adjoint_mix",
    )(matrix, depths, *parts)


def unfold(main, halo, groups):
    cols = main.shape[1]
    width = cols // groups
    below = halo[:STEPS]
    above = pltpu.roll(halo[STEPS:], width, 1)
    return jnp.concatenate(
        [above] + [main] + [pltpu.roll(main, cols - a * width, 1) for a in range(1, groups)] + [below], axis=0
    )


def turn_kernel(pieces, *refs):
    groups = len(pieces[0][0])
    depths, parts, (out, held, depth_i, depth_j) = refs[:-4 - groups], refs[-4 - groups:-4], refs[-4:]
    _, width, order = out.shape
    half = order // 2
    count = half // groups
    cols = width * groups
    source = position()[2]
    planes, base = [], 0
    for starts, rows in pieces:
        planes += [(base + i, rows, i, starts) for i in range(rows)]
        base += 2 * count * rows
    for k, (first, rows, _, _) in enumerate(planes):
        for d, part in enumerate(parts):
            for side in range(2):
                at = pl.multiple_of(side * half + source[d] * count, 8)
                held[k, pl.ds(at, count), :] = part[pl.ds(first + side * count * rows, count, rows), :]

    no_halo = jnp.zeros((2 * STEPS, cols), jnp.float32)
    depth = unfold(depths[0][...], depths[1][...] if len(depths) > 1 else no_halo, groups)
    tall = depth.shape[0]
    lane = lax.broadcasted_iota(jnp.int32, depth.shape, 1)
    right = jnp.where(lane == width - 1, depth, pltpu.roll(depth, cols - 1, 1))
    depth_j[...] = jnp.minimum(depth, right)
    depth_i[pl.ds(0, tall - 1), :] = jnp.minimum(depth[:-1], depth[1:])
    depth_i[pl.ds(tall - 1, 1), :] = depth[tall - 1:]

    def fold(ref, starts, rows):
        group = lane_groups(rows, cols, groups)
        x = ref[pl.ds(starts[0], rows), :]
        for a in range(1, groups):
            x = jnp.where(group == a, pltpu.roll(ref[pl.ds(starts[a], rows), :], a * width, 1), x)
        return x

    folded = [(fold(depth_i, *piece), fold(depth_j, *piece)) for piece in pieces]
    level = lax.broadcasted_iota(jnp.int32, (half, cols), 0).astype(jnp.float32)
    at = 0
    for n, (starts, rows) in enumerate(pieces):
        for i in range(rows):
            k = at // groups + i
            along_i = jnp.where(level < folded[n][0][i:i + 1], held[k, pl.ds(0, half), :], 0.0)
            along_j = jnp.where(level < folded[n][1][i:i + 1], held[k, pl.ds(half, half), :], 0.0)
            turned = jnp.concatenate([along_i, along_j], axis=0).T
            for a in range(groups):
                out[at + a * rows + i] = turned[a * width:(a + 1) * width]
        at += groups * rows


def turn_weights(pieces, depths, parts, order):
    groups = len(parts)
    cols = parts[0].shape[1]
    rows = sum(n for _, n in pieces)
    tall = depths[0].shape[0] * groups + 2 * STEPS
    return pl.pallas_call(
        functools.partial(turn_kernel, pieces),
        in_specs=[vmem()] * (len(depths) + groups),
        out_specs=vmem(),
        out_shape=jax.ShapeDtypeStruct((rows * groups, cols // groups, order), jnp.float32),
        scratch_shapes=[pltpu.VMEM((rows, order, cols), jnp.float32)] + [pltpu.VMEM((tall, cols), jnp.float32)] * 2,
        compiler_params=params(),
        name="turn_weights",
    )(*depths, *parts)


def edge_masks(depths, order):
    groups = lax.axis_size("lev")
    slot = position()[0][0]
    gy = lax.axis_index("gy")
    start = (slot == 0) & (gy == 0)
    end = (slot == groups - 1) & (gy == lax.axis_size("gy") - 1)
    no_halo = jnp.zeros((2 * STEPS, depths[0].shape[1]), jnp.float32)
    masks = []
    for k, out in enumerate((start, end)):
        x = unfold(depths[k][...], depths[2 + k][...] if len(depths) > 2 else no_halo, groups)
        x = jnp.where(out, 0.0, x)
        x = jnp.broadcast_to(x[:, :1], (x.shape[0], order))
        lane = lax.broadcasted_iota(jnp.int32, x.shape, 1)
        level = lax.rem(lane, order // 2).astype(jnp.float32)
        masks.append(jnp.where((lane < order // 2) | (level < x), 1.0, 0.0))
    return masks


def spread_kernel(windows, field_rows, weight_rows, count, matrix, *refs):
    depths, refs = refs[:count], refs[count:]
    pieces = [refs[3 * k:3 * k + 3] for k in range(len(field_rows) + len(weight_rows))]
    outs, (a, b, wi, wj, masks, terms) = refs[3 * len(pieces):-6], refs[-6:]
    width, order = pieces[0][0].shape[1:]
    half = order // 2
    _, ext, wide, _ = a.shape
    lane = lax.broadcasted_iota(jnp.int32, (wide, order), 1)
    last = lax.broadcasted_iota(jnp.int32, (PAD, order), 0) == PAD - 1
    nothing = jnp.zeros((PAD - STEPS, order), jnp.float32)
    masks[0], masks[1] = edge_masks(depths, order)

    def row_of(some, rows, r):
        piece = [k for k in range(len(rows)) if r in rows[k]][0]
        main, left, right = some[piece]
        k = rows[piece].index(r)
        side = pl.ds(k * STEPS, STEPS)
        return [jnp.concatenate([nothing, left[side, :]], axis=0), main[k], jnp.concatenate([right[side, :], nothing], axis=0)]

    for n, window in enumerate(windows):
        for e, r in enumerate(window):
            a[n, e] = jnp.concatenate(row_of(pieces[:len(field_rows)], field_rows, r), axis=0)
            left, mid, right = row_of(pieces[len(field_rows):], weight_rows, r)
            at = pl.ds(STEPS + r, 1)
            left = jnp.where(last, left * masks[0, at, :], left)
            end = mid[width - PAD:]
            end = jnp.where(last, end * masks[1, at, :], end)
            w = jnp.concatenate([left, mid[:width - PAD], end, right], axis=0)
            other = pltpu.roll(w, half, 1)
            wi[n, e] = jnp.where(lane < half, w, other)
            wj[n, e] = jnp.where(lane < half, other, w)

    src, dst = a, b
    for step in range(STEPS):
        begin, stop = step + 1, ext - 1 - step
        for n in range(len(windows)):

            def one(r, carry, n=n, src=src, dst=dst):
                v, before = carry
                after = src[n, r + 1]
                flux = wi[n, r] * (after - v)
                across = wj[n, r] * (pltpu.roll(v, wide - 1, 0) - v)
                dst[n, r] = v + (flux - before) + (across - pltpu.roll(across, 1, 0))
                return after, flux

            v = src[n, begin]
            lax.fori_loop(begin, stop, one, (v, wi[n, begin - 1] * (v - src[n, begin - 1])), unroll=2)
        src, dst = dst, src

    groups = len(outs)
    count = order // groups
    rows = len(windows) * (ext - 2 * STEPS) // groups
    each = groups // len(windows)

    terms[...] = left_terms(matrix[...])

    def mix(pair, carry):
        planes = [2 * pair, 2 * pair + 1]
        x = jnp.concatenate(
            [src[g // each, STEPS + g % each * rows + i, pl.ds(PAD, width), :] for i in planes for g in range(groups)],
            axis=0,
        )
        y = lax.dot_general(
            terms[...], right_terms(x, 1), (((1,), (1,)), ((), ())), preferred_element_type=jnp.float32
        )
        cols = groups * width
        for k, i in enumerate(planes):
            for d, out in enumerate(outs):
                out[pl.ds(i, count, rows), :] = y[d * count:(d + 1) * count, k * cols:(k + 1) * cols]
        return carry

    lax.fori_loop(0, rows // 2, mix, 0, unroll=2)


def spread_mix(windows, matrix, depths, field, weights, groups):
    width, order = field[0][1].shape[1:]
    cols = width * groups
    ext = len(windows[0])
    rows = len(windows) * (ext - 2 * STEPS) // groups
    shape = jax.ShapeDtypeStruct((order // groups * rows, cols), jnp.float32)
    arrays = list(depths) + [x for piece in field + weights for x in piece[1:]]
    kernel = functools.partial(
        spread_kernel, windows, [piece[0] for piece in field], [piece[0] for piece in weights], len(depths)
    )
    tall = field[0][1].shape[0] + 2 * STEPS
    return pl.pallas_call(
        kernel,
        in_specs=[vmem()] * (1 + len(arrays)),
        out_specs=[vmem()] * groups,
        out_shape=[shape] * groups,
        scratch_shapes=[pltpu.VMEM((len(windows), ext, width + 2 * PAD, order), jnp.float32)] * 4
        + [pltpu.VMEM((2, tall, order), jnp.float32), pltpu.VMEM((order, 6 * order), jnp.bfloat16)],
        compiler_params=params(),
        name="spread_mix",
    )(matrix, *arrays)


RESULT_STEPS = 4


def result_kernel(runs, gain, mask, *refs):
    parts, (out, done, out_sems) = refs[:-3], refs[-3:]
    fields, levels, _, cols = gain.shape
    groups = len(parts)
    rows = done.shape[2] // groups
    some = levels // RESULT_STEPS
    slots = position()[1]
    group = lane_groups(rows, cols, groups)

    def of_slot(slot, at):
        x = parts[0][pl.ds(at, rows), :]
        for d in range(1, groups):
            x = jnp.where(slots[d] == slot, parts[d][pl.ds(at, rows), :], x)
        return x

    stored = []
    for step in range(RESULT_STEPS):
        for level in range(step * some, (step + 1) * some):
            ocean = jnp.concatenate([mask[level, pl.ds(*run), :] for run in runs], axis=0).astype(jnp.float32)
            for field in range(fields):
                at = (field * levels + level) * rows
                blocks = swap([of_slot(slot, at) for slot in range(groups)], group, cols // groups)
                gains = jnp.concatenate([gain[field, level, pl.ds(*run), :] for run in runs], axis=0)
                done[field, level] = ocean * gains * jnp.concatenate(blocks, axis=0)
        these = pl.ds(step * some, some)
        pairs, at = [], 0
        for first, number in runs:
            pairs.append((done.at[:, these, pl.ds(at, number)], out.at[:, these, pl.ds(first, number)]))
            at += number
        stored += copies(pairs, out_sems.at[step])
    for copy in stored:
        copy.wait()


def result(runs, gain, mask, parts, before):
    fields, levels, _, cols = gain.shape
    groups = len(parts)
    rows = sum(number for _, number in runs)
    anywhere = pl.BlockSpec(memory_space=pl.ANY)
    more = [] if before is None else [before]

    def kernel(gain, mask, *refs):
        result_kernel(runs, gain, mask, *refs[:groups], *refs[groups + len(more):])

    return pl.pallas_call(
        kernel,
        in_specs=[vmem()] * (2 + groups) + [anywhere] * len(more),
        out_specs=anywhere,
        out_shape=jax.ShapeDtypeStruct(gain.shape, jnp.float32),
        scratch_shapes=[
            pltpu.VMEM((fields, levels, rows, cols), jnp.float32),
            pltpu.SemaphoreType.DMA((RESULT_STEPS, len(runs))),
        ],
        input_output_aliases={2 + groups: 0} if more else {},
        compiler_params=params(),
        name="result",
    )(gain, mask, *parts, *more)


def shards(increment, norm_gain, diffusion_i, diffusion_j, sea_mask, coupling):
    devices = lax.axis_size("lev")
    gx_size = lax.axis_size("gx")
    gy_size = lax.axis_size("gy")
    _, levels, length, cols = increment.shape
    width = cols // devices
    rows = length // devices
    order = coupling.shape[0]
    to = [lax.rem(lax.axis_index("lev") + d, devices) for d in distances(devices)]
    source = [lax.rem(lax.axis_index("lev") + devices - d, devices) for d in distances(devices)]

    def shift(x, d):
        return lax.ppermute(x, "lev", [(k, (k + d) % devices) for k in range(devices)])

    def exchange(parts):
        return [parts[0]] + [shift(x, d) for x, d in zip(parts[1:], distances(devices)[1:])]

    up = [((k + 1) % gx_size, k) for k in range(gx_size)]
    down = [(b, a) for a, b in up]
    ring = [(devices - 1 - slot if y % 2 else slot) * gy_size + y for y in range(gy_size) for slot in range(devices)]
    ahead = list(zip(ring, ring[1:] + ring[:1]))
    back = [(b, a) for a, b in ahead]

    def halo_i(first, last):
        if gx_size == 2:
            size = first.shape[0]
            both = lax.ppermute(jnp.concatenate([first, last], axis=0), "gx", up)
            return both[size:], both[:size]
        return lax.ppermute(last, "gx", down), lax.ppermute(first, "gx", up)

    def halo_j(first, last):
        return lax.ppermute(last, ("lev", "gy"), ahead), lax.ppermute(first, ("lev", "gy"), back)

    def flat(x):
        return x.reshape(-1, x.shape[-1])

    def cut(x, *sizes):
        return lax.split(x, sizes, 0)

    quarter = length // 4
    some = 2 * quarter // devices
    half = devices // 2
    inner = (quarter, 2 * quarter)
    outer = ((0, quarter), (3 * quarter, quarter))
    inner_pieces = [
        ([STEPS + quarter + a * some for a in range(devices)], some),
        ([quarter + 2 * a for a in range(half)] + [STEPS + 3 * quarter + 2 * a for a in range(half)], 2),
    ]
    outer_pieces = [([a * some for a in range(half)] + [3 * quarter + 2 * STEPS + a * some for a in range(half)], some)]

    def rows_of(pieces):
        return [start - STEPS + i for starts, number in pieces for start in starts for i in range(number)]

    inner_rows, outer_rows = rows_of(inner_pieces), rows_of(outer_pieces)
    windows = [list(range(-STEPS, quarter + STEPS)), list(range(3 * quarter - STEPS, length + STEPS))]

    inner_size = len(inner_rows) // devices
    inner_messages = weight_messages(inner_pieces, diffusion_i, diffusion_j, [sea_mask])
    *inner_messages, ends = inner_messages
    inner_parts = exchange(inner_messages)
    _, increment, norm_gain = lax.optimization_barrier((inner_messages[0], increment, norm_gain))
    messages = scaled_messages(increment, norm_gain, sea_mask, devices)
    scaled = exchange(messages)
    _, ends = lax.optimization_barrier((messages[0], ends))
    halos = halo_i(*cut(ends, ends.shape[0] // 2, ends.shape[0] // 2))
    outer_messages = weight_messages(outer_pieces, diffusion_i, diffusion_j, halos=halos)

    depth = sum(part[2 * levels * inner_size:] for part in inner_parts)
    here = turn_weights(inner_pieces, [depth], inner_parts, order)
    left, right = halo_j(
        jnp.concatenate([flat(here[:, :STEPS]), depth], axis=0),
        flat(here[:, -STEPS:]),
    )
    right, right_depth = cut(right, len(inner_rows) * STEPS, rows)

    balance = jnp.eye(order, dtype=jnp.float32) + coupling
    by_device = balance.reshape(2, devices, levels, order)
    adjoint = jnp.concatenate([by_device[:, s].reshape(2 * levels, order) for s in source], axis=0).T
    forward = jnp.concatenate([by_device[:, t].reshape(2 * levels, order) for t in to], axis=0)

    scaled[1], outer_messages = lax.optimization_barrier((scaled[1], outer_messages))
    early = shift(outer_messages[1], devices // 2)
    mixed = adjoint_mix(adjoint, depth, scaled, length, width)
    edges = flat(mixed[:, :STEPS]), flat(mixed[:, -STEPS:])
    edges, inner_weights = lax.optimization_barrier((edges, (here, left, right)))
    left, right = halo_j(*edges)
    left, right, outer_messages, early = lax.optimization_barrier((left, right, outer_messages, early))
    own, _, *others = outer_messages
    outer_parts = [own, early] + [shift(x, d) for x, d in zip(others, distances(devices)[2:])]
    field = [(list(range(length)), mixed, left, right)]
    weights = [(inner_rows, *inner_weights)]
    depths = [depth, right_depth]
    inner_mixed = spread_mix([sorted(inner_rows)], forward, depths, field, weights, devices)
    _, upper, lower = lax.optimization_barrier((left, mixed[:STEPS], mixed[-STEPS:]))
    _, outer_parts = lax.optimization_barrier((inner_mixed[0], outer_parts))
    inner_mixed = exchange(inner_mixed)
    out = result((inner,), norm_gain, sea_mask, inner_mixed, None)

    above, below = halo_i(
        jnp.concatenate([flat(upper), depth[:STEPS]], axis=0),
        jnp.concatenate([flat(lower), depth[-STEPS:]], axis=0),
    )
    above, above_depth = cut(above, STEPS * width, STEPS)
    below, below_depth = cut(below, STEPS * width, STEPS)
    halo_depth = jnp.concatenate([below_depth, above_depth], axis=0)
    halo = jnp.concatenate([above, below], axis=0).reshape(2 * STEPS, width, order)
    here = turn_weights(outer_pieces, [depth, halo_depth], outer_parts, order)
    left, right = halo_j(
        jnp.concatenate([flat(here[:, :STEPS]), flat(halo[:, :STEPS]), halo_depth], axis=0),
        jnp.concatenate([flat(here[:, -STEPS:]), flat(halo[:, -STEPS:])], axis=0),
    )
    sizes = len(outer_rows) * STEPS, 2 * STEPS * STEPS
    left, halo_left = cut(left, *sizes)
    right, halo_right, right_halo_depth = cut(right, *sizes, 2 * STEPS)
    weights.append((outer_rows, here, left, right))
    field.append((list(range(-STEPS, 0)) + list(range(length, length + STEPS)), halo, halo_left, halo_right))
    depths += [halo_depth, right_halo_depth]
    outer_mixed = exchange(spread_mix(windows, forward, depths, field, weights, devices))
    return result(outer, norm_gain, sea_mask, outer_mixed, out)


def solution(mesh):
    return jax.shard_map(
        shards,
        mesh=mesh,
        in_specs=(
            P(None, "lev", "gx", "gy"),
            P(None, "lev", "gx", "gy"),
            P("lev", "gx", "gy"),
            P("lev", "gx", "gy"),
            P("lev", "gx", "gy"),
            P(),
        ),
        out_specs=P(None, "lev", "gx", "gy"),
        check_vma=False,
    )
```

```python
import functools

import jax
import jax.numpy as jnp
from jax import lax
from jax.experimental import pallas as pl
from jax.experimental.pallas import tpu as pltpu
from jax.sharding import PartitionSpec as P

ITERS = 2
STEPS = 2 * ITERS
PAD = 8
VMEM_LIMIT = 40 * 1024 * 1024
VMEM_WHOLE = 60 * 1024 * 1024
HIGHEST = lax.Precision.HIGHEST


def params(limit=VMEM_LIMIT):
    return pltpu.CompilerParams(vmem_limit_bytes=limit)


def smem():
    return pl.BlockSpec(memory_space=pltpu.SMEM)


def vmem():
    return pl.BlockSpec(memory_space=pltpu.VMEM)


def distances(devices):
    return list(range(devices))


def position():
    devices = lax.axis_size("lev")
    me = lax.axis_index("lev")
    flipped = lax.rem(lax.axis_index("gy"), 2) == 1

    def slot(lev):
        return jnp.where(flipped, devices - 1 - lev, lev)

    to = [lax.rem(me + d, devices) for d in distances(devices)]
    source = [lax.rem(me + devices - d, devices) for d in distances(devices)]
    return [slot(lev) for lev in to], [slot(lev) for lev in source], source


def swap(blocks, group, width, axis=1):
    blocks = list(blocks)
    cols = blocks[0].shape[axis]
    bit = len(blocks) // 2
    while bit:
        shift = bit * width
        low = (group & bit) == 0
        for a in range(len(blocks)):
            if not a & bit:
                x, y = blocks[a], blocks[a + bit]
                blocks[a] = jnp.where(low, x, pltpu.roll(y, shift, axis))
                blocks[a + bit] = jnp.where(low, pltpu.roll(x, cols - shift, axis), y)
        bit //= 2
    return blocks


def lane_groups(rows, cols, groups):
    return lax.broadcasted_iota(jnp.int32, (rows, cols), 1) // (cols // groups)


def copies(pairs, sems):
    made = [pltpu.make_async_copy(src, dst, sems.at[k]) for k, (src, dst) in enumerate(pairs)]
    for copy in made:
        copy.start()
    return made


SCALED_STEPS = 4


def scaled_kernel(increment, gain, mask, *refs):
    outs, (inc, gn, sea, held, sems, out_sems) = refs[:-6], refs[-6:]
    fields, levels, length, cols = increment.shape
    groups = len(outs)
    rows = length // groups
    some = levels // SCALED_STEPS
    group = lane_groups(rows, cols, groups)
    fetched = []
    for step in range(SCALED_STEPS):
        part = pl.ds(step * some, some)
        fetched.append(
            copies(
                [
                    (increment.at[:, part], inc.at[:, part]),
                    (gain.at[:, part], gn.at[:, part]),
                    (mask.at[part], sea.at[part]),
                ],
                sems.at[step],
            )
        )

    for step in range(SCALED_STEPS):
        for copy in fetched[step]:
            copy.wait()

        def one(level, carry):
            ocean = sea[level].astype(jnp.float32)
            for field in range(fields):
                at = pl.multiple_of((field * levels + level) * rows, rows)
                x = ocean * gn[field, level] * inc[field, level]
                blocks = swap([x[a * rows:(a + 1) * rows] for a in range(groups)], group, cols // groups)
                for slot, block in enumerate(blocks):
                    held[slot, pl.ds(at, rows), :] = block
            return carry

        lax.fori_loop(step * some, (step + 1) * some, one, 0, unroll=True)
    slots = position()[0]
    for copy in copies([(held.at[slots[d]], out) for d, out in enumerate(outs)], out_sems):
        copy.wait()


def scaled_messages(increment, gain, mask, groups):
    fields, levels, length, cols = increment.shape
    shape = (fields * levels * length // groups, cols)
    return pl.pallas_call(
        scaled_kernel,
        in_specs=[pl.BlockSpec(memory_space=pl.ANY)] * 3,
        out_specs=[pl.BlockSpec(memory_space=pl.ANY)] * groups,
        out_shape=[jax.ShapeDtypeStruct(shape, jnp.float32)] * groups,
        scratch_shapes=[
            pltpu.VMEM(increment.shape, jnp.float32),
            pltpu.VMEM(gain.shape, jnp.float32),
            pltpu.VMEM(mask.shape, mask.dtype),
            pltpu.VMEM((groups, *shape), jnp.float32),
            pltpu.SemaphoreType.DMA((SCALED_STEPS, 3)),
            pltpu.SemaphoreType.DMA((groups,)),
        ],
        compiler_params=params(VMEM_WHOLE),
        name="scaled_messages",
    )(increment, gain, mask)


def pack_kernel(pieces, masked, *refs):
    sources, refs = refs[:2 + masked], refs[2 + masked:]
    groups = len(pieces[0][0])
    outs, refs = refs[:groups], refs[groups:]
    targets, (slots_held, sems, fetch_sems) = refs[:2 + masked], refs[2 + masked:]
    levels, length, cols = sources[0].shape
    width = cols // groups
    unroll = groups
    fetched = []
    for side, (source, target) in enumerate(zip(sources, targets)):
        pairs = [(source.at[pl.ds(k, unroll)], target.at[pl.ds(k, unroll)]) for k in range(0, levels, unroll)]
        fetched.append(copies(pairs, fetch_sems.at[side]))

    def put(at, blocks):
        for slot, block in enumerate(blocks):
            slots_held[slot, pl.ds(at, block.shape[0]), :] = block

    for side, weight in enumerate(targets[:2]):
        for outer in range(levels // unroll):
            fetched[side][outer].wait()
            some = range(outer * unroll, (outer + 1) * unroll)
            base = 0
            for starts, rows in pieces:
                at = base + (side * levels + outer * unroll) * rows
                base += 2 * levels * rows
                if rows == 2:
                    low, high = starts[0], starts[groups // 2]
                    row = lax.broadcasted_iota(jnp.int32, (8, cols), 0)
                    blocks = []
                    for level in some:
                        x, y = [weight[level, pl.ds(first // 8 * 8, 8), :] for first in (low, high)]
                        x = pltpu.roll(x, 8 - low % 8, 0) if low % 8 else x
                        y = pltpu.roll(y, 4, 0) if high % 8 == 0 else y
                        blocks.append(jnp.where(row < 4, x, y))
                    blocks = swap(blocks, row // 2, 2, 0)
                    put(at, swap(blocks, lane_groups(8, cols, groups), width))
                else:
                    group = lane_groups(rows, cols, groups)
                    packed = [
                        swap([weight[level, pl.ds(start, rows), :] for start in starts], group, width) for level in some
                    ]
                    put(at, [jnp.concatenate([x[slot] for x in packed], axis=0) for slot in range(groups)])
    if masked:
        sea = targets[2]
        depth = jnp.zeros((length, cols), sea.dtype)
        for outer in range(levels // unroll):
            fetched[2][outer].wait()
            for level in range(outer * unroll, (outer + 1) * unroll):
                depth = depth + sea[level]
        depth = depth.astype(jnp.float32)
        size = length // groups
        blocks = [depth[a * size:(a + 1) * size] for a in range(groups)]
        put(2 * levels * sum(n for _, n in pieces), swap(blocks, lane_groups(size, cols, groups), width))
    slots = position()[0]
    for copy in copies([(slots_held.at[slots[d]], out) for d, out in enumerate(outs)], sems):
        copy.wait()


def weight_messages(pieces, along_i, along_j, *mask):
    levels, length, cols = along_i.shape
    groups = len(pieces[0][0])
    shape = (2 * levels * sum(rows for _, rows in pieces) + len(mask) * length // groups, cols)
    anywhere = pl.BlockSpec(memory_space=pl.ANY)
    return list(
        pl.pallas_call(
            functools.partial(pack_kernel, pieces, len(mask)),
            in_specs=[anywhere] * (2 + len(mask)),
            out_specs=[anywhere] * groups,
            out_shape=[jax.ShapeDtypeStruct(shape, jnp.float32)] * groups,
            scratch_shapes=[pltpu.VMEM(x.shape, x.dtype) for x in (along_i, along_j, *mask)]
            + [
                pltpu.VMEM((groups, *shape), jnp.float32),
                pltpu.SemaphoreType.DMA((groups,)),
                pltpu.SemaphoreType.DMA((3, levels // groups)),
            ],
            compiler_params=params(VMEM_WHOLE if mask else VMEM_LIMIT),
            name="weight_messages",
        )(along_i, along_j, *mask)
    )


def three(x):
    high = x.astype(jnp.bfloat16)
    rest = x - high.astype(jnp.float32)
    middle = rest.astype(jnp.bfloat16)
    return high, middle, (rest - middle.astype(jnp.float32)).astype(jnp.bfloat16)


def left_terms(x):
    high, middle, low = three(x)
    return jnp.concatenate([high, middle, low, high, middle, high], axis=1)


def right_terms(x, axis):
    high, middle, low = three(x)
    return jnp.concatenate([high, high, high, middle, middle, low], axis=axis)


def adjoint_kernel(matrix, depths, *refs):
    parts, out, terms = refs[:-2], refs[-2], refs[-1]
    length, width, order = out.shape
    groups = len(parts)
    rows = length // groups
    cols = groups * width
    count = order // groups
    level = lax.rem(lax.broadcasted_iota(jnp.int32, (order, cols), 0), order // 2).astype(jnp.float32)

    terms[...] = left_terms(matrix[...])

    def two(pair, carry):
        planes = [2 * pair, 2 * pair + 1]
        x = jnp.concatenate(
            [jnp.concatenate([part[pl.ds(i, count, rows), :] for part in parts], axis=0) for i in planes], axis=1
        )
        y = jnp.dot(terms[...], right_terms(x, 0), preferred_element_type=jnp.float32)
        for k, i in enumerate(planes):
            z = jnp.where(level < depths[pl.ds(i, 1), :], y[:, k * cols:(k + 1) * cols], 0.0).T
            for a in range(groups):
                out[a * rows + i] = z[a * width:(a + 1) * width]
        return carry

    lax.fori_loop(0, rows // 2, two, 0, unroll=2)


def adjoint_mix(matrix, depths, parts, length, width):
    return pl.pallas_call(
        adjoint_kernel,
        in_specs=[vmem()] * (2 + len(parts)),
        out_specs=vmem(),
        out_shape=jax.ShapeDtypeStruct((length, width, matrix.shape[0]), jnp.float32),
        scratch_shapes=[pltpu.VMEM((matrix.shape[0], 6 * matrix.shape[0]), jnp.bfloat16)],
        compiler_params=params(),
        name="adjoint_mix",
    )(matrix, depths, *parts)


def unfold(main, halo, groups):
    cols = main.shape[1]
    width = cols // groups
    below = halo[:STEPS]
    above = pltpu.roll(halo[STEPS:], width, 1)
    return jnp.concatenate(
        [above] + [main] + [pltpu.roll(main, cols - a * width, 1) for a in range(1, groups)] + [below], axis=0
    )


def turn_kernel(pieces, *refs):
    groups = len(pieces[0][0])
    depths, parts, (out, held, depth_i, depth_j) = refs[:-4 - groups], refs[-4 - groups:-4], refs[-4:]
    _, width, order = out.shape
    half = order // 2
    count = half // groups
    cols = width * groups
    source = position()[2]
    planes, base = [], 0
    for starts, rows in pieces:
        planes += [(base + i, rows, i, starts) for i in range(rows)]
        base += 2 * count * rows
    for k, (first, rows, _, _) in enumerate(planes):
        for d, part in enumerate(parts):
            for side in range(2):
                at = pl.multiple_of(side * half + source[d] * count, 8)
                held[k, pl.ds(at, count), :] = part[pl.ds(first + side * count * rows, count, rows), :]

    depth = unfold(depths[0][...], depths[1][...], groups)
    tall = depth.shape[0]
    lane = lax.broadcasted_iota(jnp.int32, depth.shape, 1)
    right = jnp.where(lane == width - 1, depth, pltpu.roll(depth, cols - 1, 1))
    depth_j[...] = jnp.minimum(depth, right)
    depth_i[pl.ds(0, tall - 1), :] = jnp.minimum(depth[:-1], depth[1:])
    depth_i[pl.ds(tall - 1, 1), :] = depth[tall - 1:]

    def fold(ref, starts, rows):
        group = lane_groups(rows, cols, groups)
        x = ref[pl.ds(STEPS + starts[0], rows), :]
        for a in range(1, groups):
            x = jnp.where(group == a, pltpu.roll(ref[pl.ds(STEPS + starts[a], rows), :], a * width, 1), x)
        return x

    folded = [(fold(depth_i, *piece), fold(depth_j, *piece)) for piece in pieces]
    level = lax.broadcasted_iota(jnp.int32, (half, cols), 0).astype(jnp.float32)
    at = 0
    for n, (starts, rows) in enumerate(pieces):
        for i in range(rows):
            k = at // groups + i
            along_i = jnp.where(level < folded[n][0][i:i + 1], held[k, pl.ds(0, half), :], 0.0)
            along_j = jnp.where(level < folded[n][1][i:i + 1], held[k, pl.ds(half, half), :], 0.0)
            turned = jnp.concatenate([along_i, along_j], axis=0).T
            for a in range(groups):
                out[at + a * rows + i] = turned[a * width:(a + 1) * width]
        at += groups * rows


def turn_weights(pieces, depths, parts, order):
    groups = len(parts)
    cols = parts[0].shape[1]
    rows = sum(n for _, n in pieces)
    tall = depths[0].shape[0] * groups + 2 * STEPS
    return pl.pallas_call(
        functools.partial(turn_kernel, pieces),
        in_specs=[vmem()] * (len(depths) + groups),
        out_specs=vmem(),
        out_shape=jax.ShapeDtypeStruct((rows * groups, cols // groups, order), jnp.float32),
        scratch_shapes=[pltpu.VMEM((rows, order, cols), jnp.float32)] + [pltpu.VMEM((tall, cols), jnp.float32)] * 2,
        compiler_params=params(),
        name="turn_weights",
    )(*depths, *parts)


def edge_masks(depths, order):
    groups = lax.axis_size("lev")
    slot = position()[0][0]
    gy = lax.axis_index("gy")
    start = (slot == 0) & (gy == 0)
    end = (slot == groups - 1) & (gy == lax.axis_size("gy") - 1)
    no_halo = jnp.zeros((2 * STEPS, depths[0].shape[1]), jnp.float32)
    masks = []
    for k, out in enumerate((start, end)):
        x = unfold(depths[k][...], depths[2 + k][...] if len(depths) > 2 else no_halo, groups)
        x = jnp.where(out, 0.0, x)
        x = jnp.broadcast_to(x[:, :1], (x.shape[0], order))
        lane = lax.broadcasted_iota(jnp.int32, x.shape, 1)
        level = lax.rem(lane, order // 2).astype(jnp.float32)
        masks.append(jnp.where((lane < order // 2) | (level < x), 1.0, 0.0))
    return masks


def spread_kernel(windows, field_rows, weight_rows, count, matrix, *refs):
    depths, refs = refs[:count], refs[count:]
    pieces = [refs[3 * k:3 * k + 3] for k in range(len(field_rows) + len(weight_rows))]
    outs, (a, b, wi, wj, masks, terms) = refs[3 * len(pieces):-6], refs[-6:]
    width, order = pieces[0][0].shape[1:]
    half = order // 2
    _, ext, wide, _ = a.shape
    lane = lax.broadcasted_iota(jnp.int32, (wide, order), 1)
    last = lax.broadcasted_iota(jnp.int32, (PAD, order), 0) == PAD - 1
    nothing = jnp.zeros((PAD - STEPS, order), jnp.float32)
    masks[0], masks[1] = edge_masks(depths, order)

    def row_of(some, rows, r):
        piece = [k for k in range(len(rows)) if r in rows[k]][0]
        main, left, right = some[piece]
        k = rows[piece].index(r)
        side = pl.ds(k * STEPS, STEPS)
        return [jnp.concatenate([nothing, left[side, :]], axis=0), main[k], jnp.concatenate([right[side, :], nothing], axis=0)]

    for n, window in enumerate(windows):
        for e, r in enumerate(window):
            a[n, e] = jnp.concatenate(row_of(pieces[:len(field_rows)], field_rows, r), axis=0)
            left, mid, right = row_of(pieces[len(field_rows):], weight_rows, r)
            at = pl.ds(STEPS + r, 1)
            left = jnp.where(last, left * masks[0, at, :], left)
            end = mid[width - PAD:]
            end = jnp.where(last, end * masks[1, at, :], end)
            w = jnp.concatenate([left, mid[:width - PAD], end, right], axis=0)
            other = pltpu.roll(w, half, 1)
            wi[n, e] = jnp.where(lane < half, w, other)
            wj[n, e] = jnp.where(lane < half, other, w)

    src, dst = a, b
    for step in range(STEPS):
        begin, stop = step + 1, ext - 1 - step
        for n in range(len(windows)):

            def one(r, carry, n=n, src=src, dst=dst):
                v, before = carry
                after = src[n, r + 1]
                flux = wi[n, r] * (after - v)
                across = wj[n, r] * (pltpu.roll(v, wide - 1, 0) - v)
                dst[n, r] = v + (flux - before) + (across - pltpu.roll(across, 1, 0))
                return after, flux

            v = src[n, begin]
            lax.fori_loop(begin, stop, one, (v, wi[n, begin - 1] * (v - src[n, begin - 1])), unroll=2)
        src, dst = dst, src

    groups = len(outs)
    count = order // groups
    rows = len(windows) * (ext - 2 * STEPS) // groups
    each = groups // len(windows)

    terms[...] = left_terms(matrix[...])

    def mix(pair, carry):
        planes = [2 * pair, 2 * pair + 1]
        x = jnp.concatenate(
            [src[g // each, STEPS + g % each * rows + i, pl.ds(PAD, width), :] for i in planes for g in range(groups)],
            axis=0,
        )
        y = lax.dot_general(
            terms[...], right_terms(x, 1), (((1,), (1,)), ((), ())), preferred_element_type=jnp.float32
        )
        cols = groups * width
        for k, i in enumerate(planes):
            for d, out in enumerate(outs):
                out[pl.ds(i, count, rows), :] = y[d * count:(d + 1) * count, k * cols:(k + 1) * cols]
        return carry

    lax.fori_loop(0, rows // 2, mix, 0, unroll=2)


def spread_mix(windows, matrix, depths, field, weights, groups):
    width, order = field[0][1].shape[1:]
    cols = width * groups
    ext = len(windows[0])
    rows = len(windows) * (ext - 2 * STEPS) // groups
    shape = jax.ShapeDtypeStruct((order // groups * rows, cols), jnp.float32)
    arrays = list(depths) + [x for piece in field + weights for x in piece[1:]]
    kernel = functools.partial(
        spread_kernel, windows, [piece[0] for piece in field], [piece[0] for piece in weights], len(depths)
    )
    tall = field[0][1].shape[0] + 2 * STEPS
    return pl.pallas_call(
        kernel,
        in_specs=[vmem()] * (1 + len(arrays)),
        out_specs=[vmem()] * groups,
        out_shape=[shape] * groups,
        scratch_shapes=[pltpu.VMEM((len(windows), ext, width + 2 * PAD, order), jnp.float32)] * 4
        + [pltpu.VMEM((2, tall, order), jnp.float32), pltpu.VMEM((order, 6 * order), jnp.bfloat16)],
        compiler_params=params(),
        name="spread_mix",
    )(matrix, *arrays)


RESULT_STEPS = 4


def result_kernel(runs, gain, mask, *refs):
    parts, (out, done, out_sems) = refs[:-3], refs[-3:]
    fields, levels, _, cols = gain.shape
    groups = len(parts)
    rows = done.shape[2] // groups
    some = levels // RESULT_STEPS
    slots = position()[1]
    group = lane_groups(rows, cols, groups)

    def of_slot(slot, at):
        x = parts[0][pl.ds(at, rows), :]
        for d in range(1, groups):
            x = jnp.where(slots[d] == slot, parts[d][pl.ds(at, rows), :], x)
        return x

    stored = []
    for step in range(RESULT_STEPS):
        for level in range(step * some, (step + 1) * some):
            ocean = jnp.concatenate([mask[level, pl.ds(*run), :] for run in runs], axis=0).astype(jnp.float32)
            for field in range(fields):
                at = (field * levels + level) * rows
                blocks = swap([of_slot(slot, at) for slot in range(groups)], group, cols // groups)
                gains = jnp.concatenate([gain[field, level, pl.ds(*run), :] for run in runs], axis=0)
                done[field, level] = ocean * gains * jnp.concatenate(blocks, axis=0)
        these = pl.ds(step * some, some)
        pairs, at = [], 0
        for first, number in runs:
            pairs.append((done.at[:, these, pl.ds(at, number)], out.at[:, these, pl.ds(first, number)]))
            at += number
        stored += copies(pairs, out_sems.at[step])
    for copy in stored:
        copy.wait()


def result(runs, gain, mask, parts, before):
    fields, levels, _, cols = gain.shape
    groups = len(parts)
    rows = sum(number for _, number in runs)
    anywhere = pl.BlockSpec(memory_space=pl.ANY)
    more = [] if before is None else [before]

    def kernel(gain, mask, *refs):
        result_kernel(runs, gain, mask, *refs[:groups], *refs[groups + len(more):])

    return pl.pallas_call(
        kernel,
        in_specs=[vmem()] * (2 + groups) + [anywhere] * len(more),
        out_specs=anywhere,
        out_shape=jax.ShapeDtypeStruct(gain.shape, jnp.float32),
        scratch_shapes=[
            pltpu.VMEM((fields, levels, rows, cols), jnp.float32),
            pltpu.SemaphoreType.DMA((RESULT_STEPS, len(runs))),
        ],
        input_output_aliases={2 + groups: 0} if more else {},
        compiler_params=params(),
        name="result",
    )(gain, mask, *parts, *more)


def shards(increment, norm_gain, diffusion_i, diffusion_j, sea_mask, coupling):
    devices = lax.axis_size("lev")
    gx_size = lax.axis_size("gx")
    gy_size = lax.axis_size("gy")
    _, levels, length, cols = increment.shape
    width = cols // devices
    rows = length // devices
    order = coupling.shape[0]
    to = [lax.rem(lax.axis_index("lev") + d, devices) for d in distances(devices)]
    source = [lax.rem(lax.axis_index("lev") + devices - d, devices) for d in distances(devices)]

    def shift(x, d):
        return lax.ppermute(x, "lev", [(k, (k + d) % devices) for k in range(devices)])

    def exchange(parts):
        return [parts[0]] + [shift(x, d) for x, d in zip(parts[1:], distances(devices)[1:])]

    up = [((k + 1) % gx_size, k) for k in range(gx_size)]
    down = [(b, a) for a, b in up]
    ring = [(devices - 1 - slot if y % 2 else slot) * gy_size + y for y in range(gy_size) for slot in range(devices)]
    ahead = list(zip(ring, ring[1:] + ring[:1]))
    back = [(b, a) for a, b in ahead]

    def halo_i(first, last):
        if gx_size == 2:
            size = first.shape[0]
            both = lax.ppermute(jnp.concatenate([first, last], axis=0), "gx", up)
            return both[size:], both[:size]
        return lax.ppermute(last, "gx", down), lax.ppermute(first, "gx", up)

    def halo_j(first, last):
        return lax.ppermute(last, ("lev", "gy"), ahead), lax.ppermute(first, ("lev", "gy"), back)

    def flat(x):
        return x.reshape(-1, x.shape[-1])

    def cut(x, *sizes):
        return lax.split(x, sizes, 0)

    quarter = length // 4
    some = 2 * quarter // devices
    half = devices // 2
    inner = (quarter, 2 * quarter)
    outer = ((0, quarter), (3 * quarter, quarter))
    rest = (quarter - 2 * STEPS) // half
    inner_pieces = [
        ([quarter + a * some for a in range(devices)], some),
        ([quarter - STEPS + 2 * a for a in range(half)] + [3 * quarter + 2 * a for a in range(half)], 2),
        ([2 * a for a in range(half)] + [length - STEPS + 2 * a for a in range(half)], 2),
    ]
    outer_pieces = [
        ([STEPS + a * rest for a in range(half)] + [3 * quarter + STEPS + a * rest for a in range(half)], rest)
    ]

    def rows_of(pieces):
        return [start + i for starts, number in pieces for start in starts for i in range(number)]

    inner_rows, outer_rows = rows_of(inner_pieces), rows_of(outer_pieces)
    inner_window = list(range(quarter - STEPS, 3 * quarter + STEPS))
    halo_rows = list(range(-STEPS, 0)) + list(range(length, length + STEPS))
    windows = [list(range(-STEPS, quarter + STEPS)), list(range(3 * quarter - STEPS, length + STEPS))]

    inner_messages = weight_messages(inner_pieces, diffusion_i, diffusion_j, sea_mask)
    inner_parts = exchange(inner_messages)
    _, increment, norm_gain = lax.optimization_barrier((inner_messages[0], increment, norm_gain))
    messages = scaled_messages(increment, norm_gain, sea_mask, devices)
    scaled = exchange(messages)
    _, diffusion_i, diffusion_j = lax.optimization_barrier((messages[0], diffusion_i, diffusion_j))
    outer_messages = weight_messages(outer_pieces, diffusion_i, diffusion_j)

    size = 2 * levels * len(inner_rows) // devices
    depth = sum(part[size:] for part in inner_parts)
    above, below = halo_i(depth[:STEPS], depth[-STEPS:])
    halo_depth = jnp.concatenate([below, above], axis=0)
    here = turn_weights(inner_pieces, [depth, halo_depth], inner_parts, order)
    ends = flat(here[-2 * STEPS:-STEPS]), flat(here[-STEPS:])
    left, right = halo_j(
        jnp.concatenate([flat(here[:, :STEPS]), depth, halo_depth], axis=0), flat(here[:, -STEPS:])
    )
    right, right_depth, right_halo_depth = cut(right, len(inner_rows) * STEPS, rows, 2 * STEPS)
    depths = [depth, right_depth, halo_depth, right_halo_depth]

    balance = jnp.eye(order, dtype=jnp.float32) + coupling
    by_device = balance.reshape(2, devices, levels, order)
    adjoint = jnp.concatenate([by_device[:, s].reshape(2 * levels, order) for s in source], axis=0).T
    forward = jnp.concatenate([by_device[:, t].reshape(2 * levels, order) for t in to], axis=0)

    middle = devices // 2
    scaled[1], outer_messages = lax.optimization_barrier((scaled[1], outer_messages))
    early = shift(outer_messages[middle], middle)
    mixed = adjoint_mix(adjoint, depth, scaled, length, width)
    edges = flat(mixed[:, :STEPS]), flat(mixed[:, -STEPS:])
    edges, inner_weights = lax.optimization_barrier((edges, (here, left, right)))
    left, right = halo_j(*edges)
    left, right, outer_messages, early = lax.optimization_barrier((left, right, outer_messages, early))
    outer_parts = [
        early if d == middle else shift(outer_messages[d], d) if d else outer_messages[0] for d in range(devices)
    ]
    field = [(list(range(length)), mixed, left, right)]
    weights = [(inner_rows, *inner_weights)]
    inner_mixed = spread_mix([inner_window], forward, depths[:2], field, weights, devices)
    _, upper, lower = lax.optimization_barrier((left, mixed[:STEPS], mixed[-STEPS:]))
    _, outer_parts = lax.optimization_barrier((inner_mixed[0], outer_parts))
    above, below = halo_i(*[jnp.concatenate(pair, axis=0) for pair in zip((flat(upper), flat(lower)), ends)])
    size = STEPS * width
    halo, halo_weight = [
        jnp.concatenate(pair, axis=0).reshape(2 * STEPS, width, order)
        for pair in zip(cut(above, size, size), cut(below, size, size))
    ]
    here = turn_weights(outer_pieces, [depth, halo_depth], outer_parts, order)
    inner_mixed = list(inner_mixed)
    _, inner_mixed[2:] = lax.optimization_barrier(((here, halo), inner_mixed[2:]))
    inner_mixed = exchange(inner_mixed)
    out = result((inner,), norm_gain, sea_mask, inner_mixed, None)
    left, right = halo_j(
        *[
            jnp.concatenate([flat(x[:, at]) for x in (here, halo, halo_weight)], axis=0)
            for at in (slice(0, STEPS), slice(-STEPS, None))
        ]
    )
    sizes = [rows * STEPS for rows in (len(outer_rows), 2 * STEPS, 2 * STEPS)]
    left, halo_left, weight_left = cut(left, *sizes)
    right, halo_right, weight_right = cut(right, *sizes)
    weights += [(halo_rows, halo_weight, weight_left, weight_right), (outer_rows, here, left, right)]
    field.append((halo_rows, halo, halo_left, halo_right))
    outer_mixed = exchange(spread_mix(windows, forward, depths, field, weights, devices))
    return result(outer, norm_gain, sea_mask, outer_mixed, out)


def solution(mesh):
    return jax.shard_map(
        shards,
        mesh=mesh,
        in_specs=(
            P(None, "lev", "gx", "gy"),
            P(None, "lev", "gx", "gy"),
            P("lev", "gx", "gy"),
            P("lev", "gx", "gy"),
            P("lev", "gx", "gy"),
            P(),
        ),
        out_specs=P(None, "lev", "gx", "gy"),
        check_vma=False,
    )
```

```python
import functools

import jax
import jax.numpy as jnp
from jax import lax
from jax.experimental import pallas as pl
from jax.experimental.pallas import tpu as pltpu
from jax.sharding import PartitionSpec as P

ITERS = 2
STEPS = 2 * ITERS
PAD = 8
VMEM_LIMIT = 40 * 1024 * 1024
VMEM_WHOLE = 60 * 1024 * 1024
HIGHEST = lax.Precision.HIGHEST


def params(limit=VMEM_LIMIT):
    return pltpu.CompilerParams(vmem_limit_bytes=limit)


def smem():
    return pl.BlockSpec(memory_space=pltpu.SMEM)


def vmem():
    return pl.BlockSpec(memory_space=pltpu.VMEM)


def distances(devices):
    return list(range(devices))


def position():
    devices = lax.axis_size("lev")
    me = lax.axis_index("lev")
    flipped = lax.rem(lax.axis_index("gy"), 2) == 1

    def slot(lev):
        return jnp.where(flipped, devices - 1 - lev, lev)

    to = [lax.rem(me + d, devices) for d in distances(devices)]
    source = [lax.rem(me + devices - d, devices) for d in distances(devices)]
    return [slot(lev) for lev in to], [slot(lev) for lev in source], source


def swap(blocks, group, width, axis=1):
    blocks = list(blocks)
    cols = blocks[0].shape[axis]
    bit = len(blocks) // 2
    while bit:
        shift = bit * width
        low = (group & bit) == 0
        for a in range(len(blocks)):
            if not a & bit:
                x, y = blocks[a], blocks[a + bit]
                blocks[a] = jnp.where(low, x, pltpu.roll(y, shift, axis))
                blocks[a + bit] = jnp.where(low, pltpu.roll(x, cols - shift, axis), y)
        bit //= 2
    return blocks


def lane_groups(rows, cols, groups):
    return lax.broadcasted_iota(jnp.int32, (rows, cols), 1) // (cols // groups)


def copies(pairs, sems):
    made = [pltpu.make_async_copy(src, dst, sems.at[k]) for k, (src, dst) in enumerate(pairs)]
    for copy in made:
        copy.start()
    return made


SCALED_STEPS = 4


def scaled_kernel(increment, gain, mask, *refs):
    outs, (inc, gn, sea, held, sems, out_sems) = refs[:-6], refs[-6:]
    fields, levels, length, cols = increment.shape
    groups = len(outs)
    rows = length // groups
    some = levels // SCALED_STEPS
    group = lane_groups(rows, cols, groups)
    fetched = []
    for step in range(SCALED_STEPS):
        part = pl.ds(step * some, some)
        fetched.append(
            copies(
                [
                    (increment.at[:, part], inc.at[:, part]),
                    (gain.at[:, part], gn.at[:, part]),
                    (mask.at[part], sea.at[part]),
                ],
                sems.at[step],
            )
        )

    for step in range(SCALED_STEPS):
        for copy in fetched[step]:
            copy.wait()

        def one(level, carry):
            ocean = sea[level].astype(jnp.float32)
            for field in range(fields):
                at = pl.multiple_of((field * levels + level) * rows, rows)
                x = ocean * gn[field, level] * inc[field, level]
                blocks = swap([x[a * rows:(a + 1) * rows] for a in range(groups)], group, cols // groups)
                for slot, block in enumerate(blocks):
                    held[slot, pl.ds(at, rows), :] = block
            return carry

        lax.fori_loop(step * some, (step + 1) * some, one, 0, unroll=True)
    slots = position()[0]
    for copy in copies([(held.at[slots[d]], out) for d, out in enumerate(outs)], out_sems):
        copy.wait()


def scaled_messages(increment, gain, mask, groups):
    fields, levels, length, cols = increment.shape
    shape = (fields * levels * length // groups, cols)
    return pl.pallas_call(
        scaled_kernel,
        in_specs=[pl.BlockSpec(memory_space=pl.ANY)] * 3,
        out_specs=[pl.BlockSpec(memory_space=pl.ANY)] * groups,
        out_shape=[jax.ShapeDtypeStruct(shape, jnp.float32)] * groups,
        scratch_shapes=[
            pltpu.VMEM(increment.shape, jnp.float32),
            pltpu.VMEM(gain.shape, jnp.float32),
            pltpu.VMEM(mask.shape, mask.dtype),
            pltpu.VMEM((groups, *shape), jnp.float32),
            pltpu.SemaphoreType.DMA((SCALED_STEPS, 3)),
            pltpu.SemaphoreType.DMA((groups,)),
        ],
        compiler_params=params(VMEM_WHOLE),
        name="scaled_messages",
    )(increment, gain, mask)


def pack_kernel(pieces, masked, along_i, along_j, *refs):
    levels, length, cols = along_i.shape
    groups = len(pieces[0][0])
    width = cols // groups
    halos, outs = refs[masked:-4 - groups - 3 * masked], refs[-4 - groups - 3 * masked:-4 - 3 * masked]
    held, slots_held, sems, fetch_sems = refs[-4:]
    unroll = held.shape[0]
    number = levels // unroll
    starts, rows = pieces[0]
    group = lane_groups(rows, cols, groups)
    if masked:
        sources, (along_i, along_j, sea) = (along_i, along_j, refs[0]), refs[-7:-4]
        fetched = []
        for side, (source, target) in enumerate(zip(sources, (along_i, along_j, sea))):
            pairs = [(source.at[pl.ds(k * unroll, unroll)], target.at[pl.ds(k * unroll, unroll)]) for k in range(number)]
            fetched.append(copies(pairs, fetch_sems.at[side]))

    def put(at, blocks):
        for slot, block in enumerate(blocks):
            slots_held[slot, pl.ds(at, block.shape[0]), :] = block

    for side, weight in enumerate((along_i, along_j)):
        for outer in range(number):
            if masked:
                fetched[side][outer].wait()
            edges = []
            for k in range(unroll):
                level = outer * unroll + k
                index = side * levels + level
                if halos:
                    for halo, at in zip(halos, (0, STEPS + length)):
                        held[k, pl.ds(at, STEPS), :] = halo[pl.ds(index * STEPS, STEPS), :]
                    held[k, pl.ds(STEPS, length), :] = weight[level]
                    blocks = [held[k, pl.ds(start, rows), :] for start in starts]
                else:
                    blocks = [weight[level, pl.ds(start - STEPS, rows), :] for start in starts]
                put(index * rows, swap(blocks, group, width))
                if len(pieces) > 1:
                    small = pieces[1][0]
                    low, high = small[0] - 2 * STEPS, small[groups // 2] - STEPS
                    row = lax.broadcasted_iota(jnp.int32, (2 * STEPS, cols), 0)
                    upper = pltpu.roll(weight[level, pl.ds(low, 2 * STEPS), :], STEPS, 0)
                    lower = pltpu.roll(weight[level, pl.ds(high, 2 * STEPS), :], STEPS, 0)
                    edges.append(jnp.where(row < STEPS, upper, lower))
            if edges:
                each = pieces[1][1]
                pairs = lax.broadcasted_iota(jnp.int32, edges[0].shape, 0) // each
                edges = swap(edges, pairs, each, 0)
                at = 2 * levels * rows + (side * levels + outer * unroll) * each
                put(at, swap(edges, lane_groups(unroll * each, cols, groups), width))
    if masked:
        depth = jnp.zeros((length, cols), sea.dtype)
        for outer in range(number):
            fetched[2][outer].wait()
            for level in range(outer * unroll, (outer + 1) * unroll):
                depth = depth + sea[level]
        depth = depth.astype(jnp.float32)
        size = length // groups
        blocks = [depth[a * size:(a + 1) * size] for a in range(groups)]
        put(2 * levels * sum(n for _, n in pieces), swap(blocks, lane_groups(size, cols, groups), width))
    slots = position()[0]
    for copy in copies([(slots_held.at[slots[d]], out) for d, out in enumerate(outs)], sems):
        copy.wait()


def weight_messages(pieces, along_i, along_j, mask=(), halos=()):
    levels, length, cols = along_i.shape
    groups = len(pieces[0][0])
    shape = (2 * levels * sum(rows for _, rows in pieces) + len(mask) * length // groups, cols)
    unroll = 4
    return list(
        pl.pallas_call(
            functools.partial(pack_kernel, pieces, len(mask)),
            in_specs=[pl.BlockSpec(memory_space=pl.ANY) if mask else vmem()] * (2 + len(mask) + len(halos)),
            out_specs=[pl.BlockSpec(memory_space=pl.ANY)] * groups,
            out_shape=[jax.ShapeDtypeStruct(shape, jnp.float32)] * groups,
            scratch_shapes=[pltpu.VMEM(x.shape, x.dtype) for x in ([along_i, along_j, *mask] if mask else [])]
            + [
                pltpu.VMEM((unroll, length + 2 * STEPS, cols), jnp.float32),
                pltpu.VMEM((groups, *shape), jnp.float32),
                pltpu.SemaphoreType.DMA((groups,)),
                pltpu.SemaphoreType.DMA((3, levels // unroll)),
            ],
            compiler_params=params(VMEM_WHOLE if mask else VMEM_LIMIT),
            name="weight_messages",
        )(along_i, along_j, *mask, *halos)
    )


def three(x):
    high = x.astype(jnp.bfloat16)
    rest = x - high.astype(jnp.float32)
    middle = rest.astype(jnp.bfloat16)
    return high, middle, (rest - middle.astype(jnp.float32)).astype(jnp.bfloat16)


def left_terms(x):
    high, middle, low = three(x)
    return jnp.concatenate([high, middle, low, high, middle, high], axis=1)


def right_terms(x, axis):
    high, middle, low = three(x)
    return jnp.concatenate([high, high, high, middle, middle, low], axis=axis)


def adjoint_kernel(matrix, depths, *refs):
    parts, out, terms = refs[:-2], refs[-2], refs[-1]
    length, width, order = out.shape
    groups = len(parts)
    rows = length // groups
    cols = groups * width
    count = order // groups
    level = lax.rem(lax.broadcasted_iota(jnp.int32, (order, cols), 0), order // 2).astype(jnp.float32)

    terms[...] = left_terms(matrix[...])

    def two(pair, carry):
        planes = [2 * pair, 2 * pair + 1]
        x = jnp.concatenate(
            [jnp.concatenate([part[pl.ds(i, count, rows), :] for part in parts], axis=0) for i in planes], axis=1
        )
        y = jnp.dot(terms[...], right_terms(x, 0), preferred_element_type=jnp.float32)
        for k, i in enumerate(planes):
            z = jnp.where(level < depths[pl.ds(i, 1), :], y[:, k * cols:(k + 1) * cols], 0.0).T
            for a in range(groups):
                out[a * rows + i] = z[a * width:(a + 1) * width]
        return carry

    lax.fori_loop(0, rows // 2, two, 0, unroll=2)


def adjoint_mix(matrix, depths, parts, length, width):
    return pl.pallas_call(
        adjoint_kernel,
        in_specs=[vmem()] * (2 + len(parts)),
        out_specs=vmem(),
        out_shape=jax.ShapeDtypeStruct((length, width, matrix.shape[0]), jnp.float32),
        scratch_shapes=[pltpu.VMEM((matrix.shape[0], 6 * matrix.shape[0]), jnp.bfloat16)],
        compiler_params=params(),
        name="adjoint_mix",
    )(matrix, depths, *parts)


def unfold(main, halo, groups):
    cols = main.shape[1]
    width = cols // groups
    below = halo[:STEPS]
    above = pltpu.roll(halo[STEPS:], width, 1)
    return jnp.concatenate(
        [above] + [main] + [pltpu.roll(main, cols - a * width, 1) for a in range(1, groups)] + [below], axis=0
    )


def turn_kernel(pieces, *refs):
    groups = len(pieces[0][0])
    depths, parts, (out, held, depth_i, depth_j) = refs[:-4 - groups], refs[-4 - groups:-4], refs[-4:]
    _, width, order = out.shape
    half = order // 2
    count = half // groups
    cols = width * groups
    source = position()[2]
    planes, base = [], 0
    for starts, rows in pieces:
        planes += [(base + i, rows, i, starts) for i in range(rows)]
        base += 2 * count * rows
    for k, (first, rows, _, _) in enumerate(planes):
        for d, part in enumerate(parts):
            for side in range(2):
                at = pl.multiple_of(side * half + source[d] * count, 8)
                held[k, pl.ds(at, count), :] = part[pl.ds(first + side * count * rows, count, rows), :]

    no_halo = jnp.zeros((2 * STEPS, cols), jnp.float32)
    depth = unfold(depths[0][...], depths[1][...] if len(depths) > 1 else no_halo, groups)
    tall = depth.shape[0]
    lane = lax.broadcasted_iota(jnp.int32, depth.shape, 1)
    right = jnp.where(lane == width - 1, depth, pltpu.roll(depth, cols - 1, 1))
    depth_j[...] = jnp.minimum(depth, right)
    depth_i[pl.ds(0, tall - 1), :] = jnp.minimum(depth[:-1], depth[1:])
    depth_i[pl.ds(tall - 1, 1), :] = depth[tall - 1:]

    def fold(ref, starts, rows):
        group = lane_groups(rows, cols, groups)
        x = ref[pl.ds(starts[0], rows), :]
        for a in range(1, groups):
            x = jnp.where(group == a, pltpu.roll(ref[pl.ds(starts[a], rows), :], a * width, 1), x)
        return x

    folded = [(fold(depth_i, *piece), fold(depth_j, *piece)) for piece in pieces]
    level = lax.broadcasted_iota(jnp.int32, (half, cols), 0).astype(jnp.float32)
    at = 0
    for n, (starts, rows) in enumerate(pieces):
        for i in range(rows):
            k = at // groups + i
            along_i = jnp.where(level < folded[n][0][i:i + 1], held[k, pl.ds(0, half), :], 0.0)
            along_j = jnp.where(level < folded[n][1][i:i + 1], held[k, pl.ds(half, half), :], 0.0)
            turned = jnp.concatenate([along_i, along_j], axis=0).T
            for a in range(groups):
                out[at + a * rows + i] = turned[a * width:(a + 1) * width]
        at += groups * rows


def turn_weights(pieces, depths, parts, order):
    groups = len(parts)
    cols = parts[0].shape[1]
    rows = sum(n for _, n in pieces)
    tall = depths[0].shape[0] * groups + 2 * STEPS
    return pl.pallas_call(
        functools.partial(turn_kernel, pieces),
        in_specs=[vmem()] * (len(depths) + groups),
        out_specs=vmem(),
        out_shape=jax.ShapeDtypeStruct((rows * groups, cols // groups, order), jnp.float32),
        scratch_shapes=[pltpu.VMEM((rows, order, cols), jnp.float32)] + [pltpu.VMEM((tall, cols), jnp.float32)] * 2,
        compiler_params=params(),
        name="turn_weights",
    )(*depths, *parts)


def edge_masks(depths, order):
    groups = lax.axis_size("lev")
    slot = position()[0][0]
    gy = lax.axis_index("gy")
    start = (slot == 0) & (gy == 0)
    end = (slot == groups - 1) & (gy == lax.axis_size("gy") - 1)
    no_halo = jnp.zeros((2 * STEPS, depths[0].shape[1]), jnp.float32)
    masks = []
    for k, out in enumerate((start, end)):
        x = unfold(depths[k][...], depths[2 + k][...] if len(depths) > 2 else no_halo, groups)
        x = jnp.where(out, 0.0, x)
        x = jnp.broadcast_to(x[:, :1], (x.shape[0], order))
        lane = lax.broadcasted_iota(jnp.int32, x.shape, 1)
        level = lax.rem(lane, order // 2).astype(jnp.float32)
        masks.append(jnp.where((lane < order // 2) | (level < x), 1.0, 0.0))
    return masks


def spread_kernel(windows, field_rows, weight_rows, count, matrix, *refs):
    depths, refs = refs[:count], refs[count:]
    pieces = [refs[3 * k:3 * k + 3] for k in range(len(field_rows) + len(weight_rows))]
    outs, (a, b, wi, wj, masks, terms) = refs[3 * len(pieces):-6], refs[-6:]
    width, order = pieces[0][0].shape[1:]
    half = order // 2
    _, ext, wide, _ = a.shape
    lane = lax.broadcasted_iota(jnp.int32, (wide, order), 1)
    last = lax.broadcasted_iota(jnp.int32, (PAD, order), 0) == PAD - 1
    nothing = jnp.zeros((PAD - STEPS, order), jnp.float32)
    masks[0], masks[1] = edge_masks(depths, order)

    def row_of(some, rows, r):
        piece = [k for k in range(len(rows)) if r in rows[k]][0]
        main, left, right = some[piece]
        k = rows[piece].index(r)
        side = pl.ds(k * STEPS, STEPS)
        return [jnp.concatenate([nothing, left[side, :]], axis=0), main[k], jnp.concatenate([right[side, :], nothing], axis=0)]

    for n, window in enumerate(windows):
        for e, r in enumerate(window):
            a[n, e] = jnp.concatenate(row_of(pieces[:len(field_rows)], field_rows, r), axis=0)
            left, mid, right = row_of(pieces[len(field_rows):], weight_rows, r)
            at = pl.ds(STEPS + r, 1)
            left = jnp.where(last, left * masks[0, at, :], left)
            end = mid[width - PAD:]
            end = jnp.where(last, end * masks[1, at, :], end)
            w = jnp.concatenate([left, mid[:width - PAD], end, right], axis=0)
            other = pltpu.roll(w, half, 1)
            wi[n, e] = jnp.where(lane < half, w, other)
            wj[n, e] = jnp.where(lane < half, other, w)

    src, dst = a, b
    for step in range(STEPS):
        begin, stop = step + 1, ext - 1 - step
        for n in range(len(windows)):

            def one(r, carry, n=n, src=src, dst=dst):
                v, before = carry
                after = src[n, r + 1]
                flux = wi[n, r] * (after - v)
                across = wj[n, r] * (pltpu.roll(v, wide - 1, 0) - v)
                dst[n, r] = v + (flux - before) + (across - pltpu.roll(across, 1, 0))
                return after, flux

            v = src[n, begin]
            lax.fori_loop(begin, stop, one, (v, wi[n, begin - 1] * (v - src[n, begin - 1])), unroll=2)
        src, dst = dst, src

    groups = len(outs)
    count = order // groups
    rows = len(windows) * (ext - 2 * STEPS) // groups
    each = groups // len(windows)

    terms[...] = left_terms(matrix[...])

    def mix(pair, carry):
        planes = [2 * pair, 2 * pair + 1]
        x = jnp.concatenate(
            [src[g // each, STEPS + g % each * rows + i, pl.ds(PAD, width), :] for i in planes for g in range(groups)],
            axis=0,
        )
        y = lax.dot_general(
            terms[...], right_terms(x, 1), (((1,), (1,)), ((), ())), preferred_element_type=jnp.float32
        )
        cols = groups * width
        for k, i in enumerate(planes):
            for d, out in enumerate(outs):
                out[pl.ds(i, count, rows), :] = y[d * count:(d + 1) * count, k * cols:(k + 1) * cols]
        return carry

    lax.fori_loop(0, rows // 2, mix, 0, unroll=2)


def spread_mix(windows, matrix, depths, field, weights, groups):
    width, order = field[0][1].shape[1:]
    cols = width * groups
    ext = len(windows[0])
    rows = len(windows) * (ext - 2 * STEPS) // groups
    shape = jax.ShapeDtypeStruct((order // groups * rows, cols), jnp.float32)
    arrays = list(depths) + [x for piece in field + weights for x in piece[1:]]
    kernel = functools.partial(
        spread_kernel, windows, [piece[0] for piece in field], [piece[0] for piece in weights], len(depths)
    )
    tall = field[0][1].shape[0] + 2 * STEPS
    return pl.pallas_call(
        kernel,
        in_specs=[vmem()] * (1 + len(arrays)),
        out_specs=[vmem()] * groups,
        out_shape=[shape] * groups,
        scratch_shapes=[pltpu.VMEM((len(windows), ext, width + 2 * PAD, order), jnp.float32)] * 4
        + [pltpu.VMEM((2, tall, order), jnp.float32), pltpu.VMEM((order, 6 * order), jnp.bfloat16)],
        compiler_params=params(),
        name="spread_mix",
    )(matrix, *arrays)


RESULT_STEPS = 4


def result_kernel(runs, gain, mask, *refs):
    parts, (out, done, out_sems) = refs[:-3], refs[-3:]
    fields, levels, _, cols = gain.shape
    groups = len(parts)
    rows = done.shape[2] // groups
    some = levels // RESULT_STEPS
    slots = position()[1]
    group = lane_groups(rows, cols, groups)

    def of_slot(slot, at):
        x = parts[0][pl.ds(at, rows), :]
        for d in range(1, groups):
            x = jnp.where(slots[d] == slot, parts[d][pl.ds(at, rows), :], x)
        return x

    stored = []
    for step in range(RESULT_STEPS):
        for level in range(step * some, (step + 1) * some):
            ocean = jnp.concatenate([mask[level, pl.ds(*run), :] for run in runs], axis=0).astype(jnp.float32)
            for field in range(fields):
                at = (field * levels + level) * rows
                blocks = swap([of_slot(slot, at) for slot in range(groups)], group, cols // groups)
                gains = jnp.concatenate([gain[field, level, pl.ds(*run), :] for run in runs], axis=0)
                done[field, level] = ocean * gains * jnp.concatenate(blocks, axis=0)
        these = pl.ds(step * some, some)
        pairs, at = [], 0
        for first, number in runs:
            pairs.append((done.at[:, these, pl.ds(at, number)], out.at[:, these, pl.ds(first, number)]))
            at += number
        stored += copies(pairs, out_sems.at[step])
    for copy in stored:
        copy.wait()


def result(runs, gain, mask, parts, before):
    fields, levels, _, cols = gain.shape
    groups = len(parts)
    rows = sum(number for _, number in runs)
    anywhere = pl.BlockSpec(memory_space=pl.ANY)
    more = [] if before is None else [before]

    def kernel(gain, mask, *refs):
        result_kernel(runs, gain, mask, *refs[:groups], *refs[groups + len(more):])

    return pl.pallas_call(
        kernel,
        in_specs=[vmem()] * (2 + groups) + [anywhere] * len(more),
        out_specs=anywhere,
        out_shape=jax.ShapeDtypeStruct(gain.shape, jnp.float32),
        scratch_shapes=[
            pltpu.VMEM((fields, levels, rows, cols), jnp.float32),
            pltpu.SemaphoreType.DMA((RESULT_STEPS, len(runs))),
        ],
        input_output_aliases={2 + groups: 0} if more else {},
        compiler_params=params(),
        name="result",
    )(gain, mask, *parts, *more)


def shards(increment, norm_gain, diffusion_i, diffusion_j, sea_mask, coupling):
    devices = lax.axis_size("lev")
    gx_size = lax.axis_size("gx")
    gy_size = lax.axis_size("gy")
    _, levels, length, cols = increment.shape
    width = cols // devices
    rows = length // devices
    order = coupling.shape[0]
    to = [lax.rem(lax.axis_index("lev") + d, devices) for d in distances(devices)]
    source = [lax.rem(lax.axis_index("lev") + devices - d, devices) for d in distances(devices)]

    def shift(x, d):
        return lax.ppermute(x, "lev", [(k, (k + d) % devices) for k in range(devices)])

    def exchange(parts):
        return [parts[0]] + [shift(x, d) for x, d in zip(parts[1:], distances(devices)[1:])]

    up = [((k + 1) % gx_size, k) for k in range(gx_size)]
    down = [(b, a) for a, b in up]
    ring = [(devices - 1 - slot if y % 2 else slot) * gy_size + y for y in range(gy_size) for slot in range(devices)]
    ahead = list(zip(ring, ring[1:] + ring[:1]))
    back = [(b, a) for a, b in ahead]

    def halo_i(first, last):
        if gx_size == 2:
            size = first.shape[0]
            both = lax.ppermute(jnp.concatenate([first, last], axis=0), "gx", up)
            return both[size:], both[:size]
        return lax.ppermute(last, "gx", down), lax.ppermute(first, "gx", up)

    def halo_j(first, last):
        return lax.ppermute(last, ("lev", "gy"), ahead), lax.ppermute(first, ("lev", "gy"), back)

    def flat(x):
        return x.reshape(-1, x.shape[-1])

    def cut(x, *sizes):
        return lax.split(x, sizes, 0)

    quarter = length // 4
    some = 2 * quarter // devices
    half = devices // 2
    inner = (quarter, 2 * quarter)
    outer = ((0, quarter), (3 * quarter, quarter))
    inner_pieces = [
        ([STEPS + quarter + a * some for a in range(devices)], some),
        ([quarter + 2 * a for a in range(half)] + [STEPS + 3 * quarter + 2 * a for a in range(half)], 2),
    ]
    outer_pieces = [([a * some for a in range(half)] + [3 * quarter + 2 * STEPS + a * some for a in range(half)], some)]

    def rows_of(pieces):
        return [start - STEPS + i for starts, number in pieces for start in starts for i in range(number)]

    inner_rows, outer_rows = rows_of(inner_pieces), rows_of(outer_pieces)
    windows = [list(range(-STEPS, quarter + STEPS)), list(range(3 * quarter - STEPS, length + STEPS))]

    inner_size = len(inner_rows) // devices
    inner_messages = weight_messages(inner_pieces, diffusion_i, diffusion_j, [sea_mask])
    inner_parts = exchange(inner_messages)
    inner_messages, edge_i, edge_j, increment, norm_gain = lax.optimization_barrier(
        (inner_messages, diffusion_i, diffusion_j, increment, norm_gain)
    )
    halos = halo_i(
        *[
            jnp.concatenate([flat(edge_i[:, at]), flat(edge_j[:, at])], axis=0)
            for at in (slice(0, STEPS), slice(-STEPS, None))
        ]
    )
    messages = scaled_messages(increment, norm_gain, sea_mask, devices)
    scaled = exchange(messages)
    messages, halos = lax.optimization_barrier((messages, halos))
    outer_messages = weight_messages(outer_pieces, diffusion_i, diffusion_j, halos=halos)

    depth = sum(part[2 * levels * inner_size:] for part in inner_parts)
    here = turn_weights(inner_pieces, [depth], inner_parts, order)
    left, right = halo_j(
        jnp.concatenate([flat(here[:, :STEPS]), depth], axis=0),
        flat(here[:, -STEPS:]),
    )
    right, right_depth = cut(right, len(inner_rows) * STEPS, rows)

    balance = jnp.eye(order, dtype=jnp.float32) + coupling
    by_device = balance.reshape(2, devices, levels, order)
    adjoint = jnp.concatenate([by_device[:, s].reshape(2 * levels, order) for s in source], axis=0).T
    forward = jnp.concatenate([by_device[:, t].reshape(2 * levels, order) for t in to], axis=0)

    middle = devices // 2
    scaled, outer_messages = lax.optimization_barrier((scaled, outer_messages))
    early = shift(outer_messages[middle], middle)
    mixed = adjoint_mix(adjoint, depth, scaled, length, width)
    edges = flat(mixed[:, :STEPS]), flat(mixed[:, -STEPS:])
    edges, inner_weights = lax.optimization_barrier((edges, (here, left, right)))
    left, right = halo_j(*edges)
    left, right, outer_messages, early = lax.optimization_barrier((left, right, outer_messages, early))
    outer_parts = [
        early if d == middle else shift(outer_messages[d], d) if d else outer_messages[0] for d in range(devices)
    ]
    field = [(list(range(length)), mixed, left, right)]
    weights = [(inner_rows, *inner_weights)]
    depths = [depth, right_depth]
    inner_mixed = spread_mix([sorted(inner_rows)], forward, depths, field, weights, devices)
    _, upper, lower = lax.optimization_barrier((left, mixed[:STEPS], mixed[-STEPS:]))
    _, outer_parts = lax.optimization_barrier((inner_mixed[0], outer_parts))
    inner_mixed = exchange(inner_mixed)
    out = result((inner,), norm_gain, sea_mask, inner_mixed, None)

    above, below = halo_i(
        jnp.concatenate([flat(upper), depth[:STEPS]], axis=0),
        jnp.concatenate([flat(lower), depth[-STEPS:]], axis=0),
    )
    above, above_depth = cut(above, STEPS * width, STEPS)
    below, below_depth = cut(below, STEPS * width, STEPS)
    halo_depth = jnp.concatenate([below_depth, above_depth], axis=0)
    halo = jnp.concatenate([above, below], axis=0).reshape(2 * STEPS, width, order)
    here = turn_weights(outer_pieces, [depth, halo_depth], outer_parts, order)
    left, right = halo_j(
        jnp.concatenate([flat(here[:, :STEPS]), flat(halo[:, :STEPS]), halo_depth], axis=0),
        jnp.concatenate([flat(here[:, -STEPS:]), flat(halo[:, -STEPS:])], axis=0),
    )
    sizes = len(outer_rows) * STEPS, 2 * STEPS * STEPS
    left, halo_left = cut(left, *sizes)
    right, halo_right, right_halo_depth = cut(right, *sizes, 2 * STEPS)
    weights.append((outer_rows, here, left, right))
    field.append((list(range(-STEPS, 0)) + list(range(length, length + STEPS)), halo, halo_left, halo_right))
    depths += [halo_depth, right_halo_depth]
    outer_mixed = exchange(spread_mix(windows, forward, depths, field, weights, devices))
    return result(outer, norm_gain, sea_mask, outer_mixed, out)


def solution(mesh):
    return jax.shard_map(
        shards,
        mesh=mesh,
        in_specs=(
            P(None, "lev", "gx", "gy"),
            P(None, "lev", "gx", "gy"),
            P("lev", "gx", "gy"),
            P("lev", "gx", "gy"),
            P("lev", "gx", "gy"),
            P(),
        ),
        out_specs=P(None, "lev", "gx", "gy"),
        check_vma=False,
    )
```

```python
import functools

import jax
import jax.numpy as jnp
from jax import lax
from jax.experimental import pallas as pl
from jax.experimental.pallas import tpu as pltpu
from jax.sharding import PartitionSpec as P

ITERS = 2
STEPS = 2 * ITERS
PAD = 8
VMEM_LIMIT = 40 * 1024 * 1024
VMEM_WHOLE = 60 * 1024 * 1024
HIGHEST = lax.Precision.HIGHEST


def params(limit=VMEM_LIMIT):
    return pltpu.CompilerParams(vmem_limit_bytes=limit)


def smem():
    return pl.BlockSpec(memory_space=pltpu.SMEM)


def vmem():
    return pl.BlockSpec(memory_space=pltpu.VMEM)


def distances(devices):
    return list(range(devices))


def position():
    devices = lax.axis_size("lev")
    me = lax.axis_index("lev")
    flipped = lax.rem(lax.axis_index("gy"), 2) == 1

    def slot(lev):
        return jnp.where(flipped, devices - 1 - lev, lev)

    to = [lax.rem(me + d, devices) for d in distances(devices)]
    source = [lax.rem(me + devices - d, devices) for d in distances(devices)]
    return [slot(lev) for lev in to], [slot(lev) for lev in source], source


def swap(blocks, group, width, axis=1):
    blocks = list(blocks)
    cols = blocks[0].shape[axis]
    bit = len(blocks) // 2
    while bit:
        shift = bit * width
        low = (group & bit) == 0
        for a in range(len(blocks)):
            if not a & bit:
                x, y = blocks[a], blocks[a + bit]
                blocks[a] = jnp.where(low, x, pltpu.roll(y, shift, axis))
                blocks[a + bit] = jnp.where(low, pltpu.roll(x, cols - shift, axis), y)
        bit //= 2
    return blocks


def lane_groups(rows, cols, groups):
    return lax.broadcasted_iota(jnp.int32, (rows, cols), 1) // (cols // groups)


def copies(pairs, sems):
    made = [pltpu.make_async_copy(src, dst, sems.at[k]) for k, (src, dst) in enumerate(pairs)]
    for copy in made:
        copy.start()
    return made


SCALED_STEPS = 4


def scaled_kernel(increment, gain, mask, *refs):
    outs, (inc, gn, sea, held, sems, out_sems) = refs[:-6], refs[-6:]
    fields, levels, length, cols = increment.shape
    groups = len(outs)
    rows = length // groups
    some = levels // SCALED_STEPS
    group = lane_groups(rows, cols, groups)
    fetched = []
    for step in range(SCALED_STEPS):
        part = pl.ds(step * some, some)
        fetched.append(
            copies(
                [
                    (increment.at[:, part], inc.at[:, part]),
                    (gain.at[:, part], gn.at[:, part]),
                    (mask.at[part], sea.at[part]),
                ],
                sems.at[step],
            )
        )

    for step in range(SCALED_STEPS):
        for copy in fetched[step]:
            copy.wait()

        def one(level, carry):
            ocean = sea[level].astype(jnp.float32)
            for field in range(fields):
                at = pl.multiple_of((field * levels + level) * rows, rows)
                x = ocean * gn[field, level] * inc[field, level]
                blocks = swap([x[a * rows:(a + 1) * rows] for a in range(groups)], group, cols // groups)
                for slot, block in enumerate(blocks):
                    held[slot, pl.ds(at, rows), :] = block
            return carry

        lax.fori_loop(step * some, (step + 1) * some, one, 0, unroll=True)
    slots = position()[0]
    for copy in copies([(held.at[slots[d]], out) for d, out in enumerate(outs)], out_sems):
        copy.wait()


def scaled_messages(increment, gain, mask, groups):
    fields, levels, length, cols = increment.shape
    shape = (fields * levels * length // groups, cols)
    return pl.pallas_call(
        scaled_kernel,
        in_specs=[pl.BlockSpec(memory_space=pl.ANY)] * 3,
        out_specs=[pl.BlockSpec(memory_space=pl.ANY)] * groups,
        out_shape=[jax.ShapeDtypeStruct(shape, jnp.float32)] * groups,
        scratch_shapes=[
            pltpu.VMEM(increment.shape, jnp.float32),
            pltpu.VMEM(gain.shape, jnp.float32),
            pltpu.VMEM(mask.shape, mask.dtype),
            pltpu.VMEM((groups, *shape), jnp.float32),
            pltpu.SemaphoreType.DMA((SCALED_STEPS, 3)),
            pltpu.SemaphoreType.DMA((groups,)),
        ],
        compiler_params=params(VMEM_WHOLE),
        name="scaled_messages",
    )(increment, gain, mask)


def pack_kernel(pieces, masked, along_i, along_j, *refs):
    levels, length, cols = along_i.shape
    groups = len(pieces[0][0])
    width = cols // groups
    halos, outs = refs[masked:-4 - groups - 3 * masked], refs[-4 - groups - 3 * masked:-4 - 3 * masked]
    held, slots_held, sems, fetch_sems = refs[-4:]
    unroll = held.shape[0]
    number = levels // unroll
    starts, rows = pieces[0]
    group = lane_groups(rows, cols, groups)
    if masked:
        sources, (along_i, along_j, sea) = (along_i, along_j, refs[0]), refs[-7:-4]
        fetched = []
        for side, (source, target) in enumerate(zip(sources, (along_i, along_j, sea))):
            pairs = [(source.at[pl.ds(k * unroll, unroll)], target.at[pl.ds(k * unroll, unroll)]) for k in range(number)]
            fetched.append(copies(pairs, fetch_sems.at[side]))

    def put(at, blocks):
        for slot, block in enumerate(blocks):
            slots_held[slot, pl.ds(at, block.shape[0]), :] = block

    for side, weight in enumerate((along_i, along_j)):
        for outer in range(number):
            if masked:
                fetched[side][outer].wait()
            edges = []
            for k in range(unroll):
                level = outer * unroll + k
                index = side * levels + level
                if halos:
                    for halo, at in zip(halos, (0, STEPS + length)):
                        held[k, pl.ds(at, STEPS), :] = halo[pl.ds(index * STEPS, STEPS), :]
                    held[k, pl.ds(STEPS, length), :] = weight[level]
                    blocks = [held[k, pl.ds(start, rows), :] for start in starts]
                else:
                    blocks = [weight[level, pl.ds(start - STEPS, rows), :] for start in starts]
                put(index * rows, swap(blocks, group, width))
                if len(pieces) > 1:
                    small = pieces[1][0]
                    low, high = small[0] - 2 * STEPS, small[groups // 2] - STEPS
                    row = lax.broadcasted_iota(jnp.int32, (2 * STEPS, cols), 0)
                    upper = pltpu.roll(weight[level, pl.ds(low, 2 * STEPS), :], STEPS, 0)
                    lower = pltpu.roll(weight[level, pl.ds(high, 2 * STEPS), :], STEPS, 0)
                    edges.append(jnp.where(row < STEPS, upper, lower))
            if edges:
                each = pieces[1][1]
                pairs = lax.broadcasted_iota(jnp.int32, edges[0].shape, 0) // each
                edges = swap(edges, pairs, each, 0)
                at = 2 * levels * rows + (side * levels + outer * unroll) * each
                put(at, swap(edges, lane_groups(unroll * each, cols, groups), width))
    if masked:
        depth = jnp.zeros((length, cols), sea.dtype)
        for outer in range(number):
            fetched[2][outer].wait()
            for level in range(outer * unroll, (outer + 1) * unroll):
                depth = depth + sea[level]
        depth = depth.astype(jnp.float32)
        size = length // groups
        blocks = [depth[a * size:(a + 1) * size] for a in range(groups)]
        put(2 * levels * sum(n for _, n in pieces), swap(blocks, lane_groups(size, cols, groups), width))
    slots = position()[0]
    for copy in copies([(slots_held.at[slots[d]], out) for d, out in enumerate(outs)], sems):
        copy.wait()


def weight_messages(pieces, along_i, along_j, mask=(), halos=()):
    levels, length, cols = along_i.shape
    groups = len(pieces[0][0])
    shape = (2 * levels * sum(rows for _, rows in pieces) + len(mask) * length // groups, cols)
    unroll = 4
    return list(
        pl.pallas_call(
            functools.partial(pack_kernel, pieces, len(mask)),
            in_specs=[pl.BlockSpec(memory_space=pl.ANY) if mask else vmem()] * (2 + len(mask) + len(halos)),
            out_specs=[pl.BlockSpec(memory_space=pl.ANY)] * groups,
            out_shape=[jax.ShapeDtypeStruct(shape, jnp.float32)] * groups,
            scratch_shapes=[pltpu.VMEM(x.shape, x.dtype) for x in ([along_i, along_j, *mask] if mask else [])]
            + [
                pltpu.VMEM((unroll, length + 2 * STEPS, cols), jnp.float32),
                pltpu.VMEM((groups, *shape), jnp.float32),
                pltpu.SemaphoreType.DMA((groups,)),
                pltpu.SemaphoreType.DMA((3, levels // unroll)),
            ],
            compiler_params=params(VMEM_WHOLE if mask else VMEM_LIMIT),
            name="weight_messages",
        )(along_i, along_j, *mask, *halos)
    )


def three(x):
    high = x.astype(jnp.bfloat16)
    rest = x - high.astype(jnp.float32)
    middle = rest.astype(jnp.bfloat16)
    return high, middle, (rest - middle.astype(jnp.float32)).astype(jnp.bfloat16)


def left_terms(x):
    high, middle, low = three(x)
    return jnp.concatenate([high, middle, low, high, middle, high], axis=1)


def right_terms(x, axis):
    high, middle, low = three(x)
    return jnp.concatenate([high, high, high, middle, middle, low], axis=axis)


def adjoint_kernel(matrix, depths, *refs):
    parts, out, terms = refs[:-2], refs[-2], refs[-1]
    length, width, order = out.shape
    groups = len(parts)
    rows = length // groups
    cols = groups * width
    count = order // groups
    level = lax.rem(lax.broadcasted_iota(jnp.int32, (order, cols), 0), order // 2).astype(jnp.float32)

    terms[...] = left_terms(matrix[...])

    def two(pair, carry):
        planes = [2 * pair, 2 * pair + 1]
        x = jnp.concatenate(
            [jnp.concatenate([part[pl.ds(i, count, rows), :] for part in parts], axis=0) for i in planes], axis=1
        )
        y = jnp.dot(terms[...], right_terms(x, 0), preferred_element_type=jnp.float32)
        for k, i in enumerate(planes):
            z = jnp.where(level < depths[pl.ds(i, 1), :], y[:, k * cols:(k + 1) * cols], 0.0).T
            for a in range(groups):
                out[a * rows + i] = z[a * width:(a + 1) * width]
        return carry

    lax.fori_loop(0, rows // 2, two, 0, unroll=2)


def adjoint_mix(matrix, depths, parts, length, width):
    return pl.pallas_call(
        adjoint_kernel,
        in_specs=[vmem()] * (2 + len(parts)),
        out_specs=vmem(),
        out_shape=jax.ShapeDtypeStruct((length, width, matrix.shape[0]), jnp.float32),
        scratch_shapes=[pltpu.VMEM((matrix.shape[0], 6 * matrix.shape[0]), jnp.bfloat16)],
        compiler_params=params(),
        name="adjoint_mix",
    )(matrix, depths, *parts)


def unfold(main, halo, groups):
    cols = main.shape[1]
    width = cols // groups
    below = halo[:STEPS]
    above = pltpu.roll(halo[STEPS:], width, 1)
    return jnp.concatenate(
        [above] + [main] + [pltpu.roll(main, cols - a * width, 1) for a in range(1, groups)] + [below], axis=0
    )


def turn_kernel(pieces, *refs):
    groups = len(pieces[0][0])
    depths, parts, (out, held, depth_i, depth_j) = refs[:-4 - groups], refs[-4 - groups:-4], refs[-4:]
    _, width, order = out.shape
    half = order // 2
    count = half // groups
    cols = width * groups
    source = position()[2]
    planes, base = [], 0
    for starts, rows in pieces:
        planes += [(base + i, rows, i, starts) for i in range(rows)]
        base += 2 * count * rows
    for k, (first, rows, _, _) in enumerate(planes):
        for d, part in enumerate(parts):
            for side in range(2):
                at = pl.multiple_of(side * half + source[d] * count, 8)
                held[k, pl.ds(at, count), :] = part[pl.ds(first + side * count * rows, count, rows), :]

    no_halo = jnp.zeros((2 * STEPS, cols), jnp.float32)
    depth = unfold(depths[0][...], depths[1][...] if len(depths) > 1 else no_halo, groups)
    tall = depth.shape[0]
    lane = lax.broadcasted_iota(jnp.int32, depth.shape, 1)
    right = jnp.where(lane == width - 1, depth, pltpu.roll(depth, cols - 1, 1))
    depth_j[...] = jnp.minimum(depth, right)
    depth_i[pl.ds(0, tall - 1), :] = jnp.minimum(depth[:-1], depth[1:])
    depth_i[pl.ds(tall - 1, 1), :] = depth[tall - 1:]

    def fold(ref, starts, rows):
        group = lane_groups(rows, cols, groups)
        x = ref[pl.ds(starts[0], rows), :]
        for a in range(1, groups):
            x = jnp.where(group == a, pltpu.roll(ref[pl.ds(starts[a], rows), :], a * width, 1), x)
        return x

    folded = [(fold(depth_i, *piece), fold(depth_j, *piece)) for piece in pieces]
    level = lax.broadcasted_iota(jnp.int32, (half, cols), 0).astype(jnp.float32)
    at = 0
    for n, (starts, rows) in enumerate(pieces):
        for i in range(rows):
            k = at // groups + i
            along_i = jnp.where(level < folded[n][0][i:i + 1], held[k, pl.ds(0, half), :], 0.0)
            along_j = jnp.where(level < folded[n][1][i:i + 1], held[k, pl.ds(half, half), :], 0.0)
            turned = jnp.concatenate([along_i, along_j], axis=0).T
            for a in range(groups):
                out[at + a * rows + i] = turned[a * width:(a + 1) * width]
        at += groups * rows


def turn_weights(pieces, depths, parts, order):
    groups = len(parts)
    cols = parts[0].shape[1]
    rows = sum(n for _, n in pieces)
    tall = depths[0].shape[0] * groups + 2 * STEPS
    return pl.pallas_call(
        functools.partial(turn_kernel, pieces),
        in_specs=[vmem()] * (len(depths) + groups),
        out_specs=vmem(),
        out_shape=jax.ShapeDtypeStruct((rows * groups, cols // groups, order), jnp.float32),
        scratch_shapes=[pltpu.VMEM((rows, order, cols), jnp.float32)] + [pltpu.VMEM((tall, cols), jnp.float32)] * 2,
        compiler_params=params(),
        name="turn_weights",
    )(*depths, *parts)


def edge_masks(depths, order):
    groups = lax.axis_size("lev")
    slot = position()[0][0]
    gy = lax.axis_index("gy")
    start = (slot == 0) & (gy == 0)
    end = (slot == groups - 1) & (gy == lax.axis_size("gy") - 1)
    no_halo = jnp.zeros((2 * STEPS, depths[0].shape[1]), jnp.float32)
    masks = []
    for k, out in enumerate((start, end)):
        x = unfold(depths[k][...], depths[2 + k][...] if len(depths) > 2 else no_halo, groups)
        x = jnp.where(out, 0.0, x)
        x = jnp.broadcast_to(x[:, :1], (x.shape[0], order))
        lane = lax.broadcasted_iota(jnp.int32, x.shape, 1)
        level = lax.rem(lane, order // 2).astype(jnp.float32)
        masks.append(jnp.where((lane < order // 2) | (level < x), 1.0, 0.0))
    return masks


def spread_kernel(windows, field_rows, weight_rows, count, matrix, *refs):
    depths, refs = refs[:count], refs[count:]
    pieces = [refs[3 * k:3 * k + 3] for k in range(len(field_rows) + len(weight_rows))]
    outs, (a, b, wi, wj, masks, terms) = refs[3 * len(pieces):-6], refs[-6:]
    width, order = pieces[0][0].shape[1:]
    half = order // 2
    _, ext, wide, _ = a.shape
    lane = lax.broadcasted_iota(jnp.int32, (wide, order), 1)
    last = lax.broadcasted_iota(jnp.int32, (PAD, order), 0) == PAD - 1
    nothing = jnp.zeros((PAD - STEPS, order), jnp.float32)
    masks[0], masks[1] = edge_masks(depths, order)

    def row_of(some, rows, r):
        piece = [k for k in range(len(rows)) if r in rows[k]][0]
        main, left, right = some[piece]
        k = rows[piece].index(r)
        side = pl.ds(k * STEPS, STEPS)
        return [jnp.concatenate([nothing, left[side, :]], axis=0), main[k], jnp.concatenate([right[side, :], nothing], axis=0)]

    for n, window in enumerate(windows):
        for e, r in enumerate(window):
            a[n, e] = jnp.concatenate(row_of(pieces[:len(field_rows)], field_rows, r), axis=0)
            left, mid, right = row_of(pieces[len(field_rows):], weight_rows, r)
            at = pl.ds(STEPS + r, 1)
            left = jnp.where(last, left * masks[0, at, :], left)
            end = mid[width - PAD:]
            end = jnp.where(last, end * masks[1, at, :], end)
            w = jnp.concatenate([left, mid[:width - PAD], end, right], axis=0)
            other = pltpu.roll(w, half, 1)
            wi[n, e] = jnp.where(lane < half, w, other)
            wj[n, e] = jnp.where(lane < half, other, w)

    src, dst = a, b
    for step in range(STEPS):
        begin, stop = step + 1, ext - 1 - step
        for n in range(len(windows)):

            def one(r, carry, n=n, src=src, dst=dst):
                v, before = carry
                after = src[n, r + 1]
                flux = wi[n, r] * (after - v)
                across = wj[n, r] * (pltpu.roll(v, wide - 1, 0) - v)
                dst[n, r] = v + (flux - before) + (across - pltpu.roll(across, 1, 0))
                return after, flux

            v = src[n, begin]
            lax.fori_loop(begin, stop, one, (v, wi[n, begin - 1] * (v - src[n, begin - 1])), unroll=2)
        src, dst = dst, src

    groups = len(outs)
    count = order // groups
    rows = len(windows) * (ext - 2 * STEPS) // groups
    each = groups // len(windows)

    terms[...] = left_terms(matrix[...])

    def mix(pair, carry):
        planes = [2 * pair, 2 * pair + 1]
        x = jnp.concatenate(
            [src[g // each, STEPS + g % each * rows + i, pl.ds(PAD, width), :] for i in planes for g in range(groups)],
            axis=0,
        )
        y = lax.dot_general(
            terms[...], right_terms(x, 1), (((1,), (1,)), ((), ())), preferred_element_type=jnp.float32
        )
        cols = groups * width
        for k, i in enumerate(planes):
            for d, out in enumerate(outs):
                out[pl.ds(i, count, rows), :] = y[d * count:(d + 1) * count, k * cols:(k + 1) * cols]
        return carry

    lax.fori_loop(0, rows // 2, mix, 0, unroll=2)


def spread_mix(windows, matrix, depths, field, weights, groups):
    width, order = field[0][1].shape[1:]
    cols = width * groups
    ext = len(windows[0])
    rows = len(windows) * (ext - 2 * STEPS) // groups
    shape = jax.ShapeDtypeStruct((order // groups * rows, cols), jnp.float32)
    arrays = list(depths) + [x for piece in field + weights for x in piece[1:]]
    kernel = functools.partial(
        spread_kernel, windows, [piece[0] for piece in field], [piece[0] for piece in weights], len(depths)
    )
    tall = field[0][1].shape[0] + 2 * STEPS
    return pl.pallas_call(
        kernel,
        in_specs=[vmem()] * (1 + len(arrays)),
        out_specs=[vmem()] * groups,
        out_shape=[shape] * groups,
        scratch_shapes=[pltpu.VMEM((len(windows), ext, width + 2 * PAD, order), jnp.float32)] * 4
        + [pltpu.VMEM((2, tall, order), jnp.float32), pltpu.VMEM((order, 6 * order), jnp.bfloat16)],
        compiler_params=params(),
        name="spread_mix",
    )(matrix, *arrays)


RESULT_STEPS = 4


def result_kernel(runs, gain, mask, *refs):
    parts, (out, done, out_sems) = refs[:-3], refs[-3:]
    fields, levels, _, cols = gain.shape
    groups = len(parts)
    rows = done.shape[2] // groups
    some = levels // RESULT_STEPS
    slots = position()[1]
    group = lane_groups(rows, cols, groups)

    def of_slot(slot, at):
        x = parts[0][pl.ds(at, rows), :]
        for d in range(1, groups):
            x = jnp.where(slots[d] == slot, parts[d][pl.ds(at, rows), :], x)
        return x

    stored = []
    for step in range(RESULT_STEPS):
        for level in range(step * some, (step + 1) * some):
            ocean = jnp.concatenate([mask[level, pl.ds(*run), :] for run in runs], axis=0).astype(jnp.float32)
            for field in range(fields):
                at = (field * levels + level) * rows
                blocks = swap([of_slot(slot, at) for slot in range(groups)], group, cols // groups)
                gains = jnp.concatenate([gain[field, level, pl.ds(*run), :] for run in runs], axis=0)
                done[field, level] = ocean * gains * jnp.concatenate(blocks, axis=0)
        these = pl.ds(step * some, some)
        pairs, at = [], 0
        for first, number in runs:
            pairs.append((done.at[:, these, pl.ds(at, number)], out.at[:, these, pl.ds(first, number)]))
            at += number
        stored += copies(pairs, out_sems.at[step])
    for copy in stored:
        copy.wait()


def result(runs, gain, mask, parts, before):
    fields, levels, _, cols = gain.shape
    groups = len(parts)
    rows = sum(number for _, number in runs)
    anywhere = pl.BlockSpec(memory_space=pl.ANY)
    more = [] if before is None else [before]

    def kernel(gain, mask, *refs):
        result_kernel(runs, gain, mask, *refs[:groups], *refs[groups + len(more):])

    return pl.pallas_call(
        kernel,
        in_specs=[vmem()] * (2 + groups) + [anywhere] * len(more),
        out_specs=anywhere,
        out_shape=jax.ShapeDtypeStruct(gain.shape, jnp.float32),
        scratch_shapes=[
            pltpu.VMEM((fields, levels, rows, cols), jnp.float32),
            pltpu.SemaphoreType.DMA((RESULT_STEPS, len(runs))),
        ],
        input_output_aliases={2 + groups: 0} if more else {},
        compiler_params=params(),
        name="result",
    )(gain, mask, *parts, *more)


def shards(increment, norm_gain, diffusion_i, diffusion_j, sea_mask, coupling):
    devices = lax.axis_size("lev")
    gx_size = lax.axis_size("gx")
    gy_size = lax.axis_size("gy")
    _, levels, length, cols = increment.shape
    width = cols // devices
    rows = length // devices
    order = coupling.shape[0]
    to = [lax.rem(lax.axis_index("lev") + d, devices) for d in distances(devices)]
    source = [lax.rem(lax.axis_index("lev") + devices - d, devices) for d in distances(devices)]

    def shift(x, d):
        return lax.ppermute(x, "lev", [(k, (k + d) % devices) for k in range(devices)])

    def exchange(parts):
        return [parts[0]] + [shift(x, d) for x, d in zip(parts[1:], distances(devices)[1:])]

    up = [((k + 1) % gx_size, k) for k in range(gx_size)]
    down = [(b, a) for a, b in up]
    ring = [(devices - 1 - slot if y % 2 else slot) * gy_size + y for y in range(gy_size) for slot in range(devices)]
    ahead = list(zip(ring, ring[1:] + ring[:1]))
    back = [(b, a) for a, b in ahead]

    def halo_i(first, last):
        if gx_size == 2:
            size = first.shape[0]
            both = lax.ppermute(jnp.concatenate([first, last], axis=0), "gx", up)
            return both[size:], both[:size]
        return lax.ppermute(last, "gx", down), lax.ppermute(first, "gx", up)

    def halo_j(first, last):
        return lax.ppermute(last, ("lev", "gy"), ahead), lax.ppermute(first, ("lev", "gy"), back)

    def flat(x):
        return x.reshape(-1, x.shape[-1])

    def cut(x, *sizes):
        return lax.split(x, sizes, 0)

    quarter = length // 4
    some = 2 * quarter // devices
    half = devices // 2
    inner = (quarter, 2 * quarter)
    outer = ((0, quarter), (3 * quarter, quarter))
    inner_pieces = [
        ([STEPS + quarter + a * some for a in range(devices)], some),
        ([quarter + 2 * a for a in range(half)] + [STEPS + 3 * quarter + 2 * a for a in range(half)], 2),
    ]
    outer_pieces = [([a * some for a in range(half)] + [3 * quarter + 2 * STEPS + a * some for a in range(half)], some)]

    def rows_of(pieces):
        return [start - STEPS + i for starts, number in pieces for start in starts for i in range(number)]

    inner_rows, outer_rows = rows_of(inner_pieces), rows_of(outer_pieces)
    windows = [list(range(-STEPS, quarter + STEPS)), list(range(3 * quarter - STEPS, length + STEPS))]

    inner_size = len(inner_rows) // devices
    inner_messages = weight_messages(inner_pieces, diffusion_i, diffusion_j, [sea_mask])
    inner_parts = exchange(inner_messages)
    inner_messages, edge_i, edge_j, increment, norm_gain = lax.optimization_barrier(
        (inner_messages, diffusion_i, diffusion_j, increment, norm_gain)
    )
    halos = halo_i(
        *[
            jnp.concatenate([flat(edge_i[:, at]), flat(edge_j[:, at])], axis=0)
            for at in (slice(0, STEPS), slice(-STEPS, None))
        ]
    )
    messages = scaled_messages(increment, norm_gain, sea_mask, devices)
    scaled = exchange(messages)
    messages, halos = lax.optimization_barrier((messages, halos))
    outer_messages = weight_messages(outer_pieces, diffusion_i, diffusion_j, halos=halos)

    depth = sum(part[2 * levels * inner_size:] for part in inner_parts)
    here = turn_weights(inner_pieces, [depth], inner_parts, order)
    left, right = halo_j(
        jnp.concatenate([flat(here[:, :STEPS]), depth], axis=0),
        flat(here[:, -STEPS:]),
    )
    right, right_depth = cut(right, len(inner_rows) * STEPS, rows)

    balance = jnp.eye(order, dtype=jnp.float32) + coupling
    by_device = balance.reshape(2, devices, levels, order)
    adjoint = jnp.concatenate([by_device[:, s].reshape(2 * levels, order) for s in source], axis=0).T
    forward = jnp.concatenate([by_device[:, t].reshape(2 * levels, order) for t in to], axis=0)

    middle = devices // 2
    scaled, outer_messages = lax.optimization_barrier((scaled, outer_messages))
    early = shift(outer_messages[middle], middle)
    mixed = adjoint_mix(adjoint, depth, scaled, length, width)
    edges = flat(mixed[:, :STEPS]), flat(mixed[:, -STEPS:])
    edges, inner_weights = lax.optimization_barrier((edges, (here, left, right)))
    left, right = halo_j(*edges)
    left, right, outer_messages, early = lax.optimization_barrier((left, right, outer_messages, early))
    outer_parts = [
        early if d == middle else shift(outer_messages[d], d) if d else outer_messages[0] for d in range(devices)
    ]
    field = [(list(range(length)), mixed, left, right)]
    weights = [(inner_rows, *inner_weights)]
    depths = [depth, right_depth]
    inner_mixed = spread_mix([sorted(inner_rows)], forward, depths, field, weights, devices)
    _, upper, lower = lax.optimization_barrier((left, mixed[:STEPS], mixed[-STEPS:]))
    _, outer_parts = lax.optimization_barrier((inner_mixed[0], outer_parts))
    inner_mixed = exchange(inner_mixed)

    above, below = halo_i(
        jnp.concatenate([flat(upper), depth[:STEPS]], axis=0),
        jnp.concatenate([flat(lower), depth[-STEPS:]], axis=0),
    )
    above, above_depth = cut(above, STEPS * width, STEPS)
    below, below_depth = cut(below, STEPS * width, STEPS)
    halo_depth = jnp.concatenate([below_depth, above_depth], axis=0)
    halo = jnp.concatenate([above, below], axis=0).reshape(2 * STEPS, width, order)
    here = turn_weights(outer_pieces, [depth, halo_depth], outer_parts, order)
    left, right = halo_j(
        jnp.concatenate([flat(here[:, :STEPS]), flat(halo[:, :STEPS]), halo_depth], axis=0),
        jnp.concatenate([flat(here[:, -STEPS:]), flat(halo[:, -STEPS:])], axis=0),
    )
    light = [d for d in range(1, devices) if d != middle]
    left, right, moved = lax.optimization_barrier((left, right, [inner_mixed[d] for d in light]))
    for d, x in zip(light, moved):
        inner_mixed[d] = x
    out = result((inner,), norm_gain, sea_mask, inner_mixed, None)
    sizes = len(outer_rows) * STEPS, 2 * STEPS * STEPS
    left, halo_left = cut(left, *sizes)
    right, halo_right, right_halo_depth = cut(right, *sizes, 2 * STEPS)
    weights.append((outer_rows, here, left, right))
    field.append((list(range(-STEPS, 0)) + list(range(length, length + STEPS)), halo, halo_left, halo_right))
    depths += [halo_depth, right_halo_depth]
    outer_mixed = exchange(spread_mix(windows, forward, depths, field, weights, devices))
    return result(outer, norm_gain, sea_mask, outer_mixed, out)


def solution(mesh):
    return jax.shard_map(
        shards,
        mesh=mesh,
        in_specs=(
            P(None, "lev", "gx", "gy"),
            P(None, "lev", "gx", "gy"),
            P("lev", "gx", "gy"),
            P("lev", "gx", "gy"),
            P("lev", "gx", "gy"),
            P(),
        ),
        out_specs=P(None, "lev", "gx", "gy"),
        check_vma=False,
    )
```

```python
import functools

import jax
import jax.numpy as jnp
from jax import lax
from jax.experimental import pallas as pl
from jax.experimental.pallas import tpu as pltpu
from jax.sharding import PartitionSpec as P

ITERS = 2
STEPS = 2 * ITERS
PAD = 8
VMEM_LIMIT = 40 * 1024 * 1024
VMEM_WHOLE = 60 * 1024 * 1024
HIGHEST = lax.Precision.HIGHEST


def params(limit=VMEM_LIMIT):
    return pltpu.CompilerParams(vmem_limit_bytes=limit)


def smem():
    return pl.BlockSpec(memory_space=pltpu.SMEM)


def vmem():
    return pl.BlockSpec(memory_space=pltpu.VMEM)


def distances(devices):
    return list(range(devices))


def position():
    devices = lax.axis_size("lev")
    me = lax.axis_index("lev")
    flipped = lax.rem(lax.axis_index("gy"), 2) == 1

    def slot(lev):
        return jnp.where(flipped, devices - 1 - lev, lev)

    to = [lax.rem(me + d, devices) for d in distances(devices)]
    source = [lax.rem(me + devices - d, devices) for d in distances(devices)]
    return [slot(lev) for lev in to], [slot(lev) for lev in source], source


def swap(blocks, group, width, axis=1):
    blocks = list(blocks)
    cols = blocks[0].shape[axis]
    bit = len(blocks) // 2
    while bit:
        shift = bit * width
        low = (group & bit) == 0
        for a in range(len(blocks)):
            if not a & bit:
                x, y = blocks[a], blocks[a + bit]
                blocks[a] = jnp.where(low, x, pltpu.roll(y, shift, axis))
                blocks[a + bit] = jnp.where(low, pltpu.roll(x, cols - shift, axis), y)
        bit //= 2
    return blocks


def lane_groups(rows, cols, groups):
    return lax.broadcasted_iota(jnp.int32, (rows, cols), 1) // (cols // groups)


def copies(pairs, sems):
    made = [pltpu.make_async_copy(src, dst, sems.at[k]) for k, (src, dst) in enumerate(pairs)]
    for copy in made:
        copy.start()
    return made


SCALED_STEPS = 4


def scaled_kernel(increment, gain, mask, *refs):
    outs, (inc, gn, sea, held, sems, out_sems) = refs[:-6], refs[-6:]
    fields, levels, length, cols = increment.shape
    groups = len(outs)
    rows = length // groups
    some = levels // SCALED_STEPS
    group = lane_groups(rows, cols, groups)
    fetched = []
    for step in range(SCALED_STEPS):
        part = pl.ds(step * some, some)
        fetched.append(
            copies(
                [
                    (increment.at[:, part], inc.at[:, part]),
                    (gain.at[:, part], gn.at[:, part]),
                    (mask.at[part], sea.at[part]),
                ],
                sems.at[step],
            )
        )

    for step in range(SCALED_STEPS):
        for copy in fetched[step]:
            copy.wait()

        def one(level, carry):
            ocean = sea[level].astype(jnp.float32)
            for field in range(fields):
                at = pl.multiple_of((field * levels + level) * rows, rows)
                x = ocean * gn[field, level] * inc[field, level]
                blocks = swap([x[a * rows:(a + 1) * rows] for a in range(groups)], group, cols // groups)
                for slot, block in enumerate(blocks):
                    held[slot, pl.ds(at, rows), :] = block
            return carry

        lax.fori_loop(step * some, (step + 1) * some, one, 0, unroll=True)
    slots = position()[0]
    for copy in copies([(held.at[slots[d]], out) for d, out in enumerate(outs)], out_sems):
        copy.wait()


def scaled_messages(increment, gain, mask, groups):
    fields, levels, length, cols = increment.shape
    shape = (fields * levels * length // groups, cols)
    return pl.pallas_call(
        scaled_kernel,
        in_specs=[pl.BlockSpec(memory_space=pl.ANY)] * 3,
        out_specs=[pl.BlockSpec(memory_space=pl.ANY)] * groups,
        out_shape=[jax.ShapeDtypeStruct(shape, jnp.float32)] * groups,
        scratch_shapes=[
            pltpu.VMEM(increment.shape, jnp.float32),
            pltpu.VMEM(gain.shape, jnp.float32),
            pltpu.VMEM(mask.shape, mask.dtype),
            pltpu.VMEM((groups, *shape), jnp.float32),
            pltpu.SemaphoreType.DMA((SCALED_STEPS, 3)),
            pltpu.SemaphoreType.DMA((groups,)),
        ],
        compiler_params=params(VMEM_WHOLE),
        name="scaled_messages",
    )(increment, gain, mask)


def pack_kernel(pieces, masked, along_i, along_j, *refs):
    levels, length, cols = along_i.shape
    groups = len(pieces[0][0])
    width = cols // groups
    halos, outs = refs[masked:-4 - groups - 3 * masked], refs[-4 - groups - 3 * masked:-4 - 3 * masked]
    held, slots_held, sems, fetch_sems = refs[-4:]
    unroll = held.shape[0]
    number = levels // unroll
    starts, rows = pieces[0]
    group = lane_groups(rows, cols, groups)
    if masked:
        sources, (along_i, along_j, sea) = (along_i, along_j, refs[0]), refs[-7:-4]
        fetched = []
        for side, (source, target) in enumerate(zip(sources, (along_i, along_j, sea))):
            pairs = [(source.at[pl.ds(k * unroll, unroll)], target.at[pl.ds(k * unroll, unroll)]) for k in range(number)]
            fetched.append(copies(pairs, fetch_sems.at[side]))

    def put(at, blocks):
        for slot, block in enumerate(blocks):
            slots_held[slot, pl.ds(at, block.shape[0]), :] = block

    for side, weight in enumerate((along_i, along_j)):
        for outer in range(number):
            if masked:
                fetched[side][outer].wait()
            edges = []
            for k in range(unroll):
                level = outer * unroll + k
                index = side * levels + level
                if halos:
                    for halo, at in zip(halos, (0, STEPS + length)):
                        held[k, pl.ds(at, STEPS), :] = halo[pl.ds(index * STEPS, STEPS), :]
                    held[k, pl.ds(STEPS, length), :] = weight[level]
                    blocks = [held[k, pl.ds(start, rows), :] for start in starts]
                else:
                    blocks = [weight[level, pl.ds(start - STEPS, rows), :] for start in starts]
                put(index * rows, swap(blocks, group, width))
                if len(pieces) > 1:
                    small = pieces[1][0]
                    low, high = small[0] - 2 * STEPS, small[groups // 2] - STEPS
                    row = lax.broadcasted_iota(jnp.int32, (2 * STEPS, cols), 0)
                    upper = pltpu.roll(weight[level, pl.ds(low, 2 * STEPS), :], STEPS, 0)
                    lower = pltpu.roll(weight[level, pl.ds(high, 2 * STEPS), :], STEPS, 0)
                    edges.append(jnp.where(row < STEPS, upper, lower))
            if edges:
                each = pieces[1][1]
                pairs = lax.broadcasted_iota(jnp.int32, edges[0].shape, 0) // each
                edges = swap(edges, pairs, each, 0)
                at = 2 * levels * rows + (side * levels + outer * unroll) * each
                put(at, swap(edges, lane_groups(unroll * each, cols, groups), width))
    if masked:
        depth = jnp.zeros((length, cols), sea.dtype)
        for outer in range(number):
            fetched[2][outer].wait()
            for level in range(outer * unroll, (outer + 1) * unroll):
                depth = depth + sea[level]
        depth = depth.astype(jnp.float32)
        size = length // groups
        blocks = [depth[a * size:(a + 1) * size] for a in range(groups)]
        put(2 * levels * sum(n for _, n in pieces), swap(blocks, lane_groups(size, cols, groups), width))
    slots = position()[0]
    for copy in copies([(slots_held.at[slots[d]], out) for d, out in enumerate(outs)], sems):
        copy.wait()


def weight_messages(pieces, along_i, along_j, mask=(), halos=()):
    levels, length, cols = along_i.shape
    groups = len(pieces[0][0])
    shape = (2 * levels * sum(rows for _, rows in pieces) + len(mask) * length // groups, cols)
    unroll = 4
    return list(
        pl.pallas_call(
            functools.partial(pack_kernel, pieces, len(mask)),
            in_specs=[pl.BlockSpec(memory_space=pl.ANY) if mask else vmem()] * (2 + len(mask) + len(halos)),
            out_specs=[pl.BlockSpec(memory_space=pl.ANY)] * groups,
            out_shape=[jax.ShapeDtypeStruct(shape, jnp.float32)] * groups,
            scratch_shapes=[pltpu.VMEM(x.shape, x.dtype) for x in ([along_i, along_j, *mask] if mask else [])]
            + [
                pltpu.VMEM((unroll, length + 2 * STEPS, cols), jnp.float32),
                pltpu.VMEM((groups, *shape), jnp.float32),
                pltpu.SemaphoreType.DMA((groups,)),
                pltpu.SemaphoreType.DMA((3, levels // unroll)),
            ],
            compiler_params=params(VMEM_WHOLE if mask else VMEM_LIMIT),
            name="weight_messages",
        )(along_i, along_j, *mask, *halos)
    )


def three(x):
    high = x.astype(jnp.bfloat16)
    rest = x - high.astype(jnp.float32)
    middle = rest.astype(jnp.bfloat16)
    return high, middle, (rest - middle.astype(jnp.float32)).astype(jnp.bfloat16)


def left_terms(x):
    high, middle, low = three(x)
    return jnp.concatenate([high, middle, low, high, middle, high], axis=1)


def right_terms(x, axis):
    high, middle, low = three(x)
    return jnp.concatenate([high, high, high, middle, middle, low], axis=axis)


def adjoint_kernel(matrix, depths, *refs):
    parts, out, terms = refs[:-2], refs[-2], refs[-1]
    length, width, order = out.shape
    groups = len(parts)
    rows = length // groups
    cols = groups * width
    count = order // groups
    level = lax.rem(lax.broadcasted_iota(jnp.int32, (order, cols), 0), order // 2).astype(jnp.float32)

    terms[...] = left_terms(matrix[...])

    def two(pair, carry):
        planes = [2 * pair, 2 * pair + 1]
        x = jnp.concatenate(
            [jnp.concatenate([part[pl.ds(i, count, rows), :] for part in parts], axis=0) for i in planes], axis=1
        )
        y = jnp.dot(terms[...], right_terms(x, 0), preferred_element_type=jnp.float32)
        for k, i in enumerate(planes):
            z = jnp.where(level < depths[pl.ds(i, 1), :], y[:, k * cols:(k + 1) * cols], 0.0).T
            for a in range(groups):
                out[a * rows + i] = z[a * width:(a + 1) * width]
        return carry

    lax.fori_loop(0, rows // 2, two, 0, unroll=rows // 2)


def adjoint_mix(matrix, depths, parts, length, width):
    return pl.pallas_call(
        adjoint_kernel,
        in_specs=[vmem()] * (2 + len(parts)),
        out_specs=vmem(),
        out_shape=jax.ShapeDtypeStruct((length, width, matrix.shape[0]), jnp.float32),
        scratch_shapes=[pltpu.VMEM((matrix.shape[0], 6 * matrix.shape[0]), jnp.bfloat16)],
        compiler_params=params(),
        name="adjoint_mix",
    )(matrix, depths, *parts)


def unfold(main, halo, groups):
    cols = main.shape[1]
    width = cols // groups
    below = halo[:STEPS]
    above = pltpu.roll(halo[STEPS:], width, 1)
    return jnp.concatenate(
        [above] + [main] + [pltpu.roll(main, cols - a * width, 1) for a in range(1, groups)] + [below], axis=0
    )


def turn_kernel(pieces, *refs):
    groups = len(pieces[0][0])
    depths, parts, (out, held, depth_i, depth_j) = refs[:-4 - groups], refs[-4 - groups:-4], refs[-4:]
    _, width, order = out.shape
    half = order // 2
    count = half // groups
    cols = width * groups
    source = position()[2]
    planes, base = [], 0
    for starts, rows in pieces:
        planes += [(base + i, rows, i, starts) for i in range(rows)]
        base += 2 * count * rows
    for k, (first, rows, _, _) in enumerate(planes):
        for d, part in enumerate(parts):
            for side in range(2):
                at = pl.multiple_of(side * half + source[d] * count, 8)
                held[k, pl.ds(at, count), :] = part[pl.ds(first + side * count * rows, count, rows), :]

    no_halo = jnp.zeros((2 * STEPS, cols), jnp.float32)
    depth = unfold(depths[0][...], depths[1][...] if len(depths) > 1 else no_halo, groups)
    tall = depth.shape[0]
    lane = lax.broadcasted_iota(jnp.int32, depth.shape, 1)
    right = jnp.where(lane == width - 1, depth, pltpu.roll(depth, cols - 1, 1))
    depth_j[...] = jnp.minimum(depth, right)
    depth_i[pl.ds(0, tall - 1), :] = jnp.minimum(depth[:-1], depth[1:])
    depth_i[pl.ds(tall - 1, 1), :] = depth[tall - 1:]

    def fold(ref, starts, rows):
        group = lane_groups(rows, cols, groups)
        x = ref[pl.ds(starts[0], rows), :]
        for a in range(1, groups):
            x = jnp.where(group == a, pltpu.roll(ref[pl.ds(starts[a], rows), :], a * width, 1), x)
        return x

    folded = [(fold(depth_i, *piece), fold(depth_j, *piece)) for piece in pieces]
    level = lax.broadcasted_iota(jnp.int32, (half, cols), 0).astype(jnp.float32)
    at = 0
    for n, (starts, rows) in enumerate(pieces):
        for i in range(rows):
            k = at // groups + i
            along_i = jnp.where(level < folded[n][0][i:i + 1], held[k, pl.ds(0, half), :], 0.0)
            along_j = jnp.where(level < folded[n][1][i:i + 1], held[k, pl.ds(half, half), :], 0.0)
            turned = jnp.concatenate([along_i, along_j], axis=0).T
            for a in range(groups):
                out[at + a * rows + i] = turned[a * width:(a + 1) * width]
        at += groups * rows


def turn_weights(pieces, depths, parts, order):
    groups = len(parts)
    cols = parts[0].shape[1]
    rows = sum(n for _, n in pieces)
    tall = depths[0].shape[0] * groups + 2 * STEPS
    return pl.pallas_call(
        functools.partial(turn_kernel, pieces),
        in_specs=[vmem()] * (len(depths) + groups),
        out_specs=vmem(),
        out_shape=jax.ShapeDtypeStruct((rows * groups, cols // groups, order), jnp.float32),
        scratch_shapes=[pltpu.VMEM((rows, order, cols), jnp.float32)] + [pltpu.VMEM((tall, cols), jnp.float32)] * 2,
        compiler_params=params(),
        name="turn_weights",
    )(*depths, *parts)


def edge_masks(depths, order):
    groups = lax.axis_size("lev")
    slot = position()[0][0]
    gy = lax.axis_index("gy")
    start = (slot == 0) & (gy == 0)
    end = (slot == groups - 1) & (gy == lax.axis_size("gy") - 1)
    no_halo = jnp.zeros((2 * STEPS, depths[0].shape[1]), jnp.float32)
    masks = []
    for k, out in enumerate((start, end)):
        x = unfold(depths[k][...], depths[2 + k][...] if len(depths) > 2 else no_halo, groups)
        x = jnp.where(out, 0.0, x)
        x = jnp.broadcast_to(x[:, :1], (x.shape[0], order))
        lane = lax.broadcasted_iota(jnp.int32, x.shape, 1)
        level = lax.rem(lane, order // 2).astype(jnp.float32)
        masks.append(jnp.where((lane < order // 2) | (level < x), 1.0, 0.0))
    return masks


def spread_kernel(windows, field_rows, weight_rows, count, matrix, *refs):
    depths, refs = refs[:count], refs[count:]
    pieces = [refs[3 * k:3 * k + 3] for k in range(len(field_rows) + len(weight_rows))]
    outs, (a, b, wi, wj, masks, terms) = refs[3 * len(pieces):-6], refs[-6:]
    width, order = pieces[0][0].shape[1:]
    half = order // 2
    _, ext, wide, _ = a.shape
    lane = lax.broadcasted_iota(jnp.int32, (wide, order), 1)
    last = lax.broadcasted_iota(jnp.int32, (PAD, order), 0) == PAD - 1
    nothing = jnp.zeros((PAD - STEPS, order), jnp.float32)
    masks[0], masks[1] = edge_masks(depths, order)

    def row_of(some, rows, r):
        piece = [k for k in range(len(rows)) if r in rows[k]][0]
        main, left, right = some[piece]
        k = rows[piece].index(r)
        side = pl.ds(k * STEPS, STEPS)
        return [jnp.concatenate([nothing, left[side, :]], axis=0), main[k], jnp.concatenate([right[side, :], nothing], axis=0)]

    for n, window in enumerate(windows):
        for e, r in enumerate(window):
            a[n, e] = jnp.concatenate(row_of(pieces[:len(field_rows)], field_rows, r), axis=0)
            left, mid, right = row_of(pieces[len(field_rows):], weight_rows, r)
            at = pl.ds(STEPS + r, 1)
            left = jnp.where(last, left * masks[0, at, :], left)
            end = mid[width - PAD:]
            end = jnp.where(last, end * masks[1, at, :], end)
            w = jnp.concatenate([left, mid[:width - PAD], end, right], axis=0)
            other = pltpu.roll(w, half, 1)
            wi[n, e] = jnp.where(lane < half, w, other)
            wj[n, e] = jnp.where(lane < half, other, w)

    src, dst = a, b
    for step in range(STEPS):
        begin, stop = step + 1, ext - 1 - step
        for n in range(len(windows)):

            def one(r, carry, n=n, src=src, dst=dst):
                v, before = carry
                after = src[n, r + 1]
                flux = wi[n, r] * (after - v)
                across = wj[n, r] * (pltpu.roll(v, wide - 1, 0) - v)
                dst[n, r] = v + (flux - before) + (across - pltpu.roll(across, 1, 0))
                return after, flux

            v = src[n, begin]
            carry = v, wi[n, begin - 1] * (v - src[n, begin - 1])
            whole = (stop - begin) // 4 * 4
            carry = lax.fori_loop(begin, begin + whole, one, carry, unroll=4)
            for r in range(begin + whole, stop):
                carry = one(r, carry)
        src, dst = dst, src

    groups = len(outs)
    count = order // groups
    rows = len(windows) * (ext - 2 * STEPS) // groups
    each = groups // len(windows)

    terms[...] = left_terms(matrix[...])

    def mix(pair, carry):
        planes = [2 * pair, 2 * pair + 1]
        x = jnp.concatenate(
            [src[g // each, STEPS + g % each * rows + i, pl.ds(PAD, width), :] for i in planes for g in range(groups)],
            axis=0,
        )
        y = lax.dot_general(
            terms[...], right_terms(x, 1), (((1,), (1,)), ((), ())), preferred_element_type=jnp.float32
        )
        cols = groups * width
        for k, i in enumerate(planes):
            for d, out in enumerate(outs):
                out[pl.ds(i, count, rows), :] = y[d * count:(d + 1) * count, k * cols:(k + 1) * cols]
        return carry

    lax.fori_loop(0, rows // 2, mix, 0, unroll=rows // 2)


def spread_mix(windows, matrix, depths, field, weights, groups):
    width, order = field[0][1].shape[1:]
    cols = width * groups
    ext = len(windows[0])
    rows = len(windows) * (ext - 2 * STEPS) // groups
    shape = jax.ShapeDtypeStruct((order // groups * rows, cols), jnp.float32)
    arrays = list(depths) + [x for piece in field + weights for x in piece[1:]]
    kernel = functools.partial(
        spread_kernel, windows, [piece[0] for piece in field], [piece[0] for piece in weights], len(depths)
    )
    tall = field[0][1].shape[0] + 2 * STEPS
    return pl.pallas_call(
        kernel,
        in_specs=[vmem()] * (1 + len(arrays)),
        out_specs=[vmem()] * groups,
        out_shape=[shape] * groups,
        scratch_shapes=[pltpu.VMEM((len(windows), ext, width + 2 * PAD, order), jnp.float32)] * 4
        + [pltpu.VMEM((2, tall, order), jnp.float32), pltpu.VMEM((order, 6 * order), jnp.bfloat16)],
        compiler_params=params(),
        name="spread_mix",
    )(matrix, *arrays)


RESULT_STEPS = 4


def result_kernel(runs, gain, mask, *refs):
    parts, (out, done, out_sems) = refs[:-3], refs[-3:]
    fields, levels, _, cols = gain.shape
    groups = len(parts)
    rows = done.shape[2] // groups
    some = levels // RESULT_STEPS
    slots = position()[1]
    group = lane_groups(rows, cols, groups)

    def of_slot(slot, at):
        x = parts[0][pl.ds(at, rows), :]
        for d in range(1, groups):
            x = jnp.where(slots[d] == slot, parts[d][pl.ds(at, rows), :], x)
        return x

    stored = []
    for step in range(RESULT_STEPS):
        for level in range(step * some, (step + 1) * some):
            ocean = jnp.concatenate([mask[level, pl.ds(*run), :] for run in runs], axis=0).astype(jnp.float32)
            for field in range(fields):
                at = (field * levels + level) * rows
                blocks = swap([of_slot(slot, at) for slot in range(groups)], group, cols // groups)
                gains = jnp.concatenate([gain[field, level, pl.ds(*run), :] for run in runs], axis=0)
                done[field, level] = ocean * gains * jnp.concatenate(blocks, axis=0)
        these = pl.ds(step * some, some)
        pairs, at = [], 0
        for first, number in runs:
            pairs.append((done.at[:, these, pl.ds(at, number)], out.at[:, these, pl.ds(first, number)]))
            at += number
        stored += copies(pairs, out_sems.at[step])
    for copy in stored:
        copy.wait()


def result(runs, gain, mask, parts, before):
    fields, levels, _, cols = gain.shape
    groups = len(parts)
    rows = sum(number for _, number in runs)
    anywhere = pl.BlockSpec(memory_space=pl.ANY)
    more = [] if before is None else [before]

    def kernel(gain, mask, *refs):
        result_kernel(runs, gain, mask, *refs[:groups], *refs[groups + len(more):])

    return pl.pallas_call(
        kernel,
        in_specs=[vmem()] * (2 + groups) + [anywhere] * len(more),
        out_specs=anywhere,
        out_shape=jax.ShapeDtypeStruct(gain.shape, jnp.float32),
        scratch_shapes=[
            pltpu.VMEM((fields, levels, rows, cols), jnp.float32),
            pltpu.SemaphoreType.DMA((RESULT_STEPS, len(runs))),
        ],
        input_output_aliases={2 + groups: 0} if more else {},
        compiler_params=params(),
        name="result",
    )(gain, mask, *parts, *more)


def shards(increment, norm_gain, diffusion_i, diffusion_j, sea_mask, coupling):
    devices = lax.axis_size("lev")
    gx_size = lax.axis_size("gx")
    gy_size = lax.axis_size("gy")
    _, levels, length, cols = increment.shape
    width = cols // devices
    rows = length // devices
    order = coupling.shape[0]
    to = [lax.rem(lax.axis_index("lev") + d, devices) for d in distances(devices)]
    source = [lax.rem(lax.axis_index("lev") + devices - d, devices) for d in distances(devices)]

    def shift(x, d):
        return lax.ppermute(x, "lev", [(k, (k + d) % devices) for k in range(devices)])

    def exchange(parts):
        return [parts[0]] + [shift(x, d) for x, d in zip(parts[1:], distances(devices)[1:])]

    up = [((k + 1) % gx_size, k) for k in range(gx_size)]
    down = [(b, a) for a, b in up]
    ring = [(devices - 1 - slot if y % 2 else slot) * gy_size + y for y in range(gy_size) for slot in range(devices)]
    ahead = list(zip(ring, ring[1:] + ring[:1]))
    back = [(b, a) for a, b in ahead]

    def halo_i(first, last):
        if gx_size == 2:
            size = first.shape[0]
            both = lax.ppermute(jnp.concatenate([first, last], axis=0), "gx", up)
            return both[size:], both[:size]
        return lax.ppermute(last, "gx", down), lax.ppermute(first, "gx", up)

    def halo_j(first, last):
        return lax.ppermute(last, ("lev", "gy"), ahead), lax.ppermute(first, ("lev", "gy"), back)

    def flat(x):
        return x.reshape(-1, x.shape[-1])

    def cut(x, *sizes):
        return lax.split(x, sizes, 0)

    quarter = length // 4
    some = 2 * quarter // devices
    half = devices // 2
    inner = (quarter, 2 * quarter)
    outer = ((0, quarter), (3 * quarter, quarter))
    inner_pieces = [
        ([STEPS + quarter + a * some for a in range(devices)], some),
        ([quarter + 2 * a for a in range(half)] + [STEPS + 3 * quarter + 2 * a for a in range(half)], 2),
    ]
    outer_pieces = [([a * some for a in range(half)] + [3 * quarter + 2 * STEPS + a * some for a in range(half)], some)]

    def rows_of(pieces):
        return [start - STEPS + i for starts, number in pieces for start in starts for i in range(number)]

    inner_rows, outer_rows = rows_of(inner_pieces), rows_of(outer_pieces)
    windows = [list(range(-STEPS, quarter + STEPS)), list(range(3 * quarter - STEPS, length + STEPS))]

    inner_size = len(inner_rows) // devices
    inner_messages = weight_messages(inner_pieces, diffusion_i, diffusion_j, [sea_mask])
    inner_parts = exchange(inner_messages)
    inner_messages, edge_i, edge_j, increment, norm_gain = lax.optimization_barrier(
        (inner_messages, diffusion_i, diffusion_j, increment, norm_gain)
    )
    halos = halo_i(
        *[
            jnp.concatenate([flat(edge_i[:, at]), flat(edge_j[:, at])], axis=0)
            for at in (slice(0, STEPS), slice(-STEPS, None))
        ]
    )
    messages = scaled_messages(increment, norm_gain, sea_mask, devices)
    scaled = exchange(messages)
    messages, halos = lax.optimization_barrier((messages, halos))
    outer_messages = weight_messages(outer_pieces, diffusion_i, diffusion_j, halos=halos)

    depth = sum(part[2 * levels * inner_size:] for part in inner_parts)
    here = turn_weights(inner_pieces, [depth], inner_parts, order)
    left, right = halo_j(
        jnp.concatenate([flat(here[:, :STEPS]), depth], axis=0),
        flat(here[:, -STEPS:]),
    )
    right, right_depth = cut(right, len(inner_rows) * STEPS, rows)

    balance = jnp.eye(order, dtype=jnp.float32) + coupling
    by_device = balance.reshape(2, devices, levels, order)
    adjoint = jnp.concatenate([by_device[:, s].reshape(2 * levels, order) for s in source], axis=0).T
    forward = jnp.concatenate([by_device[:, t].reshape(2 * levels, order) for t in to], axis=0)

    middle = devices // 2
    scaled, outer_messages = lax.optimization_barrier((scaled, outer_messages))
    early = shift(outer_messages[middle], middle)
    mixed = adjoint_mix(adjoint, depth, scaled, length, width)
    edges = flat(mixed[:, :STEPS]), flat(mixed[:, -STEPS:])
    edges, inner_weights = lax.optimization_barrier((edges, (here, left, right)))
    left, right = halo_j(*edges)
    left, right, outer_messages, early = lax.optimization_barrier((left, right, outer_messages, early))
    outer_parts = [
        early if d == middle else shift(outer_messages[d], d) if d else outer_messages[0] for d in range(devices)
    ]
    field = [(list(range(length)), mixed, left, right)]
    weights = [(inner_rows, *inner_weights)]
    depths = [depth, right_depth]
    inner_mixed = spread_mix([sorted(inner_rows)], forward, depths, field, weights, devices)
    _, upper, lower = lax.optimization_barrier((left, mixed[:STEPS], mixed[-STEPS:]))
    _, outer_parts = lax.optimization_barrier((inner_mixed[0], outer_parts))
    inner_mixed = exchange(inner_mixed)

    above, below = halo_i(
        jnp.concatenate([flat(upper), depth[:STEPS]], axis=0),
        jnp.concatenate([flat(lower), depth[-STEPS:]], axis=0),
    )
    above, above_depth = cut(above, STEPS * width, STEPS)
    below, below_depth = cut(below, STEPS * width, STEPS)
    halo_depth = jnp.concatenate([below_depth, above_depth], axis=0)
    halo = jnp.concatenate([above, below], axis=0).reshape(2 * STEPS, width, order)
    here = turn_weights(outer_pieces, [depth, halo_depth], outer_parts, order)
    left, right = halo_j(
        jnp.concatenate([flat(here[:, :STEPS]), flat(halo[:, :STEPS]), halo_depth], axis=0),
        jnp.concatenate([flat(here[:, -STEPS:]), flat(halo[:, -STEPS:])], axis=0),
    )
    light = [d for d in range(1, devices) if d != middle]
    left, right, moved = lax.optimization_barrier((left, right, [inner_mixed[d] for d in light]))
    for d, x in zip(light, moved):
        inner_mixed[d] = x
    out = result((inner,), norm_gain, sea_mask, inner_mixed, None)
    sizes = len(outer_rows) * STEPS, 2 * STEPS * STEPS
    left, halo_left = cut(left, *sizes)
    right, halo_right, right_halo_depth = cut(right, *sizes, 2 * STEPS)
    weights.append((outer_rows, here, left, right))
    field.append((list(range(-STEPS, 0)) + list(range(length, length + STEPS)), halo, halo_left, halo_right))
    depths += [halo_depth, right_halo_depth]
    outer_mixed = exchange(spread_mix(windows, forward, depths, field, weights, devices))
    return result(outer, norm_gain, sea_mask, outer_mixed, out)


def solution(mesh):
    return jax.shard_map(
        shards,
        mesh=mesh,
        in_specs=(
            P(None, "lev", "gx", "gy"),
            P(None, "lev", "gx", "gy"),
            P("lev", "gx", "gy"),
            P("lev", "gx", "gy"),
            P("lev", "gx", "gy"),
            P(),
        ),
        out_specs=P(None, "lev", "gx", "gy"),
        check_vma=False,
    )
```

```python
import functools

import jax
import jax.numpy as jnp
from jax import lax
from jax.experimental import pallas as pl
from jax.experimental.pallas import tpu as pltpu
from jax.sharding import PartitionSpec as P

ITERS = 2
STEPS = 2 * ITERS
PAD = 8
VMEM_LIMIT = 40 * 1024 * 1024
VMEM_WHOLE = 60 * 1024 * 1024
HIGHEST = lax.Precision.HIGHEST


def params(limit=VMEM_LIMIT):
    return pltpu.CompilerParams(vmem_limit_bytes=limit)


def smem():
    return pl.BlockSpec(memory_space=pltpu.SMEM)


def vmem():
    return pl.BlockSpec(memory_space=pltpu.VMEM)


def distances(devices):
    return list(range(devices))


def position():
    devices = lax.axis_size("lev")
    me = lax.axis_index("lev")
    flipped = lax.rem(lax.axis_index("gy"), 2) == 1

    def slot(lev):
        return jnp.where(flipped, devices - 1 - lev, lev)

    to = [lax.rem(me + d, devices) for d in distances(devices)]
    source = [lax.rem(me + devices - d, devices) for d in distances(devices)]
    return [slot(lev) for lev in to], [slot(lev) for lev in source], source


def swap(blocks, group, width, axis=1):
    blocks = list(blocks)
    cols = blocks[0].shape[axis]
    bit = len(blocks) // 2
    while bit:
        shift = bit * width
        low = (group & bit) == 0
        for a in range(len(blocks)):
            if not a & bit:
                x, y = blocks[a], blocks[a + bit]
                blocks[a] = jnp.where(low, x, pltpu.roll(y, shift, axis))
                blocks[a + bit] = jnp.where(low, pltpu.roll(x, cols - shift, axis), y)
        bit //= 2
    return blocks


def lane_groups(rows, cols, groups):
    return lax.broadcasted_iota(jnp.int32, (rows, cols), 1) // (cols // groups)


def copies(pairs, sems):
    made = [pltpu.make_async_copy(src, dst, sems.at[k]) for k, (src, dst) in enumerate(pairs)]
    for copy in made:
        copy.start()
    return made


SCALED_STEPS = 4


def scaled_kernel(increment, gain, mask, *refs):
    outs, (inc, gn, sea, held, sems, out_sems) = refs[:-6], refs[-6:]
    fields, levels, length, cols = increment.shape
    groups = len(outs)
    rows = length // groups
    some = levels // SCALED_STEPS
    group = lane_groups(rows, cols, groups)
    fetched = []
    for step in range(SCALED_STEPS):
        part = pl.ds(step * some, some)
        fetched.append(
            copies(
                [
                    (increment.at[:, part], inc.at[:, part]),
                    (gain.at[:, part], gn.at[:, part]),
                    (mask.at[part], sea.at[part]),
                ],
                sems.at[step],
            )
        )

    for step in range(SCALED_STEPS):
        for copy in fetched[step]:
            copy.wait()

        def one(level, carry):
            ocean = sea[level].astype(jnp.float32)
            for field in range(fields):
                at = pl.multiple_of((field * levels + level) * rows, rows)
                x = ocean * gn[field, level] * inc[field, level]
                blocks = swap([x[a * rows:(a + 1) * rows] for a in range(groups)], group, cols // groups)
                for slot, block in enumerate(blocks):
                    held[slot, pl.ds(at, rows), :] = block
            return carry

        lax.fori_loop(step * some, (step + 1) * some, one, 0, unroll=True)
    slots = position()[0]
    for copy in copies([(held.at[slots[d]], out) for d, out in enumerate(outs)], out_sems):
        copy.wait()


def scaled_messages(increment, gain, mask, groups):
    fields, levels, length, cols = increment.shape
    shape = (fields * levels * length // groups, cols)
    return pl.pallas_call(
        scaled_kernel,
        in_specs=[pl.BlockSpec(memory_space=pl.ANY)] * 3,
        out_specs=[pl.BlockSpec(memory_space=pl.ANY)] * groups,
        out_shape=[jax.ShapeDtypeStruct(shape, jnp.float32)] * groups,
        scratch_shapes=[
            pltpu.VMEM(increment.shape, jnp.float32),
            pltpu.VMEM(gain.shape, jnp.float32),
            pltpu.VMEM(mask.shape, mask.dtype),
            pltpu.VMEM((groups, *shape), jnp.float32),
            pltpu.SemaphoreType.DMA((SCALED_STEPS, 3)),
            pltpu.SemaphoreType.DMA((groups,)),
        ],
        compiler_params=params(VMEM_WHOLE),
        name="scaled_messages",
    )(increment, gain, mask)


def pack_kernel(pieces, masked, along_i, along_j, *refs):
    levels, length, cols = along_i.shape
    groups = len(pieces[0][0])
    width = cols // groups
    halos, outs = refs[masked:-4 - groups - 3 * masked], refs[-4 - groups - 3 * masked:-4 - 3 * masked]
    held, slots_held, sems, fetch_sems = refs[-4:]
    unroll = held.shape[0]
    number = levels // unroll
    starts, rows = pieces[0]
    group = lane_groups(rows, cols, groups)
    if masked:
        sources, (along_i, along_j, sea) = (along_i, along_j, refs[0]), refs[-7:-4]
        fetched = []
        for side, (source, target) in enumerate(zip(sources, (along_i, along_j, sea))):
            pairs = [(source.at[pl.ds(k * unroll, unroll)], target.at[pl.ds(k * unroll, unroll)]) for k in range(number)]
            fetched.append(copies(pairs, fetch_sems.at[side]))

    def put(at, blocks):
        for slot, block in enumerate(blocks):
            slots_held[slot, pl.ds(at, block.shape[0]), :] = block

    for side, weight in enumerate((along_i, along_j)):
        for outer in range(number):
            if masked:
                fetched[side][outer].wait()
            edges = []
            for k in range(unroll):
                level = outer * unroll + k
                index = side * levels + level
                if halos:
                    for halo, at in zip(halos, (0, STEPS + length)):
                        held[k, pl.ds(at, STEPS), :] = halo[pl.ds(index * STEPS, STEPS), :]
                    held[k, pl.ds(STEPS, length), :] = weight[level]
                    blocks = [held[k, pl.ds(start, rows), :] for start in starts]
                else:
                    blocks = [weight[level, pl.ds(start - STEPS, rows), :] for start in starts]
                put(index * rows, swap(blocks, group, width))
                if len(pieces) > 1:
                    small = pieces[1][0]
                    low, high = small[0] - 2 * STEPS, small[groups // 2] - STEPS
                    row = lax.broadcasted_iota(jnp.int32, (2 * STEPS, cols), 0)
                    upper = pltpu.roll(weight[level, pl.ds(low, 2 * STEPS), :], STEPS, 0)
                    lower = pltpu.roll(weight[level, pl.ds(high, 2 * STEPS), :], STEPS, 0)
                    edges.append(jnp.where(row < STEPS, upper, lower))
            if edges:
                each = pieces[1][1]
                pairs = lax.broadcasted_iota(jnp.int32, edges[0].shape, 0) // each
                edges = swap(edges, pairs, each, 0)
                at = 2 * levels * rows + (side * levels + outer * unroll) * each
                put(at, swap(edges, lane_groups(unroll * each, cols, groups), width))
    if masked:
        depth = jnp.zeros((length, cols), sea.dtype)
        for outer in range(number):
            fetched[2][outer].wait()
            for level in range(outer * unroll, (outer + 1) * unroll):
                depth = depth + sea[level]
        depth = depth.astype(jnp.float32)
        size = length // groups
        blocks = [depth[a * size:(a + 1) * size] for a in range(groups)]
        put(2 * levels * sum(n for _, n in pieces), swap(blocks, lane_groups(size, cols, groups), width))
    slots = position()[0]
    for copy in copies([(slots_held.at[slots[d]], out) for d, out in enumerate(outs)], sems):
        copy.wait()


def weight_messages(pieces, along_i, along_j, mask=(), halos=()):
    levels, length, cols = along_i.shape
    groups = len(pieces[0][0])
    shape = (2 * levels * sum(rows for _, rows in pieces) + len(mask) * length // groups, cols)
    unroll = 4
    return list(
        pl.pallas_call(
            functools.partial(pack_kernel, pieces, len(mask)),
            in_specs=[pl.BlockSpec(memory_space=pl.ANY) if mask else vmem()] * (2 + len(mask) + len(halos)),
            out_specs=[pl.BlockSpec(memory_space=pl.ANY)] * groups,
            out_shape=[jax.ShapeDtypeStruct(shape, jnp.float32)] * groups,
            scratch_shapes=[pltpu.VMEM(x.shape, x.dtype) for x in ([along_i, along_j, *mask] if mask else [])]
            + [
                pltpu.VMEM((unroll, length + 2 * STEPS, cols), jnp.float32),
                pltpu.VMEM((groups, *shape), jnp.float32),
                pltpu.SemaphoreType.DMA((groups,)),
                pltpu.SemaphoreType.DMA((3, levels // unroll)),
            ],
            compiler_params=params(VMEM_WHOLE if mask else VMEM_LIMIT),
            name="weight_messages",
        )(along_i, along_j, *mask, *halos)
    )


def three(x):
    high = x.astype(jnp.bfloat16)
    rest = x - high.astype(jnp.float32)
    middle = rest.astype(jnp.bfloat16)
    return high, middle, (rest - middle.astype(jnp.float32)).astype(jnp.bfloat16)


def left_terms(x):
    high, middle, low = three(x)
    return jnp.concatenate([high, middle, low, high, middle, high], axis=1)


def right_terms(x, axis):
    high, middle, low = three(x)
    return jnp.concatenate([high, high, high, middle, middle, low], axis=axis)


def adjoint_kernel(matrix, depths, *refs):
    parts, out, terms = refs[:-2], refs[-2], refs[-1]
    length, width, order = out.shape
    groups = len(parts)
    rows = length // groups
    cols = groups * width
    count = order // groups
    level = lax.rem(lax.broadcasted_iota(jnp.int32, (order, cols), 0), order // 2).astype(jnp.float32)

    terms[...] = left_terms(matrix[...])

    def two(pair, carry):
        planes = [2 * pair, 2 * pair + 1]
        x = jnp.concatenate(
            [jnp.concatenate([part[pl.ds(i, count, rows), :] for part in parts], axis=0) for i in planes], axis=1
        )
        y = jnp.dot(terms[...], right_terms(x, 0), preferred_element_type=jnp.float32)
        for k, i in enumerate(planes):
            z = jnp.where(level < depths[pl.ds(i, 1), :], y[:, k * cols:(k + 1) * cols], 0.0).T
            for a in range(groups):
                out[a * rows + i] = z[a * width:(a + 1) * width]
        return carry

    lax.fori_loop(0, rows // 2, two, 0, unroll=rows // 2)


def adjoint_mix(matrix, depths, parts, length, width):
    return pl.pallas_call(
        adjoint_kernel,
        in_specs=[vmem()] * (2 + len(parts)),
        out_specs=vmem(),
        out_shape=jax.ShapeDtypeStruct((length, width, matrix.shape[0]), jnp.float32),
        scratch_shapes=[pltpu.VMEM((matrix.shape[0], 6 * matrix.shape[0]), jnp.bfloat16)],
        compiler_params=params(),
        name="adjoint_mix",
    )(matrix, depths, *parts)


def unfold(main, halo, groups):
    cols = main.shape[1]
    width = cols // groups
    below = halo[:STEPS]
    above = pltpu.roll(halo[STEPS:], width, 1)
    return jnp.concatenate(
        [above] + [main] + [pltpu.roll(main, cols - a * width, 1) for a in range(1, groups)] + [below], axis=0
    )


def turn_kernel(pieces, *refs):
    groups = len(pieces[0][0])
    depths, parts, (out, held, depth_i, depth_j) = refs[:-4 - groups], refs[-4 - groups:-4], refs[-4:]
    _, width, order = out.shape
    half = order // 2
    count = half // groups
    cols = width * groups
    source = position()[2]
    planes, base = [], 0
    for starts, rows in pieces:
        planes += [(base + i, rows, i, starts) for i in range(rows)]
        base += 2 * count * rows
    for k, (first, rows, _, _) in enumerate(planes):
        for d, part in enumerate(parts):
            for side in range(2):
                at = pl.multiple_of(side * half + source[d] * count, 8)
                held[k, pl.ds(at, count), :] = part[pl.ds(first + side * count * rows, count, rows), :]

    no_halo = jnp.zeros((2 * STEPS, cols), jnp.float32)
    depth = unfold(depths[0][...], depths[1][...] if len(depths) > 1 else no_halo, groups)
    tall = depth.shape[0]
    lane = lax.broadcasted_iota(jnp.int32, depth.shape, 1)
    right = jnp.where(lane == width - 1, depth, pltpu.roll(depth, cols - 1, 1))
    depth_j[...] = jnp.minimum(depth, right)
    depth_i[pl.ds(0, tall - 1), :] = jnp.minimum(depth[:-1], depth[1:])
    depth_i[pl.ds(tall - 1, 1), :] = depth[tall - 1:]

    def fold(ref, starts, rows):
        group = lane_groups(rows, cols, groups)
        x = ref[pl.ds(starts[0], rows), :]
        for a in range(1, groups):
            x = jnp.where(group == a, pltpu.roll(ref[pl.ds(starts[a], rows), :], a * width, 1), x)
        return x

    folded = [(fold(depth_i, *piece), fold(depth_j, *piece)) for piece in pieces]
    level = lax.broadcasted_iota(jnp.int32, (half, cols), 0).astype(jnp.float32)
    at = 0
    for n, (starts, rows) in enumerate(pieces):
        for i in range(rows):
            k = at // groups + i
            along_i = jnp.where(level < folded[n][0][i:i + 1], held[k, pl.ds(0, half), :], 0.0)
            along_j = jnp.where(level < folded[n][1][i:i + 1], held[k, pl.ds(half, half), :], 0.0)
            turned = jnp.concatenate([along_i, along_j], axis=0).T
            for a in range(groups):
                out[at + a * rows + i] = turned[a * width:(a + 1) * width]
        at += groups * rows


def turn_weights(pieces, depths, parts, order):
    groups = len(parts)
    cols = parts[0].shape[1]
    rows = sum(n for _, n in pieces)
    tall = depths[0].shape[0] * groups + 2 * STEPS
    return pl.pallas_call(
        functools.partial(turn_kernel, pieces),
        in_specs=[vmem()] * (len(depths) + groups),
        out_specs=vmem(),
        out_shape=jax.ShapeDtypeStruct((rows * groups, cols // groups, order), jnp.float32),
        scratch_shapes=[pltpu.VMEM((rows, order, cols), jnp.float32)] + [pltpu.VMEM((tall, cols), jnp.float32)] * 2,
        compiler_params=params(),
        name="turn_weights",
    )(*depths, *parts)


def edge_masks(depths, order):
    groups = lax.axis_size("lev")
    slot = position()[0][0]
    gy = lax.axis_index("gy")
    start = (slot == 0) & (gy == 0)
    end = (slot == groups - 1) & (gy == lax.axis_size("gy") - 1)
    no_halo = jnp.zeros((2 * STEPS, depths[0].shape[1]), jnp.float32)
    masks = []
    for k, out in enumerate((start, end)):
        x = unfold(depths[k][...], depths[2 + k][...] if len(depths) > 2 else no_halo, groups)
        x = jnp.where(out, 0.0, x)
        x = jnp.broadcast_to(x[:, :1], (x.shape[0], order))
        lane = lax.broadcasted_iota(jnp.int32, x.shape, 1)
        level = lax.rem(lane, order // 2).astype(jnp.float32)
        masks.append(jnp.where((lane < order // 2) | (level < x), 1.0, 0.0))
    return masks


def spread_kernel(windows, field_rows, weight_rows, count, matrix, *refs):
    depths, refs = refs[:count], refs[count:]
    pieces = [refs[3 * k:3 * k + 3] for k in range(len(field_rows) + len(weight_rows))]
    outs, (a, b, wi, wj, masks, terms) = refs[3 * len(pieces):-6], refs[-6:]
    width, order = pieces[0][0].shape[1:]
    half = order // 2
    _, ext, wide, _ = a.shape
    lane = lax.broadcasted_iota(jnp.int32, (wide, order), 1)
    last = lax.broadcasted_iota(jnp.int32, (PAD, order), 0) == PAD - 1
    nothing = jnp.zeros((PAD - STEPS, order), jnp.float32)
    masks[0], masks[1] = edge_masks(depths, order)

    def row_of(some, rows, r):
        piece = [k for k in range(len(rows)) if r in rows[k]][0]
        main, left, right = some[piece]
        k = rows[piece].index(r)
        side = pl.ds(k * STEPS, STEPS)
        return [jnp.concatenate([nothing, left[side, :]], axis=0), main[k], jnp.concatenate([right[side, :], nothing], axis=0)]

    for n, window in enumerate(windows):
        for e, r in enumerate(window):
            a[n, e] = jnp.concatenate(row_of(pieces[:len(field_rows)], field_rows, r), axis=0)
            left, mid, right = row_of(pieces[len(field_rows):], weight_rows, r)
            at = pl.ds(STEPS + r, 1)
            left = jnp.where(last, left * masks[0, at, :], left)
            end = mid[width - PAD:]
            end = jnp.where(last, end * masks[1, at, :], end)
            w = jnp.concatenate([left, mid[:width - PAD], end, right], axis=0)
            other = pltpu.roll(w, half, 1)
            wi[n, e] = jnp.where(lane < half, w, other)
            wj[n, e] = jnp.where(lane < half, other, w)

    src, dst = a, b
    for step in range(STEPS):
        begin, stop = step + 1, ext - 1 - step
        for n in range(len(windows)):

            def one(r, carry, n=n, src=src, dst=dst):
                v, before = carry
                after = src[n, r + 1]
                flux = wi[n, r] * (after - v)
                across = wj[n, r] * (pltpu.roll(v, wide - 1, 0) - v)
                dst[n, r] = v + (flux - before) + (across - pltpu.roll(across, 1, 0))
                return after, flux

            v = src[n, begin]
            carry = v, wi[n, begin - 1] * (v - src[n, begin - 1])
            whole = (stop - begin) // 8 * 8
            carry = lax.fori_loop(begin, begin + whole, one, carry, unroll=8)
            for r in range(begin + whole, stop):
                carry = one(r, carry)
        src, dst = dst, src

    groups = len(outs)
    count = order // groups
    rows = len(windows) * (ext - 2 * STEPS) // groups
    each = groups // len(windows)

    terms[...] = left_terms(matrix[...])

    def mix(pair, carry):
        planes = [2 * pair, 2 * pair + 1]
        x = jnp.concatenate(
            [src[g // each, STEPS + g % each * rows + i, pl.ds(PAD, width), :] for i in planes for g in range(groups)],
            axis=0,
        )
        y = lax.dot_general(
            terms[...], right_terms(x, 1), (((1,), (1,)), ((), ())), preferred_element_type=jnp.float32
        )
        cols = groups * width
        for k, i in enumerate(planes):
            for d, out in enumerate(outs):
                out[pl.ds(i, count, rows), :] = y[d * count:(d + 1) * count, k * cols:(k + 1) * cols]
        return carry

    lax.fori_loop(0, rows // 2, mix, 0, unroll=rows // 2)


def spread_mix(windows, matrix, depths, field, weights, groups):
    width, order = field[0][1].shape[1:]
    cols = width * groups
    ext = len(windows[0])
    rows = len(windows) * (ext - 2 * STEPS) // groups
    shape = jax.ShapeDtypeStruct((order // groups * rows, cols), jnp.float32)
    arrays = list(depths) + [x for piece in field + weights for x in piece[1:]]
    kernel = functools.partial(
        spread_kernel, windows, [piece[0] for piece in field], [piece[0] for piece in weights], len(depths)
    )
    tall = field[0][1].shape[0] + 2 * STEPS
    return pl.pallas_call(
        kernel,
        in_specs=[vmem()] * (1 + len(arrays)),
        out_specs=[vmem()] * groups,
        out_shape=[shape] * groups,
        scratch_shapes=[pltpu.VMEM((len(windows), ext, width + 2 * PAD, order), jnp.float32)] * 4
        + [pltpu.VMEM((2, tall, order), jnp.float32), pltpu.VMEM((order, 6 * order), jnp.bfloat16)],
        compiler_params=params(),
        name="spread_mix",
    )(matrix, *arrays)


RESULT_STEPS = 4


def result_kernel(runs, gain, mask, *refs):
    parts, (out, done, out_sems) = refs[:-3], refs[-3:]
    fields, levels, _, cols = gain.shape
    groups = len(parts)
    rows = done.shape[2] // groups
    some = levels // RESULT_STEPS
    slots = position()[1]
    group = lane_groups(rows, cols, groups)

    def of_slot(slot, at):
        x = parts[0][pl.ds(at, rows), :]
        for d in range(1, groups):
            x = jnp.where(slots[d] == slot, parts[d][pl.ds(at, rows), :], x)
        return x

    stored = []
    for step in range(RESULT_STEPS):
        for level in range(step * some, (step + 1) * some):
            ocean = jnp.concatenate([mask[level, pl.ds(*run), :] for run in runs], axis=0).astype(jnp.float32)
            for field in range(fields):
                at = (field * levels + level) * rows
                blocks = swap([of_slot(slot, at) for slot in range(groups)], group, cols // groups)
                gains = jnp.concatenate([gain[field, level, pl.ds(*run), :] for run in runs], axis=0)
                done[field, level] = ocean * gains * jnp.concatenate(blocks, axis=0)
        these = pl.ds(step * some, some)
        pairs, at = [], 0
        for first, number in runs:
            pairs.append((done.at[:, these, pl.ds(at, number)], out.at[:, these, pl.ds(first, number)]))
            at += number
        stored += copies(pairs, out_sems.at[step])
    for copy in stored:
        copy.wait()


def result(runs, gain, mask, parts, before):
    fields, levels, _, cols = gain.shape
    groups = len(parts)
    rows = sum(number for _, number in runs)
    anywhere = pl.BlockSpec(memory_space=pl.ANY)
    more = [] if before is None else [before]

    def kernel(gain, mask, *refs):
        result_kernel(runs, gain, mask, *refs[:groups], *refs[groups + len(more):])

    return pl.pallas_call(
        kernel,
        in_specs=[vmem()] * (2 + groups) + [anywhere] * len(more),
        out_specs=anywhere,
        out_shape=jax.ShapeDtypeStruct(gain.shape, jnp.float32),
        scratch_shapes=[
            pltpu.VMEM((fields, levels, rows, cols), jnp.float32),
            pltpu.SemaphoreType.DMA((RESULT_STEPS, len(runs))),
        ],
        input_output_aliases={2 + groups: 0} if more else {},
        compiler_params=params(),
        name="result",
    )(gain, mask, *parts, *more)


def shards(increment, norm_gain, diffusion_i, diffusion_j, sea_mask, coupling):
    devices = lax.axis_size("lev")
    gx_size = lax.axis_size("gx")
    gy_size = lax.axis_size("gy")
    _, levels, length, cols = increment.shape
    width = cols // devices
    rows = length // devices
    order = coupling.shape[0]
    to = [lax.rem(lax.axis_index("lev") + d, devices) for d in distances(devices)]
    source = [lax.rem(lax.axis_index("lev") + devices - d, devices) for d in distances(devices)]

    def shift(x, d):
        return lax.ppermute(x, "lev", [(k, (k + d) % devices) for k in range(devices)])

    def exchange(parts):
        return [parts[0]] + [shift(x, d) for x, d in zip(parts[1:], distances(devices)[1:])]

    up = [((k + 1) % gx_size, k) for k in range(gx_size)]
    down = [(b, a) for a, b in up]
    ring = [(devices - 1 - slot if y % 2 else slot) * gy_size + y for y in range(gy_size) for slot in range(devices)]
    ahead = list(zip(ring, ring[1:] + ring[:1]))
    back = [(b, a) for a, b in ahead]

    def halo_i(first, last):
        if gx_size == 2:
            size = first.shape[0]
            both = lax.ppermute(jnp.concatenate([first, last], axis=0), "gx", up)
            return both[size:], both[:size]
        return lax.ppermute(last, "gx", down), lax.ppermute(first, "gx", up)

    def halo_j(first, last):
        return lax.ppermute(last, ("lev", "gy"), ahead), lax.ppermute(first, ("lev", "gy"), back)

    def flat(x):
        return x.reshape(-1, x.shape[-1])

    def cut(x, *sizes):
        return lax.split(x, sizes, 0)

    quarter = length // 4
    some = 2 * quarter // devices
    half = devices // 2
    inner = (quarter, 2 * quarter)
    outer = ((0, quarter), (3 * quarter, quarter))
    inner_pieces = [
        ([STEPS + quarter + a * some for a in range(devices)], some),
        ([quarter + 2 * a for a in range(half)] + [STEPS + 3 * quarter + 2 * a for a in range(half)], 2),
    ]
    outer_pieces = [([a * some for a in range(half)] + [3 * quarter + 2 * STEPS + a * some for a in range(half)], some)]

    def rows_of(pieces):
        return [start - STEPS + i for starts, number in pieces for start in starts for i in range(number)]

    inner_rows, outer_rows = rows_of(inner_pieces), rows_of(outer_pieces)
    windows = [list(range(-STEPS, quarter + STEPS)), list(range(3 * quarter - STEPS, length + STEPS))]

    inner_size = len(inner_rows) // devices
    inner_messages = weight_messages(inner_pieces, diffusion_i, diffusion_j, [sea_mask])
    inner_parts = exchange(inner_messages)
    inner_messages, edge_i, edge_j, increment, norm_gain = lax.optimization_barrier(
        (inner_messages, diffusion_i, diffusion_j, increment, norm_gain)
    )
    halos = halo_i(
        *[
            jnp.concatenate([flat(edge_i[:, at]), flat(edge_j[:, at])], axis=0)
            for at in (slice(0, STEPS), slice(-STEPS, None))
        ]
    )
    messages = scaled_messages(increment, norm_gain, sea_mask, devices)
    scaled = exchange(messages)
    messages, halos = lax.optimization_barrier((messages, halos))
    outer_messages = weight_messages(outer_pieces, diffusion_i, diffusion_j, halos=halos)

    depth = sum(part[2 * levels * inner_size:] for part in inner_parts)
    here = turn_weights(inner_pieces, [depth], inner_parts, order)
    left, right = halo_j(
        jnp.concatenate([flat(here[:, :STEPS]), depth], axis=0),
        flat(here[:, -STEPS:]),
    )
    right, right_depth = cut(right, len(inner_rows) * STEPS, rows)

    balance = jnp.eye(order, dtype=jnp.float32) + coupling
    by_device = balance.reshape(2, devices, levels, order)
    adjoint = jnp.concatenate([by_device[:, s].reshape(2 * levels, order) for s in source], axis=0).T
    forward = jnp.concatenate([by_device[:, t].reshape(2 * levels, order) for t in to], axis=0)

    middle = devices // 2
    scaled, outer_messages = lax.optimization_barrier((scaled, outer_messages))
    early = shift(outer_messages[middle], middle)
    mixed = adjoint_mix(adjoint, depth, scaled, length, width)
    edges = flat(mixed[:, :STEPS]), flat(mixed[:, -STEPS:])
    edges, inner_weights = lax.optimization_barrier((edges, (here, left, right)))
    left, right = halo_j(*edges)
    left, right, outer_messages, early = lax.optimization_barrier((left, right, outer_messages, early))
    outer_parts = [
        early if d == middle else shift(outer_messages[d], d) if d else outer_messages[0] for d in range(devices)
    ]
    field = [(list(range(length)), mixed, left, right)]
    weights = [(inner_rows, *inner_weights)]
    depths = [depth, right_depth]
    inner_mixed = spread_mix([sorted(inner_rows)], forward, depths, field, weights, devices)
    _, upper, lower = lax.optimization_barrier((left, mixed[:STEPS], mixed[-STEPS:]))
    _, outer_parts = lax.optimization_barrier((inner_mixed[0], outer_parts))
    inner_mixed = exchange(inner_mixed)

    above, below = halo_i(
        jnp.concatenate([flat(upper), depth[:STEPS]], axis=0),
        jnp.concatenate([flat(lower), depth[-STEPS:]], axis=0),
    )
    above, above_depth = cut(above, STEPS * width, STEPS)
    below, below_depth = cut(below, STEPS * width, STEPS)
    halo_depth = jnp.concatenate([below_depth, above_depth], axis=0)
    halo = jnp.concatenate([above, below], axis=0).reshape(2 * STEPS, width, order)
    here = turn_weights(outer_pieces, [depth, halo_depth], outer_parts, order)
    left, right = halo_j(
        jnp.concatenate([flat(here[:, :STEPS]), flat(halo[:, :STEPS]), halo_depth], axis=0),
        jnp.concatenate([flat(here[:, -STEPS:]), flat(halo[:, -STEPS:])], axis=0),
    )
    light = [d for d in range(1, devices) if d != middle]
    left, right, moved = lax.optimization_barrier((left, right, [inner_mixed[d] for d in light]))
    for d, x in zip(light, moved):
        inner_mixed[d] = x
    out = result((inner,), norm_gain, sea_mask, inner_mixed, None)
    sizes = len(outer_rows) * STEPS, 2 * STEPS * STEPS
    left, halo_left = cut(left, *sizes)
    right, halo_right, right_halo_depth = cut(right, *sizes, 2 * STEPS)
    weights.append((outer_rows, here, left, right))
    field.append((list(range(-STEPS, 0)) + list(range(length, length + STEPS)), halo, halo_left, halo_right))
    depths += [halo_depth, right_halo_depth]
    outer_mixed = exchange(spread_mix(windows, forward, depths, field, weights, devices))
    return result(outer, norm_gain, sea_mask, outer_mixed, out)


def solution(mesh):
    return jax.shard_map(
        shards,
        mesh=mesh,
        in_specs=(
            P(None, "lev", "gx", "gy"),
            P(None, "lev", "gx", "gy"),
            P("lev", "gx", "gy"),
            P("lev", "gx", "gy"),
            P("lev", "gx", "gy"),
            P(),
        ),
        out_specs=P(None, "lev", "gx", "gy"),
        check_vma=False,
    )
```

```python
import functools

import jax
import jax.numpy as jnp
from jax import lax
from jax.experimental import pallas as pl
from jax.experimental.pallas import tpu as pltpu
from jax.sharding import PartitionSpec as P

ITERS = 2
STEPS = 2 * ITERS
PAD = 8
VMEM_LIMIT = 40 * 1024 * 1024
VMEM_WHOLE = 60 * 1024 * 1024
HIGHEST = lax.Precision.HIGHEST


def params(limit=VMEM_LIMIT):
    return pltpu.CompilerParams(vmem_limit_bytes=limit)


def smem():
    return pl.BlockSpec(memory_space=pltpu.SMEM)


def vmem():
    return pl.BlockSpec(memory_space=pltpu.VMEM)


def distances(devices):
    return list(range(devices))


def position():
    devices = lax.axis_size("lev")
    me = lax.axis_index("lev")
    flipped = lax.rem(lax.axis_index("gy"), 2) == 1

    def slot(lev):
        return jnp.where(flipped, devices - 1 - lev, lev)

    to = [lax.rem(me + d, devices) for d in distances(devices)]
    source = [lax.rem(me + devices - d, devices) for d in distances(devices)]
    return [slot(lev) for lev in to], [slot(lev) for lev in source], source


def swap(blocks, group, width, axis=1):
    blocks = list(blocks)
    cols = blocks[0].shape[axis]
    bit = len(blocks) // 2
    while bit:
        shift = bit * width
        low = (group & bit) == 0
        for a in range(len(blocks)):
            if not a & bit:
                x, y = blocks[a], blocks[a + bit]
                blocks[a] = jnp.where(low, x, pltpu.roll(y, shift, axis))
                blocks[a + bit] = jnp.where(low, pltpu.roll(x, cols - shift, axis), y)
        bit //= 2
    return blocks


def lane_groups(rows, cols, groups):
    return lax.broadcasted_iota(jnp.int32, (rows, cols), 1) // (cols // groups)


def copies(pairs, sems):
    made = [pltpu.make_async_copy(src, dst, sems.at[k]) for k, (src, dst) in enumerate(pairs)]
    for copy in made:
        copy.start()
    return made


SCALED_STEPS = 4


def scaled_kernel(increment, gain, mask, *refs):
    outs, (inc, gn, sea, held, sems, out_sems) = refs[:-6], refs[-6:]
    fields, levels, length, cols = increment.shape
    groups = len(outs)
    rows = length // groups
    some = levels // SCALED_STEPS
    group = lane_groups(rows, cols, groups)
    fetched = []
    for step in range(SCALED_STEPS):
        part = pl.ds(step * some, some)
        fetched.append(
            copies(
                [
                    (increment.at[:, part], inc.at[:, part]),
                    (gain.at[:, part], gn.at[:, part]),
                    (mask.at[part], sea.at[part]),
                ],
                sems.at[step],
            )
        )

    for step in range(SCALED_STEPS):
        for copy in fetched[step]:
            copy.wait()

        def one(level, carry):
            ocean = sea[level].astype(jnp.float32)
            for field in range(fields):
                at = pl.multiple_of((field * levels + level) * rows, rows)
                x = ocean * gn[field, level] * inc[field, level]
                blocks = swap([x[a * rows:(a + 1) * rows] for a in range(groups)], group, cols // groups)
                for slot, block in enumerate(blocks):
                    held[slot, pl.ds(at, rows), :] = block
            return carry

        lax.fori_loop(step * some, (step + 1) * some, one, 0, unroll=True)
    slots = position()[0]
    for copy in copies([(held.at[slots[d]], out) for d, out in enumerate(outs)], out_sems):
        copy.wait()


def scaled_messages(increment, gain, mask, groups):
    fields, levels, length, cols = increment.shape
    shape = (fields * levels * length // groups, cols)
    return pl.pallas_call(
        scaled_kernel,
        in_specs=[pl.BlockSpec(memory_space=pl.ANY)] * 3,
        out_specs=[pl.BlockSpec(memory_space=pl.ANY)] * groups,
        out_shape=[jax.ShapeDtypeStruct(shape, jnp.float32)] * groups,
        scratch_shapes=[
            pltpu.VMEM(increment.shape, jnp.float32),
            pltpu.VMEM(gain.shape, jnp.float32),
            pltpu.VMEM(mask.shape, mask.dtype),
            pltpu.VMEM((groups, *shape), jnp.float32),
            pltpu.SemaphoreType.DMA((SCALED_STEPS, 3)),
            pltpu.SemaphoreType.DMA((groups,)),
        ],
        compiler_params=params(VMEM_WHOLE),
        name="scaled_messages",
    )(increment, gain, mask)


def pack_kernel(pieces, masked, along_i, along_j, *refs):
    levels, length, cols = along_i.shape
    groups = len(pieces[0][0])
    width = cols // groups
    halos, outs = refs[masked:-4 - groups - 3 * masked], refs[-4 - groups - 3 * masked:-4 - 3 * masked]
    held, slots_held, sems, fetch_sems = refs[-4:]
    unroll = held.shape[0]
    number = levels // unroll
    starts, rows = pieces[0]
    group = lane_groups(rows, cols, groups)
    if masked:
        sources, (along_i, along_j, sea) = (along_i, along_j, refs[0]), refs[-7:-4]
        fetched = []
        for side, (source, target) in enumerate(zip(sources, (along_i, along_j, sea))):
            pairs = [(source.at[pl.ds(k * unroll, unroll)], target.at[pl.ds(k * unroll, unroll)]) for k in range(number)]
            fetched.append(copies(pairs, fetch_sems.at[side]))

    def put(at, blocks):
        for slot, block in enumerate(blocks):
            slots_held[slot, pl.ds(at, block.shape[0]), :] = block

    for side, weight in enumerate((along_i, along_j)):
        for outer in range(number):
            if masked:
                fetched[side][outer].wait()
            edges = []
            for k in range(unroll):
                level = outer * unroll + k
                index = side * levels + level
                if halos:
                    for halo, at in zip(halos, (0, STEPS + length)):
                        held[k, pl.ds(at, STEPS), :] = halo[pl.ds(index * STEPS, STEPS), :]
                    held[k, pl.ds(STEPS, length), :] = weight[level]
                    blocks = [held[k, pl.ds(start, rows), :] for start in starts]
                else:
                    blocks = [weight[level, pl.ds(start - STEPS, rows), :] for start in starts]
                put(index * rows, swap(blocks, group, width))
                if len(pieces) > 1:
                    small = pieces[1][0]
                    low, high = small[0] - 2 * STEPS, small[groups // 2] - STEPS
                    row = lax.broadcasted_iota(jnp.int32, (2 * STEPS, cols), 0)
                    upper = pltpu.roll(weight[level, pl.ds(low, 2 * STEPS), :], STEPS, 0)
                    lower = pltpu.roll(weight[level, pl.ds(high, 2 * STEPS), :], STEPS, 0)
                    edges.append(jnp.where(row < STEPS, upper, lower))
            if edges:
                each = pieces[1][1]
                pairs = lax.broadcasted_iota(jnp.int32, edges[0].shape, 0) // each
                edges = swap(edges, pairs, each, 0)
                at = 2 * levels * rows + (side * levels + outer * unroll) * each
                put(at, swap(edges, lane_groups(unroll * each, cols, groups), width))
    if masked:
        depth = jnp.zeros((length, cols), sea.dtype)
        for outer in range(number):
            fetched[2][outer].wait()
            for level in range(outer * unroll, (outer + 1) * unroll):
                depth = depth + sea[level]
        depth = depth.astype(jnp.float32)
        size = length // groups
        blocks = [depth[a * size:(a + 1) * size] for a in range(groups)]
        put(2 * levels * sum(n for _, n in pieces), swap(blocks, lane_groups(size, cols, groups), width))
    slots = position()[0]
    for copy in copies([(slots_held.at[slots[d]], out) for d, out in enumerate(outs)], sems):
        copy.wait()


def weight_messages(pieces, along_i, along_j, mask=(), halos=()):
    levels, length, cols = along_i.shape
    groups = len(pieces[0][0])
    shape = (2 * levels * sum(rows for _, rows in pieces) + len(mask) * length // groups, cols)
    unroll = 4
    return list(
        pl.pallas_call(
            functools.partial(pack_kernel, pieces, len(mask)),
            in_specs=[pl.BlockSpec(memory_space=pl.ANY) if mask else vmem()] * (2 + len(mask) + len(halos)),
            out_specs=[pl.BlockSpec(memory_space=pl.ANY)] * groups,
            out_shape=[jax.ShapeDtypeStruct(shape, jnp.float32)] * groups,
            scratch_shapes=[pltpu.VMEM(x.shape, x.dtype) for x in ([along_i, along_j, *mask] if mask else [])]
            + [
                pltpu.VMEM((unroll, length + 2 * STEPS, cols), jnp.float32),
                pltpu.VMEM((groups, *shape), jnp.float32),
                pltpu.SemaphoreType.DMA((groups,)),
                pltpu.SemaphoreType.DMA((3, levels // unroll)),
            ],
            compiler_params=params(VMEM_WHOLE if mask else VMEM_LIMIT),
            name="weight_messages",
        )(along_i, along_j, *mask, *halos)
    )


def three(x):
    high = x.astype(jnp.bfloat16)
    rest = x - high.astype(jnp.float32)
    middle = rest.astype(jnp.bfloat16)
    return high, middle, (rest - middle.astype(jnp.float32)).astype(jnp.bfloat16)


def left_terms(x):
    high, middle, low = three(x)
    return jnp.concatenate([high, middle, low, high, middle, high], axis=1)


def right_terms(x, axis):
    high, middle, low = three(x)
    return jnp.concatenate([high, high, high, middle, middle, low], axis=axis)


def adjoint_kernel(matrix, depths, *refs):
    parts, out, terms = refs[:-2], refs[-2], refs[-1]
    length, width, order = out.shape
    groups = len(parts)
    rows = length // groups
    cols = groups * width
    count = order // groups
    level = lax.rem(lax.broadcasted_iota(jnp.int32, (order, cols), 0), order // 2).astype(jnp.float32)

    terms[...] = left_terms(matrix[...])

    def two(pair, carry):
        planes = [2 * pair, 2 * pair + 1]
        x = jnp.concatenate(
            [jnp.concatenate([part[pl.ds(i, count, rows), :] for part in parts], axis=0) for i in planes], axis=1
        )
        y = jnp.dot(terms[...], right_terms(x, 0), preferred_element_type=jnp.float32)
        for k, i in enumerate(planes):
            z = jnp.where(level < depths[pl.ds(i, 1), :], y[:, k * cols:(k + 1) * cols], 0.0).T
            for a in range(groups):
                out[a * rows + i] = z[a * width:(a + 1) * width]
        return carry

    lax.fori_loop(0, rows // 2, two, 0, unroll=rows // 2)


def adjoint_mix(matrix, depths, parts, length, width):
    return pl.pallas_call(
        adjoint_kernel,
        in_specs=[vmem()] * (2 + len(parts)),
        out_specs=vmem(),
        out_shape=jax.ShapeDtypeStruct((length, width, matrix.shape[0]), jnp.float32),
        scratch_shapes=[pltpu.VMEM((matrix.shape[0], 6 * matrix.shape[0]), jnp.bfloat16)],
        compiler_params=params(),
        name="adjoint_mix",
    )(matrix, depths, *parts)


def unfold(main, halo, groups):
    cols = main.shape[1]
    width = cols // groups
    below = halo[:STEPS]
    above = pltpu.roll(halo[STEPS:], width, 1)
    return jnp.concatenate(
        [above] + [main] + [pltpu.roll(main, cols - a * width, 1) for a in range(1, groups)] + [below], axis=0
    )


def turn_kernel(pieces, *refs):
    groups = len(pieces[0][0])
    depths, parts, (out, held, depth_i, depth_j) = refs[:-4 - groups], refs[-4 - groups:-4], refs[-4:]
    _, width, order = out.shape
    half = order // 2
    count = half // groups
    cols = width * groups
    source = position()[2]
    planes, base = [], 0
    for starts, rows in pieces:
        planes += [(base + i, rows, i, starts) for i in range(rows)]
        base += 2 * count * rows
    for k, (first, rows, _, _) in enumerate(planes):
        for d, part in enumerate(parts):
            for side in range(2):
                at = pl.multiple_of(side * half + source[d] * count, 8)
                held[k, pl.ds(at, count), :] = part[pl.ds(first + side * count * rows, count, rows), :]

    no_halo = jnp.zeros((2 * STEPS, cols), jnp.float32)
    depth = unfold(depths[0][...], depths[1][...] if len(depths) > 1 else no_halo, groups)
    tall = depth.shape[0]
    lane = lax.broadcasted_iota(jnp.int32, depth.shape, 1)
    right = jnp.where(lane == width - 1, depth, pltpu.roll(depth, cols - 1, 1))
    depth_j[...] = jnp.minimum(depth, right)
    depth_i[pl.ds(0, tall - 1), :] = jnp.minimum(depth[:-1], depth[1:])
    depth_i[pl.ds(tall - 1, 1), :] = depth[tall - 1:]

    def fold(ref, starts, rows):
        group = lane_groups(rows, cols, groups)
        x = ref[pl.ds(starts[0], rows), :]
        for a in range(1, groups):
            x = jnp.where(group == a, pltpu.roll(ref[pl.ds(starts[a], rows), :], a * width, 1), x)
        return x

    folded = [(fold(depth_i, *piece), fold(depth_j, *piece)) for piece in pieces]
    level = lax.broadcasted_iota(jnp.int32, (half, cols), 0).astype(jnp.float32)
    at = 0
    for n, (starts, rows) in enumerate(pieces):
        for i in range(rows):
            k = at // groups + i
            along_i = jnp.where(level < folded[n][0][i:i + 1], held[k, pl.ds(0, half), :], 0.0)
            along_j = jnp.where(level < folded[n][1][i:i + 1], held[k, pl.ds(half, half), :], 0.0)
            turned = jnp.concatenate([along_i, along_j], axis=0).T
            for a in range(groups):
                out[at + a * rows + i] = turned[a * width:(a + 1) * width]
        at += groups * rows


def turn_weights(pieces, depths, parts, order):
    groups = len(parts)
    cols = parts[0].shape[1]
    rows = sum(n for _, n in pieces)
    tall = depths[0].shape[0] * groups + 2 * STEPS
    return pl.pallas_call(
        functools.partial(turn_kernel, pieces),
        in_specs=[vmem()] * (len(depths) + groups),
        out_specs=vmem(),
        out_shape=jax.ShapeDtypeStruct((rows * groups, cols // groups, order), jnp.float32),
        scratch_shapes=[pltpu.VMEM((rows, order, cols), jnp.float32)] + [pltpu.VMEM((tall, cols), jnp.float32)] * 2,
        compiler_params=params(),
        name="turn_weights",
    )(*depths, *parts)


def edge_masks(depths, order):
    groups = lax.axis_size("lev")
    slot = position()[0][0]
    gy = lax.axis_index("gy")
    start = (slot == 0) & (gy == 0)
    end = (slot == groups - 1) & (gy == lax.axis_size("gy") - 1)
    no_halo = jnp.zeros((2 * STEPS, depths[0].shape[1]), jnp.float32)
    masks = []
    for k, out in enumerate((start, end)):
        x = unfold(depths[k][...], depths[2 + k][...] if len(depths) > 2 else no_halo, groups)
        x = jnp.where(out, 0.0, x)
        x = jnp.broadcast_to(x[:, :1], (x.shape[0], order))
        lane = lax.broadcasted_iota(jnp.int32, x.shape, 1)
        level = lax.rem(lane, order // 2).astype(jnp.float32)
        masks.append(jnp.where((lane < order // 2) | (level < x), 1.0, 0.0))
    return masks


def spread_kernel(windows, field_rows, weight_rows, count, matrix, *refs):
    depths, refs = refs[:count], refs[count:]
    pieces = [refs[3 * k:3 * k + 3] for k in range(len(field_rows) + len(weight_rows))]
    outs, (a, b, wi, wj, masks, terms) = refs[3 * len(pieces):-6], refs[-6:]
    width, order = pieces[0][0].shape[1:]
    half = order // 2
    _, ext, wide, _ = a.shape
    lane = lax.broadcasted_iota(jnp.int32, (wide, order), 1)
    last = lax.broadcasted_iota(jnp.int32, (PAD, order), 0) == PAD - 1
    nothing = jnp.zeros((PAD - STEPS, order), jnp.float32)
    masks[0], masks[1] = edge_masks(depths, order)

    def row_of(some, rows, r):
        piece = [k for k in range(len(rows)) if r in rows[k]][0]
        main, left, right = some[piece]
        k = rows[piece].index(r)
        side = pl.ds(k * STEPS, STEPS)
        return [jnp.concatenate([nothing, left[side, :]], axis=0), main[k], jnp.concatenate([right[side, :], nothing], axis=0)]

    for n, window in enumerate(windows):
        for e, r in enumerate(window):
            a[n, e] = jnp.concatenate(row_of(pieces[:len(field_rows)], field_rows, r), axis=0)
            left, mid, right = row_of(pieces[len(field_rows):], weight_rows, r)
            at = pl.ds(STEPS + r, 1)
            left = jnp.where(last, left * masks[0, at, :], left)
            end = mid[width - PAD:]
            end = jnp.where(last, end * masks[1, at, :], end)
            w = jnp.concatenate([left, mid[:width - PAD], end, right], axis=0)
            other = pltpu.roll(w, half, 1)
            wi[n, e] = jnp.where(lane < half, w, other)
            wj[n, e] = jnp.where(lane < half, other, w)

    src, dst = a, b
    for step in range(STEPS):
        begin, stop = step + 1, ext - 1 - step
        for n in range(len(windows)):

            def one(r, carry, n=n, src=src, dst=dst):
                v, before = carry
                after = src[n, r + 1]
                flux = wi[n, r] * (after - v)
                across = wj[n, r] * (pltpu.roll(v, wide - 1, 0) - v)
                dst[n, r] = v + (flux - before) + (across - pltpu.roll(across, 1, 0))
                return after, flux

            v = src[n, begin]
            carry = v, wi[n, begin - 1] * (v - src[n, begin - 1])
            whole = (stop - begin) // 12 * 12
            carry = lax.fori_loop(begin, begin + whole, one, carry, unroll=12)
            for r in range(begin + whole, stop):
                carry = one(r, carry)
        src, dst = dst, src

    groups = len(outs)
    count = order // groups
    rows = len(windows) * (ext - 2 * STEPS) // groups
    each = groups // len(windows)

    terms[...] = left_terms(matrix[...])

    def mix(pair, carry):
        planes = [2 * pair, 2 * pair + 1]
        x = jnp.concatenate(
            [src[g // each, STEPS + g % each * rows + i, pl.ds(PAD, width), :] for i in planes for g in range(groups)],
            axis=0,
        )
        y = lax.dot_general(
            terms[...], right_terms(x, 1), (((1,), (1,)), ((), ())), preferred_element_type=jnp.float32
        )
        cols = groups * width
        for k, i in enumerate(planes):
            for d, out in enumerate(outs):
                out[pl.ds(i, count, rows), :] = y[d * count:(d + 1) * count, k * cols:(k + 1) * cols]
        return carry

    lax.fori_loop(0, rows // 2, mix, 0, unroll=rows // 2)


def spread_mix(windows, matrix, depths, field, weights, groups):
    width, order = field[0][1].shape[1:]
    cols = width * groups
    ext = len(windows[0])
    rows = len(windows) * (ext - 2 * STEPS) // groups
    shape = jax.ShapeDtypeStruct((order // groups * rows, cols), jnp.float32)
    arrays = list(depths) + [x for piece in field + weights for x in piece[1:]]
    kernel = functools.partial(
        spread_kernel, windows, [piece[0] for piece in field], [piece[0] for piece in weights], len(depths)
    )
    tall = field[0][1].shape[0] + 2 * STEPS
    return pl.pallas_call(
        kernel,
        in_specs=[vmem()] * (1 + len(arrays)),
        out_specs=[vmem()] * groups,
        out_shape=[shape] * groups,
        scratch_shapes=[pltpu.VMEM((len(windows), ext, width + 2 * PAD, order), jnp.float32)] * 4
        + [pltpu.VMEM((2, tall, order), jnp.float32), pltpu.VMEM((order, 6 * order), jnp.bfloat16)],
        compiler_params=params(),
        name="spread_mix",
    )(matrix, *arrays)


RESULT_STEPS = 4


def result_kernel(runs, gain, mask, *refs):
    parts, (out, done, out_sems) = refs[:-3], refs[-3:]
    fields, levels, _, cols = gain.shape
    groups = len(parts)
    rows = done.shape[2] // groups
    some = levels // RESULT_STEPS
    slots = position()[1]
    group = lane_groups(rows, cols, groups)

    def of_slot(slot, at):
        x = parts[0][pl.ds(at, rows), :]
        for d in range(1, groups):
            x = jnp.where(slots[d] == slot, parts[d][pl.ds(at, rows), :], x)
        return x

    stored = []
    for step in range(RESULT_STEPS):
        for level in range(step * some, (step + 1) * some):
            ocean = jnp.concatenate([mask[level, pl.ds(*run), :] for run in runs], axis=0).astype(jnp.float32)
            for field in range(fields):
                at = (field * levels + level) * rows
                blocks = swap([of_slot(slot, at) for slot in range(groups)], group, cols // groups)
                gains = jnp.concatenate([gain[field, level, pl.ds(*run), :] for run in runs], axis=0)
                done[field, level] = ocean * gains * jnp.concatenate(blocks, axis=0)
        these = pl.ds(step * some, some)
        pairs, at = [], 0
        for first, number in runs:
            pairs.append((done.at[:, these, pl.ds(at, number)], out.at[:, these, pl.ds(first, number)]))
            at += number
        stored += copies(pairs, out_sems.at[step])
    for copy in stored:
        copy.wait()


def result(runs, gain, mask, parts, before):
    fields, levels, _, cols = gain.shape
    groups = len(parts)
    rows = sum(number for _, number in runs)
    anywhere = pl.BlockSpec(memory_space=pl.ANY)
    more = [] if before is None else [before]

    def kernel(gain, mask, *refs):
        result_kernel(runs, gain, mask, *refs[:groups], *refs[groups + len(more):])

    return pl.pallas_call(
        kernel,
        in_specs=[vmem()] * (2 + groups) + [anywhere] * len(more),
        out_specs=anywhere,
        out_shape=jax.ShapeDtypeStruct(gain.shape, jnp.float32),
        scratch_shapes=[
            pltpu.VMEM((fields, levels, rows, cols), jnp.float32),
            pltpu.SemaphoreType.DMA((RESULT_STEPS, len(runs))),
        ],
        input_output_aliases={2 + groups: 0} if more else {},
        compiler_params=params(),
        name="result",
    )(gain, mask, *parts, *more)


def shards(increment, norm_gain, diffusion_i, diffusion_j, sea_mask, coupling):
    devices = lax.axis_size("lev")
    gx_size = lax.axis_size("gx")
    gy_size = lax.axis_size("gy")
    _, levels, length, cols = increment.shape
    width = cols // devices
    rows = length // devices
    order = coupling.shape[0]
    to = [lax.rem(lax.axis_index("lev") + d, devices) for d in distances(devices)]
    source = [lax.rem(lax.axis_index("lev") + devices - d, devices) for d in distances(devices)]

    def shift(x, d):
        return lax.ppermute(x, "lev", [(k, (k + d) % devices) for k in range(devices)])

    def exchange(parts):
        return [parts[0]] + [shift(x, d) for x, d in zip(parts[1:], distances(devices)[1:])]

    up = [((k + 1) % gx_size, k) for k in range(gx_size)]
    down = [(b, a) for a, b in up]
    ring = [(devices - 1 - slot if y % 2 else slot) * gy_size + y for y in range(gy_size) for slot in range(devices)]
    ahead = list(zip(ring, ring[1:] + ring[:1]))
    back = [(b, a) for a, b in ahead]

    def halo_i(first, last):
        if gx_size == 2:
            size = first.shape[0]
            both = lax.ppermute(jnp.concatenate([first, last], axis=0), "gx", up)
            return both[size:], both[:size]
        return lax.ppermute(last, "gx", down), lax.ppermute(first, "gx", up)

    def halo_j(first, last):
        return lax.ppermute(last, ("lev", "gy"), ahead), lax.ppermute(first, ("lev", "gy"), back)

    def flat(x):
        return x.reshape(-1, x.shape[-1])

    def cut(x, *sizes):
        return lax.split(x, sizes, 0)

    quarter = length // 4
    some = 2 * quarter // devices
    half = devices // 2
    inner = (quarter, 2 * quarter)
    outer = ((0, quarter), (3 * quarter, quarter))
    inner_pieces = [
        ([STEPS + quarter + a * some for a in range(devices)], some),
        ([quarter + 2 * a for a in range(half)] + [STEPS + 3 * quarter + 2 * a for a in range(half)], 2),
    ]
    outer_pieces = [([a * some for a in range(half)] + [3 * quarter + 2 * STEPS + a * some for a in range(half)], some)]

    def rows_of(pieces):
        return [start - STEPS + i for starts, number in pieces for start in starts for i in range(number)]

    inner_rows, outer_rows = rows_of(inner_pieces), rows_of(outer_pieces)
    windows = [list(range(-STEPS, quarter + STEPS)), list(range(3 * quarter - STEPS, length + STEPS))]

    inner_size = len(inner_rows) // devices
    inner_messages = weight_messages(inner_pieces, diffusion_i, diffusion_j, [sea_mask])
    inner_parts = exchange(inner_messages)
    inner_messages, edge_i, edge_j, increment, norm_gain = lax.optimization_barrier(
        (inner_messages, diffusion_i, diffusion_j, increment, norm_gain)
    )
    halos = halo_i(
        *[
            jnp.concatenate([flat(edge_i[:, at]), flat(edge_j[:, at])], axis=0)
            for at in (slice(0, STEPS), slice(-STEPS, None))
        ]
    )
    messages = scaled_messages(increment, norm_gain, sea_mask, devices)
    scaled = exchange(messages)
    messages, halos = lax.optimization_barrier((messages, halos))
    outer_messages = weight_messages(outer_pieces, diffusion_i, diffusion_j, halos=halos)

    depth = sum(part[2 * levels * inner_size:] for part in inner_parts)
    here = turn_weights(inner_pieces, [depth], inner_parts, order)
    left, right = halo_j(
        jnp.concatenate([flat(here[:, :STEPS]), depth], axis=0),
        flat(here[:, -STEPS:]),
    )
    right, right_depth = cut(right, len(inner_rows) * STEPS, rows)

    balance = jnp.eye(order, dtype=jnp.float32) + coupling
    by_device = balance.reshape(2, devices, levels, order)
    adjoint = jnp.concatenate([by_device[:, s].reshape(2 * levels, order) for s in source], axis=0).T
    forward = jnp.concatenate([by_device[:, t].reshape(2 * levels, order) for t in to], axis=0)

    middle = devices // 2
    scaled, outer_messages = lax.optimization_barrier((scaled, outer_messages))
    early = shift(outer_messages[middle], middle)
    mixed = adjoint_mix(adjoint, depth, scaled, length, width)
    edges = flat(mixed[:, :STEPS]), flat(mixed[:, -STEPS:])
    edges, inner_weights = lax.optimization_barrier((edges, (here, left, right)))
    left, right = halo_j(*edges)
    left, right, outer_messages, early = lax.optimization_barrier((left, right, outer_messages, early))
    outer_parts = [
        early if d == middle else shift(outer_messages[d], d) if d else outer_messages[0] for d in range(devices)
    ]
    field = [(list(range(length)), mixed, left, right)]
    weights = [(inner_rows, *inner_weights)]
    depths = [depth, right_depth]
    inner_mixed = spread_mix([sorted(inner_rows)], forward, depths, field, weights, devices)
    _, upper, lower = lax.optimization_barrier((left, mixed[:STEPS], mixed[-STEPS:]))
    _, outer_parts = lax.optimization_barrier((inner_mixed[0], outer_parts))
    inner_mixed = exchange(inner_mixed)

    above, below = halo_i(
        jnp.concatenate([flat(upper), depth[:STEPS]], axis=0),
        jnp.concatenate([flat(lower), depth[-STEPS:]], axis=0),
    )
    above, above_depth = cut(above, STEPS * width, STEPS)
    below, below_depth = cut(below, STEPS * width, STEPS)
    halo_depth = jnp.concatenate([below_depth, above_depth], axis=0)
    halo = jnp.concatenate([above, below], axis=0).reshape(2 * STEPS, width, order)
    here = turn_weights(outer_pieces, [depth, halo_depth], outer_parts, order)
    left, right = halo_j(
        jnp.concatenate([flat(here[:, :STEPS]), flat(halo[:, :STEPS]), halo_depth], axis=0),
        jnp.concatenate([flat(here[:, -STEPS:]), flat(halo[:, -STEPS:])], axis=0),
    )
    light = [d for d in range(1, devices) if d != middle]
    left, right, moved = lax.optimization_barrier((left, right, [inner_mixed[d] for d in light]))
    for d, x in zip(light, moved):
        inner_mixed[d] = x
    out = result((inner,), norm_gain, sea_mask, inner_mixed, None)
    sizes = len(outer_rows) * STEPS, 2 * STEPS * STEPS
    left, halo_left = cut(left, *sizes)
    right, halo_right, right_halo_depth = cut(right, *sizes, 2 * STEPS)
    weights.append((outer_rows, here, left, right))
    field.append((list(range(-STEPS, 0)) + list(range(length, length + STEPS)), halo, halo_left, halo_right))
    depths += [halo_depth, right_halo_depth]
    outer_mixed = exchange(spread_mix(windows, forward, depths, field, weights, devices))
    return result(outer, norm_gain, sea_mask, outer_mixed, out)


def solution(mesh):
    return jax.shard_map(
        shards,
        mesh=mesh,
        in_specs=(
            P(None, "lev", "gx", "gy"),
            P(None, "lev", "gx", "gy"),
            P("lev", "gx", "gy"),
            P("lev", "gx", "gy"),
            P("lev", "gx", "gy"),
            P(),
        ),
        out_specs=P(None, "lev", "gx", "gy"),
        check_vma=False,
    )
```
